32 devices in a mesh: blk: 8 (over y, x, core), sub: 4 (over z).
Axes of the slice: x: 2, y: 2, z: 4, core: 2. Of those that a mesh axis runs over, the one named last changes fastest.
Arguments:
- left_emb: float32 [2, 200, 16384], P(None, None, ('blk', 'sub')), may hold values from -1.8 to 1.8
- left_state: float32 [16384], P(('blk', 'sub')), may hold values from 0.003 to 0.1
- right_emb: float32 [2, 200, 16384], P(None, None, ('blk', 'sub')), may hold values from -1.8 to 1.8
- right_state: float32 [16384], P(('blk', 'sub')), may hold values from 0.003 to 0.1
- relation_emb: float32 [2, 200, 1280], replicated, may hold values from -4.2 to 4.2
- relation_state: float32 [1280], replicated, may hold values from 0.003 to 0.1
- hub_emb: float32 [2, 200, 4096], replicated, may hold values from -1.8 to 1.8
- hub_state: float32 [4096], replicated, may hold values from 0.003 to 0.1
- heads: int32 [2, 16384], P(None, ('blk', 'sub')), may hold values from 0 to 511
- relations: int32 [2, 16384], P(None, ('blk', 'sub')), may hold values from 0 to 1279
- tails: int32 [2, 16384], P(None, ('blk', 'sub')), may hold values from 0 to 511
- negatives: int32 [2, 32768], P(None, ('blk', 'sub')), may hold values from 0 to 511
- hub_ids: int32 [2, 8192], P(None, ('blk', 'sub')), may hold values from 0 to 4095
Outputs:
- left_out: float32 [2, 200, 16384], P(None, None, ('blk', 'sub'))
- right_out: float32 [2, 200, 16384], P(None, None, ('blk', 'sub'))
- relation_out: float32 [2, 200, 1280], replicated
- hub_out: float32 [2, 200, 4096], replicated
The draws below stay inside these ranges and needn't reach their ends.
Inputs may be any that keep to these rules, and one draw needn't show every extreme that they name: `heads`: local row indices of the head-side block. `relations`: relation types. `tails`: local row indices of the tail-side block held in that bucket. `negatives`: local row indices of the tail-side block held in that bucket; indices may repeat. `hub_ids`: hub rows; indices may repeat.
All inputs are finite; a program needn't handle non-finite values.
Results may differ from the reference program's by a relative error of at most 0.0001.
Values sent between devices are 32-bit elements; how exact they have to be, the bound alone decides.
No kernel may reach another device: no remote copies, remote signals or barrier semaphores. Data moves between devices by JAX's collectives and lax.ppermute only.
A program may use at most 128 MiB of HBM per device.

```python
import math
import jax
import jax.numpy as jnp
import numpy as np
from jax import lax

CDIM = 200
NREL = 1280
ROWS = 512
EDGES = 512
NEG = 1024
HUB = 4096
HUB_NEG = 256
BUCKETS = 2
ENTITIES = 16384
ALL_EDGES = 16384
ALL_NEG = 32768
ALL_HUB_NEG = 8192
N_BLK = 8
N_SUB = 4


def set_ends(drawn, rng, smallest, high):
    longest = drawn.shape.index(max(drawn.shape))
    spots = []
    for shift in (0, 1):
        where = [jax.random.randint(jax.random.fold_in(rng, axis), (), 0, length) for axis, length in enumerate(drawn.shape)]
        where[longest] = (where[longest] + shift) % drawn.shape[longest]
        spots.append(tuple(where))
    return drawn.at[spots[0]].set(smallest).at[spots[1]].set(high)


def level_of(stream_key, dims, split, low, top_value):
    loudness, own = 1.0, jax.random.fold_in(stream_key, 6)
    for axis_at, parts in split:
        steps = jnp.exp(jax.random.uniform(jax.random.fold_in(own, axis_at), (parts,), jnp.float32, low / len(split), top_value / len(split)))
        loudness = loudness * jnp.repeat(steps, dims[axis_at] // parts).reshape([-1 if axis == axis_at else 1 for axis in range(len(dims))])
    return loudness


def rank_bounds(amount, slope):
    portions = [(1 << 20) // math.isqrt(standing ** slope) + 1 for standing in range(1, amount + 1)]
    deviation = 1 + sum(portions) // (1 << 30)
    return np.cumsum(np.array([max(1, weight // deviation) for weight in portions]))


def ranked_ids(own_key, dims, amount, slope):
    table = rank_bounds(amount, slope)
    lot = jax.random.randint(jax.random.fold_in(own_key, 1), dims, 0, int(table[amount - 1]))
    standing = jnp.searchsorted(jnp.asarray(table, jnp.int32), lot, side="right")
    return jax.random.permutation(jax.random.fold_in(own_key, 2), amount)[standing].astype(jnp.int32)


def normal_values(own_key, extent, deviation, most, pieces=(), dtype=jnp.bfloat16):
    drawn = deviation * jax.random.normal(own_key, extent, jnp.float32)
    if pieces:
        drawn = drawn * level_of(own_key, extent, pieces, -0.22, 0.18)
    return jnp.clip(drawn, -most, most).astype(dtype)


def setup_inputs(seed: int = 0) -> dict:
    keys = jax.random.split(jax.random.key(seed), 14)
    left_emb = normal_values(keys[0], (2, CDIM, ENTITIES), 0.3, 1.8, ((2, 32),), jnp.float32)
    left_state = jnp.clip(jnp.exp(math.log(0.1) - 3.506558 * jax.random.uniform(keys[1], (ENTITIES,), jnp.float32) ** level_of(keys[1], (ENTITIES,), ((0, 32),), -0.2, 0.2)), 0.003, 0.1)
    right_emb = normal_values(keys[2], (2, CDIM, ENTITIES), 0.3, 1.8, ((2, 32),), jnp.float32)
    right_state = jnp.clip(jnp.exp(math.log(0.1) - 3.506558 * jax.random.uniform(keys[3], (ENTITIES,), jnp.float32) ** level_of(keys[3], (ENTITIES,), ((0, 32),), -0.2, 0.2)), 0.003, 0.1)
    relation_emb = normal_values(keys[4], (2, CDIM, NREL), 0.7, 4.2, (), jnp.float32)
    relation_state = jnp.clip(jnp.exp(jax.random.uniform(keys[5], (NREL,), jnp.float32, math.log(0.003), math.log(0.1))), 0.003, 0.1)
    hub_emb = normal_values(keys[6], (2, CDIM, HUB), 0.3, 1.8, (), jnp.float32)
    hub_state = jnp.clip(jnp.exp(jax.random.uniform(keys[7], (HUB,), jnp.float32, math.log(0.003), math.log(0.1))), 0.003, 0.1)
    heads = set_ends(jax.random.randint(keys[8], (BUCKETS, ALL_EDGES), 0, ROWS), jax.random.fold_in(keys[8], 1), 0, ROWS - 1).astype(jnp.int32)
    relations = set_ends(ranked_ids(keys[9], (BUCKETS, ALL_EDGES), NREL, 2), jax.random.fold_in(keys[9], 3), 0, NREL - 1).astype(jnp.int32)
    tails = set_ends(jax.random.randint(keys[10], (BUCKETS, ALL_EDGES), 0, ROWS), jax.random.fold_in(keys[10], 1), 0, ROWS - 1).astype(jnp.int32)
    negatives = set_ends(jax.random.randint(keys[11], (BUCKETS, ALL_NEG), 0, ROWS), jax.random.fold_in(keys[11], 1), 0, ROWS - 1).astype(jnp.int32)
    hub_ids = set_ends(jax.random.randint(keys[12], (BUCKETS, ALL_HUB_NEG), 0, HUB), jax.random.fold_in(keys[12], 1), 0, HUB - 1).astype(jnp.int32)
    return dict(left_emb=left_emb, left_state=left_state, right_emb=right_emb, right_state=right_state, relation_emb=relation_emb, relation_state=relation_state, hub_emb=hub_emb, hub_state=hub_state, heads=heads, relations=relations, tails=tails, negatives=negatives, hub_ids=hub_ids)


step_rate = 0.25
exact = lax.Precision.HIGHEST

def adagrad(table, state, grads):
    new_state = state + lax.optimization_barrier(jnp.mean(grads * grads, axis=(-3, -2)))
    return (table - step_rate * grads / jnp.sqrt(new_state)[..., None, None, :], new_state)

def bucket_grads(left_block, right_block, relation_emb, hub_emb, head_idx, rel_idx, tail_idx, neg_idx, hub_idx):
    head_rows = left_block[:, :, head_idx]
    rel_rows = relation_emb[:, :, rel_idx]
    tail_rows = right_block[:, :, tail_idx]
    neg_rows = right_block[:, :, neg_idx]
    hub_rows = hub_emb[:, :, hub_idx]
    queries = jnp.stack([head_rows[0] * rel_rows[0] - head_rows[1] * rel_rows[1], head_rows[0] * rel_rows[1] + head_rows[1] * rel_rows[0]])
    positive = lax.optimization_barrier(jnp.sum(queries * tail_rows, axis=(0, 1)))
    neg_scores = jnp.einsum('khe,khn->en', queries, neg_rows, precision=exact)
    hub_scores = jnp.einsum('khe,khn->en', queries, hub_rows, precision=exact)
    weight = 1.0 / (neg_idx.shape[0] + hub_idx.shape[0])
    coef_pos = jax.nn.sigmoid(positive) - 1.0
    coef_neg = jax.nn.sigmoid(neg_scores) * weight
    coef_hub = jax.nn.sigmoid(hub_scores) * weight
    grad_query = coef_pos * tail_rows + jnp.einsum('en,khn->khe', coef_neg, neg_rows, precision=exact) + jnp.einsum('en,khn->khe', coef_hub, hub_rows, precision=exact)
    grad_tail = coef_pos * queries
    grad_neg = jnp.einsum('en,khe->khn', coef_neg, queries, precision=exact)
    grad_hub = jnp.einsum('en,khe->khn', coef_hub, queries, precision=exact)
    grad_head = jnp.stack([grad_query[0] * rel_rows[0] + grad_query[1] * rel_rows[1], grad_query[1] * rel_rows[0] - grad_query[0] * rel_rows[1]])
    grad_rel = jnp.stack([grad_query[0] * head_rows[0] + grad_query[1] * head_rows[1], grad_query[1] * head_rows[0] - grad_query[0] * head_rows[1]])
    left_grad = jnp.zeros_like(left_block).at[:, :, head_idx].add(grad_head)
    right_grad = jnp.zeros_like(right_block).at[:, :, tail_idx].add(grad_tail).at[:, :, neg_idx].add(grad_neg)
    rel_grad = jnp.zeros_like(relation_emb).at[:, :, rel_idx].add(grad_rel)
    hub_grad = jnp.zeros_like(hub_emb).at[:, :, hub_idx].add(grad_hub)
    return (left_grad, right_grad, rel_grad, hub_grad)

def reference(left_emb, left_state, right_emb, right_state, relation_emb, relation_state, hub_emb, hub_state, heads, relations, tails, negatives, hub_ids):
    blocks = N_BLK * N_SUB

    def split_table(table):
        return table.reshape(2, CDIM, blocks, ROWS).transpose(2, 0, 1, 3)

    def join_table(table):
        return table.transpose(1, 2, 0, 3).reshape(2, CDIM, blocks * ROWS)
    left_table = split_table(left_emb)
    right_table = split_table(right_emb)
    left_sums = left_state.reshape(blocks, ROWS)
    right_sums = right_state.reshape(blocks, ROWS)
    rel_total = jnp.zeros_like(relation_emb)
    hub_total = jnp.zeros_like(hub_emb)
    per_block = jax.vmap(bucket_grads, in_axes=(0, 0, None, None, 0, 0, 0, 0, 0))
    for bucket in range(BUCKETS):
        left_grad, right_grad, rel_grad, hub_grad = per_block(left_table, right_table, relation_emb, hub_emb, heads[bucket].reshape(blocks, EDGES), relations[bucket].reshape(blocks, EDGES), tails[bucket].reshape(blocks, EDGES), negatives[bucket].reshape(blocks, NEG), hub_ids[bucket].reshape(blocks, HUB_NEG))
        left_table, left_sums = adagrad(left_table, left_sums, left_grad)
        right_table, right_sums = adagrad(right_table, right_sums, right_grad)
        rel_total = rel_total + lax.optimization_barrier(jnp.sum(rel_grad, axis=0))
        hub_total = hub_total + lax.optimization_barrier(jnp.sum(hub_grad, axis=0))
        if bucket < BUCKETS - 1:
            right_table = jnp.roll(right_table.reshape(N_BLK, N_SUB, 2, CDIM, ROWS), 1, axis=0).reshape(blocks, 2, CDIM, ROWS)
            right_sums = jnp.roll(right_sums.reshape(N_BLK, N_SUB, ROWS), 1, axis=0).reshape(blocks, ROWS)
    relation_out, unused_rel = adagrad(relation_emb, relation_state, rel_total)
    hub_out, unused_hub = adagrad(hub_emb, hub_state, hub_total)
    return (join_table(left_table), join_table(right_table), relation_out, hub_out)
```

```python
import functools
import jax
import jax.numpy as jnp
from jax import lax
from jax.experimental import pallas as pl
from jax.experimental.pallas import tpu as pltpu
from jax.sharding import PartitionSpec as P

step_rate = 0.25
F32, BF16 = jnp.float32, jnp.bfloat16
NN = (((1,), (0,)), ((), ()))
NT = (((1,), (1,)), ((), ()))
TN = (((0,), (0,)), ((), ()))
VMEM = pl.BlockSpec(memory_space=pltpu.VMEM)
PARAMS = pltpu.CompilerParams(vmem_limit_bytes=48 * 1024 * 1024)


def split(x):
    hi = x.astype(BF16)
    return hi, (x - hi.astype(F32)).astype(BF16)


def dot(a, b, dims):
    return lax.dot_general(a, b, dims, preferred_element_type=F32)


def dot3(a, b, dims):
    return dot(a[0], b[0], dims) + (dot(a[0], b[1], dims) + dot(a[1], b[0], dims))


def dot2(a, onehot, dims):
    return dot(a[0], onehot, dims) + dot(a[1], onehot, dims)


def onehot(first, rows, idx):
    place = lax.broadcasted_iota(jnp.int32, (rows, idx.shape[1]), 0) + first
    return jnp.where(place == idx, 1.0, 0.0).astype(BF16)


def gather_kernel(tile, idx_ref, table_ref, out_ref):
    step = pl.program_id(0)
    part = dot2(split(table_ref[...]), onehot(step * tile, tile, idx_ref[...]), NN)

    @pl.when(step == 0)
    def _():
        out_ref[...] = part

    @pl.when(step > 0)
    def _():
        out_ref[...] += part


def gather_columns(table, idx, steps):
    features, rows = table.shape
    count = idx.shape[1]
    tile = rows // steps
    return pl.pallas_call(
        functools.partial(gather_kernel, tile),
        grid=(steps,),
        in_specs=[
            pl.BlockSpec((1, count), lambda k: (0, 0)),
            pl.BlockSpec((features, tile), lambda k: (0, k)),
        ],
        out_specs=pl.BlockSpec((features, count), lambda k: (0, 0)),
        out_shape=jax.ShapeDtypeStruct((features, count), F32),
        compiler_params=PARAMS,
        cost_estimate=pl.CostEstimate(
            flops=4 * features * rows * count, bytes_accessed=4 * features * rows, transcendentals=0
        ),
    )(idx, table)


def scatter_kernel(tile, idx_ref, grads_ref, out_ref):
    step = pl.program_id(0)
    out_ref[...] = dot2(split(grads_ref[...]), onehot(step * tile, tile, idx_ref[...]), NT)


def scatter_columns(grads, idx, rows, steps):
    features, count = grads.shape
    tile = rows // steps
    return pl.pallas_call(
        functools.partial(scatter_kernel, tile),
        grid=(steps,),
        in_specs=[
            pl.BlockSpec((1, count), lambda k: (0, 0)),
            pl.BlockSpec((features, count), lambda k: (0, 0)),
        ],
        out_specs=pl.BlockSpec((features, tile), lambda k: (0, k)),
        out_shape=jax.ShapeDtypeStruct((features, rows), F32),
        compiler_params=PARAMS,
        cost_estimate=pl.CostEstimate(
            flops=4 * features * rows * count, bytes_accessed=4 * features * rows, transcendentals=0
        ),
    )(idx, grads)


def adagrad(table, state, grads):
    new_state = state + jnp.sum(grads * grads, axis=0, keepdims=True) * (1.0 / grads.shape[0])
    return table - grads * (step_rate / jnp.sqrt(new_state)), new_state


def bucket_kernel(
    heads_ref, tails_ref, negs_ref, left_ref, left_sums_ref, right_ref, right_sums_ref, rel_ref, hub_ref,
    left_out, left_sums_out, right_out, right_sums_out, rel_out, hub_out,
    left_hi, left_lo, both_hi, both_lo, left_grad, both_grad,
):
    features, rows = left_ref.shape
    half = features // 2
    edges = heads_ref.shape[1]
    hubs = hub_ref.shape[1]
    weight = 1.0 / (negs_ref.shape[1] + hubs)
    place = lax.broadcasted_iota(jnp.int32, (rows, negs_ref.shape[1]), 0)
    counts = jnp.sum(jnp.where(place == negs_ref[...], weight, 0.0), axis=1, keepdims=True)
    left_hi[...], left_lo[...] = split(left_ref[...])
    both_hi[:, :rows], both_lo[:, :rows] = split(right_ref[...])
    both_hi[:, rows:], both_lo[:, rows:] = split(hub_ref[...])
    left_grad[...] = jnp.zeros_like(left_grad)
    both_grad[...] = jnp.zeros_like(both_grad)
    tile = 256

    @pl.loop(0, edges // tile)
    def _(step):
        span = pl.ds(pl.multiple_of(step * tile, tile), tile)
        head_hot = onehot(0, rows, heads_ref[:, span])
        tail_here = lax.broadcasted_iota(jnp.int32, (rows, tile), 0) == tails_ref[:, span]
        h = dot2((left_hi[...], left_lo[...]), head_hot, NN)
        h0, h1 = h[:half], h[half:]
        r0, r1 = rel_ref[:half, span], rel_ref[half:, span]
        q = split(jnp.concatenate([h0 * r0 - h1 * r1, h0 * r1 + h1 * r0], axis=0))
        both = (both_hi[...], both_lo[...])
        scores = dot3(both, q, TN)
        chance = jax.nn.sigmoid(scores[:rows])
        coef = jnp.concatenate(
            [
                counts * chance + jnp.where(tail_here, chance - 1.0, 0.0),
                weight * jax.nn.sigmoid(scores[rows:]),
            ],
            axis=0,
        )
        coef = split(coef)
        dq = dot3(both, coef, NN)
        both_grad[...] += dot3(q, coef, NT)
        d0, d1 = dq[:half], dq[half:]
        dh = jnp.concatenate([d0 * r0 + d1 * r1, d1 * r0 - d0 * r1], axis=0)
        left_grad[...] += dot2(split(dh), head_hot, NT)
        rel_out[:half, span] = d0 * h0 + d1 * h1
        rel_out[half:, span] = d1 * h0 - d0 * h1

    left_out[...], left_sums_out[...] = adagrad(left_ref[...], left_sums_ref[...], left_grad[...])
    right_out[...], right_sums_out[...] = adagrad(right_ref[...], right_sums_ref[...], both_grad[:, :rows])
    hub_out[...] = both_grad[:, rows:]


def bucket_step(heads, tails, negs, left, left_sums, right, right_sums, rel_rows, hub_rows):
    features, rows = left.shape
    edges, hubs = heads.shape[1], hub_rows.shape[1]
    width = rows + hubs
    like = lambda x: jax.ShapeDtypeStruct(x.shape, x.dtype)
    return pl.pallas_call(
        bucket_kernel,
        in_specs=[VMEM] * 9,
        out_specs=[VMEM] * 6,
        out_shape=[like(left), like(left_sums), like(right), like(right_sums), like(rel_rows), like(hub_rows)],
        scratch_shapes=[
            pltpu.VMEM((features, rows), BF16),
            pltpu.VMEM((features, rows), BF16),
            pltpu.VMEM((features, width), BF16),
            pltpu.VMEM((features, width), BF16),
            pltpu.VMEM((features, rows), F32),
            pltpu.VMEM((features, width), F32),
        ],
        compiler_params=PARAMS,
        cost_estimate=pl.CostEstimate(
            flops=18 * features * edges * width, bytes_accessed=24 * features * rows, transcendentals=edges * width
        ),
    )(heads, tails, negs, left, left_sums, right, right_sums, rel_rows, hub_rows)


def from_behind(x, axis, by):
    size = lax.axis_size(axis)
    return lax.ppermute(x, axis, [(i, (i + by) % size) for i in range(size)])


def shards(
    left_emb, left_state, right_emb, right_state, relation_emb, relation_state, hub_emb, hub_state,
    heads, relations, tails, negatives, hub_ids,
):
    components, half_width, row_count = left_emb.shape
    features = components * half_width
    left = left_emb.reshape(features, row_count)
    right = right_emb.reshape(features, row_count)
    rel_table = relation_emb.reshape(features, relation_emb.shape[2])
    hub_table = hub_emb.reshape(features, hub_emb.shape[2])
    left_sums = left_state.reshape(1, row_count)
    right_sums = right_state.reshape(1, row_count)
    buckets, edges = heads.shape
    hubs = hub_ids.shape[1]
    all_rel = relations.reshape(1, buckets * edges)
    all_hub = hub_ids.reshape(1, buckets * hubs)
    rel_rows = gather_columns(rel_table, all_rel, 1)
    hub_rows = gather_columns(hub_table, all_hub, 4)
    rel_parts, hub_parts = [], []
    for b in range(buckets):
        left, left_sums, right, right_sums, rel_part, hub_part = bucket_step(
            heads[b : b + 1], tails[b : b + 1], negatives[b : b + 1],
            left, left_sums, right, right_sums,
            rel_rows[:, b * edges : (b + 1) * edges], hub_rows[:, b * hubs : (b + 1) * hubs],
        )
        rel_parts.append(rel_part)
        hub_parts.append(hub_part)
        if b < buckets - 1:
            right, right_sums = from_behind((right, right_sums), "blk", 1)
    rel_total = scatter_columns(jnp.concatenate(rel_parts, axis=1), all_rel, rel_table.shape[1], 1)
    hub_total = scatter_columns(jnp.concatenate(hub_parts, axis=1), all_hub, hub_table.shape[1], 4)
    rel_total, hub_total = lax.psum((rel_total, hub_total), ("blk", "sub"))
    rel_new, unused_rel = adagrad(rel_table, relation_state[None], rel_total)
    hub_new, unused_hub = adagrad(hub_table, hub_state[None], hub_total)
    return (
        left.reshape(components, half_width, row_count),
        right.reshape(components, half_width, row_count),
        rel_new.reshape(relation_emb.shape),
        hub_new.reshape(hub_emb.shape),
    )


def solution(mesh):
    both = ("blk", "sub")
    block, table, whole = P(None, None, both), P(None, both), P()
    return jax.shard_map(
        shards,
        mesh=mesh,
        in_specs=(block, P(both), block, P(both), whole, whole, whole, whole, table, table, table, table, table),
        out_specs=(block, block, whole, whole),
        check_vma=False,
    )
```

```python
import functools
import jax
import jax.numpy as jnp
from jax import lax
from jax.experimental import pallas as pl
from jax.experimental.pallas import tpu as pltpu
from jax.sharding import PartitionSpec as P

step_rate = 0.25
F32, BF16 = jnp.float32, jnp.bfloat16
NN = (((1,), (0,)), ((), ()))
NT = (((1,), (1,)), ((), ()))
TN = (((0,), (0,)), ((), ()))
VMEM = pl.BlockSpec(memory_space=pltpu.VMEM)
PARAMS = pltpu.CompilerParams(vmem_limit_bytes=48 * 1024 * 1024)


def split(x):
    hi = x.astype(BF16)
    return hi, (x - hi.astype(F32)).astype(BF16)


def dot(a, b, dims):
    return lax.dot_general(a, b, dims, preferred_element_type=F32)


def dot3(a, b, dims):
    return dot(a[0], b[0], dims) + (dot(a[0], b[1], dims) + dot(a[1], b[0], dims))


def dot2(a, onehot, dims):
    return dot(a[0], onehot, dims) + dot(a[1], onehot, dims)


def onehot(first, rows, idx):
    place = lax.broadcasted_iota(jnp.int32, (rows, idx.shape[1]), 0) + first
    return jnp.where(place == idx, 1.0, 0.0).astype(BF16)


def gather_kernel(tile, idx_ref, table_ref, out_ref):
    step = pl.program_id(0)
    part = dot2(split(table_ref[...]), onehot(step * tile, tile, idx_ref[...]), NN)

    @pl.when(step == 0)
    def _():
        out_ref[...] = part

    @pl.when(step > 0)
    def _():
        out_ref[...] += part


def gather_columns(table, idx, steps):
    features, rows = table.shape
    count = idx.shape[1]
    tile = rows // steps
    return pl.pallas_call(
        functools.partial(gather_kernel, tile),
        grid=(steps,),
        in_specs=[
            pl.BlockSpec((1, count), lambda k: (0, 0)),
            pl.BlockSpec((features, tile), lambda k: (0, k)),
        ],
        out_specs=pl.BlockSpec((features, count), lambda k: (0, 0)),
        out_shape=jax.ShapeDtypeStruct((features, count), F32),
        compiler_params=PARAMS,
        cost_estimate=pl.CostEstimate(
            flops=4 * features * rows * count, bytes_accessed=4 * features * rows, transcendentals=0
        ),
    )(idx, table)


def spread_bits(place, order):
    bits = len(order)
    return sum((((place >> p) & 1) << (bits - 1 - i)) for i, p in enumerate(order))


def put_chunk(index, value, send_ref, keep_ref):
    half = keep_ref.shape[0]
    spot = index & (half - 1)

    @pl.when(index >= half)
    def _():
        send_ref[spot] = value

    @pl.when(index < half)
    def _():
        keep_ref[spot] = value


def load_columns(idx_refs, grad_refs, idx_all, hi_all, lo_all):
    at = 0
    for ref in idx_refs:
        idx_all[:, at : at + ref.shape[1]] = ref[...]
        at += ref.shape[1]
    at = 0
    for ref in grad_refs:
        width = ref.shape[1]
        hi_all[:, at : at + width], lo_all[:, at : at + width] = split(ref[...])
        at += width


def hub_chunks_kernel(orders, spans, grads, chip_ref, *refs):
    idx_refs, grad_refs, refs = refs[:2], refs[2 : 2 + grads], refs[2 + grads :]
    streams = len(orders)
    sends, keeps = refs[:streams], refs[streams : 2 * streams]
    idx_all, hi_all, lo_all = refs[2 * streams :]
    load_columns(idx_refs, grad_refs, idx_all, hi_all, lo_all)
    chunks, width = 2 * keeps[0].shape[0], keeps[0].shape[2]

    @pl.loop(0, chunks)
    def _(place):
        hot = onehot((chip_ref[0] ^ place) * width, width, idx_all[...])
        chunk = dot2((hi_all[...], lo_all[...]), hot, NT)
        for order, (low, high), send_ref, keep_ref in zip(orders, spans, sends, keeps):
            put_chunk(spread_bits(place, order), chunk[low:high], send_ref, keep_ref)


def rel_chunks_kernel(orders, spans, grads, chip_ref, *refs):
    idx_refs, grad_refs, refs = refs[:2], refs[2 : 2 + grads], refs[2 + grads :]
    streams = len(orders)
    sends, keeps = refs[:streams], refs[streams : 2 * streams]
    idx_all, hi_all, lo_all, dense = refs[2 * streams :]
    load_columns(idx_refs, grad_refs, idx_all, hi_all, lo_all)
    chunks, width = 2 * keeps[0].shape[0], keeps[0].shape[2]
    tile = 256

    @pl.loop(0, dense.shape[1] // tile)
    def _(step):
        hot = onehot(step * tile, tile, idx_all[...])
        dense[:, pl.ds(pl.multiple_of(step * tile, tile), tile)] = dot2((hi_all[...], lo_all[...]), hot, NT)

    for chunk in range(chunks):
        place = chip_ref[0] ^ chunk
        for order, (low, high), send_ref, keep_ref in zip(orders, spans, sends, keeps):
            value = dense[low:high, chunk * width : (chunk + 1) * width]
            put_chunk(spread_bits(place, order), value, send_ref, keep_ref)


SMEM = pl.BlockSpec(memory_space=pltpu.SMEM)


def chunk_columns(kernel, rows, chip, idx, grads, orders, spans):
    chunks = 1 << len(orders[0])
    width = rows // chunks
    half_width = grads[0].shape[0]
    count = sum(g.shape[1] for g in grads)
    shapes = [jax.ShapeDtypeStruct((chunks // 2, high - low, width), F32) for low, high in spans] * 2
    dense = [pltpu.VMEM((half_width, rows), F32)] if kernel is rel_chunks_kernel else []
    out = pl.pallas_call(
        functools.partial(kernel, orders, spans, len(grads)),
        in_specs=[SMEM] + [VMEM] * (2 + len(grads)),
        out_specs=[VMEM] * len(shapes),
        out_shape=shapes,
        scratch_shapes=[
            pltpu.VMEM((1, count), jnp.int32),
            pltpu.VMEM((half_width, count), BF16),
            pltpu.VMEM((half_width, count), BF16),
        ]
        + dense,
        compiler_params=PARAMS,
        cost_estimate=pl.CostEstimate(
            flops=4 * half_width * rows * count, bytes_accessed=4 * half_width * rows, transcendentals=0
        ),
    )(chip, *idx, *grads)
    return out[: len(spans)], out[len(spans) :]


def place_kernel(orders, spans, spot_ref, *refs):
    streams = len(orders)
    lows, highs = refs[:streams], refs[streams : 2 * streams]
    hub_ref, rel_ref = refs[-2:]
    half = lows[0].shape[0]
    hub_width, rel_width = hub_ref.shape[2] // (2 * half), rel_ref.shape[2] // (2 * half)
    for chunk in range(2 * half):
        place = spot_ref[0] ^ chunk
        for order, (low, high), near, far in zip(orders, spans, lows, highs):
            index = spread_bits(place, order)
            spot = index & (half - 1)
            value = jnp.where(index >= half, far[spot], near[spot])
            hub_ref[0, low:high, chunk * hub_width : (chunk + 1) * hub_width] = value[:, :hub_width]
            rel_ref[0, low:high, chunk * rel_width : (chunk + 1) * rel_width] = value[:, hub_width:]


def place_chunks(spot, near, far, orders, spans, hub_shape, rel_shape, earlier):
    whole = [pl.BlockSpec(memory_space=pltpu.VMEM)] * (2 * len(spans))
    kept = [pl.BlockSpec(memory_space=pl.ANY)] * len(earlier)
    mine = lambda shape: pl.BlockSpec((1,) + shape[1:], lambda i, spot: (spot[1], 0, 0))
    return pl.pallas_call(
        functools.partial(place_kernel, orders, spans),
        grid_spec=pltpu.PrefetchScalarGridSpec(
            num_scalar_prefetch=1,
            grid=(1,),
            in_specs=whole + kept,
            out_specs=[mine(hub_shape), mine(rel_shape)],
        ),
        out_shape=[jax.ShapeDtypeStruct(hub_shape, F32), jax.ShapeDtypeStruct(rel_shape, F32)],
        input_output_aliases={1 + len(whole) + i: i for i in range(len(earlier))},
        compiler_params=PARAMS,
        cost_estimate=pl.CostEstimate(flops=0, bytes_accessed=2 * 4 * (hub_shape[1] * (hub_shape[2] + rel_shape[2])), transcendentals=0),
    )(spot, *near, *far, *earlier)


def adagrad(table, state, grads):
    new_state = state + jnp.sum(grads * grads, axis=0, keepdims=True) * (1.0 / grads.shape[0])
    return table - grads * (step_rate / jnp.sqrt(new_state)), new_state


def keep_and_send(core, first, second):
    return jnp.where(core == 0, first, second), jnp.where(core == 0, second, first)


def table_counts(rows, negs, weight):
    place = lax.broadcasted_iota(jnp.int32, (rows, negs.shape[1]), 0)
    return jnp.sum(jnp.where(place == negs, weight, 0.0), axis=1, keepdims=True)


def turned(x, r, half):
    x0, x1, r0, r1 = x[:half], x[half:], r[:half], r[half:]
    return jnp.concatenate([x0 * r0 - x1 * r1, x0 * r1 + x1 * r0], axis=0)


def turned_back(x, r, half):
    x0, x1, r0, r1 = x[:half], x[half:], r[:half], r[half:]
    return x0 * r0 + x1 * r1, x1 * r0 - x0 * r1


EDGE_TILE = 256


def bucket_kernel(
    core_ref, heads_ref, tails_ref, negs_ref, left_ref, left_sums_ref, right_ref, right_sums_ref, rel_ref, hub_ref,
    left_out, left_sums_out, right_out, right_sums_out, rel_keep, rel_send, hub_keep, hub_send,
    left_hi, left_lo, both_hi, both_lo, left_grad, both_grad,
):
    features, rows = left_ref.shape
    half = features // 2
    core = core_ref[0]
    weight = 1.0 / (negs_ref.shape[1] + hub_ref.shape[1])
    counts = table_counts(rows, negs_ref[...], weight)
    left_hi[...], left_lo[...] = split(left_ref[...])
    both_hi[:, :rows], both_lo[:, :rows] = split(right_ref[...])
    both_hi[:, rows:], both_lo[:, rows:] = split(hub_ref[...])
    left_grad[...] = jnp.zeros_like(left_grad)
    both_grad[...] = jnp.zeros_like(both_grad)
    tile = EDGE_TILE

    @pl.loop(0, heads_ref.shape[1] // tile)
    def _(step):
        span = pl.ds(pl.multiple_of(step * tile, tile), tile)
        head_hot = onehot(0, rows, heads_ref[:, span])
        tail_here = lax.broadcasted_iota(jnp.int32, (rows, tile), 0) == tails_ref[:, span]
        h = dot2((left_hi[...], left_lo[...]), head_hot, NN)
        r = rel_ref[:, span]
        q = split(turned(h, r, half))
        both = (both_hi[...], both_lo[...])
        scores = dot3(both, q, TN)
        chance = jax.nn.sigmoid(scores[:rows])
        coef = jnp.concatenate(
            [
                counts * chance + jnp.where(tail_here, chance - 1.0, 0.0),
                weight * jax.nn.sigmoid(scores[rows:]),
            ],
            axis=0,
        )
        coef = split(coef)
        dq = dot3(both, coef, NN)
        both_grad[...] += dot3(q, coef, NT)
        dh = jnp.concatenate(turned_back(dq, r, half), axis=0)
        left_grad[...] += dot2(split(dh), head_hot, NT)
        rel_keep[:, span], rel_send[:, span] = keep_and_send(core, *turned_back(dq, h, half))

    left_out[...], left_sums_out[...] = adagrad(left_ref[...], left_sums_ref[...], left_grad[...])
    right_out[...], right_sums_out[...] = adagrad(right_ref[...], right_sums_ref[...], both_grad[:, :rows])
    hub_keep[...], hub_send[...] = keep_and_send(core, both_grad[:half, rows:], both_grad[half:, rows:])


def like(x, rows=None):
    return jax.ShapeDtypeStruct((rows or x.shape[0], x.shape[1]), x.dtype)


def bucket_step(core, heads, tails, negs, left, left_sums, right, right_sums, rel_rows, hub_rows):
    features, rows = left.shape
    half = features // 2
    edges, hubs = heads.shape[1], hub_rows.shape[1]
    width = rows + hubs
    return pl.pallas_call(
        bucket_kernel,
        in_specs=[SMEM] + [VMEM] * 9,
        out_specs=[VMEM] * 8,
        out_shape=[like(left), like(left_sums), like(right), like(right_sums)]
        + [like(rel_rows, half)] * 2
        + [like(hub_rows, half)] * 2,
        scratch_shapes=[
            pltpu.VMEM((features, rows), BF16),
            pltpu.VMEM((features, rows), BF16),
            pltpu.VMEM((features, width), BF16),
            pltpu.VMEM((features, width), BF16),
            pltpu.VMEM((features, rows), F32),
            pltpu.VMEM((features, width), F32),
        ],
        compiler_params=PARAMS,
        cost_estimate=pl.CostEstimate(
            flops=18 * features * edges * width, bytes_accessed=24 * features * rows, transcendentals=edges * width
        ),
    )(core, heads, tails, negs, left, left_sums, right, right_sums, rel_rows, hub_rows)


def hub_kernel(
    negatives, core_ref, heads_ref, left_ref, rel_ref, hub_ref,
    head_out, query_grad, hub_keep, hub_send,
    left_hi, left_lo, hub_hi, hub_lo, hub_grad,
):
    features, rows = left_ref.shape
    half = features // 2
    weight = 1.0 / (negatives + hub_ref.shape[1])
    left_hi[...], left_lo[...] = split(left_ref[...])
    hub_hi[...], hub_lo[...] = split(hub_ref[...])
    hub_grad[...] = jnp.zeros_like(hub_grad)
    tile = EDGE_TILE

    @pl.loop(0, heads_ref.shape[1] // tile)
    def _(step):
        span = pl.ds(pl.multiple_of(step * tile, tile), tile)
        h = dot2((left_hi[...], left_lo[...]), onehot(0, rows, heads_ref[:, span]), NN)
        head_out[:, span] = h
        q = split(turned(h, rel_ref[:, span], half))
        hub = (hub_hi[...], hub_lo[...])
        coef = split(weight * jax.nn.sigmoid(dot3(hub, q, TN)))
        query_grad[:, span] = dot3(hub, coef, NN)
        hub_grad[...] += dot3(q, coef, NT)

    hub_keep[...], hub_send[...] = keep_and_send(core_ref[0], hub_grad[:half], hub_grad[half:])


def hub_step(core, heads, left, rel_rows, hub_rows, negatives):
    features, rows = left.shape
    edges, hubs = heads.shape[1], hub_rows.shape[1]
    return pl.pallas_call(
        functools.partial(hub_kernel, negatives),
        in_specs=[SMEM] + [VMEM] * 4,
        out_specs=[VMEM] * 4,
        out_shape=[like(rel_rows), like(rel_rows)] + [like(hub_rows, features // 2)] * 2,
        scratch_shapes=[
            pltpu.VMEM((features, rows), BF16),
            pltpu.VMEM((features, rows), BF16),
            pltpu.VMEM((features, hubs), BF16),
            pltpu.VMEM((features, hubs), BF16),
            pltpu.VMEM((features, hubs), F32),
        ],
        compiler_params=PARAMS,
        cost_estimate=pl.CostEstimate(
            flops=18 * features * edges * hubs + 4 * features * edges * rows,
            bytes_accessed=24 * features * rows,
            transcendentals=edges * hubs,
        ),
    )(core, heads, left, rel_rows, hub_rows)


def tables_kernel(
    hubs, core_ref, heads_ref, tails_ref, negs_ref, head_rows, query_grad,
    left_ref, left_sums_ref, right_ref, right_sums_ref, rel_ref,
    left_out, right_out, rel_keep, rel_send,
    right_hi, right_lo, left_grad, right_grad,
):
    features, rows = left_ref.shape
    half = features // 2
    core = core_ref[0]
    counts = table_counts(rows, negs_ref[...], 1.0 / (negs_ref.shape[1] + hubs))
    right_hi[...], right_lo[...] = split(right_ref[...])
    left_grad[...] = jnp.zeros_like(left_grad)
    right_grad[...] = jnp.zeros_like(right_grad)
    tile = EDGE_TILE

    @pl.loop(0, heads_ref.shape[1] // tile)
    def _(step):
        span = pl.ds(pl.multiple_of(step * tile, tile), tile)
        head_hot = onehot(0, rows, heads_ref[:, span])
        tail_here = lax.broadcasted_iota(jnp.int32, (rows, tile), 0) == tails_ref[:, span]
        h, r = head_rows[:, span], rel_ref[:, span]
        q = split(turned(h, r, half))
        right = (right_hi[...], right_lo[...])
        chance = jax.nn.sigmoid(dot3(right, q, TN))
        coef = split(counts * chance + jnp.where(tail_here, chance - 1.0, 0.0))
        dq = dot3(right, coef, NN) + query_grad[:, span]
        right_grad[...] += dot3(q, coef, NT)
        rel_keep[:, span], rel_send[:, span] = keep_and_send(core, *turned_back(dq, h, half))
        dh = jnp.concatenate(turned_back(dq, r, half), axis=0)
        left_grad[...] += dot2(split(dh), head_hot, NT)

    left_out[...], unused = adagrad(left_ref[...], left_sums_ref[...], left_grad[...])
    right_out[...], unused = adagrad(right_ref[...], right_sums_ref[...], right_grad[...])


def tables_step(hubs, core, heads, tails, negs, head_rows, query_grad, left, left_sums, right, right_sums, rel_rows):
    features, rows = left.shape
    edges = heads.shape[1]
    return pl.pallas_call(
        functools.partial(tables_kernel, hubs),
        in_specs=[SMEM] + [VMEM] * 10,
        out_specs=[VMEM] * 4,
        out_shape=[like(left), like(right)] + [like(rel_rows, features // 2)] * 2,
        scratch_shapes=[
            pltpu.VMEM((features, rows), BF16),
            pltpu.VMEM((features, rows), BF16),
            pltpu.VMEM((features, rows), F32),
            pltpu.VMEM((features, rows), F32),
        ],
        compiler_params=PARAMS,
        cost_estimate=pl.CostEstimate(
            flops=22 * features * edges * rows, bytes_accessed=24 * features * rows, transcendentals=edges * rows
        ),
    )(core, heads, tails, negs, head_rows, query_grad, left, left_sums, right, right_sums, rel_rows)


def from_behind(x, axis, by):
    size = lax.axis_size(axis)
    return lax.ppermute(x, axis, [(i, (i + by) % size) for i in range(size)])


def flipped(x, axis, bit):
    return lax.ppermute(x, axis, [(i, i ^ (1 << bit)) for i in range(lax.axis_size(axis))])


def other_core(x):
    return flipped(x, "blk", 0)


def across(x, place):
    sub_bits = lax.axis_size("sub").bit_length() - 1
    if place < sub_bits:
        return flipped(x, "sub", place)
    return flipped(x, "blk", place - sub_bits + 1)


def stream_orders():
    sub_bits = lax.axis_size("sub").bit_length() - 1
    bits = sub_bits + lax.axis_size("blk").bit_length() - 2
    x, y, z, far = sub_bits, sub_bits + 1, 0, 1
    rest = [p for p in range(bits) if p not in (x, y, z, far)]
    return [[x, y, z, far] + rest, [y, z, x, far] + rest, [z, x, far, y] + rest]


def row_spans(rows, parts):
    ends = [-(-rows * (i + 1) // (8 * parts)) * 8 for i in range(parts - 1)] + [rows]
    return list(zip([0] + ends[:-1], ends))


def shards(
    left_emb, left_state, right_emb, right_state, relation_emb, relation_state, hub_emb, hub_state,
    heads, relations, tails, negatives, hub_ids,
):
    components, half_width, row_count = left_emb.shape
    features = components * half_width
    rel_count, hub_count = relation_emb.shape[2], hub_emb.shape[2]
    left = left_emb.reshape(features, row_count)
    right = right_emb.reshape(features, row_count)
    rel_table = relation_emb.reshape(features, rel_count)
    hub_table = hub_emb.reshape(features, hub_count)
    left_sums = left_state.reshape(1, row_count)
    right_sums = right_state.reshape(1, row_count)
    buckets, edges = heads.shape
    hubs = hub_ids.shape[1]

    core_id = lax.axis_index("blk") % 2
    chip_id = (lax.axis_index("blk") // 2) * lax.axis_size("sub") + lax.axis_index("sub")
    core, chip = core_id.astype(jnp.int32).reshape(1), chip_id.astype(jnp.int32).reshape(1)
    orders = stream_orders()
    spans = row_spans(half_width, len(orders))
    chunks = 1 << len(orders[0])
    hub_width, rel_width = hub_count // chunks, rel_count // chunks

    all_rel = relations.reshape(1, buckets * edges)
    all_hub = hub_ids.reshape(1, buckets * hubs)
    far_rel, far_hub = other_core((all_rel, all_hub))
    rel_rows = gather_columns(rel_table, all_rel, 1)
    hub_rows = [gather_columns(hub_table, hub_ids[b : b + 1], 4) for b in range(buckets)]
    rel_keep, rel_far, hub_keep, hub_far = [], [], [], []
    for b in range(buckets):
        rows_b = rel_rows[:, b * edges : (b + 1) * edges]
        at = slice(b, b + 1)
        if b < buckets - 1:
            left, left_sums, right, right_sums, rk, rs, hk, hs = bucket_step(
                core, heads[at], tails[at], negatives[at], left, left_sums, right, right_sums, rows_b, hub_rows[b]
            )
            right, right_sums = from_behind((right, right_sums), "blk", 1)
            hub_far.append(other_core(hs))
            rel_far.append(other_core(rs))
            hub_keep.append(hk)
            rel_keep.append(rk)
        else:
            head_rows, query_grad, hk, hs = hub_step(core, heads[at], left, rows_b, hub_rows[b], negatives.shape[1])
            hub_far.append(other_core(hs))
            hub_keep.append(hk)
            hub_send, hub_own = chunk_columns(
                hub_chunks_kernel, hub_count, chip, (all_hub, far_hub), hub_keep + hub_far, orders, spans
            )
            hub_got = [across(x, order[0]) for x, order in zip(hub_send, orders)]
            left, right, rk, rs = tables_step(
                hubs, core, heads[at], tails[at], negatives[at], head_rows, query_grad,
                left, left_sums, right, right_sums, rows_b,
            )
            rel_far.append(other_core(rs))
            rel_keep.append(rk)
    rel_send, rel_own = chunk_columns(
        rel_chunks_kernel, rel_count, chip, (all_rel, far_rel), rel_keep + rel_far, orders, spans
    )
    rel_got = [across(x, order[0]) for x, order in zip(rel_send, orders)]

    totals = []
    for s, order in enumerate(orders):
        half = chunks // 4

        def joined(part):
            return jnp.concatenate(
                [hub_own[s][part] + hub_got[s][part], rel_own[s][part] + rel_got[s][part]], axis=2
            )

        send, own = joined(slice(half, None)), joined(slice(0, half))
        for step, place in enumerate(order[1:]):
            got = across(send, place)
            if half > 1:
                half //= 2
                send, own = own[half:] + got[half:], own[:half] + got[:half]
            else:
                own = own + got
        totals.append(own[0])

    squares = sum(jnp.sum(g * g, axis=0, keepdims=True) for g in totals)
    squares = squares + other_core(squares)
    cut = lambda x, width: lax.dynamic_slice(x, (core_id, 0, chip_id * width), (1, half_width, width))[0]
    cut_sums = lambda x, width: lax.dynamic_slice(x, (chip_id * width,), (width,))
    owned = jnp.concatenate([cut(hub_emb, hub_width), cut(relation_emb, rel_width)], axis=1)
    sums = jnp.concatenate([cut_sums(hub_state, hub_width), cut_sums(relation_state, rel_width)])[None]
    scale = step_rate / jnp.sqrt(sums + squares * (1.0 / features))
    near, far = [], []
    for (low, high), g, order in zip(spans, totals, orders):
        have = (owned[low:high] - g * scale)[None]
        for place in order[:0:-1]:
            have = jnp.concatenate([have, across(have, place)], axis=0)
        near.append(have)
        far.append(across(have, order[0]))
    shapes = (hub_emb.shape, relation_emb.shape)
    out = place_chunks(jnp.concatenate([chip, core]), near, far, orders, spans, *shapes, ())
    out = place_chunks(
        jnp.concatenate([chip, 1 - core]), other_core(near), other_core(far), orders, spans, *shapes, tuple(out)
    )
    return (
        left.reshape(components, half_width, row_count),
        right.reshape(components, half_width, row_count),
        out[1],
        out[0],
    )


def solution(mesh):
    both = ("blk", "sub")
    block, table, whole = P(None, None, both), P(None, both), P()
    return jax.shard_map(
        shards,
        mesh=mesh,
        in_specs=(block, P(both), block, P(both), whole, whole, whole, whole, table, table, table, table, table),
        out_specs=(block, block, whole, whole),
        check_vma=False,
    )
```

```python
import functools
import jax
import jax.numpy as jnp
from jax import lax
from jax.experimental import pallas as pl
from jax.experimental.pallas import tpu as pltpu
from jax.sharding import PartitionSpec as P

step_rate = 0.25
F32, BF16 = jnp.float32, jnp.bfloat16
NN = (((1,), (0,)), ((), ()))
NT = (((1,), (1,)), ((), ()))
TN = (((0,), (0,)), ((), ()))
VMEM = pl.BlockSpec(memory_space=pltpu.VMEM)
SMEM = pl.BlockSpec(memory_space=pltpu.SMEM)
PARAMS = pltpu.CompilerParams(vmem_limit_bytes=24 * 1024 * 1024)
COST = pl.CostEstimate(flops=10000, bytes_accessed=10000, transcendentals=0)


def split(x):
    hi = x.astype(BF16)
    return hi, (x - hi.astype(F32)).astype(BF16)


def dot(a, b, dims):
    return lax.dot_general(a, b, dims, preferred_element_type=F32)


def dot3(a, b, dims):
    return dot(a[0], b[0], dims) + (dot(a[0], b[1], dims) + dot(a[1], b[0], dims))


def dot2(a, onehot, dims):
    return dot(a[0], onehot, dims) + dot(a[1], onehot, dims)


def onehot(first, rows, idx):
    place = lax.broadcasted_iota(jnp.int32, (rows, idx.shape[1]), 0) + first
    return jnp.where(place == idx, 1.0, 0.0).astype(BF16)


def laid_out(idx):
    return jnp.concatenate([idx[b : b + 1] for b in range(idx.shape[0])], axis=1)


def add_part(first, part, out_ref):
    @pl.when(first)
    def _():
        out_ref[...] = part

    @pl.when(jnp.logical_not(first))
    def _():
        out_ref[...] += part


def gather_kernel(hub_steps, hub_idx, rel_idx, hub_ref, rel_ref, hub_out, rel_out):
    step = pl.program_id(0)

    @pl.when(step < hub_steps)
    def _():
        tile = hub_ref.shape[1]
        hot = onehot(step * tile, tile, laid_out(hub_idx[...]))
        add_part(step == 0, dot2(split(hub_ref[...]), hot, NN), hub_out)

    @pl.when(step >= hub_steps)
    def _():
        tile = rel_ref.shape[1]
        hot = onehot((step - hub_steps) * tile, tile, laid_out(rel_idx[...]))
        add_part(step == hub_steps, dot2(split(rel_ref[...]), hot, NN), rel_out)


def gather_rows(hub_table, hub_idx, rel_table, rel_idx):
    features = hub_table.shape[0]
    hub_steps, rel_steps = 4, 2
    fixed = lambda shape: pl.BlockSpec(shape, lambda k: (0, 0))
    shapes = [(features, hub_idx.size), (features, rel_idx.size)]
    return pl.pallas_call(
        functools.partial(gather_kernel, hub_steps),
        grid=(hub_steps + rel_steps,),
        in_specs=[
            fixed(hub_idx.shape),
            fixed(rel_idx.shape),
            pl.BlockSpec((features, hub_table.shape[1] // hub_steps), lambda k: (0, jnp.minimum(k, hub_steps - 1))),
            pl.BlockSpec((features, rel_table.shape[1] // rel_steps), lambda k: (0, jnp.maximum(k - hub_steps, 0))),
        ],
        out_specs=[fixed(shape) for shape in shapes],
        out_shape=[jax.ShapeDtypeStruct(shape, F32) for shape in shapes],
        compiler_params=PARAMS,
        cost_estimate=COST,
    )(hub_idx, rel_idx, hub_table, rel_table)


def spread_bits(place, order):
    bits = len(order)
    return sum((((place >> p) & 1) << (bits - 1 - i)) for i, p in enumerate(order))


def load_columns(idx_refs, grad_refs, idx_down, hi_all, lo_all):
    idx = jnp.concatenate([laid_out(ref[...]) for ref in idx_refs], axis=1)
    idx_down[...] = jnp.transpose(jnp.broadcast_to(idx, (128, idx.shape[1])))
    at = 0
    for ref in grad_refs:
        width = ref.shape[1]
        hi_all[:, at : at + width], lo_all[:, at : at + width] = split(ref[...])
        at += width


def onehot_across(idx_down, targets):
    width = targets.shape[1]
    idx = idx_down[...]
    wide = jnp.concatenate([idx] * -(-width // 128), axis=1)[:, :width]
    return jnp.where(wide == targets, 1.0, 0.0).astype(BF16)


def out_for(place, order, sends, keeps, s):
    index = spread_bits(place, order)
    half = keeps[s].shape[0]
    return sends[s].at[index - half] if index >= half else keeps[s].at[index]


def hub_chunks_kernel(orders, spans, grads, chip_ref, *refs):
    idx_refs, grad_refs, refs = refs[:2], refs[2 : 2 + grads], refs[2 + grads :]
    streams = len(orders)
    sends, keeps = refs[:streams], refs[streams : 2 * streams]
    idx_down, hi_all, lo_all = refs[2 * streams :]
    load_columns(idx_refs, grad_refs, idx_down, hi_all, lo_all)
    chunks, width = 2 * keeps[0].shape[0], keeps[0].shape[2]
    lane = lax.broadcasted_iota(jnp.int32, (1, width), 1)
    for place in range(chunks):
        hot = onehot_across(idx_down, lane + (chip_ref[0] ^ place) * width)
        chunk = dot2((hi_all[...], lo_all[...]), hot, NN)
        for s, (low, high) in enumerate(spans):
            out_for(place, orders[s], sends, keeps, s)[...] = chunk[low:high]


def third_of(spans):
    return -(-max(high - low for low, high in spans) // 24) * 8


def packed_pieces(spans):
    third = third_of(spans)
    for block, (low, high) in enumerate(spans):
        for s in range(len(spans)):
            count = min(third, high - low - third * s)
            if count > 0:
                yield block, s, low + third * s, count


def rel_chunks_kernel(orders, spans, rows, grads, chip_ref, *refs):
    idx_refs, grad_refs, refs = refs[:2], refs[2 : 2 + grads], refs[2 + grads :]
    streams = len(orders)
    sends, keeps = refs[:streams], refs[streams : 2 * streams]
    idx_down, hi_all, lo_all = refs[2 * streams :]
    load_columns(idx_refs, grad_refs, idx_down, hi_all, lo_all)
    for ref in refs[: 2 * streams]:
        ref[...] = jnp.zeros_like(ref)
    chunks, lanes = 2 * keeps[0].shape[0], keeps[0].shape[2]
    width = rows // chunks
    group = lanes // width
    lane = lax.broadcasted_iota(jnp.int32, (1, lanes), 1)
    for first in range(0, chunks, group):
        targets = jnp.full((1, lanes), -1, jnp.int32)
        places = range(first, min(first + group, chunks))
        for slot, place in enumerate(places):
            here = (lane >= slot * width) & (lane < (slot + 1) * width)
            targets = jnp.where(here, lane + ((chip_ref[0] ^ place) * width - slot * width), targets)
        dense = dot2((hi_all[...], lo_all[...]), onehot_across(idx_down, targets), NN)
        for slot, place in enumerate(places):
            chunk = dense[:, slot * width : (slot + 1) * width]
            for block, s, low, count in packed_pieces(spans):
                out = out_for(place, orders[s], sends, keeps, s)
                out[:count, block * width : (block + 1) * width] = chunk[low : low + count]


def chunk_columns(kernel, heights, lanes, chip, idx, grads, chunks):
    half_width = grads[0].shape[0]
    count = sum(g.shape[1] for g in grads)
    shapes = [jax.ShapeDtypeStruct((chunks // 2, height, lanes), F32) for height in heights] * 2
    out = pl.pallas_call(
        kernel,
        in_specs=[SMEM] + [VMEM] * (2 + len(grads)),
        out_specs=[VMEM] * len(shapes),
        out_shape=shapes,
        scratch_shapes=[
            pltpu.VMEM((count, 128), jnp.int32),
            pltpu.VMEM((half_width, count), BF16),
            pltpu.VMEM((half_width, count), BF16),
        ],
        compiler_params=PARAMS,
        cost_estimate=COST,
    )(chip, *idx, *grads)
    return out[: len(heights)], out[len(heights) :]


def call(kernel, ins, shapes):
    return pl.pallas_call(
        kernel,
        in_specs=[VMEM] * len(ins),
        out_specs=[VMEM] * len(shapes),
        out_shape=[jax.ShapeDtypeStruct(shape, F32) for shape in shapes],
        compiler_params=PARAMS,
        cost_estimate=COST,
    )(*ins)


def first_sums_kernel(*refs):
    streams = len(refs) // 6
    hub_own, hub_got, rel_own, rel_got, sends, keeps = [refs[i * streams : (i + 1) * streams] for i in range(6)]
    for s in range(streams):
        half, height = sends[s].shape[0], hub_own[s].shape[1]
        for out, part in ((sends[s], pl.ds(half, half)), (keeps[s], pl.ds(0, half))):
            out[:, :height] = hub_own[s][part] + hub_got[s][part]
            out[:, height:] = rel_own[s][part] + rel_got[s][part]


def sums_kernel(*refs):
    streams = len(refs) // 4
    own, got, sends, keeps = [refs[i * streams : (i + 1) * streams] for i in range(4)]
    for s in range(streams):
        half = sends[s].shape[0]
        sends[s][...] = own[s][half:] + got[s][half:]
        keeps[s][...] = own[s][:half] + got[s][:half]


def halves(kernel, groups, shapes):
    shapes = [(shape[0] // 2,) + shape[1:] for shape in shapes]
    out = call(kernel, [x for group in groups for x in group], shapes * 2)
    return out[: len(shapes)], out[len(shapes) :]


def join_kernel(*refs):
    streams = len(refs) // 3
    for s in range(streams):
        own, got, out = refs[s], refs[streams + s], refs[2 * streams + s]
        count = own.shape[0]
        out[:count] = own[...]
        out[count:] = got[...]


def join(own, got):
    return call(join_kernel, [*own, *got], [(2 * x.shape[0],) + x.shape[1:] for x in own])


def squares_kernel(spans, width, *refs):
    streams = len(spans)
    own, got, totals, out = [refs[i * streams : (i + 1) * streams] for i in range(3)] + [refs[-1]]
    lanes = out.shape[1]
    hub, rel = jnp.zeros((1, lanes), F32), jnp.zeros((1, lanes), F32)
    for s, (low, high) in enumerate(spans):
        total = own[s][0] + got[s][0]
        totals[s][0] = total
        square = total * total
        hub += jnp.sum(square[: high - low], axis=0, keepdims=True)
        rel += jnp.sum(square[high - low :], axis=0, keepdims=True)
    out[...] = jnp.zeros_like(out)
    out[0:1] = hub
    out[1:2, :width] = sum(rel[:, b * width : (b + 1) * width] for b in range(streams))


def update_kernel(spans, width, features, *refs):
    streams = len(spans)
    totals, news = refs[:streams], refs[-streams:]
    mine, other, hub_ref, rel_ref, hub_sums, rel_sums = refs[streams:-streams]
    means = (mine[...] + other[...]) * (1.0 / features)
    hub_scale = step_rate / jnp.sqrt(hub_sums[...] + means[0:1])
    rel_scale = step_rate / jnp.sqrt(rel_sums[...] + means[1:2, :width])
    for s, (low, high) in enumerate(spans):
        height = high - low
        news[s][0, :height] = hub_ref[low:high] - totals[s][0, :height] * hub_scale
        news[s][0, height:] = jnp.zeros_like(news[s][0, height:])
    for block, s, low, count in packed_pieces(spans):
        at = spans[s][1] - spans[s][0]
        lanes = slice(block * width, (block + 1) * width)
        news[s][0, at : at + count, lanes] = (
            rel_ref[low : low + count] - totals[s][0, at : at + count, lanes] * rel_scale
        )


def place_kernel(orders, spans, spot_ref, *refs):
    streams = len(orders)
    lows, highs = refs[:streams], refs[streams : 2 * streams]
    hub_ref, rel_ref = refs[-2:]
    half = lows[0].shape[0]
    width, rel_width = hub_ref.shape[2] // (2 * half), rel_ref.shape[2] // (2 * half)
    pieces = list(packed_pieces(spans))
    for chunk in range(2 * half):
        place = spot_ref[0] ^ chunk
        for s, (low, high) in enumerate(spans):
            index = spread_bits(place, orders[s])
            spot = index & (half - 1)
            value = jnp.where(index >= half, highs[s][spot], lows[s][spot])
            height = high - low
            hub_ref[0, low:high, chunk * width : (chunk + 1) * width] = value[:height]
            for block, stream, row, count in pieces:
                if stream == s:
                    part = value[height : height + count, block * rel_width : (block + 1) * rel_width]
                    rel_ref[0, row : row + count, chunk * rel_width : (chunk + 1) * rel_width] = part


def place_chunks(spot, near, far, orders, spans, hub_shape, rel_shape, earlier):
    whole = [pl.BlockSpec(memory_space=pltpu.VMEM)] * (2 * len(spans))
    kept = [pl.BlockSpec(memory_space=pl.ANY)] * len(earlier)
    mine = lambda shape: pl.BlockSpec((1,) + shape[1:], lambda i, spot: (spot[1], 0, 0))
    return pl.pallas_call(
        functools.partial(place_kernel, orders, spans),
        grid_spec=pltpu.PrefetchScalarGridSpec(
            num_scalar_prefetch=1,
            grid=(1,),
            in_specs=whole + kept,
            out_specs=[mine(hub_shape), mine(rel_shape)],
        ),
        out_shape=[jax.ShapeDtypeStruct(hub_shape, F32), jax.ShapeDtypeStruct(rel_shape, F32)],
        input_output_aliases={1 + len(whole) + i: i for i in range(len(earlier))},
        compiler_params=PARAMS,
        cost_estimate=COST,
    )(spot, *near, *far, *earlier)


def adagrad(table, state, grads):
    new_state = state + jnp.sum(grads * grads, axis=0, keepdims=True) * (1.0 / grads.shape[0])
    return table - grads * (step_rate / jnp.sqrt(new_state)), new_state


def keep_and_send(core, first, second):
    return jnp.where(core == 0, first, second), jnp.where(core == 0, second, first)


def table_counts(rows, negs, weight):
    place = lax.broadcasted_iota(jnp.int32, (rows, negs.shape[1]), 0)
    return jnp.sum(jnp.where(place == negs, weight, 0.0), axis=1, keepdims=True)


def turned(x, r, half):
    x0, x1, r0, r1 = x[:half], x[half:], r[:half], r[half:]
    return jnp.concatenate([x0 * r0 - x1 * r1, x0 * r1 + x1 * r0], axis=0)


def turned_back(x, r, half):
    x0, x1, r0, r1 = x[:half], x[half:], r[:half], r[half:]
    return x0 * r0 + x1 * r1, x1 * r0 - x0 * r1


EDGE_TILE = 256


def edge_spans(step, bucket, edges):
    tile = EDGE_TILE
    here = pl.multiple_of(step * tile, tile)
    return pl.ds(here, tile), pl.ds(pl.multiple_of(bucket * edges + here, tile), tile)


def lay_down(idx, out_ref):
    out_ref[...] = jnp.transpose(jnp.broadcast_to(idx, (128, idx.shape[1])))


def head_hot_down(heads_down, span, rows):
    return onehot_across(heads_down.at[span], lax.broadcasted_iota(jnp.int32, (1, rows), 1))


def bucket_kernel(
    bucket, core_ref, heads_ref, tails_ref, negs_ref, left_ref, left_sums_ref, right_ref, right_sums_ref, rel_ref, hub_ref,
    left_out, left_sums_out, right_out, right_sums_out, rel_keep, rel_send, hub_keep, hub_send,
    left_hi, left_lo, both_hi, both_lo, down_hi, down_lo, left_grad, both_grad, heads_down,
):
    features, rows = left_ref.shape
    half = features // 2
    core = core_ref[0]
    edges, hubs = heads_ref.shape[1], hub_keep.shape[1]
    at = slice(bucket, bucket + 1)
    hub_rows = hub_ref[:, bucket * hubs : (bucket + 1) * hubs]
    weight = 1.0 / (negs_ref.shape[1] + hubs)
    counts = table_counts(rows, negs_ref[at], weight)
    lay_down(heads_ref[at], heads_down)
    left_hi[...], left_lo[...] = split(left_ref[...])
    both_hi[:, :rows], both_lo[:, :rows] = split(right_ref[...])
    both_hi[:, rows:], both_lo[:, rows:] = split(hub_rows)
    down_hi[:rows], down_lo[:rows] = split(jnp.transpose(right_ref[...]))
    down_hi[rows:], down_lo[rows:] = split(jnp.transpose(hub_rows))
    left_grad[...] = jnp.zeros_like(left_grad)
    both_grad[...] = jnp.zeros_like(both_grad)

    @pl.loop(0, edges // EDGE_TILE)
    def _(step):
        span, wide_span = edge_spans(step, bucket, edges)
        tail_here = lax.broadcasted_iota(jnp.int32, (rows, EDGE_TILE), 0) == tails_ref[at, span]
        h = dot2((left_hi[...], left_lo[...]), onehot(0, rows, heads_ref[at, span]), NN)
        r = rel_ref[:, wide_span]
        q = split(turned(h, r, half))
        scores = dot3((down_hi[...], down_lo[...]), q, NN)
        chance = jax.nn.sigmoid(scores[:rows])
        coef = jnp.concatenate(
            [
                counts * chance + jnp.where(tail_here, chance - 1.0, 0.0),
                weight * jax.nn.sigmoid(scores[rows:]),
            ],
            axis=0,
        )
        coef = split(coef)
        dq = dot3((both_hi[...], both_lo[...]), coef, NN)
        both_grad[...] += dot3(q, coef, NT)
        dh = jnp.concatenate(turned_back(dq, r, half), axis=0)
        left_grad[...] += dot2(split(dh), head_hot_down(heads_down, span, rows), NN)
        rel_keep[:, span], rel_send[:, span] = keep_and_send(core, *turned_back(dq, h, half))

    left_out[...], left_sums_out[...] = adagrad(left_ref[...], left_sums_ref[...], left_grad[...])
    right_out[...], right_sums_out[...] = adagrad(right_ref[...], right_sums_ref[...], both_grad[:, :rows])
    hub_keep[...], hub_send[...] = keep_and_send(core, both_grad[:half, rows:], both_grad[half:, rows:])


def bucket_step(bucket, core, heads, tails, negs, left, left_sums, right, right_sums, rel_rows, hub_rows):
    features, rows = left.shape
    edges, hubs = heads.shape[1], hub_rows.shape[1] // heads.shape[0]
    width = rows + hubs
    shapes = [(features, rows), (1, rows)] * 2 + [(features // 2, edges)] * 2 + [(features // 2, hubs)] * 2
    return pl.pallas_call(
        functools.partial(bucket_kernel, bucket),
        in_specs=[SMEM] + [VMEM] * 9,
        out_specs=[VMEM] * 8,
        out_shape=[jax.ShapeDtypeStruct(shape, F32) for shape in shapes],
        scratch_shapes=[pltpu.VMEM((features, rows), BF16)] * 2
        + [pltpu.VMEM((features, width), BF16)] * 2
        + [pltpu.VMEM((width, features), BF16)] * 2
        + [
            pltpu.VMEM((features, rows), F32),
            pltpu.VMEM((features, width), F32),
            pltpu.VMEM((edges, 128), jnp.int32),
        ],
        compiler_params=PARAMS,
        cost_estimate=COST,
    )(core, heads, tails, negs, left, left_sums, right, right_sums, rel_rows, hub_rows)


def hub_kernel(
    bucket, negatives, core_ref, heads_ref, left_ref, rel_ref, hub_ref,
    head_out, query_grad, hub_keep, hub_send,
    left_hi, left_lo, hub_hi, hub_lo, down_hi, down_lo, hub_grad,
):
    features, rows = left_ref.shape
    half = features // 2
    edges, hubs = heads_ref.shape[1], hub_keep.shape[1]
    at = slice(bucket, bucket + 1)
    hub_rows = hub_ref[:, bucket * hubs : (bucket + 1) * hubs]
    weight = 1.0 / (negatives + hubs)
    left_hi[...], left_lo[...] = split(left_ref[...])
    hub_hi[...], hub_lo[...] = split(hub_rows)
    down_hi[...], down_lo[...] = split(jnp.transpose(hub_rows))
    hub_grad[...] = jnp.zeros_like(hub_grad)

    @pl.loop(0, edges // EDGE_TILE)
    def _(step):
        span, wide_span = edge_spans(step, bucket, edges)
        h = dot2((left_hi[...], left_lo[...]), onehot(0, rows, heads_ref[at, span]), NN)
        head_out[:, span] = h
        q = split(turned(h, rel_ref[:, wide_span], half))
        coef = split(weight * jax.nn.sigmoid(dot3((down_hi[...], down_lo[...]), q, NN)))
        query_grad[:, span] = dot3((hub_hi[...], hub_lo[...]), coef, NN)
        hub_grad[...] += dot3(q, coef, NT)

    hub_keep[...], hub_send[...] = keep_and_send(core_ref[0], hub_grad[:half], hub_grad[half:])


def hub_step(bucket, negatives, core, heads, left, rel_rows, hub_rows):
    features, rows = left.shape
    edges, hubs = heads.shape[1], hub_rows.shape[1] // heads.shape[0]
    shapes = [(features, edges)] * 2 + [(features // 2, hubs)] * 2
    return pl.pallas_call(
        functools.partial(hub_kernel, bucket, negatives),
        in_specs=[SMEM] + [VMEM] * 4,
        out_specs=[VMEM] * 4,
        out_shape=[jax.ShapeDtypeStruct(shape, F32) for shape in shapes],
        scratch_shapes=[pltpu.VMEM((features, rows), BF16)] * 2
        + [pltpu.VMEM((features, hubs), BF16)] * 2
        + [pltpu.VMEM((hubs, features), BF16)] * 2
        + [pltpu.VMEM((features, hubs), F32)],
        compiler_params=PARAMS,
        cost_estimate=COST,
    )(core, heads, left, rel_rows, hub_rows)


def tables_kernel(
    bucket, hubs, core_ref, heads_ref, tails_ref, negs_ref, head_rows, query_grad,
    left_ref, left_sums_ref, right_ref, right_sums_ref, rel_ref,
    left_out, right_out, rel_keep, rel_send,
    right_hi, right_lo, down_hi, down_lo, left_grad, right_grad, heads_down,
):
    features, rows = left_ref.shape
    half = features // 2
    edges = heads_ref.shape[1]
    at = slice(bucket, bucket + 1)
    core = core_ref[0]
    counts = table_counts(rows, negs_ref[at], 1.0 / (negs_ref.shape[1] + hubs))
    lay_down(heads_ref[at], heads_down)
    right_hi[...], right_lo[...] = split(right_ref[...])
    down_hi[...], down_lo[...] = split(jnp.transpose(right_ref[...]))
    left_grad[...] = jnp.zeros_like(left_grad)
    right_grad[...] = jnp.zeros_like(right_grad)

    @pl.loop(0, edges // EDGE_TILE)
    def _(step):
        span, wide_span = edge_spans(step, bucket, edges)
        tail_here = lax.broadcasted_iota(jnp.int32, (rows, EDGE_TILE), 0) == tails_ref[at, span]
        h, r = head_rows[:, span], rel_ref[:, wide_span]
        q = split(turned(h, r, half))
        chance = jax.nn.sigmoid(dot3((down_hi[...], down_lo[...]), q, NN))
        coef = split(counts * chance + jnp.where(tail_here, chance - 1.0, 0.0))
        dq = dot3((right_hi[...], right_lo[...]), coef, NN) + query_grad[:, span]
        right_grad[...] += dot3(q, coef, NT)
        rel_keep[:, span], rel_send[:, span] = keep_and_send(core, *turned_back(dq, h, half))
        dh = jnp.concatenate(turned_back(dq, r, half), axis=0)
        left_grad[...] += dot2(split(dh), head_hot_down(heads_down, span, rows), NN)

    left_out[...], unused = adagrad(left_ref[...], left_sums_ref[...], left_grad[...])
    right_out[...], unused = adagrad(right_ref[...], right_sums_ref[...], right_grad[...])


def tables_step(bucket, hubs, core, heads, tails, negs, head_rows, query_grad, left, left_sums, right, right_sums, rel_rows):
    features, rows = left.shape
    edges = heads.shape[1]
    shapes = [(features, rows)] * 2 + [(features // 2, edges)] * 2
    return pl.pallas_call(
        functools.partial(tables_kernel, bucket, hubs),
        in_specs=[SMEM] + [VMEM] * 10,
        out_specs=[VMEM] * 4,
        out_shape=[jax.ShapeDtypeStruct(shape, F32) for shape in shapes],
        scratch_shapes=[pltpu.VMEM((features, rows), BF16)] * 2
        + [pltpu.VMEM((rows, features), BF16)] * 2
        + [pltpu.VMEM((features, rows), F32)] * 2
        + [pltpu.VMEM((edges, 128), jnp.int32)],
        compiler_params=PARAMS,
        cost_estimate=COST,
    )(core, heads, tails, negs, head_rows, query_grad, left, left_sums, right, right_sums, rel_rows)


def from_behind(x, axis, by):
    size = lax.axis_size(axis)
    return lax.ppermute(x, axis, [(i, (i + by) % size) for i in range(size)])


def flipped(x, axis, bit):
    return lax.ppermute(x, axis, [(i, i ^ (1 << bit)) for i in range(lax.axis_size(axis))])


def other_core(x):
    return flipped(x, "blk", 0)


def across(x, place):
    sub_bits = lax.axis_size("sub").bit_length() - 1
    if place < sub_bits:
        return flipped(x, "sub", place)
    return flipped(x, "blk", place - sub_bits + 1)


def stream_orders():
    sub_bits = lax.axis_size("sub").bit_length() - 1
    bits = sub_bits + lax.axis_size("blk").bit_length() - 2
    x, y, z, far = sub_bits, sub_bits + 1, 0, 1
    rest = [p for p in range(bits) if p not in (x, y, z, far)]
    return [[x, y, z, far] + rest, [y, z, x, far] + rest, [z, x, far, y] + rest]


def row_spans(rows, parts):
    ends = [-(-rows * (i + 1) // (8 * parts)) * 8 for i in range(parts - 1)] + [rows]
    return list(zip([0] + ends[:-1], ends))


def shards(
    left_emb, left_state, right_emb, right_state, relation_emb, relation_state, hub_emb, hub_state,
    heads, relations, tails, negatives, hub_ids,
):
    components, half_width, row_count = left_emb.shape
    features = components * half_width
    rel_count, hub_count = relation_emb.shape[2], hub_emb.shape[2]
    left = left_emb.reshape(features, row_count)
    right = right_emb.reshape(features, row_count)
    left_sums = left_state.reshape(1, row_count)
    right_sums = right_state.reshape(1, row_count)
    buckets, hubs = heads.shape[0], hub_ids.shape[1]

    core_id = lax.axis_index("blk") % 2
    chip_id = (lax.axis_index("blk") // 2) * lax.axis_size("sub") + lax.axis_index("sub")
    core, chip = core_id.astype(jnp.int32).reshape(1), chip_id.astype(jnp.int32).reshape(1)
    orders = stream_orders()
    spans = row_spans(half_width, len(orders))
    heights = [high - low for low, high in spans]
    third = third_of(spans)
    chunks = 1 << len(orders[0])
    width, rel_width = hub_count // chunks, rel_count // chunks

    def exchanged(parts, step):
        return [across(x, order[step]) for x, order in zip(parts, orders)]

    far_rel, far_hub = other_core((relations, hub_ids))
    hub_rows, rel_rows = gather_rows(
        hub_emb.reshape(features, hub_count), hub_ids, relation_emb.reshape(features, rel_count), relations
    )
    rel_keep, rel_far, hub_keep, hub_far = [], [], [], []
    for b in range(buckets - 1):
        left, left_sums, right, right_sums, rk, rs, hk, hs = bucket_step(
            b, core, heads, tails, negatives, left, left_sums, right, right_sums, rel_rows, hub_rows
        )
        right, right_sums = from_behind((right, right_sums), "blk", 1)
        hub_far.append(other_core(hs))
        rel_far.append(other_core(rs))
        hub_keep.append(hk)
        rel_keep.append(rk)
    last = buckets - 1
    head_rows, query_grad, hk, hs = hub_step(last, negatives.shape[1], core, heads, left, rel_rows, hub_rows)
    hub_grads = hub_keep + [hk] + hub_far + [other_core(hs)]
    hub_send, hub_own = chunk_columns(
        functools.partial(hub_chunks_kernel, orders, spans, len(hub_grads)),
        heights, width, chip, (hub_ids, far_hub), hub_grads, chunks,
    )
    hub_got = exchanged(hub_send, 0)
    left, right, rk, rs = tables_step(
        last, hubs, core, heads, tails, negatives, head_rows, query_grad, left, left_sums, right, right_sums, rel_rows
    )
    rel_grads = rel_keep + [rk] + rel_far + [other_core(rs)]
    rel_send, rel_own = chunk_columns(
        functools.partial(rel_chunks_kernel, orders, spans, rel_count, len(rel_grads)),
        [third] * len(spans), width, chip, (relations, far_rel), rel_grads, chunks,
    )
    rel_got = exchanged(rel_send, 0)

    send, own = halves(
        first_sums_kernel,
        (hub_own, hub_got, rel_own, rel_got),
        [(chunks // 2, height + third, width) for height in heights],
    )
    for step in range(1, len(orders[0]) - 1):
        got = exchanged(send, step)
        send, own = halves(sums_kernel, (own, got), [x.shape for x in own])
    late, send = lax.optimization_barrier((jnp.stack([core_id, chip_id]), send))
    got = exchanged(send, -1)
    *totals, squares = call(
        functools.partial(squares_kernel, spans, rel_width), [*own, *got], [x.shape for x in own] + [(2, width)]
    )
    far_squares = other_core(squares)
    cut = lambda x, span: lax.dynamic_slice(x, (late[0], 0, late[1] * span), (1, half_width, span))[0]
    cut_sums = lambda x, span: lax.dynamic_slice(x[None], (0, late[1] * span), (1, span))
    have = call(
        functools.partial(update_kernel, spans, rel_width, features),
        [
            *totals, squares, far_squares, cut(hub_emb, width), cut(relation_emb, rel_width),
            cut_sums(hub_state, width), cut_sums(relation_state, rel_width),
        ],
        [x.shape for x in totals],
    )
    for step in range(len(orders[0]) - 1, 0, -1):
        have = join(have, exchanged(have, step))
    far = exchanged(have, 0)
    shapes = (hub_emb.shape, relation_emb.shape)
    out = place_chunks(jnp.concatenate([chip, core]), have, far, orders, spans, *shapes, ())
    out = place_chunks(
        jnp.concatenate([chip, 1 - core]), other_core(have), other_core(far), orders, spans, *shapes, tuple(out)
    )
    return (
        left.reshape(components, half_width, row_count),
        right.reshape(components, half_width, row_count),
        out[1],
        out[0],
    )


def solution(mesh):
    both = ("blk", "sub")
    block, table, whole = P(None, None, both), P(None, both), P()
    return jax.shard_map(
        shards,
        mesh=mesh,
        in_specs=(block, P(both), block, P(both), whole, whole, whole, whole, table, table, table, table, table),
        out_specs=(block, block, whole, whole),
        check_vma=False,
    )
```

```python
import functools
import jax
import jax.numpy as jnp
from jax import lax
from jax.experimental import pallas as pl
from jax.experimental.pallas import tpu as pltpu
from jax.sharding import PartitionSpec as P

step_rate = 0.25
F32, BF16 = jnp.float32, jnp.bfloat16
NN = (((1,), (0,)), ((), ()))
NT = (((1,), (1,)), ((), ()))
TN = (((0,), (0,)), ((), ()))
VMEM = pl.BlockSpec(memory_space=pltpu.VMEM)
SMEM = pl.BlockSpec(memory_space=pltpu.SMEM)
PARAMS = pltpu.CompilerParams(vmem_limit_bytes=16 * 1024 * 1024)
ALL_VMEM = pltpu.CompilerParams(vmem_limit_bytes=56 * 1024 * 1024)
COST = pl.CostEstimate(flops=10000, bytes_accessed=10000, transcendentals=0)


def split(x):
    hi = x.astype(BF16)
    return hi, (x - hi.astype(F32)).astype(BF16)


def dot(a, b, dims):
    return lax.dot_general(a, b, dims, preferred_element_type=F32)


def dot3(a, b, dims):
    return dot(a[0], b[0], dims) + (dot(a[0], b[1], dims) + dot(a[1], b[0], dims))


def dot2(a, onehot, dims):
    return dot(a[0], onehot, dims) + dot(a[1], onehot, dims)


def onehot(first, rows, idx):
    place = lax.broadcasted_iota(jnp.int32, (rows, idx.shape[1]), 0) + first
    return jnp.where(place == idx, 1.0, 0.0).astype(BF16)


def laid_out(idx):
    return jnp.concatenate([idx[b : b + 1] for b in range(idx.shape[0])], axis=1)


def add_part(first, part, out_ref):
    @pl.when(first)
    def _():
        out_ref[...] = part

    @pl.when(jnp.logical_not(first))
    def _():
        out_ref[...] += part


def gather_kernel(hub_steps, hub_idx, rel_idx, hub_ref, rel_ref, hub_out, rel_out):
    step = pl.program_id(0)

    @pl.when(step < hub_steps)
    def _():
        tile = hub_ref.shape[1]
        hot = onehot(step * tile, tile, laid_out(hub_idx[...]))
        add_part(step == 0, dot2(split(hub_ref[...]), hot, NN), hub_out)

    @pl.when(step >= hub_steps)
    def _():
        tile = rel_ref.shape[1]
        hot = onehot((step - hub_steps) * tile, tile, laid_out(rel_idx[...]))
        add_part(step == hub_steps, dot2(split(rel_ref[...]), hot, NN), rel_out)


def gather_rows(hub_table, hub_idx, rel_table, rel_idx):
    features = hub_table.shape[0]
    hub_steps, rel_steps = 4, 2
    fixed = lambda shape: pl.BlockSpec(shape, lambda k: (0, 0))
    shapes = [(features, hub_idx.size), (features, rel_idx.size)]
    return pl.pallas_call(
        functools.partial(gather_kernel, hub_steps),
        grid=(hub_steps + rel_steps,),
        in_specs=[
            fixed(hub_idx.shape),
            fixed(rel_idx.shape),
            pl.BlockSpec((features, hub_table.shape[1] // hub_steps), lambda k: (0, jnp.minimum(k, hub_steps - 1))),
            pl.BlockSpec((features, rel_table.shape[1] // rel_steps), lambda k: (0, jnp.maximum(k - hub_steps, 0))),
        ],
        out_specs=[fixed(shape) for shape in shapes],
        out_shape=[jax.ShapeDtypeStruct(shape, F32) for shape in shapes],
        compiler_params=ALL_VMEM,
        cost_estimate=COST,
    )(hub_idx, rel_idx, hub_table, rel_table)


def spread_bits(place, order):
    bits = len(order)
    return sum((((place >> p) & 1) << (bits - 1 - i)) for i, p in enumerate(order))


def gather_bits(index, order):
    bits = len(order)
    return sum((((index >> (bits - 1 - i)) & 1) << p) for i, p in enumerate(order))


def load_columns(id_refs, id_lanes, grad_refs, idx_down, hi_all, lo_all):
    low, high = id_lanes
    idx = jnp.concatenate([laid_out(ref[:, low:high]) for ref in id_refs], axis=1)
    idx_down[...] = jnp.transpose(jnp.broadcast_to(idx, (128, idx.shape[1])))
    at = 0
    for ref, (low, high) in grad_refs:
        width = high - low
        hi_all[:, at : at + width], lo_all[:, at : at + width] = split(ref[:, low:high])
        at += width


def onehot_across(idx_down, targets):
    width = targets.shape[1]
    idx = idx_down[...]
    wide = jnp.concatenate([idx] * -(-width // 128), axis=1)[:, :width]
    return jnp.where(wide == targets, 1.0, 0.0).astype(BF16)


def out_for(place, order, sends, keeps, s):
    index = spread_bits(place, order)
    half = keeps[s].shape[0]
    return sends[s].at[index - half] if index >= half else keeps[s].at[index]


def chunk_refs(orders, grad_lanes, refs):
    ids, refs = refs[:2], refs[2:]
    grads, refs = list(zip(refs, grad_lanes)), refs[len(grad_lanes) :]
    streams = len(orders)
    return ids, grads, refs[:streams], refs[streams : 2 * streams], refs[2 * streams :]


def hub_chunks_kernel(orders, spans, id_lanes, grad_lanes, chip_ref, *refs):
    ids, grads, sends, keeps, (idx_down, hi_all, lo_all) = chunk_refs(orders, grad_lanes, refs)
    load_columns(ids, id_lanes, grads, idx_down, hi_all, lo_all)
    chunks, width = 2 * keeps[0].shape[0], keeps[0].shape[2]
    lane = lax.broadcasted_iota(jnp.int32, (1, width), 1)
    for place in range(chunks):
        hot = onehot_across(idx_down, lane + (chip_ref[0] ^ place) * width)
        chunk = dot2((hi_all[...], lo_all[...]), hot, NN)
        for s, (low, high) in enumerate(spans):
            out_for(place, orders[s], sends, keeps, s)[...] = chunk[low:high]


def rel_layout(half_width, streams):
    blocks = row_spans(half_width, 3)
    spans = row_spans(max(high - low for low, high in blocks), streams)
    pieces = []
    for block, (low, high) in enumerate(blocks):
        for s, (first, end) in enumerate(spans):
            count = min(end, high - low) - first
            if count > 0:
                pieces.append((block, s, low + first, count))
    return spans, pieces


def rel_chunks_kernel(orders, pieces, rows, id_lanes, grad_lanes, chip_ref, *refs):
    ids, grads, sends, keeps, (idx_down, hi_all, lo_all) = chunk_refs(orders, grad_lanes, refs)
    load_columns(ids, id_lanes, grads, idx_down, hi_all, lo_all)
    for ref in [*sends, *keeps]:
        ref[...] = jnp.zeros_like(ref)
    chunks, lanes = 2 * keeps[0].shape[0], keeps[0].shape[2]
    width = rows // chunks
    group = lanes // width
    lane = lax.broadcasted_iota(jnp.int32, (1, lanes), 1)
    for first in range(0, chunks, group):
        targets = jnp.full((1, lanes), -1, jnp.int32)
        places = range(first, min(first + group, chunks))
        for slot, place in enumerate(places):
            here = (lane >= slot * width) & (lane < (slot + 1) * width)
            targets = jnp.where(here, lane + ((chip_ref[0] ^ place) * width - slot * width), targets)
        dense = dot2((hi_all[...], lo_all[...]), onehot_across(idx_down, targets), NN)
        for slot, place in enumerate(places):
            chunk = dense[:, slot * width : (slot + 1) * width]
            for block, s, low, count in pieces:
                out = out_for(place, orders[s], sends, keeps, s)
                out[:count, block * width : (block + 1) * width] = chunk[low : low + count]


def chunk_columns(kernel, heights, lanes, chip, ids, grads, chunks):
    half_width = grads[0][0].shape[0]
    grad_lanes = [lanes_of for unused, lanes_of in grads]
    count = sum(high - low for low, high in grad_lanes)
    shapes = [jax.ShapeDtypeStruct((chunks // 2, height, lanes), F32) for height in heights] * 2
    out = pl.pallas_call(
        functools.partial(kernel, grad_lanes),
        in_specs=[SMEM] + [VMEM] * (2 + len(grads)),
        out_specs=[VMEM] * len(shapes),
        out_shape=shapes,
        scratch_shapes=[
            pltpu.VMEM((count, 128), jnp.int32),
            pltpu.VMEM((half_width, count), BF16),
            pltpu.VMEM((half_width, count), BF16),
        ],
        compiler_params=PARAMS,
        cost_estimate=COST,
    )(chip, *ids, *[g for g, unused in grads])
    return out[: len(heights)], out[len(heights) :]


def call(kernel, ins, shapes):
    return pl.pallas_call(
        kernel,
        in_specs=[VMEM] * len(ins),
        out_specs=[VMEM] * len(shapes),
        out_shape=[jax.ShapeDtypeStruct(shape, F32) for shape in shapes],
        compiler_params=PARAMS,
        cost_estimate=COST,
    )(*ins)


def sums_kernel(*refs):
    streams = len(refs) // 4
    own, got, sends, keeps = [refs[i * streams : (i + 1) * streams] for i in range(4)]
    for s in range(streams):
        half = sends[s].shape[0]
        sends[s][...] = own[s][half:] + got[s][half:]
        keeps[s][...] = own[s][:half] + got[s][:half]


def halves(own, got):
    shapes = [(x.shape[0] // 2,) + x.shape[1:] for x in own]
    out = call(sums_kernel, [*own, *got], shapes * 2)
    return out[: len(shapes)], out[len(shapes) :]


def join_kernel(*refs):
    streams = len(refs) // 3
    for s in range(streams):
        own, got, out = refs[s], refs[streams + s], refs[2 * streams + s]
        count = own.shape[0]
        out[:count] = own[...]
        out[count:] = got[...]


def join(own, got):
    return call(join_kernel, [*own, *got], [(2 * x.shape[0],) + x.shape[1:] for x in own])


def squares_kernel(*refs):
    streams = len(refs) // 3
    own, got, totals, out = [refs[i * streams : (i + 1) * streams] for i in range(3)] + [refs[-1]]
    squares = jnp.zeros(out.shape, F32)
    for s in range(streams):
        total = own[s][0] + got[s][0]
        totals[s][0] = total
        squares += jnp.sum(total * total, axis=0, keepdims=True)
    out[...] = squares


def squares_of(own, got):
    *totals, squares = call(squares_kernel, [*own, *got], [x.shape for x in own] + [(1, own[0].shape[2])])
    return totals, squares


def hub_update_kernel(spans, features, *refs):
    streams = len(spans)
    totals, news = refs[:streams], refs[-streams:]
    mine, other, table_ref, sums_ref = refs[streams:-streams]
    scale = step_rate / jnp.sqrt(sums_ref[...] + (mine[...] + other[...]) * (1.0 / features))
    for s, (low, high) in enumerate(spans):
        news[s][0] = table_ref[low:high] - totals[s][0] * scale


def rel_update_kernel(streams, pieces, features, *refs):
    totals, news = refs[:streams], refs[-streams:]
    mine, other, table_ref, sums_ref = refs[streams:-streams]
    width = table_ref.shape[1]
    squares = mine[...] + other[...]
    squares = sum(squares[:, b * width : (b + 1) * width] for b in range(3))
    scale = step_rate / jnp.sqrt(sums_ref[...] + squares * (1.0 / features))
    for new in news:
        new[...] = jnp.zeros_like(new)
    for block, s, low, count in pieces:
        lanes = slice(block * width, (block + 1) * width)
        news[s][0, :count, lanes] = table_ref[low : low + count] - totals[s][0, :count, lanes] * scale


def place_kernel(orders, pieces, spot_ref, *refs):
    streams = len(orders)
    lows, highs, out_ref = refs[:streams], refs[streams : 2 * streams], refs[-1]
    half = lows[0].shape[0]
    width = out_ref.shape[2] // (2 * half)
    for chunk in range(2 * half):
        place = spot_ref[0] ^ chunk
        for s in range(streams):
            index = spread_bits(place, orders[s])
            spot = index & (half - 1)
            value = jnp.where(index >= half, highs[s][spot], lows[s][spot])
            for block, stream, row, count in pieces:
                if stream == s:
                    part = value[:count, block * width : (block + 1) * width]
                    out_ref[0, row : row + count, chunk * width : (chunk + 1) * width] = part


def place_chunks(spot, near, far, orders, pieces, shape, earlier):
    whole = [pl.BlockSpec(memory_space=pltpu.VMEM)] * (2 * len(orders))
    kept = [pl.BlockSpec(memory_space=pl.ANY)] * len(earlier)
    return pl.pallas_call(
        functools.partial(place_kernel, orders, pieces),
        grid_spec=pltpu.PrefetchScalarGridSpec(
            num_scalar_prefetch=1,
            grid=(1,),
            in_specs=whole + kept,
            out_specs=pl.BlockSpec((1,) + shape[1:], lambda i, spot: (spot[1], 0, 0)),
        ),
        out_shape=jax.ShapeDtypeStruct(shape, F32),
        input_output_aliases={1 + len(whole): 0} if earlier else {},
        compiler_params=PARAMS,
        cost_estimate=COST,
    )(spot, *near, *far, *earlier)


def copy_kernel(orders, spans, upper, spot_ref, *refs):
    streams = len(orders)
    parts, out_ref, sems = refs[:streams], refs[-2], refs[-1]
    half, width = parts[0].shape[0], parts[0].shape[2]
    copies = []
    for s, (low, high) in enumerate(spans):
        for index in range(half):
            chunk = spot_ref[0] ^ gather_bits(index + half * upper, orders[s])
            lanes = pl.ds(pl.multiple_of(chunk * width, width), width)
            target = out_ref.at[spot_ref[1], pl.ds(low, high - low), lanes]
            copies.append(pltpu.make_async_copy(parts[s].at[index], target, sems.at[len(copies)]))
    for copy in copies:
        copy.start()
    for copy in copies:
        copy.wait()


def copy_chunks(spot, parts, upper, orders, spans, shape, earlier):
    anywhere = pl.BlockSpec(memory_space=pl.ANY)
    return pl.pallas_call(
        functools.partial(copy_kernel, orders, spans, upper),
        in_specs=[SMEM] + [anywhere] * (len(parts) + len(earlier)),
        out_specs=anywhere,
        out_shape=jax.ShapeDtypeStruct(shape, F32),
        scratch_shapes=[pltpu.SemaphoreType.DMA((len(parts) * parts[0].shape[0],))],
        input_output_aliases={1 + len(parts): 0} if earlier else {},
        compiler_params=PARAMS,
        cost_estimate=COST,
    )(spot, *parts, *earlier)


def adagrad(table, state, grads):
    new_state = state + jnp.sum(grads * grads, axis=0, keepdims=True) * (1.0 / grads.shape[0])
    return table - grads * (step_rate / jnp.sqrt(new_state)), new_state


def keep_and_send(core, first, second):
    return jnp.where(core == 0, first, second), jnp.where(core == 0, second, first)


def table_counts(rows, negs, weight):
    place = lax.broadcasted_iota(jnp.int32, (rows, negs.shape[1]), 0)
    return jnp.sum(jnp.where(place == negs, weight, 0.0), axis=1, keepdims=True)


def turned(x, r, half):
    x0, x1, r0, r1 = x[:half], x[half:], r[:half], r[half:]
    return jnp.concatenate([x0 * r0 - x1 * r1, x0 * r1 + x1 * r0], axis=0)


def turned_back(x, r, half):
    x0, x1, r0, r1 = x[:half], x[half:], r[:half], r[half:]
    return x0 * r0 + x1 * r1, x1 * r0 - x0 * r1


EDGE_TILE = 256


def edge_spans(step, bucket, edges):
    tile = EDGE_TILE
    here = pl.multiple_of(step * tile, tile)
    return pl.ds(here, tile), pl.ds(pl.multiple_of(bucket * edges + here, tile), tile)


def lay_down(idx, out_ref):
    out_ref[...] = jnp.transpose(jnp.broadcast_to(idx, (128, idx.shape[1])))


def head_hot_down(heads_down, span, rows):
    return onehot_across(heads_down.at[span], lax.broadcasted_iota(jnp.int32, (1, rows), 1))


def bucket_kernel(
    bucket, core_ref, heads_ref, tails_ref, negs_ref, left_ref, left_sums_ref, right_ref, right_sums_ref, rel_ref, hub_ref,
    left_out, left_sums_out, right_out, keep_out, send_out,
    left_hi, left_lo, both_hi, both_lo, left_grad, both_grad, heads_down,
):
    features, rows = left_ref.shape
    half = features // 2
    core = core_ref[0]
    edges = heads_ref.shape[1]
    hubs = keep_out.shape[1] - edges
    at = slice(bucket, bucket + 1)
    hub_rows = hub_ref[:, bucket * hubs : (bucket + 1) * hubs]
    weight = 1.0 / (negs_ref.shape[1] + hubs)
    counts = table_counts(rows, negs_ref[at], weight)
    lay_down(heads_ref[at], heads_down)
    left_hi[...], left_lo[...] = split(left_ref[...])
    both_hi[:, :rows], both_lo[:, :rows] = split(right_ref[...])
    both_hi[:, rows:], both_lo[:, rows:] = split(hub_rows)
    left_grad[...] = jnp.zeros_like(left_grad)
    both_grad[...] = jnp.zeros_like(both_grad)

    @pl.loop(0, edges // EDGE_TILE)
    def _(step):
        span, wide_span = edge_spans(step, bucket, edges)
        tail_here = lax.broadcasted_iota(jnp.int32, (rows, EDGE_TILE), 0) == tails_ref[at, span]
        h = dot2((left_hi[...], left_lo[...]), onehot(0, rows, heads_ref[at, span]), NN)
        r = rel_ref[:, wide_span]
        q = split(turned(h, r, half))
        both = (both_hi[...], both_lo[...])
        scores = dot3(both, q, TN)
        chance = jax.nn.sigmoid(scores[:rows])
        coef = jnp.concatenate(
            [
                counts * chance + jnp.where(tail_here, chance - 1.0, 0.0),
                weight * jax.nn.sigmoid(scores[rows:]),
            ],
            axis=0,
        )
        coef = split(coef)
        dq = dot3(both, coef, NN)
        both_grad[...] += dot3(q, coef, NT)
        dh = jnp.concatenate(turned_back(dq, r, half), axis=0)
        left_grad[...] += dot2(split(dh), head_hot_down(heads_down, span, rows), NN)
        out_span = pl.ds(pl.multiple_of(hubs + step * EDGE_TILE, 128), EDGE_TILE)
        keep_out[:, out_span], send_out[:, out_span] = keep_and_send(core, *turned_back(dq, h, half))

    left_out[...], left_sums_out[...] = adagrad(left_ref[...], left_sums_ref[...], left_grad[...])
    new_right, new_sums = adagrad(right_ref[...], right_sums_ref[...], both_grad[:, :rows])
    right_out[:features] = new_right
    right_out[features:] = jnp.broadcast_to(new_sums, (right_out.shape[0] - features, rows))
    keep_out[:, :hubs], send_out[:, :hubs] = keep_and_send(core, both_grad[:half, rows:], both_grad[half:, rows:])


def bucket_step(bucket, core, heads, tails, negs, left, left_sums, right, right_sums, rel_rows, hub_rows):
    features, rows = left.shape
    edges, hubs = heads.shape[1], hub_rows.shape[1] // heads.shape[0]
    width = rows + hubs
    shapes = [(features, rows), (1, rows), (features + 8, rows)] + [(features // 2, hubs + edges)] * 2
    return pl.pallas_call(
        functools.partial(bucket_kernel, bucket),
        in_specs=[SMEM] + [VMEM] * 9,
        out_specs=[VMEM] * 5,
        out_shape=[jax.ShapeDtypeStruct(shape, F32) for shape in shapes],
        scratch_shapes=[pltpu.VMEM((features, rows), BF16)] * 2
        + [pltpu.VMEM((features, width), BF16)] * 2
        + [
            pltpu.VMEM((features, rows), F32),
            pltpu.VMEM((features, width), F32),
            pltpu.VMEM((edges, 128), jnp.int32),
        ],
        compiler_params=PARAMS,
        cost_estimate=COST,
    )(core, heads, tails, negs, left, left_sums, right, right_sums, rel_rows, hub_rows)


def hub_kernel(
    bucket, negatives, core_ref, heads_ref, left_ref, rel_ref, hub_ref,
    head_out, query_grad, hub_keep, hub_send,
    left_hi, left_lo, hub_hi, hub_lo, hub_grad,
):
    features, rows = left_ref.shape
    half = features // 2
    edges, hubs = heads_ref.shape[1], hub_keep.shape[1]
    at = slice(bucket, bucket + 1)
    hub_rows = hub_ref[:, bucket * hubs : (bucket + 1) * hubs]
    weight = 1.0 / (negatives + hubs)
    left_hi[...], left_lo[...] = split(left_ref[...])
    hub_hi[...], hub_lo[...] = split(hub_rows)
    hub_grad[...] = jnp.zeros_like(hub_grad)

    @pl.loop(0, edges // EDGE_TILE)
    def _(step):
        span, wide_span = edge_spans(step, bucket, edges)
        h = dot2((left_hi[...], left_lo[...]), onehot(0, rows, heads_ref[at, span]), NN)
        head_out[:, span] = h
        q = split(turned(h, rel_ref[:, wide_span], half))
        hub = (hub_hi[...], hub_lo[...])
        coef = split(weight * jax.nn.sigmoid(dot3(hub, q, TN)))
        query_grad[:, span] = dot3(hub, coef, NN)
        hub_grad[...] += dot3(q, coef, NT)

    hub_keep[...], hub_send[...] = keep_and_send(core_ref[0], hub_grad[:half], hub_grad[half:])


def hub_step(bucket, negatives, core, heads, left, rel_rows, hub_rows):
    features, rows = left.shape
    edges, hubs = heads.shape[1], hub_rows.shape[1] // heads.shape[0]
    shapes = [(features, edges)] * 2 + [(features // 2, hubs)] * 2
    return pl.pallas_call(
        functools.partial(hub_kernel, bucket, negatives),
        in_specs=[SMEM] + [VMEM] * 4,
        out_specs=[VMEM] * 4,
        out_shape=[jax.ShapeDtypeStruct(shape, F32) for shape in shapes],
        scratch_shapes=[pltpu.VMEM((features, rows), BF16)] * 2
        + [pltpu.VMEM((features, hubs), BF16)] * 2
        + [pltpu.VMEM((features, hubs), F32)],
        compiler_params=PARAMS,
        cost_estimate=COST,
    )(core, heads, left, rel_rows, hub_rows)


def tables_kernel(
    bucket, hubs, core_ref, heads_ref, tails_ref, negs_ref, head_rows, query_grad,
    left_ref, left_sums_ref, right_ref, rel_ref,
    left_out, right_out, rel_keep, rel_send,
    right_hi, right_lo, left_grad, right_grad, heads_down,
):
    features, rows = left_ref.shape
    half = features // 2
    edges = heads_ref.shape[1]
    at = slice(bucket, bucket + 1)
    core = core_ref[0]
    counts = table_counts(rows, negs_ref[at], 1.0 / (negs_ref.shape[1] + hubs))
    lay_down(heads_ref[at], heads_down)
    right_hi[...], right_lo[...] = split(right_ref[:features])
    left_grad[...] = jnp.zeros_like(left_grad)
    right_grad[...] = jnp.zeros_like(right_grad)

    @pl.loop(0, edges // EDGE_TILE)
    def _(step):
        span, wide_span = edge_spans(step, bucket, edges)
        tail_here = lax.broadcasted_iota(jnp.int32, (rows, EDGE_TILE), 0) == tails_ref[at, span]
        h, r = head_rows[:, span], rel_ref[:, wide_span]
        q = split(turned(h, r, half))
        right = (right_hi[...], right_lo[...])
        chance = jax.nn.sigmoid(dot3(right, q, TN))
        coef = split(counts * chance + jnp.where(tail_here, chance - 1.0, 0.0))
        dq = dot3(right, coef, NN) + query_grad[:, span]
        right_grad[...] += dot3(q, coef, NT)
        rel_keep[:, span], rel_send[:, span] = keep_and_send(core, *turned_back(dq, h, half))
        dh = jnp.concatenate(turned_back(dq, r, half), axis=0)
        left_grad[...] += dot2(split(dh), head_hot_down(heads_down, span, rows), NN)

    left_out[...], unused = adagrad(left_ref[...], left_sums_ref[...], left_grad[...])
    right_out[...], unused = adagrad(right_ref[:features], right_ref[features : features + 1], right_grad[...])


def tables_step(bucket, hubs, core, heads, tails, negs, head_rows, query_grad, left, left_sums, right, rel_rows):
    features, rows = left.shape
    edges = heads.shape[1]
    shapes = [(features, rows)] * 2 + [(features // 2, edges)] * 2
    return pl.pallas_call(
        functools.partial(tables_kernel, bucket, hubs),
        in_specs=[SMEM] + [VMEM] * 9,
        out_specs=[VMEM] * 4,
        out_shape=[jax.ShapeDtypeStruct(shape, F32) for shape in shapes],
        scratch_shapes=[pltpu.VMEM((features, rows), BF16)] * 2
        + [pltpu.VMEM((features, rows), F32)] * 2
        + [pltpu.VMEM((edges, 128), jnp.int32)],
        compiler_params=PARAMS,
        cost_estimate=COST,
    )(core, heads, tails, negs, head_rows, query_grad, left, left_sums, right, rel_rows)


def from_behind(x, axis, by):
    size = lax.axis_size(axis)
    return lax.ppermute(x, axis, [(i, (i + by) % size) for i in range(size)])


def flipped(x, axis, bit):
    return lax.ppermute(x, axis, [(i, i ^ (1 << bit)) for i in range(lax.axis_size(axis))])


def other_core(x):
    return flipped(x, "blk", 0)


def across(x, place):
    sub_bits = lax.axis_size("sub").bit_length() - 1
    if place < sub_bits:
        return flipped(x, "sub", place)
    return flipped(x, "blk", place - sub_bits + 1)


def stream_orders():
    sub_bits = lax.axis_size("sub").bit_length() - 1
    bits = sub_bits + lax.axis_size("blk").bit_length() - 2
    x, y, z, far = sub_bits, sub_bits + 1, 0, 1
    rest = [p for p in range(bits) if p not in (x, y, z, far)]
    return [[x, y, z, far] + rest, [y, z, x, far] + rest, [z, x, far, y] + rest]


def row_spans(rows, parts):
    ends = [-(-rows * (i + 1) // (8 * parts)) * 8 for i in range(parts - 1)] + [rows]
    return list(zip([0] + ends[:-1], ends))


def shards(
    left_emb, left_state, right_emb, right_state, relation_emb, relation_state, hub_emb, hub_state,
    heads, relations, tails, negatives, hub_ids,
):
    components, half_width, row_count = left_emb.shape
    features = components * half_width
    rel_count, hub_count = relation_emb.shape[2], hub_emb.shape[2]
    left = left_emb.reshape(features, row_count)
    right = right_emb.reshape(features, row_count)
    left_sums = left_state.reshape(1, row_count)
    right_sums = right_state.reshape(1, row_count)
    buckets, edges = heads.shape
    hubs = hub_ids.shape[1]

    core_id = lax.axis_index("blk") % 2
    chip_id = (lax.axis_index("blk") // 2) * lax.axis_size("sub") + lax.axis_index("sub")
    core, chip = core_id.astype(jnp.int32).reshape(1), chip_id.astype(jnp.int32).reshape(1)
    hub_orders = stream_orders()
    rel_orders = hub_orders[:2]
    spans = row_spans(half_width, len(hub_orders))
    hub_pieces = [(0, s, low, high - low) for s, (low, high) in enumerate(spans)]
    rel_spans, rel_pieces = rel_layout(half_width, len(rel_orders))
    heights, rel_heights = [[high - low for low, high in x] for x in (spans, rel_spans)]
    stages = len(hub_orders[0])
    chunks = 1 << stages
    width, rel_width = hub_count // chunks, rel_count // chunks
    hub_lanes, rel_lanes = (0, hubs), (hubs, hubs + edges)

    def exchanged(parts, orders, step):
        return [across(x, order[step]) for x, order in zip(parts, orders)]

    def in_turn(first, then):
        return lax.optimization_barrier((first, then))

    ids = jnp.concatenate([hub_ids, relations], axis=1)
    far_ids = other_core(ids)
    hub_rows, rel_rows = gather_rows(
        hub_emb.reshape(features, hub_count), hub_ids, relation_emb.reshape(features, rel_count), relations
    )
    far_ids, rel_rows = in_turn(far_ids, rel_rows)
    keeps, fars = [], []
    for b in range(buckets - 1):
        if b > 0:
            right, right_sums = right[:features], right[features : features + 1]
        left, left_sums, right, keep, send = bucket_step(
            b, core, heads, tails, negatives, left, left_sums, right, right_sums, rel_rows, hub_rows
        )
        right = from_behind(right, "blk", 1)
        keeps.append(keep)
        fars.append(other_core(send))
    last = buckets - 1
    head_rows, query_grad, hub_keep, hub_send = hub_step(
        last, negatives.shape[1], core, heads, left, rel_rows, hub_rows
    )
    hub_far = other_core(hub_send)
    grads = lambda early, late, lanes: [(x, lanes) for x in early] + [(late, (0, late.shape[1]))]
    send, own = chunk_columns(
        functools.partial(hub_chunks_kernel, hub_orders, spans, hub_lanes),
        heights, width, chip, (ids, far_ids),
        grads(keeps, hub_keep, hub_lanes) + grads(fars, hub_far, hub_lanes), chunks,
    )
    got = exchanged(send, hub_orders, 0)
    left, right, rel_keep, rel_send = tables_step(
        last, hubs, core, heads, tails, negatives, head_rows, query_grad, left, left_sums, right, rel_rows
    )
    rel_far = other_core(rel_send)

    rel_keep, got = in_turn(rel_keep, got)
    send, own = halves(own, got)
    got = exchanged(send, hub_orders, 1)
    own, rel_far = in_turn(own, rel_far)
    rel_out, rel_own = chunk_columns(
        functools.partial(rel_chunks_kernel, rel_orders, rel_pieces, rel_count, rel_lanes),
        rel_heights, width, chip, (ids, far_ids),
        grads(keeps, rel_keep, rel_lanes) + grads(fars, rel_far, rel_lanes), chunks,
    )
    rel_got = exchanged(rel_out, rel_orders, 0)
    for step in range(2, stages):
        rel_own, got = in_turn(rel_own, got)
        send, own = halves(own, got)
        got = exchanged(send, hub_orders, step)
        own, rel_got = in_turn(own, rel_got)
        rel_out, rel_own = halves(rel_own, rel_got)
        rel_got = exchanged(rel_out, rel_orders, step - 1)

    late, rel_own, got = lax.optimization_barrier((jnp.stack([core_id, chip_id]), rel_own, got))
    cut = lambda x, span: lax.dynamic_slice(x, (late[0], 0, late[1] * span), (1, half_width, span))[0]
    cut_sums = lambda x, span: lax.dynamic_slice(x[None], (0, late[1] * span), (1, span))
    totals, squares = squares_of(own, got)
    far_squares = other_core(squares)
    totals, rel_got = in_turn(totals, rel_got)
    rel_out, rel_own = halves(rel_own, rel_got)
    rel_got = exchanged(rel_out, rel_orders, stages - 1)
    rel_own, far_squares = in_turn(rel_own, far_squares)
    have = call(
        functools.partial(hub_update_kernel, spans, features),
        [*totals, squares, far_squares, cut(hub_emb, width), cut_sums(hub_state, width)],
        [x.shape for x in totals],
    )
    got = exchanged(have, hub_orders, stages - 1)
    have, rel_got = in_turn(have, rel_got)
    rel_totals, rel_squares = squares_of(rel_own, rel_got)
    rel_far_squares = other_core(rel_squares)
    rel_totals, got = in_turn(rel_totals, got)
    have = join(have, got)
    got = exchanged(have, hub_orders, stages - 2)
    have, rel_far_squares = in_turn(have, rel_far_squares)
    rel_have = call(
        functools.partial(rel_update_kernel, len(rel_orders), rel_pieces, features),
        [*rel_totals, rel_squares, rel_far_squares, cut(relation_emb, rel_width), cut_sums(relation_state, rel_width)],
        [x.shape for x in rel_totals],
    )
    rel_got = exchanged(rel_have, rel_orders, stages - 1)
    for step in range(stages - 3, -1, -1):
        rel_have, got = in_turn(rel_have, got)
        have = join(have, got)
        got = exchanged(have, hub_orders, step)
        have, rel_got = in_turn(have, rel_got)
        rel_have = join(rel_have, rel_got)
        rel_got = exchanged(rel_have, rel_orders, step + 1)
    rel_have = join(rel_have, rel_got)
    rel_got = exchanged(rel_have, rel_orders, 0)

    mine, others = jnp.concatenate([chip, core]), jnp.concatenate([chip, 1 - core])
    shape = hub_emb.shape
    if width % 128 == 0:
        hub_new = copy_chunks(mine, have, 0, hub_orders, spans, shape, ())
        hub_new = copy_chunks(others, other_core(have), 0, hub_orders, spans, shape, (hub_new,))
        hub_new = copy_chunks(mine, got, 1, hub_orders, spans, shape, (hub_new,))
        hub_new = copy_chunks(others, other_core(got), 1, hub_orders, spans, shape, (hub_new,))
    else:
        hub_new = place_chunks(mine, have, got, hub_orders, hub_pieces, shape, ())
        hub_new = place_chunks(others, other_core(have), other_core(got), hub_orders, hub_pieces, shape, (hub_new,))
    shape = relation_emb.shape
    rel_new = place_chunks(mine, rel_have, rel_got, rel_orders, rel_pieces, shape, ())
    rel_new = place_chunks(
        others, other_core(rel_have), other_core(rel_got), rel_orders, rel_pieces, shape, (rel_new,)
    )
    return (
        left.reshape(components, half_width, row_count),
        right.reshape(components, half_width, row_count),
        rel_new,
        hub_new,
    )


def solution(mesh):
    both = ("blk", "sub")
    block, table, whole = P(None, None, both), P(None, both), P()
    return jax.shard_map(
        shards,
        mesh=mesh,
        in_specs=(block, P(both), block, P(both), whole, whole, whole, whole, table, table, table, table, table),
        out_specs=(block, block, whole, whole),
        check_vma=False,
    )
```

```python
import functools
import jax
import jax.numpy as jnp
from jax import lax
from jax.experimental import pallas as pl
from jax.experimental.pallas import tpu as pltpu
from jax.sharding import PartitionSpec as P

step_rate = 0.25
F32, BF16 = jnp.float32, jnp.bfloat16
NN = (((1,), (0,)), ((), ()))
NT = (((1,), (1,)), ((), ()))
TN = (((0,), (0,)), ((), ()))
VMEM = pl.BlockSpec(memory_space=pltpu.VMEM)
SMEM = pl.BlockSpec(memory_space=pltpu.SMEM)
PARAMS = pltpu.CompilerParams(vmem_limit_bytes=16 * 1024 * 1024)
GATHER_PARAMS = pltpu.CompilerParams(vmem_limit_bytes=32 * 1024 * 1024)
COST = pl.CostEstimate(flops=10000, bytes_accessed=10000, transcendentals=0)


def split(x):
    hi = x.astype(BF16)
    return hi, (x - hi.astype(F32)).astype(BF16)


def dot(a, b, dims):
    return lax.dot_general(a, b, dims, preferred_element_type=F32)


def dot3(a, b, dims):
    return dot(a[0], b[0], dims) + (dot(a[0], b[1], dims) + dot(a[1], b[0], dims))


def dot2(stacked, onehot, dims):
    half = stacked.shape[0] // 2
    both = dot(stacked, onehot, dims)
    return both[:half] + both[half:]


def stack(parts):
    return jnp.concatenate(parts, axis=0)


def stack_into(ref, x, lanes=slice(None)):
    rows, half = x.shape[0], ref.shape[0] // 2
    hi, lo = split(x)
    ref[:rows, lanes] = hi
    ref[half : half + rows, lanes] = lo
    if half > rows:
        blank = jnp.zeros((half - rows, x.shape[1]), BF16)
        ref[rows:half, lanes] = blank
        ref[half + rows :, lanes] = blank


def dot3_stacked(stacked, b, dims):
    half = stacked.shape[0] // 2
    both = dot(stacked, b[0], dims)
    return both[:half] + (both[half:] + dot(stacked[:half], b[1], dims))


def onehot(first, rows, idx):
    place = lax.broadcasted_iota(jnp.int32, (rows, idx.shape[1]), 0) + first
    return jnp.where(place == idx, 1.0, 0.0).astype(BF16)


def laid_out(idx):
    return jnp.concatenate([idx[b : b + 1] for b in range(idx.shape[0])], axis=1)


def gather_kernel(hub_steps, rel_steps, hub_idx, rel_idx, hub_ref, rel_ref, *refs):
    buckets = hub_idx.shape[0]
    ids_out, hub_outs, rel_outs = refs[0], refs[1 : 1 + buckets], refs[1 + buckets : 1 + 2 * buckets]
    hub_buf, rel_buf, stacked, sems = refs[1 + 2 * buckets :]
    hubs, edges = hub_idx.shape[1], rel_idx.shape[1]
    hub_tile, rel_tile = hub_buf.shape[2], rel_buf.shape[2]
    steps = [(hub_ref, hub_buf, hub_tile, k) for k in range(hub_steps)]
    steps += [(rel_ref, rel_buf, rel_tile, k) for k in range(rel_steps)]
    copies = [
        pltpu.make_async_copy(table.at[:, pl.ds(k * tile, tile)], buf.at[k % 2], sems.at[i])
        for i, (table, buf, tile, k) in enumerate(steps)
    ]
    copies[0].start()
    ids_out[:, :hubs] = hub_idx[...]
    ids_out[:, hubs:] = rel_idx[...]
    for i, (table, buf, tile, k) in enumerate(steps):
        if i + 1 < len(steps):
            copies[i + 1].start()
        idx, outs = (hub_idx, hub_outs) if table is hub_ref else (rel_idx, rel_outs)
        count = idx.shape[1]
        hot = onehot(k * tile, tile, laid_out(idx[...]))
        copies[i].wait()
        stack_into(stacked, buf[k % 2], slice(0, tile))
        part = dot2(stacked[:, :tile], hot, NN)
        for b, out in enumerate(outs):
            here = part[:, b * count : (b + 1) * count]
            out[...] = here if k == 0 else out[...] + here


def gather_rows(hub_table, hub_idx, rel_table, rel_idx):
    features = hub_table.shape[0]
    hub_steps, rel_steps = 4, 2
    hub_tile, rel_tile = hub_table.shape[1] // hub_steps, rel_table.shape[1] // rel_steps
    buckets, hubs = hub_idx.shape
    edges = rel_idx.shape[1]
    shapes = [(features, hubs)] * buckets + [(features, edges)] * buckets
    anywhere = pl.BlockSpec(memory_space=pl.ANY)
    out = pl.pallas_call(
        functools.partial(gather_kernel, hub_steps, rel_steps),
        in_specs=[VMEM, VMEM, anywhere, anywhere],
        out_specs=[VMEM] * (1 + len(shapes)),
        out_shape=[jax.ShapeDtypeStruct((buckets, hubs + edges), jnp.int32)]
        + [jax.ShapeDtypeStruct(shape, F32) for shape in shapes],
        scratch_shapes=[
            pltpu.VMEM((2, features, hub_tile), F32),
            pltpu.VMEM((2, features, rel_tile), F32),
            pltpu.VMEM((2 * features, max(hub_tile, rel_tile)), BF16),
            pltpu.SemaphoreType.DMA((hub_steps + rel_steps,)),
        ],
        compiler_params=GATHER_PARAMS,
        cost_estimate=COST,
    )(hub_idx, rel_idx, hub_table, rel_table)
    return out[0], out[1 : 1 + buckets], out[1 + buckets :]


def spread_bits(place, order):
    bits = len(order)
    return sum((((place >> p) & 1) << (bits - 1 - i)) for i, p in enumerate(order))


def gather_bits(index, order):
    bits = len(order)
    return sum((((index >> (bits - 1 - i)) & 1) << p) for i, p in enumerate(order))


def load_columns(id_refs, id_lanes, grad_refs, idx_down, stacked):
    low, high = id_lanes
    idx = jnp.concatenate([laid_out(ref[:, low:high]) for ref in id_refs], axis=1)
    idx_down[...] = jnp.transpose(jnp.broadcast_to(idx, (128, idx.shape[1])))
    at = 0
    for ref, (low, high) in grad_refs:
        width = high - low
        stack_into(stacked, ref[:, low:high], slice(at, at + width))
        at += width


def onehot_across(idx_down, targets):
    width = targets.shape[1]
    idx = idx_down[...]
    wide = jnp.concatenate([idx] * -(-width // 128), axis=1)[:, :width]
    return jnp.where(wide == targets, 1.0, 0.0).astype(BF16)


def out_for(place, order, sends, keeps, s):
    index = spread_bits(place, order)
    half = keeps[s].shape[0]
    return sends[s].at[index - half] if index >= half else keeps[s].at[index]


def chunk_refs(orders, grad_lanes, refs):
    ids, refs = refs[:2], refs[2:]
    grads, refs = list(zip(refs, grad_lanes)), refs[len(grad_lanes) :]
    streams = len(orders)
    return ids, grads, refs[:streams], refs[streams : 2 * streams], refs[2 * streams :]


def hub_chunks_kernel(orders, spans, id_lanes, grad_lanes, chip_ref, *refs):
    ids, grads, sends, keeps, (idx_down, stacked) = chunk_refs(orders, grad_lanes, refs)
    load_columns(ids, id_lanes, grads, idx_down, stacked)
    chunks, width = 2 * keeps[0].shape[0], keeps[0].shape[2]
    lane = lax.broadcasted_iota(jnp.int32, (1, width), 1)
    for place in range(chunks):
        hot = onehot_across(idx_down, lane + (chip_ref[0] ^ place) * width)
        chunk = dot2(stacked[...], hot, NN)
        for s, (low, high) in enumerate(spans):
            out_for(place, orders[s], sends, keeps, s)[...] = chunk[low:high]


def rel_layout(half_width, streams):
    blocks = row_spans(half_width, 3)
    spans = row_spans(max(high - low for low, high in blocks), streams)
    pieces = []
    for block, (low, high) in enumerate(blocks):
        for s, (first, end) in enumerate(spans):
            count = min(end, high - low) - first
            if count > 0:
                pieces.append((block, s, low + first, first, count))
    return spans, pieces


def rel_chunks_kernel(orders, pieces, rows, id_lanes, grad_lanes, chip_ref, *refs):
    ids, grads, sends, keeps, (idx_down, stacked) = chunk_refs(orders, grad_lanes, refs)
    load_columns(ids, id_lanes, grads, idx_down, stacked)
    for ref in [*sends, *keeps]:
        ref[...] = jnp.zeros_like(ref)
    chunks, lanes = 2 * keeps[0].shape[0], keeps[0].shape[2]
    width = rows // chunks
    group = lanes // width
    lane = lax.broadcasted_iota(jnp.int32, (1, lanes), 1)
    for first in range(0, chunks, group):
        targets = jnp.full((1, lanes), -1, jnp.int32)
        places = range(first, min(first + group, chunks))
        for slot, place in enumerate(places):
            here = (lane >= slot * width) & (lane < (slot + 1) * width)
            targets = jnp.where(here, lane + ((chip_ref[0] ^ place) * width - slot * width), targets)
        dense = dot2(stacked[...], onehot_across(idx_down, targets), NN)
        for slot, place in enumerate(places):
            chunk = dense[:, slot * width : (slot + 1) * width]
            for block, s, low, unused, count in pieces:
                out = out_for(place, orders[s], sends, keeps, s)
                out[:count, block * width : (block + 1) * width] = chunk[low : low + count]


def chunk_columns(kernel, heights, lanes, chip, ids, grads, chunks):
    half_width = grads[0][0].shape[0]
    grad_lanes = [lanes_of for unused, lanes_of in grads]
    count = sum(high - low for low, high in grad_lanes)
    shapes = [jax.ShapeDtypeStruct((chunks // 2, height, lanes), F32) for height in heights] * 2
    out = pl.pallas_call(
        functools.partial(kernel, grad_lanes),
        in_specs=[SMEM] + [VMEM] * (2 + len(grads)),
        out_specs=[VMEM] * len(shapes),
        out_shape=shapes,
        scratch_shapes=[
            pltpu.VMEM((count, 128), jnp.int32),
            pltpu.VMEM((2 * (-(-half_width // 16) * 16), count), BF16),
        ],
        compiler_params=PARAMS,
        cost_estimate=COST,
    )(chip, *ids, *[g for g, unused in grads])
    return out[: len(heights)], out[len(heights) :]


def call(kernel, ins, shapes):
    return pl.pallas_call(
        kernel,
        in_specs=[VMEM] * len(ins),
        out_specs=[VMEM] * len(shapes),
        out_shape=[jax.ShapeDtypeStruct(shape, F32) for shape in shapes],
        compiler_params=PARAMS,
        cost_estimate=COST,
    )(*ins)


def sums_kernel(*refs):
    streams = len(refs) // 4
    own, got, sends, keeps = [refs[i * streams : (i + 1) * streams] for i in range(4)]
    for s in range(streams):
        half = sends[s].shape[0]
        sends[s][...] = own[s][half:] + got[s][half:]
        keeps[s][...] = own[s][:half] + got[s][:half]


def halves(own, got):
    shapes = [(x.shape[0] // 2,) + x.shape[1:] for x in own]
    out = call(sums_kernel, [*own, *got], shapes * 2)
    return out[: len(shapes)], out[len(shapes) :]


def join_kernel(*refs):
    streams = len(refs) // 3
    for s in range(streams):
        own, got, out = refs[s], refs[streams + s], refs[2 * streams + s]
        count = own.shape[0]
        out[:count] = own[...]
        out[count:] = got[...]


def join(own, got):
    return call(join_kernel, [*own, *got], [(2 * x.shape[0],) + x.shape[1:] for x in own])


def squares_kernel(*refs):
    streams = len(refs) // 3
    own, got, totals, out = [refs[i * streams : (i + 1) * streams] for i in range(3)] + [refs[-1]]
    squares = jnp.zeros(out.shape, F32)
    for s in range(streams):
        total = own[s][0] + got[s][0]
        totals[s][0] = total
        squares += jnp.sum(total * total, axis=0, keepdims=True)
    out[...] = squares


def squares_of(own, got):
    *totals, squares = call(squares_kernel, [*own, *got], [x.shape for x in own] + [(1, own[0].shape[2])])
    return totals, squares


def hub_update_kernel(spans, features, *refs):
    streams = len(spans)
    totals, news = refs[:streams], refs[-streams:]
    mine, other, table_ref, sums_ref = refs[streams:-streams]
    scale = step_rate / jnp.sqrt(sums_ref[...] + (mine[...] + other[...]) * (1.0 / features))
    for s, (low, high) in enumerate(spans):
        news[s][0] = table_ref[low:high] - totals[s][0] * scale


def rel_update_kernel(streams, pieces, features, *refs):
    totals, news = refs[:streams], refs[-streams:]
    mine, other, table_ref, sums_ref = refs[streams:-streams]
    width = table_ref.shape[1]
    squares = mine[...] + other[...]
    squares = sum(squares[:, b * width : (b + 1) * width] for b in range(3))
    scale = step_rate / jnp.sqrt(sums_ref[...] + squares * (1.0 / features))
    for new in news:
        new[...] = jnp.zeros_like(new)
    for block, s, low, unused, count in pieces:
        lanes = slice(block * width, (block + 1) * width)
        news[s][0, :count, lanes] = table_ref[low : low + count] - totals[s][0, :count, lanes] * scale


def combine_kernel(spans, *refs):
    streams, out = len(spans), refs[-1]
    for i, ref in enumerate(refs[:-1]):
        low, high = spans[i % streams]
        count = ref.shape[0]
        first = (i // streams) * count
        out[first : first + count, low:high] = ref[...]


def combine(spans, *groups):
    parts = [x for group in groups for x in group]
    count = sum(group[0].shape[0] for group in groups)
    return call(functools.partial(combine_kernel, spans), parts, [(count, spans[-1][1], parts[0].shape[2])])[0]


def place_kernel(orders, pieces, spot_ref, all_ref, *refs):
    out_ref = refs[-1]
    chunks = all_ref.shape[0]
    width = out_ref.shape[2] // chunks
    for chunk in range(chunks):
        place = spot_ref[0] ^ chunk
        values = [all_ref[spread_bits(place, order)] for order in orders]
        for block, s, row, source, count in pieces:
            part = values[s][source : source + count, block * width : (block + 1) * width]
            out_ref[0, row : row + count, chunk * width : (chunk + 1) * width] = part


def place_chunks(spot, parts, orders, pieces, shape, earlier):
    kept = [pl.BlockSpec(memory_space=pl.ANY)] * len(earlier)
    return pl.pallas_call(
        functools.partial(place_kernel, orders, pieces),
        grid_spec=pltpu.PrefetchScalarGridSpec(
            num_scalar_prefetch=1,
            grid=(1,),
            in_specs=[pl.BlockSpec(memory_space=pltpu.VMEM)] + kept,
            out_specs=pl.BlockSpec((1,) + shape[1:], lambda i, spot: (spot[1], 0, 0)),
        ),
        out_shape=jax.ShapeDtypeStruct(shape, F32),
        input_output_aliases={2: 0} if earlier else {},
        compiler_params=PARAMS,
        cost_estimate=pl.CostEstimate(flops=0, bytes_accessed=4 * shape[1] * shape[2], transcendentals=0),
    )(spot, parts, *earlier)


def copy_kernel(orders, spans, upper, spot_ref, *refs):
    out_ref, sems = refs[-2], refs[-1]
    copies = []
    for s, (low, high) in enumerate(spans):
        part = refs[s] if upper else refs[0].at[:, pl.ds(low, high - low)]
        half, width = part.shape[0], part.shape[2]
        for index in range(half):
            chunk = spot_ref[0] ^ gather_bits(index + half * upper, orders[s])
            lanes = pl.ds(pl.multiple_of(chunk * width, width), width)
            target = out_ref.at[spot_ref[1], pl.ds(low, high - low), lanes]
            copies.append(pltpu.make_async_copy(part.at[index], target, sems.at[len(copies)]))
    for copy in copies:
        copy.start()
    for copy in copies:
        copy.wait()


def copy_chunks(spot, parts, upper, orders, spans, shape, earlier):
    anywhere = pl.BlockSpec(memory_space=pl.ANY)
    return pl.pallas_call(
        functools.partial(copy_kernel, orders, spans, upper),
        in_specs=[SMEM] + [anywhere] * (len(parts) + len(earlier)),
        out_specs=anywhere,
        out_shape=jax.ShapeDtypeStruct(shape, F32),
        scratch_shapes=[pltpu.SemaphoreType.DMA((len(spans) * parts[0].shape[0],))],
        input_output_aliases={1 + len(parts): 0} if earlier else {},
        compiler_params=PARAMS,
        cost_estimate=pl.CostEstimate(flops=0, bytes_accessed=4 * shape[1] * shape[2], transcendentals=0),
    )(spot, *parts, *earlier)


def adagrad(table, state, grads):
    new_state = state + jnp.sum(grads * grads, axis=0, keepdims=True) * (1.0 / grads.shape[0])
    return table - grads * (step_rate / jnp.sqrt(new_state)), new_state


def keep_and_send(core, first, second):
    return jnp.where(core == 0, first, second), jnp.where(core == 0, second, first)


def table_counts(rows, negs, weight):
    place = lax.broadcasted_iota(jnp.int32, (rows, negs.shape[1]), 0)
    return jnp.sum(jnp.where(place == negs, weight, 0.0), axis=1, keepdims=True)


def turned(x, r, half):
    x0, x1, r0, r1 = x[:half], x[half:], r[:half], r[half:]
    return jnp.concatenate([x0 * r0 - x1 * r1, x0 * r1 + x1 * r0], axis=0)


def turned_back(x, r, half):
    x0, x1, r0, r1 = x[:half], x[half:], r[:half], r[half:]
    return x0 * r0 + x1 * r1, x1 * r0 - x0 * r1


EDGE_TILE = 256


def edge_span(step):
    return pl.ds(pl.multiple_of(step * EDGE_TILE, EDGE_TILE), EDGE_TILE)


def bucket_kernel(
    bucket, core_ref, heads_ref, tails_ref, negs_ref, left_ref, left_sums_ref, right_ref, right_sums_ref, rel_ref, hub_ref,
    left_out, left_sums_out, right_out, keep_out, send_out,
    left_parts, both_parts, left_grad, both_grad,
):
    features, rows = left_ref.shape
    half = features // 2
    core = core_ref[0]
    edges = heads_ref.shape[1]
    hubs = keep_out.shape[1] - edges
    at = slice(bucket, bucket + 1)
    weight = 1.0 / (negs_ref.shape[1] + hubs)
    counts = table_counts(rows, negs_ref[at], weight)
    stack_into(left_parts, left_ref[...])
    stack_into(both_parts, right_ref[...], slice(0, rows))
    stack_into(both_parts, hub_ref[...], slice(rows, rows + hubs))
    left_grad[...] = jnp.zeros_like(left_grad)
    both_grad[...] = jnp.zeros_like(both_grad)

    @pl.loop(0, edges // EDGE_TILE)
    def _(step):
        span = edge_span(step)
        tail_here = lax.broadcasted_iota(jnp.int32, (rows, EDGE_TILE), 0) == tails_ref[at, span]
        head_hot = onehot(0, rows, heads_ref[at, span])
        h = dot2(left_parts[...], head_hot, NN)
        r = rel_ref[:, span]
        q = split(turned(h, r, half))
        scores = dot3((both_parts[:features], both_parts[features:]), q, TN)
        chance = jax.nn.sigmoid(scores[:rows])
        coef = jnp.concatenate(
            [
                counts * chance + jnp.where(tail_here, chance - 1.0, 0.0),
                weight * jax.nn.sigmoid(scores[rows:]),
            ],
            axis=0,
        )
        coef = split(coef)
        dq = dot3_stacked(both_parts[...], coef, NN)
        both_grad[...] += dot3_stacked(stack(q), coef, NT)
        dh = jnp.concatenate(turned_back(dq, r, half), axis=0)
        left_grad[...] += dot2(stack(split(dh)), head_hot, NT)
        out_span = pl.ds(pl.multiple_of(hubs + step * EDGE_TILE, 128), EDGE_TILE)
        keep_out[:, out_span], send_out[:, out_span] = keep_and_send(core, *turned_back(dq, h, half))

    left_out[...], left_sums_out[...] = adagrad(left_ref[...], left_sums_ref[...], left_grad[...])
    new_right, new_sums = adagrad(right_ref[...], right_sums_ref[...], both_grad[:, :rows])
    right_out[:features] = new_right
    right_out[features:] = jnp.broadcast_to(new_sums, (right_out.shape[0] - features, rows))
    keep_out[:, :hubs], send_out[:, :hubs] = keep_and_send(core, both_grad[:half, rows:], both_grad[half:, rows:])


def bucket_step(bucket, core, heads, tails, negs, left, left_sums, right, right_sums, rel_rows, hub_rows):
    features, rows = left.shape
    edges, hubs = heads.shape[1], hub_rows.shape[1]
    width = rows + hubs
    shapes = [(features, rows), (1, rows), (features + 8, rows)] + [(features // 2, hubs + edges)] * 2
    return pl.pallas_call(
        functools.partial(bucket_kernel, bucket),
        in_specs=[SMEM] + [VMEM] * 9,
        out_specs=[VMEM] * 5,
        out_shape=[jax.ShapeDtypeStruct(shape, F32) for shape in shapes],
        scratch_shapes=[
            pltpu.VMEM((2 * features, rows), BF16),
            pltpu.VMEM((2 * features, width), BF16),
            pltpu.VMEM((features, rows), F32),
            pltpu.VMEM((features, width), F32),
        ],
        compiler_params=PARAMS,
        cost_estimate=COST,
    )(core, heads, tails, negs, left, left_sums, right, right_sums, rel_rows, hub_rows)


def hub_kernel(
    bucket, negatives, core_ref, heads_ref, left_ref, rel_ref, hub_ref,
    query_grad, hub_keep, hub_send,
    left_parts, hub_parts, hub_grad,
):
    features, rows = left_ref.shape
    half = features // 2
    edges, hubs = heads_ref.shape[1], hub_keep.shape[1]
    at = slice(bucket, bucket + 1)
    weight = 1.0 / (negatives + hubs)
    stack_into(left_parts, left_ref[...])
    stack_into(hub_parts, hub_ref[...])
    hub_grad[...] = jnp.zeros_like(hub_grad)

    @pl.loop(0, edges // EDGE_TILE)
    def _(step):
        span = edge_span(step)
        head_hot = onehot(0, rows, heads_ref[at, span])
        h = dot2(left_parts[...], head_hot, NN)
        q = split(turned(h, rel_ref[:, span], half))
        coef = split(weight * jax.nn.sigmoid(dot3((hub_parts[:features], hub_parts[features:]), q, TN)))
        query_grad[:, span] = dot3_stacked(hub_parts[...], coef, NN)
        hub_grad[...] += dot3_stacked(stack(q), coef, NT)

    hub_keep[...], hub_send[...] = keep_and_send(core_ref[0], hub_grad[:half], hub_grad[half:])


def hub_step(bucket, negatives, core, heads, left, rel_rows, hub_rows):
    features, rows = left.shape
    edges, hubs = heads.shape[1], hub_rows.shape[1]
    shapes = [(features, edges)] + [(features // 2, hubs)] * 2
    return pl.pallas_call(
        functools.partial(hub_kernel, bucket, negatives),
        in_specs=[SMEM] + [VMEM] * 4,
        out_specs=[VMEM] * 3,
        out_shape=[jax.ShapeDtypeStruct(shape, F32) for shape in shapes],
        scratch_shapes=[
            pltpu.VMEM((2 * features, rows), BF16),
            pltpu.VMEM((2 * features, hubs), BF16),
            pltpu.VMEM((features, hubs), F32),
        ],
        compiler_params=PARAMS,
        cost_estimate=COST,
    )(core, heads, left, rel_rows, hub_rows)


def tables_kernel(
    bucket, hubs, core_ref, heads_ref, tails_ref, negs_ref, query_grad,
    left_ref, left_sums_ref, right_ref, rel_ref,
    left_out, right_out, rel_keep, rel_send,
    left_parts, right_parts, left_grad, right_grad,
):
    features, rows = left_ref.shape
    half = features // 2
    edges = heads_ref.shape[1]
    at = slice(bucket, bucket + 1)
    core = core_ref[0]
    counts = table_counts(rows, negs_ref[at], 1.0 / (negs_ref.shape[1] + hubs))
    stack_into(left_parts, left_ref[...])
    stack_into(right_parts, right_ref[:features])
    left_grad[...] = jnp.zeros_like(left_grad)
    right_grad[...] = jnp.zeros_like(right_grad)

    @pl.loop(0, edges // EDGE_TILE)
    def _(step):
        span = edge_span(step)
        tail_here = lax.broadcasted_iota(jnp.int32, (rows, EDGE_TILE), 0) == tails_ref[at, span]
        head_hot = onehot(0, rows, heads_ref[at, span])
        h = dot2(left_parts[...], head_hot, NN)
        r = rel_ref[:, span]
        q = split(turned(h, r, half))
        chance = jax.nn.sigmoid(dot3((right_parts[:features], right_parts[features:]), q, TN))
        coef = split(counts * chance + jnp.where(tail_here, chance - 1.0, 0.0))
        dq = dot3_stacked(right_parts[...], coef, NN) + query_grad[:, span]
        right_grad[...] += dot3_stacked(stack(q), coef, NT)
        rel_keep[:, span], rel_send[:, span] = keep_and_send(core, *turned_back(dq, h, half))
        dh = jnp.concatenate(turned_back(dq, r, half), axis=0)
        left_grad[...] += dot2(stack(split(dh)), head_hot, NT)

    left_out[...], unused = adagrad(left_ref[...], left_sums_ref[...], left_grad[...])
    right_out[...], unused = adagrad(right_ref[:features], right_ref[features : features + 1], right_grad[...])


def tables_step(bucket, hubs, core, heads, tails, negs, query_grad, left, left_sums, right, rel_rows):
    features, rows = left.shape
    edges = heads.shape[1]
    shapes = [(features, rows)] * 2 + [(features // 2, edges)] * 2
    return pl.pallas_call(
        functools.partial(tables_kernel, bucket, hubs),
        in_specs=[SMEM] + [VMEM] * 8,
        out_specs=[VMEM] * 4,
        out_shape=[jax.ShapeDtypeStruct(shape, F32) for shape in shapes],
        scratch_shapes=[pltpu.VMEM((2 * features, rows), BF16)] * 2
        + [pltpu.VMEM((features, rows), F32)] * 2,
        compiler_params=PARAMS,
        cost_estimate=COST,
    )(core, heads, tails, negs, query_grad, left, left_sums, right, rel_rows)


def from_behind(x, axis, by):
    size = lax.axis_size(axis)
    return lax.ppermute(x, axis, [(i, (i + by) % size) for i in range(size)])


def flipped(x, axis, bit):
    return lax.ppermute(x, axis, [(i, i ^ (1 << bit)) for i in range(lax.axis_size(axis))])


def other_core(x):
    return flipped(x, "blk", 0)


def across(x, place):
    sub_bits = lax.axis_size("sub").bit_length() - 1
    if place < sub_bits:
        return flipped(x, "sub", place)
    return flipped(x, "blk", place - sub_bits + 1)


def stream_orders():
    sub_bits = lax.axis_size("sub").bit_length() - 1
    bits = sub_bits + lax.axis_size("blk").bit_length() - 2
    x, y, z, far = sub_bits, sub_bits + 1, 0, 1
    rest = [p for p in range(bits) if p not in (x, y, z, far)]
    return [[x, y, z, far] + rest, [y, z, x, far] + rest, [z, x, far, y] + rest]


def row_spans(rows, parts):
    ends = [-(-rows * (i + 1) // (8 * parts)) * 8 for i in range(parts - 1)] + [rows]
    return list(zip([0] + ends[:-1], ends))


def shards(
    left_emb, left_state, right_emb, right_state, relation_emb, relation_state, hub_emb, hub_state,
    heads, relations, tails, negatives, hub_ids,
):
    components, half_width, row_count = left_emb.shape
    features = components * half_width
    rel_count, hub_count = relation_emb.shape[2], hub_emb.shape[2]
    left = left_emb.reshape(features, row_count)
    right = right_emb.reshape(features, row_count)
    left_sums = left_state.reshape(1, row_count)
    right_sums = right_state.reshape(1, row_count)
    buckets, edges = heads.shape
    hubs = hub_ids.shape[1]

    core_id = lax.axis_index("blk") % 2
    chip_id = (lax.axis_index("blk") // 2) * lax.axis_size("sub") + lax.axis_index("sub")
    core, chip = core_id.astype(jnp.int32).reshape(1), chip_id.astype(jnp.int32).reshape(1)
    hub_orders = stream_orders()
    rel_orders = hub_orders[:2]
    spans = row_spans(half_width, len(hub_orders))
    hub_pieces = [(0, s, low, low, high - low) for s, (low, high) in enumerate(spans)]
    rel_spans, rel_pieces = rel_layout(half_width, len(rel_orders))
    heights, rel_heights = [[high - low for low, high in x] for x in (spans, rel_spans)]
    stages = len(hub_orders[0])
    chunks = 1 << stages
    width, rel_width = hub_count // chunks, rel_count // chunks
    hub_lanes, rel_lanes = (0, hubs), (hubs, hubs + edges)

    def exchanged(parts, orders, step):
        return [across(x, order[step]) for x, order in zip(parts, orders)]

    def in_turn(first, then):
        return lax.optimization_barrier((first, then))

    ids, hub_rows, rel_rows = gather_rows(
        hub_emb.reshape(features, hub_count), hub_ids, relation_emb.reshape(features, rel_count), relations
    )
    far_ids = other_core(ids)
    keeps, fars = [], []
    for b in range(buckets - 1):
        if b > 0:
            right, right_sums = right[:features], right[features : features + 1]
        left, left_sums, right, keep, send = bucket_step(
            b, core, heads, tails, negatives, left, left_sums, right, right_sums, rel_rows[b], hub_rows[b]
        )
        right = from_behind(right, "blk", 1)
        keeps.append(keep)
        fars.append(other_core(send))
    last = buckets - 1
    query_grad, hub_keep, hub_send = hub_step(
        last, negatives.shape[1], core, heads, left, rel_rows[last], hub_rows[last]
    )
    hub_far = other_core(hub_send)
    grads = lambda early, late, lanes: [(x, lanes) for x in early] + [(late, (0, late.shape[1]))]
    send, own = chunk_columns(
        functools.partial(hub_chunks_kernel, hub_orders, spans, hub_lanes),
        heights, width, chip, (ids, far_ids),
        grads(keeps, hub_keep, hub_lanes) + grads(fars, hub_far, hub_lanes), chunks,
    )
    got = exchanged(send, hub_orders, 0)
    left, right, rel_keep, rel_send = tables_step(
        last, hubs, core, heads, tails, negatives, query_grad, left, left_sums, right, rel_rows[last]
    )
    rel_far = other_core(rel_send)

    rel_keep, got = in_turn(rel_keep, got)
    send, own = halves(own, got)
    got = exchanged(send, hub_orders, 1)
    own, rel_far = in_turn(own, rel_far)
    rel_out, rel_own = chunk_columns(
        functools.partial(rel_chunks_kernel, rel_orders, rel_pieces, rel_count, rel_lanes),
        rel_heights, width, chip, (ids, far_ids),
        grads(keeps, rel_keep, rel_lanes) + grads(fars, rel_far, rel_lanes), chunks,
    )
    rel_got = exchanged(rel_out, rel_orders, 0)
    for step in range(2, stages):
        rel_own, got = in_turn(rel_own, got)
        send, own = halves(own, got)
        got = exchanged(send, hub_orders, step)
        own, rel_got = in_turn(own, rel_got)
        rel_out, rel_own = halves(rel_own, rel_got)
        rel_got = exchanged(rel_out, rel_orders, step - 1)

    late, rel_own, got = lax.optimization_barrier((jnp.stack([core_id, chip_id]), rel_own, got))
    cut = lambda x, span: lax.dynamic_slice(x, (late[0], 0, late[1] * span), (1, half_width, span))[0]
    cut_sums = lambda x, span: lax.dynamic_slice(x[None], (0, late[1] * span), (1, span))
    totals, squares = squares_of(own, got)
    far_squares = other_core(squares)
    totals, rel_got = in_turn(totals, rel_got)
    rel_out, rel_own = halves(rel_own, rel_got)
    rel_got = exchanged(rel_out, rel_orders, stages - 1)
    rel_own, far_squares = in_turn(rel_own, far_squares)
    have = call(
        functools.partial(hub_update_kernel, spans, features),
        [*totals, squares, far_squares, cut(hub_emb, width), cut_sums(hub_state, width)],
        [x.shape for x in totals],
    )
    got = exchanged(have, hub_orders, stages - 1)
    have, rel_got = in_turn(have, rel_got)
    rel_totals, rel_squares = squares_of(rel_own, rel_got)
    rel_far_squares = other_core(rel_squares)
    rel_totals, got = in_turn(rel_totals, got)
    have = join(have, got)
    got = exchanged(have, hub_orders, stages - 2)
    have, rel_far_squares = in_turn(have, rel_far_squares)
    rel_have = call(
        functools.partial(rel_update_kernel, len(rel_orders), rel_pieces, features),
        [*rel_totals, rel_squares, rel_far_squares, cut(relation_emb, rel_width), cut_sums(relation_state, rel_width)],
        [x.shape for x in rel_totals],
    )
    rel_got = exchanged(rel_have, rel_orders, stages - 1)
    rel_step, step = stages - 2, stages - 3
    turns = ["rel", "hub"] * (stages - 3) + ["rel"] * 2 + ["hub"]
    for turn in turns:
        if turn == "rel":
            have, rel_got = in_turn(have, rel_got)
            rel_have = join(rel_have, rel_got)
            rel_got = exchanged(rel_have, rel_orders, rel_step)
            rel_step -= 1
        else:
            rel_have, got = in_turn(rel_have, got)
            near = combine(spans, have, got)
            have = join(have, got)
            got = exchanged(have, hub_orders, step)
            step -= 1

    mine, others = jnp.concatenate([chip, core]), jnp.concatenate([chip, 1 - core])
    shape = hub_emb.shape
    if width % 128 == 0:
        hub_new = copy_chunks(mine, [near], 0, hub_orders, spans, shape, ())
        hub_new = copy_chunks(others, [other_core(near)], 0, hub_orders, spans, shape, (hub_new,))
        hub_new = copy_chunks(mine, got, 1, hub_orders, spans, shape, (hub_new,))
        hub_new = copy_chunks(others, other_core(got), 1, hub_orders, spans, shape, (hub_new,))
    else:
        whole = combine(spans, have, got)
        hub_new = place_chunks(mine, whole, hub_orders, hub_pieces, shape, ())
        hub_new = place_chunks(others, other_core(whole), hub_orders, hub_pieces, shape, (hub_new,))
    shape = relation_emb.shape
    rel_whole = combine(rel_spans, rel_have, rel_got)
    rel_new = place_chunks(mine, rel_whole, rel_orders, rel_pieces, shape, ())
    rel_new = place_chunks(others, other_core(rel_whole), rel_orders, rel_pieces, shape, (rel_new,))
    return (
        left.reshape(components, half_width, row_count),
        right.reshape(components, half_width, row_count),
        rel_new,
        hub_new,
    )


def solution(mesh):
    both = ("blk", "sub")
    block, table, whole = P(None, None, both), P(None, both), P()
    return jax.shard_map(
        shards,
        mesh=mesh,
        in_specs=(block, P(both), block, P(both), whole, whole, whole, whole, table, table, table, table, table),
        out_specs=(block, block, whole, whole),
        check_vma=False,
    )
```

```python
import functools
import jax
import jax.numpy as jnp
from jax import lax
from jax.experimental import pallas as pl
from jax.experimental.pallas import tpu as pltpu
from jax.sharding import PartitionSpec as P

step_rate = 0.25
F32, BF16 = jnp.float32, jnp.bfloat16
NN = (((1,), (0,)), ((), ()))
NT = (((1,), (1,)), ((), ()))
TN = (((0,), (0,)), ((), ()))
VMEM = pl.BlockSpec(memory_space=pltpu.VMEM)
SMEM = pl.BlockSpec(memory_space=pltpu.SMEM)
PARAMS = pltpu.CompilerParams(vmem_limit_bytes=16 * 1024 * 1024)
GATHER_PARAMS = pltpu.CompilerParams(vmem_limit_bytes=32 * 1024 * 1024)
HBM = pl.BlockSpec(memory_space=pltpu.HBM)
COST = pl.CostEstimate(flops=10000, bytes_accessed=10000, transcendentals=0)


def split(x):
    hi = x.astype(BF16)
    return hi, (x - hi.astype(F32)).astype(BF16)


def dot(a, b, dims):
    return lax.dot_general(a, b, dims, preferred_element_type=F32)


def dot3(a, b, dims):
    return dot(a[0], b[0], dims) + (dot(a[0], b[1], dims) + dot(a[1], b[0], dims))


def dot2(stacked, onehot, dims):
    half = stacked.shape[0] // 2
    both = dot(stacked, onehot, dims)
    return both[:half] + both[half:]


def stack(parts):
    return jnp.concatenate(parts, axis=0)


def stack_into(ref, x, lanes=slice(None)):
    rows, half = x.shape[0], ref.shape[0] // 2
    hi, lo = split(x)
    ref[:rows, lanes] = hi
    ref[half : half + rows, lanes] = lo
    if half > rows:
        blank = jnp.zeros((half - rows, x.shape[1]), BF16)
        ref[rows:half, lanes] = blank
        ref[half + rows :, lanes] = blank


def dot3_stacked(stacked, b, dims):
    half = stacked.shape[0] // 2
    both = dot(stacked, b[0], dims)
    return both[:half] + (both[half:] + dot(stacked[:half], b[1], dims))


def onehot(first, rows, idx):
    place = lax.broadcasted_iota(jnp.int32, (rows, idx.shape[1]), 0) + first
    return jnp.where(place == idx, 1.0, 0.0).astype(BF16)


def laid_out(idx):
    return jnp.concatenate([idx[b : b + 1] for b in range(idx.shape[0])], axis=1)


def gather_kernel(hub_steps, rel_steps, hub_idx, rel_idx, hub_ref, rel_ref, *refs):
    buckets = hub_idx.shape[0]
    ids_out, hub_outs, rel_outs = refs[0], refs[1 : 1 + buckets], refs[1 + buckets : 1 + 2 * buckets]
    hub_buf, rel_buf, stacked, sems = refs[1 + 2 * buckets :]
    hubs, edges = hub_idx.shape[1], rel_idx.shape[1]
    hub_tile, rel_tile = hub_buf.shape[2], rel_buf.shape[2]
    steps = [(hub_ref, hub_buf, hub_tile, k) for k in range(hub_steps)]
    steps += [(rel_ref, rel_buf, rel_tile, k) for k in range(rel_steps)]
    copies = [
        pltpu.make_async_copy(table.at[:, pl.ds(k * tile, tile)], buf.at[k % 2], sems.at[i])
        for i, (table, buf, tile, k) in enumerate(steps)
    ]
    copies[0].start()
    ids_out[:, :hubs] = hub_idx[...]
    ids_out[:, hubs:] = rel_idx[...]
    for i, (table, buf, tile, k) in enumerate(steps):
        if i + 1 < len(steps):
            copies[i + 1].start()
        idx, outs = (hub_idx, hub_outs) if table is hub_ref else (rel_idx, rel_outs)
        count = idx.shape[1]
        hot = onehot(k * tile, tile, laid_out(idx[...]))
        copies[i].wait()
        stack_into(stacked, buf[k % 2], slice(0, tile))
        part = dot2(stacked[:, :tile], hot, NN)
        for b, out in enumerate(outs):
            here = part[:, b * count : (b + 1) * count]
            out[...] = here if k == 0 else out[...] + here


def gather_rows(hub_table, hub_idx, rel_table, rel_idx):
    features = hub_table.shape[0]
    hub_steps, rel_steps = 4, 2
    hub_tile, rel_tile = hub_table.shape[1] // hub_steps, rel_table.shape[1] // rel_steps
    buckets, hubs = hub_idx.shape
    edges = rel_idx.shape[1]
    shapes = [(features, hubs)] * buckets + [(features, edges)] * buckets
    out = pl.pallas_call(
        functools.partial(gather_kernel, hub_steps, rel_steps),
        in_specs=[VMEM, VMEM, HBM, HBM],
        out_specs=[VMEM] * (1 + len(shapes)),
        out_shape=[jax.ShapeDtypeStruct((buckets, hubs + edges), jnp.int32)]
        + [jax.ShapeDtypeStruct(shape, F32) for shape in shapes],
        scratch_shapes=[
            pltpu.VMEM((2, features, hub_tile), F32),
            pltpu.VMEM((2, features, rel_tile), F32),
            pltpu.VMEM((2 * features, max(hub_tile, rel_tile)), BF16),
            pltpu.SemaphoreType.DMA((hub_steps + rel_steps,)),
        ],
        compiler_params=GATHER_PARAMS,
        cost_estimate=COST,
    )(hub_idx, rel_idx, hub_table, rel_table)
    return out[0], out[1 : 1 + buckets], out[1 + buckets :]


def spread_bits(place, order):
    bits = len(order)
    return sum((((place >> p) & 1) << (bits - 1 - i)) for i, p in enumerate(order))


def gather_bits(index, order):
    bits = len(order)
    return sum((((index >> (bits - 1 - i)) & 1) << p) for i, p in enumerate(order))


def load_columns(id_refs, id_lanes, grad_refs, idx_down, stacked):
    low, high = id_lanes
    idx = jnp.concatenate([laid_out(ref[:, low:high]) for ref in id_refs], axis=1)
    idx_down[...] = jnp.transpose(jnp.broadcast_to(idx, (128, idx.shape[1])))
    at = 0
    for ref, (low, high) in grad_refs:
        width = high - low
        stack_into(stacked, ref[:, low:high], slice(at, at + width))
        at += width


def onehot_across(idx_down, targets):
    width = targets.shape[1]
    idx = idx_down[...]
    wide = jnp.concatenate([idx] * -(-width // 128), axis=1)[:, :width]
    return jnp.where(wide == targets, 1.0, 0.0).astype(BF16)


def out_for(place, order, sends, keeps, s):
    index = spread_bits(place, order)
    half = keeps[s].shape[0]
    return sends[s].at[index - half] if index >= half else keeps[s].at[index]


def chunk_refs(grad_lanes, refs):
    ids, refs = refs[:2], refs[2:]
    grads, refs = list(zip(refs, grad_lanes)), refs[len(grad_lanes) :]
    return ids, grads, refs[:-2], refs[-2:]


def hub_chunks_kernel(orders, spans, id_lanes, grad_lanes, chip_ref, *refs):
    ids, grads, outs, (idx_down, stacked) = chunk_refs(grad_lanes, refs)
    load_columns(ids, id_lanes, grads, idx_down, stacked)
    streams = len(orders)
    sends, keeps = outs[:streams], outs[streams:]
    chunks, width = 2 * keeps[0].shape[0], keeps[0].shape[2]
    lane = lax.broadcasted_iota(jnp.int32, (1, width), 1)
    for place in range(chunks):
        hot = onehot_across(idx_down, lane + (chip_ref[0] ^ place) * width)
        chunk = dot2(stacked[...], hot, NN)
        for s, (low, high) in enumerate(spans):
            out_for(place, orders[s], sends, keeps, s)[...] = chunk[low:high]


def rel_layout(half_width, streams):
    blocks = row_spans(half_width, 3)
    spans = row_spans(max(high - low for low, high in blocks), streams)
    pieces = []
    for block, (low, high) in enumerate(blocks):
        for s, (first, end) in enumerate(spans):
            count = min(end, high - low) - first
            if count > 0:
                pieces.append((block, s, low + first, count))
    return spans, pieces


def rel_chunks_kernel(pieces, rows, id_lanes, grad_lanes, chip_ref, *refs):
    ids, grads, outs, (idx_down, stacked) = chunk_refs(grad_lanes, refs)
    load_columns(ids, id_lanes, grads, idx_down, stacked)
    for ref in outs:
        ref[...] = jnp.zeros_like(ref)
    depth, lanes = outs[0].shape[0], outs[0].shape[2]
    chunks = depth * len(outs)
    width = rows // chunks
    group = lanes // width
    lane = lax.broadcasted_iota(jnp.int32, (1, lanes), 1)
    for first in range(0, chunks, group):
        targets = jnp.full((1, lanes), -1, jnp.int32)
        places = range(first, min(first + group, chunks))
        for slot, place in enumerate(places):
            here = (lane >= slot * width) & (lane < (slot + 1) * width)
            targets = jnp.where(here, lane + ((chip_ref[0] ^ place) * width - slot * width), targets)
        dense = dot2(stacked[...], onehot_across(idx_down, targets), NN)
        for slot, place in enumerate(places):
            out = outs[place // depth].at[place % depth]
            chunk = dense[:, slot * width : (slot + 1) * width]
            for block, unused, low, count in pieces:
                out[:count, block * width : (block + 1) * width] = chunk[low : low + count]


def chunk_columns(kernel, shapes, chip, ids, grads):
    half_width = grads[0][0].shape[0]
    grad_lanes = [lanes_of for unused, lanes_of in grads]
    count = sum(high - low for low, high in grad_lanes)
    return pl.pallas_call(
        functools.partial(kernel, grad_lanes),
        in_specs=[SMEM] + [VMEM] * (2 + len(grads)),
        out_specs=[VMEM] * len(shapes),
        out_shape=[jax.ShapeDtypeStruct(shape, F32) for shape in shapes],
        scratch_shapes=[
            pltpu.VMEM((count, 128), jnp.int32),
            pltpu.VMEM((2 * (-(-half_width // 16) * 16), count), BF16),
        ],
        compiler_params=PARAMS,
        cost_estimate=COST,
    )(chip, *ids, *[g for g, unused in grads])


def call(kernel, ins, shapes):
    return pl.pallas_call(
        kernel,
        in_specs=[VMEM] * len(ins),
        out_specs=[VMEM] * len(shapes),
        out_shape=[jax.ShapeDtypeStruct(shape, F32) for shape in shapes],
        compiler_params=PARAMS,
        cost_estimate=COST,
    )(*ins)


def sums_kernel(*refs):
    streams = len(refs) // 4
    own, got, sends, keeps = [refs[i * streams : (i + 1) * streams] for i in range(4)]
    for s in range(streams):
        half = sends[s].shape[0]
        sends[s][...] = own[s][half:] + got[s][half:]
        keeps[s][...] = own[s][:half] + got[s][:half]


def halves(own, got):
    shapes = [(x.shape[0] // 2,) + x.shape[1:] for x in own]
    out = call(sums_kernel, [*own, *got], shapes * 2)
    return out[: len(shapes)], out[len(shapes) :]


def join_kernel(*refs):
    streams = len(refs) // 3
    for s in range(streams):
        own, got, out = refs[s], refs[streams + s], refs[2 * streams + s]
        count = own.shape[0]
        out[:count] = own[...]
        out[count:] = got[...]


def join(own, got):
    return call(join_kernel, [*own, *got], [(2 * x.shape[0],) + x.shape[1:] for x in own])


def plane_sums_kernel(*refs):
    ins, outs = refs[: -refs[0].shape[0]], refs[-refs[0].shape[0] :]
    for place, out in enumerate(outs):
        out[0] = sum(ref[place] for ref in ins)


def squares_kernel(streams, *refs):
    own, got, rels = refs[:streams], refs[streams : 2 * streams], refs[2 * streams : -streams - 2]
    totals, rel_total, out = refs[-streams - 2 : -2], refs[-2], refs[-1]
    squares = jnp.zeros((1, out.shape[1]), F32)
    for s in range(streams):
        total = own[s][0] + got[s][0]
        totals[s][0] = total
        squares += jnp.sum(total * total, axis=0, keepdims=True)
    total = sum(ref[0] for ref in rels)
    rel_total[0] = total
    out[0:1] = squares
    out[1:2] = jnp.sum(total * total, axis=0, keepdims=True)


def update_kernel(spans, rel_spans, pieces, features, *refs):
    streams = len(spans)
    totals, news = refs[:streams], refs[-streams:]
    rel_total, mine, other, hub_ref, hub_sums, rel_ref, rel_sums = refs[streams:-streams]
    width = rel_ref.shape[1]
    squares = mine[...] + other[...]
    hub_scale = step_rate / jnp.sqrt(hub_sums[...] + squares[0:1] * (1.0 / features))
    rel_squares = sum(squares[1:2, b * width : (b + 1) * width] for b in range(3))
    rel_scale = step_rate / jnp.sqrt(rel_sums[...] + rel_squares * (1.0 / features))
    for s, (low, high) in enumerate(spans):
        height = high - low
        news[s][0, :height] = hub_ref[low:high] - totals[s][0] * hub_scale
        news[s][0, height:] = jnp.zeros_like(news[s][0, height:])
    for block, s, low, count in pieces:
        lanes, height = slice(block * width, (block + 1) * width), spans[s][1] - spans[s][0]
        first = rel_spans[s][0]
        news[s][0, height : height + count, lanes] = (
            rel_ref[low : low + count] - rel_total[0, first : first + count, lanes] * rel_scale
        )


def join_all_kernel(bases, *refs):
    streams = len(bases)
    join_kernel(*refs[:-1])
    for s, base in enumerate(bases):
        for i, ref in enumerate((refs[s], refs[streams + s])):
            count, height = ref.shape[0], ref.shape[1]
            refs[-1][i * count : (i + 1) * count, base : base + height] = ref[...]


def join_all(own, got):
    heights = [x.shape[1] for x in own]
    bases = [sum(heights[:s]) for s in range(len(own))]
    count, width = 2 * own[0].shape[0], own[0].shape[2]
    shapes = [(count, height, width) for height in heights] + [(count, sum(heights), width)]
    *have, near = call(functools.partial(join_all_kernel, bases), [*own, *got], shapes)
    return have, near, bases


def chunk_copies(part, base, first, order, span, spot_ref, out_ref, sems, at):
    low, high = span
    width = part.shape[2]
    for index in range(part.shape[0]):
        chunk = spot_ref[0] ^ gather_bits(first + index, order)
        lanes = pl.ds(pl.multiple_of(chunk * width, width), width)
        target = out_ref.at[spot_ref[1], pl.ds(low, high - low), lanes]
        yield pltpu.make_async_copy(part.at[index, pl.ds(base, high - low)], target, sems.at[at + index])


def near_kernel(orders, spans, bases, spot_ref, near_ref, *refs):
    out_ref, sems = refs[-2:]
    copies = []
    for order, span, base in zip(orders, spans, bases):
        copies += chunk_copies(near_ref, base, 0, order, span, spot_ref, out_ref, sems, len(copies))
    for copy in copies:
        copy.start()
    for copy in copies:
        copy.wait()


def far_kernel(orders, spans, bases, pieces, by_copy, spot_ref, near_ref, *refs):
    streams = len(orders)
    fars = refs[:streams]
    hub_out, rel_out, hub_all, rel_all, sems = refs[-5:]
    half = near_ref.shape[0]
    hub_width, rel_width = hub_out.shape[2] // (2 * half), rel_out.shape[2] // (2 * half)
    copies = []
    if by_copy:
        for far, order, span in zip(fars, orders, spans):
            copies += chunk_copies(far, 0, half, order, span, spot_ref, hub_out, sems, len(copies))
        for copy in copies:
            copy.start()
    for chunk in range(2 * half):
        place = spot_ref[0] ^ chunk
        for s, (low, high) in enumerate(spans):
            index = spread_bits(place, orders[s])
            spot = index & (half - 1)
            height, end = high - low, fars[s].shape[1]
            if not by_copy:
                value = jnp.where(index >= half, fars[s][spot, :height], near_ref[spot, bases[s] : bases[s] + height])
                hub_all[low:high, chunk * hub_width : (chunk + 1) * hub_width] = value
            value = jnp.where(index >= half, fars[s][spot, height:], near_ref[spot, bases[s] + height : bases[s] + end])
            for block, stream, row, count in pieces:
                if stream == s:
                    part = value[:count, block * rel_width : (block + 1) * rel_width]
                    rel_all[row : row + count, chunk * rel_width : (chunk + 1) * rel_width] = part
    copies.append(pltpu.make_async_copy(rel_all, rel_out.at[spot_ref[1]], sems.at[len(copies)]))
    copies[-1].start()
    if not by_copy:
        copies.append(pltpu.make_async_copy(hub_all, hub_out.at[spot_ref[1]], sems.at[len(copies)]))
        copies[-1].start()
    for copy in copies:
        copy.wait()


def placed(kernel, scratch, spot, near, fars, outs, earlier):
    sems = pltpu.SemaphoreType.DMA((3 * near.shape[0] + 2,))
    return pl.pallas_call(
        kernel,
        in_specs=[SMEM] + [VMEM] * (1 + len(fars)) + [HBM] * len(earlier),
        out_specs=[HBM] * len(outs),
        out_shape=[jax.ShapeDtypeStruct(shape, F32) for shape in outs],
        scratch_shapes=scratch + [sems],
        input_output_aliases={2 + len(fars) + i: i for i in range(len(earlier))},
        compiler_params=PARAMS,
        cost_estimate=pl.CostEstimate(flops=0, bytes_accessed=4 * outs[0][1] * outs[0][2], transcendentals=0),
    )(spot, near, *fars, *earlier)


def adagrad(table, state, grads):
    new_state = state + jnp.sum(grads * grads, axis=0, keepdims=True) * (1.0 / grads.shape[0])
    return table - grads * (step_rate / jnp.sqrt(new_state)), new_state


def keep_and_send(core, first, second):
    return jnp.where(core == 0, first, second), jnp.where(core == 0, second, first)


def table_counts(rows, negs, weight):
    place = lax.broadcasted_iota(jnp.int32, (rows, negs.shape[1]), 0)
    return jnp.sum(jnp.where(place == negs, weight, 0.0), axis=1, keepdims=True)


def turned(x, r, half):
    x0, x1, r0, r1 = x[:half], x[half:], r[:half], r[half:]
    return jnp.concatenate([x0 * r0 - x1 * r1, x0 * r1 + x1 * r0], axis=0)


def turned_back(x, r, half):
    x0, x1, r0, r1 = x[:half], x[half:], r[:half], r[half:]
    return x0 * r0 + x1 * r1, x1 * r0 - x0 * r1


EDGE_TILE = 512


def edge_span(step):
    return pl.ds(pl.multiple_of(step * EDGE_TILE, EDGE_TILE), EDGE_TILE)


def bucket_kernel(
    bucket, core_ref, heads_ref, tails_ref, negs_ref, left_ref, left_sums_ref, right_ref, right_sums_ref, rel_ref, hub_ref,
    left_out, left_sums_out, right_out, keep_out, send_out,
    left_parts, both_parts, left_grad, both_grad,
):
    features, rows = left_ref.shape
    half = features // 2
    core = core_ref[0]
    edges = heads_ref.shape[1]
    hubs = keep_out.shape[1] - edges
    at = slice(bucket, bucket + 1)
    weight = 1.0 / (negs_ref.shape[1] + hubs)
    counts = table_counts(rows, negs_ref[at], weight)
    stack_into(left_parts, left_ref[...])
    stack_into(both_parts, right_ref[...], slice(0, rows))
    stack_into(both_parts, hub_ref[...], slice(rows, rows + hubs))
    left_grad[...] = jnp.zeros_like(left_grad)
    both_grad[...] = jnp.zeros_like(both_grad)

    @pl.loop(0, edges // EDGE_TILE)
    def _(step):
        span = edge_span(step)
        tail_here = lax.broadcasted_iota(jnp.int32, (rows, EDGE_TILE), 0) == tails_ref[at, span]
        head_hot = onehot(0, rows, heads_ref[at, span])
        h = dot2(left_parts[...], head_hot, NN)
        r = rel_ref[:, span]
        q = split(turned(h, r, half))
        scores = dot3((both_parts[:features], both_parts[features:]), q, TN)
        chance = jax.nn.sigmoid(scores[:rows])
        coef = jnp.concatenate(
            [
                counts * chance + jnp.where(tail_here, chance - 1.0, 0.0),
                weight * jax.nn.sigmoid(scores[rows:]),
            ],
            axis=0,
        )
        coef = split(coef)
        dq = dot3_stacked(both_parts[...], coef, NN)
        both_grad[...] += dot3_stacked(stack(q), coef, NT)
        dh = jnp.concatenate(turned_back(dq, r, half), axis=0)
        left_grad[...] += dot2(stack(split(dh)), head_hot, NT)
        out_span = pl.ds(pl.multiple_of(hubs + step * EDGE_TILE, 128), EDGE_TILE)
        keep_out[:, out_span], send_out[:, out_span] = keep_and_send(core, *turned_back(dq, h, half))

    left_out[...], left_sums_out[...] = adagrad(left_ref[...], left_sums_ref[...], left_grad[...])
    new_right, new_sums = adagrad(right_ref[...], right_sums_ref[...], both_grad[:, :rows])
    right_out[:features] = new_right
    right_out[features:] = jnp.broadcast_to(new_sums, (right_out.shape[0] - features, rows))
    keep_out[:, :hubs], send_out[:, :hubs] = keep_and_send(core, both_grad[:half, rows:], both_grad[half:, rows:])


def bucket_step(bucket, core, heads, tails, negs, left, left_sums, right, right_sums, rel_rows, hub_rows):
    features, rows = left.shape
    edges, hubs = heads.shape[1], hub_rows.shape[1]
    width = rows + hubs
    shapes = [(features, rows), (1, rows), (features + 8, rows)] + [(features // 2, hubs + edges)] * 2
    return pl.pallas_call(
        functools.partial(bucket_kernel, bucket),
        in_specs=[SMEM] + [VMEM] * 9,
        out_specs=[VMEM] * 5,
        out_shape=[jax.ShapeDtypeStruct(shape, F32) for shape in shapes],
        scratch_shapes=[
            pltpu.VMEM((2 * features, rows), BF16),
            pltpu.VMEM((2 * features, width), BF16),
            pltpu.VMEM((features, rows), F32),
            pltpu.VMEM((features, width), F32),
        ],
        compiler_params=PARAMS,
        cost_estimate=COST,
    )(core, heads, tails, negs, left, left_sums, right, right_sums, rel_rows, hub_rows)


def hub_kernel(
    bucket, negatives, core_ref, heads_ref, left_ref, rel_ref, hub_ref,
    query_grad, hub_keep, hub_send,
    left_parts, hub_parts, hub_grad,
):
    features, rows = left_ref.shape
    half = features // 2
    edges, hubs = heads_ref.shape[1], hub_keep.shape[1]
    at = slice(bucket, bucket + 1)
    weight = 1.0 / (negatives + hubs)
    stack_into(left_parts, left_ref[...])
    stack_into(hub_parts, hub_ref[...])
    hub_grad[...] = jnp.zeros_like(hub_grad)

    @pl.loop(0, edges // EDGE_TILE)
    def _(step):
        span = edge_span(step)
        head_hot = onehot(0, rows, heads_ref[at, span])
        h = dot2(left_parts[...], head_hot, NN)
        q = split(turned(h, rel_ref[:, span], half))
        coef = split(weight * jax.nn.sigmoid(dot3((hub_parts[:features], hub_parts[features:]), q, TN)))
        query_grad[:, span] = dot3_stacked(hub_parts[...], coef, NN)
        hub_grad[...] += dot3_stacked(stack(q), coef, NT)

    hub_keep[...], hub_send[...] = keep_and_send(core_ref[0], hub_grad[:half], hub_grad[half:])


def hub_step(bucket, negatives, core, heads, left, rel_rows, hub_rows):
    features, rows = left.shape
    edges, hubs = heads.shape[1], hub_rows.shape[1]
    shapes = [(features, edges)] + [(features // 2, hubs)] * 2
    return pl.pallas_call(
        functools.partial(hub_kernel, bucket, negatives),
        in_specs=[SMEM] + [VMEM] * 4,
        out_specs=[VMEM] * 3,
        out_shape=[jax.ShapeDtypeStruct(shape, F32) for shape in shapes],
        scratch_shapes=[
            pltpu.VMEM((2 * features, rows), BF16),
            pltpu.VMEM((2 * features, hubs), BF16),
            pltpu.VMEM((features, hubs), F32),
        ],
        compiler_params=PARAMS,
        cost_estimate=COST,
    )(core, heads, left, rel_rows, hub_rows)


def tables_kernel(
    bucket, hubs, core_ref, heads_ref, tails_ref, negs_ref, query_grad,
    left_ref, left_sums_ref, right_ref, rel_ref,
    left_out, right_out, rel_keep, rel_send,
    left_parts, right_parts, left_grad, right_grad,
):
    features, rows = left_ref.shape
    half = features // 2
    edges = heads_ref.shape[1]
    at = slice(bucket, bucket + 1)
    core = core_ref[0]
    counts = table_counts(rows, negs_ref[at], 1.0 / (negs_ref.shape[1] + hubs))
    stack_into(left_parts, left_ref[...])
    stack_into(right_parts, right_ref[:features])
    left_grad[...] = jnp.zeros_like(left_grad)
    right_grad[...] = jnp.zeros_like(right_grad)

    @pl.loop(0, edges // EDGE_TILE)
    def _(step):
        span = edge_span(step)
        tail_here = lax.broadcasted_iota(jnp.int32, (rows, EDGE_TILE), 0) == tails_ref[at, span]
        head_hot = onehot(0, rows, heads_ref[at, span])
        h = dot2(left_parts[...], head_hot, NN)
        r = rel_ref[:, span]
        q = split(turned(h, r, half))
        chance = jax.nn.sigmoid(dot3((right_parts[:features], right_parts[features:]), q, TN))
        coef = split(counts * chance + jnp.where(tail_here, chance - 1.0, 0.0))
        dq = dot3_stacked(right_parts[...], coef, NN) + query_grad[:, span]
        right_grad[...] += dot3_stacked(stack(q), coef, NT)
        rel_keep[:, span], rel_send[:, span] = keep_and_send(core, *turned_back(dq, h, half))
        dh = jnp.concatenate(turned_back(dq, r, half), axis=0)
        left_grad[...] += dot2(stack(split(dh)), head_hot, NT)

    left_out[...], unused = adagrad(left_ref[...], left_sums_ref[...], left_grad[...])
    right_out[...], unused = adagrad(right_ref[:features], right_ref[features : features + 1], right_grad[...])


def tables_step(bucket, hubs, core, heads, tails, negs, query_grad, left, left_sums, right, rel_rows):
    features, rows = left.shape
    edges = heads.shape[1]
    shapes = [(features, rows)] * 2 + [(features // 2, edges)] * 2
    return pl.pallas_call(
        functools.partial(tables_kernel, bucket, hubs),
        in_specs=[SMEM] + [VMEM] * 8,
        out_specs=[VMEM] * 4,
        out_shape=[jax.ShapeDtypeStruct(shape, F32) for shape in shapes],
        scratch_shapes=[pltpu.VMEM((2 * features, rows), BF16)] * 2
        + [pltpu.VMEM((features, rows), F32)] * 2,
        compiler_params=PARAMS,
        cost_estimate=COST,
    )(core, heads, tails, negs, query_grad, left, left_sums, right, rel_rows)


def from_behind(x, axis, by):
    size = lax.axis_size(axis)
    return lax.ppermute(x, axis, [(i, (i + by) % size) for i in range(size)])


def flipped(x, axis, bit):
    return lax.ppermute(x, axis, [(i, i ^ (1 << bit)) for i in range(lax.axis_size(axis))])


def flipped_by(x, axis, offset):
    return lax.ppermute(x, axis, [(i, i ^ offset) for i in range(lax.axis_size(axis))])


def other_core(x):
    return flipped(x, "blk", 0)


def across(x, place):
    sub_bits = lax.axis_size("sub").bit_length() - 1
    if place < sub_bits:
        return flipped(x, "sub", place)
    return flipped(x, "blk", place - sub_bits + 1)


def stream_orders():
    sub_bits = lax.axis_size("sub").bit_length() - 1
    bits = sub_bits + lax.axis_size("blk").bit_length() - 2
    x, y, z, far = sub_bits, sub_bits + 1, 0, 1
    rest = [p for p in range(bits) if p not in (x, y, z, far)]
    return [[x, y, z, far] + rest, [y, z, x, far] + rest, [z, x, far, y] + rest]


def row_spans(rows, parts):
    ends = [-(-rows * (i + 1) // (8 * parts)) * 8 for i in range(parts - 1)] + [rows]
    return list(zip([0] + ends[:-1], ends))


def shards(
    left_emb, left_state, right_emb, right_state, relation_emb, relation_state, hub_emb, hub_state,
    heads, relations, tails, negatives, hub_ids,
):
    components, half_width, row_count = left_emb.shape
    features = components * half_width
    rel_count, hub_count = relation_emb.shape[2], hub_emb.shape[2]
    left = left_emb.reshape(features, row_count)
    right = right_emb.reshape(features, row_count)
    left_sums = left_state.reshape(1, row_count)
    right_sums = right_state.reshape(1, row_count)
    buckets, edges = heads.shape
    hubs = hub_ids.shape[1]

    core_id = lax.axis_index("blk") % 2
    chip_id = (lax.axis_index("blk") // 2) * lax.axis_size("sub") + lax.axis_index("sub")
    core, chip = core_id.astype(jnp.int32).reshape(1), chip_id.astype(jnp.int32).reshape(1)
    orders = stream_orders()
    streams, stages = len(orders), len(orders[0])
    chunks, depth = 1 << stages, lax.axis_size("sub")
    planes = chunks // depth
    spans = row_spans(half_width, streams)
    unused, rel_pieces = rel_layout(half_width, 1)
    rel_spans, joint_pieces = rel_layout(half_width, streams)
    rel_height = rel_spans[-1][1]
    width, rel_width = hub_count // chunks, rel_count // chunks
    hub_lanes, rel_lanes = (0, hubs), (hubs, hubs + edges)

    def exchanged(parts, step):
        return [across(x, order[step]) for x, order in zip(parts, orders)]

    def in_turn(first, then):
        return lax.optimization_barrier((first, then))

    ids, hub_rows, rel_rows = gather_rows(
        hub_emb.reshape(features, hub_count), hub_ids, relation_emb.reshape(features, rel_count), relations
    )
    far_ids = other_core(ids)
    keeps, fars = [], []
    for b in range(buckets - 1):
        if b > 0:
            right, right_sums = right[:features], right[features : features + 1]
        left, left_sums, right, keep, send = bucket_step(
            b, core, heads, tails, negatives, left, left_sums, right, right_sums, rel_rows[b], hub_rows[b]
        )
        right = from_behind(right, "blk", 1)
        keeps.append(keep)
        fars.append(other_core(send))
    far_ids, left = in_turn(far_ids, left)
    last = buckets - 1
    query_grad, hub_keep, hub_send = hub_step(
        last, negatives.shape[1], core, heads, left, rel_rows[last], hub_rows[last]
    )
    hub_far = other_core(hub_send)
    grads = lambda early, late, lanes: [(x, lanes) for x in early] + [(late, (0, late.shape[1]))]
    parts = chunk_columns(
        functools.partial(hub_chunks_kernel, orders, spans, hub_lanes),
        [(chunks // 2, high - low, width) for low, high in spans] * 2, chip, (ids, far_ids),
        grads(keeps, hub_keep, hub_lanes) + grads(fars, hub_far, hub_lanes),
    )
    send, own = parts[:streams], parts[streams:]
    got = exchanged(send, 0)
    left, right, rel_keep, rel_send = tables_step(
        last, hubs, core, heads, tails, negatives, query_grad, left, left_sums, right, rel_rows[last]
    )
    rel_far = other_core(rel_send)

    rel_keep, got = in_turn(rel_keep, got)
    send, own = halves(own, got)
    got = exchanged(send, 1)
    own, rel_far = in_turn(own, rel_far)
    rel_own, *rel_out = chunk_columns(
        functools.partial(rel_chunks_kernel, rel_pieces, rel_count, rel_lanes),
        [(depth, rel_height, width)] * planes, chip, (ids, far_ids),
        grads(keeps, rel_keep, rel_lanes) + grads(fars, rel_far, rel_lanes),
    )
    rel_got = [flipped_by(x, "blk", 2 * (p + 1)) for p, x in enumerate(rel_out)]
    for step in range(2, stages):
        rel_own, got = in_turn(rel_own, got)
        send, own = halves(own, got)
        got = exchanged(send, step)
        if step == 2:
            late, own, rel_got = lax.optimization_barrier((jnp.stack([core_id, chip_id]), own, rel_got))
            rel_own, *rel_out = call(plane_sums_kernel, [rel_own, *rel_got], [(1, rel_height, width)] * depth)
            rel_got = [flipped_by(x, "sub", q + 1) for q, x in enumerate(rel_out)]

    cut = lambda x, span: lax.dynamic_slice(x, (late[0], 0, late[1] * span), (1, half_width, span))[0]
    cut_sums = lambda x, span: lax.dynamic_slice(x[None], (0, late[1] * span), (1, span))
    *totals, rel_total, squares = call(
        functools.partial(squares_kernel, streams), [*own, *got, rel_own, *rel_got],
        [x.shape for x in own] + [rel_own.shape, (2, width)],
    )
    have = call(
        functools.partial(update_kernel, spans, rel_spans, joint_pieces, features),
        [
            *totals, rel_total, squares, other_core(squares), cut(hub_emb, width), cut_sums(hub_state, width),
            cut(relation_emb, rel_width), cut_sums(relation_state, rel_width),
        ],
        [(1, high - low + end - first, width) for (low, high), (first, end) in zip(spans, rel_spans)],
    )
    for step in range(stages - 1, 1, -1):
        have = join(have, exchanged(have, step))
    have, near, bases = join_all(have, exchanged(have, 1))
    got = exchanged(have, 0)
    far_near = other_core(near)

    mine, others = jnp.concatenate([chip, core]), jnp.concatenate([chip, 1 - core])
    shapes = [hub_emb.shape, relation_emb.shape]
    by_copy = width % 128 == 0
    hub_new = []
    if by_copy:
        near_step = functools.partial(near_kernel, orders, spans, bases)
        hub_new = placed(near_step, [], mine, near, [], shapes[:1], [])
        hub_new = placed(near_step, [], others, far_near, [], shapes[:1], hub_new)
        got, hub_new = in_turn(got, hub_new)
    far_step = functools.partial(far_kernel, orders, spans, bases, joint_pieces, by_copy)
    scratch = [
        pltpu.VMEM((8, 128) if by_copy else (half_width, hub_count), F32),
        pltpu.VMEM((half_width, rel_count), F32),
    ]
    far_got = other_core(got)
    hub_new, rel_new = placed(far_step, scratch, mine, near, got, shapes, hub_new)
    hub_new, rel_new = placed(far_step, scratch, others, far_near, far_got, shapes, [hub_new, rel_new])
    return (
        left.reshape(components, half_width, row_count),
        right.reshape(components, half_width, row_count),
        rel_new,
        hub_new,
    )


def solution(mesh):
    both = ("blk", "sub")
    block, table, whole = P(None, None, both), P(None, both), P()
    return jax.shard_map(
        shards,
        mesh=mesh,
        in_specs=(block, P(both), block, P(both), whole, whole, whole, whole, table, table, table, table, table),
        out_specs=(block, block, whole, whole),
        check_vma=False,
    )
```

```python
import functools
import jax
import jax.numpy as jnp
from jax import lax
from jax.experimental import pallas as pl
from jax.experimental.pallas import tpu as pltpu
from jax.sharding import PartitionSpec as P

step_rate = 0.25
F32, BF16 = jnp.float32, jnp.bfloat16
NN = (((1,), (0,)), ((), ()))
NT = (((1,), (1,)), ((), ()))
TN = (((0,), (0,)), ((), ()))
VMEM = pl.BlockSpec(memory_space=pltpu.VMEM)
SMEM = pl.BlockSpec(memory_space=pltpu.SMEM)
PARAMS = pltpu.CompilerParams(vmem_limit_bytes=12 * 1024 * 1024)
GATHER_PARAMS = pltpu.CompilerParams(vmem_limit_bytes=48 * 1024 * 1024)
HBM = pl.BlockSpec(memory_space=pltpu.HBM)
COST = pl.CostEstimate(flops=10000, bytes_accessed=10000, transcendentals=0)


def split(x):
    hi = x.astype(BF16)
    return hi, (x - hi.astype(F32)).astype(BF16)


def dot(a, b, dims):
    return lax.dot_general(a, b, dims, preferred_element_type=F32)


def dot3(a, b, dims):
    return dot(a[0], b[0], dims) + (dot(a[0], b[1], dims) + dot(a[1], b[0], dims))


def dot2(stacked, onehot, dims):
    half = stacked.shape[0] // 2
    both = dot(stacked, onehot, dims)
    return both[:half] + both[half:]


def stack(parts):
    return jnp.concatenate(parts, axis=0)


def stack_into(ref, x, lanes=slice(None)):
    rows, half = x.shape[0], ref.shape[0] // 2
    hi, lo = split(x)
    ref[:rows, lanes] = hi
    ref[half : half + rows, lanes] = lo
    if half > rows:
        blank = jnp.zeros((half - rows, x.shape[1]), BF16)
        ref[rows:half, lanes] = blank
        ref[half + rows :, lanes] = blank


def dot3_stacked(stacked, b, dims):
    half = stacked.shape[0] // 2
    both = dot(stacked, b[0], dims)
    return both[:half] + (both[half:] + dot(stacked[:half], b[1], dims))


def onehot(first, rows, idx):
    place = lax.broadcasted_iota(jnp.int32, (rows, idx.shape[1]), 0) + first
    return jnp.where(place == idx, 1.0, 0.0).astype(BF16)


def laid_out(idx):
    return jnp.concatenate([idx[b : b + 1] for b in range(idx.shape[0])], axis=1)


def take_owned(spot_ref, chunks, span, first, piece_of, out_ref):
    width = out_ref.shape[1]
    for chunk in range(chunks):
        if first <= chunk * width < first + span:

            @pl.when(spot_ref[0] == chunk)
            def _():
                out_ref[...] = piece_of(slice(chunk * width - first, (chunk + 1) * width - first))


def gather_kernel(hub_steps, rel_steps, spot_ref, hub_idx, rel_idx, hub_sums, rel_sums, hub_ref, rel_ref, *refs):
    buckets = hub_idx.shape[0]
    hub_outs, rel_outs = refs[:buckets], refs[buckets : 2 * buckets]
    spot_out, hub_own, rel_own, hub_own_sums, rel_own_sums = refs[2 * buckets : 2 * buckets + 5]
    hub_buf, rel_buf, stacked, sems = refs[2 * buckets + 5 :]
    hub_tile, rel_tile = hub_buf.shape[2], rel_buf.shape[2]
    chunks = hub_ref.shape[1] // hub_own.shape[1]
    half = hub_own.shape[0]
    steps = [(hub_ref, hub_buf, hub_tile, k) for k in range(hub_steps)]
    steps += [(rel_ref, rel_buf, rel_tile, k) for k in range(rel_steps)]
    copies = [
        pltpu.make_async_copy(table.at[:, pl.ds(k * tile, tile)], buf.at[k % 2], sems.at[i])
        for i, (table, buf, tile, k) in enumerate(steps)
    ]
    copies[0].start()
    spot_out[0] = spot_ref[0]
    spot_out[1] = spot_ref[1]
    take_owned(spot_ref, chunks, hub_sums.shape[1], 0, lambda lanes: hub_sums[:, lanes], hub_own_sums)
    take_owned(spot_ref, chunks, rel_sums.shape[1], 0, lambda lanes: rel_sums[:, lanes], rel_own_sums)
    rows = pl.ds(pl.multiple_of(spot_ref[1] * half, 8), half)
    for i, (table, buf, tile, k) in enumerate(steps):
        if i + 1 < len(steps):
            copies[i + 1].start()
        idx, outs, own = (hub_idx, hub_outs, hub_own) if table is hub_ref else (rel_idx, rel_outs, rel_own)
        count = idx.shape[1]
        hot = onehot(k * tile, tile, laid_out(idx[...]))
        copies[i].wait()
        stack_into(stacked, buf[k % 2], slice(0, tile))
        part = dot2(stacked[:, :tile], hot, NN)
        for b, out in enumerate(outs):
            here = part[:, b * count : (b + 1) * count]
            out[...] = here if k == 0 else out[...] + here
        take_owned(spot_ref, chunks, tile, k * tile, lambda lanes: buf[k % 2, rows, lanes], own)


def gather_rows(spot, hub_table, hub_idx, hub_sums, rel_table, rel_idx, rel_sums, chunks):
    features = hub_table.shape[0]
    hub_steps, rel_steps = 4, 2
    hub_tile, rel_tile = hub_table.shape[1] // hub_steps, rel_table.shape[1] // rel_steps
    buckets, hubs = hub_idx.shape
    edges = rel_idx.shape[1]
    hub_width, rel_width = hub_table.shape[1] // chunks, rel_table.shape[1] // chunks
    shapes = [(features, hubs)] * buckets + [(features, edges)] * buckets
    own_shapes = [(features // 2, hub_width), (features // 2, rel_width), (1, hub_width), (1, rel_width)]
    floats = lambda shapes: [jax.ShapeDtypeStruct(shape, F32) for shape in shapes]
    out = pl.pallas_call(
        functools.partial(gather_kernel, hub_steps, rel_steps),
        in_specs=[SMEM] + [VMEM] * 4 + [HBM, HBM],
        out_specs=[VMEM] * len(shapes) + [SMEM] + [VMEM] * len(own_shapes),
        out_shape=floats(shapes) + [jax.ShapeDtypeStruct((2,), jnp.int32)] + floats(own_shapes),
        scratch_shapes=[
            pltpu.VMEM((2, features, hub_tile), F32),
            pltpu.VMEM((2, features, rel_tile), F32),
            pltpu.VMEM((2 * features, max(hub_tile, rel_tile)), BF16),
            pltpu.SemaphoreType.DMA((hub_steps + rel_steps,)),
        ],
        compiler_params=GATHER_PARAMS,
        cost_estimate=COST,
    )(spot, hub_idx, rel_idx, hub_sums, rel_sums, hub_table, rel_table)
    return out[:buckets], out[buckets : 2 * buckets], out[2 * buckets], out[2 * buckets + 1 :]


def spread_bits(place, order):
    bits = len(order)
    return sum((((place >> p) & 1) << (bits - 1 - i)) for i, p in enumerate(order))


def gather_bits(index, order):
    bits = len(order)
    return sum((((index >> (bits - 1 - i)) & 1) << p) for i, p in enumerate(order))


def load_columns(id_refs, grad_refs, idx_down, stacked):
    idx = jnp.concatenate([laid_out(ref[...]) for ref in id_refs], axis=1)
    idx_down[...] = jnp.transpose(jnp.broadcast_to(idx, (128, idx.shape[1])))
    at = 0
    for ref, (low, high) in grad_refs:
        width = high - low
        stack_into(stacked, ref[:, low:high], slice(at, at + width))
        at += width


def onehot_across(idx_down, targets):
    width = targets.shape[1]
    idx = idx_down[...]
    wide = jnp.concatenate([idx] * -(-width // 128), axis=1)[:, :width]
    return jnp.where(wide == targets, 1.0, 0.0).astype(BF16)


def grouped(orders, step, heights):
    groups, where = [], []
    for s, order in enumerate(orders):
        for g, (place, members) in enumerate(groups):
            if place == order[step]:
                where.append((g, sum(heights[m] for m in members)))
                members.append(s)
                break
        else:
            where.append((len(groups), 0))
            groups.append((order[step], [s]))
    return [(place, sum(heights[m] for m in members)) for place, members in groups], where


def rows_of(where, heights, s):
    group, base = where[s]
    return group, slice(base, base + heights[s])


def put_chunk(place, orders, heights, where, sends, keeps, s, value):
    index, half = spread_bits(place, orders[s]), keeps[s].shape[0]
    if index < half:
        keeps[s][index] = value
    else:
        group, rows = rows_of(where, heights, s)
        sends[group][index - half, rows] = value


def chunk_refs(grad_lanes, refs):
    ids, refs = refs[:2], refs[2:]
    grads, refs = list(zip(refs, grad_lanes)), refs[len(grad_lanes) :]
    return ids, grads, refs[:-2], refs[-2:]


def hub_chunks_kernel(orders, spans, where, grad_lanes, spot_ref, *refs):
    ids, grads, outs, (idx_down, stacked) = chunk_refs(grad_lanes, refs)
    load_columns(ids, grads, idx_down, stacked)
    streams = len(orders)
    sends, keeps = outs[:-streams], outs[-streams:]
    heights = [high - low for low, high in spans]
    chunks, width = 2 * keeps[0].shape[0], keeps[0].shape[2]
    lane = lax.broadcasted_iota(jnp.int32, (1, width), 1)
    for place in range(chunks):
        hot = onehot_across(idx_down, lane + (spot_ref[0] ^ place) * width)
        chunk = dot2(stacked[...], hot, NN)
        for s, (low, high) in enumerate(spans):
            put_chunk(place, orders, heights, where, sends, keeps, s, chunk[low:high])


def rel_layout(half_width, streams):
    blocks = row_spans(half_width, 3)
    spans = row_spans(max(high - low for low, high in blocks), streams)
    pieces = []
    for block, (low, high) in enumerate(blocks):
        for s, (first, end) in enumerate(spans):
            count = min(end, high - low) - first
            if count > 0:
                pieces.append((block, s, low + first, count))
    return spans, pieces


def rel_chunks_kernel(orders, pieces, rows, grad_lanes, spot_ref, *refs):
    ids, grads, outs, (idx_down, stacked) = chunk_refs(grad_lanes, refs)
    load_columns(ids, grads, idx_down, stacked)
    for ref in outs:
        ref[...] = jnp.zeros_like(ref)
    streams = len(orders)
    sends, keeps = outs[:streams], outs[streams:]
    half, lanes = keeps[0].shape[0], keeps[0].shape[2]
    chunks = 2 * half
    width = rows // chunks
    group = lanes // width
    lane = lax.broadcasted_iota(jnp.int32, (1, lanes), 1)
    for first in range(0, chunks, group):
        targets = jnp.full((1, lanes), -1, jnp.int32)
        places = range(first, min(first + group, chunks))
        for slot, place in enumerate(places):
            here = (lane >= slot * width) & (lane < (slot + 1) * width)
            targets = jnp.where(here, lane + ((spot_ref[0] ^ place) * width - slot * width), targets)
        dense = dot2(stacked[...], onehot_across(idx_down, targets), NN)
        for slot, place in enumerate(places):
            chunk = dense[:, slot * width : (slot + 1) * width]
            for block, s, low, count in pieces:
                index = spread_bits(place, orders[s])
                out = sends[s].at[index - half] if index >= half else keeps[s].at[index]
                out[:count, block * width : (block + 1) * width] = chunk[low : low + count]


def chunk_columns(kernel, shapes, spot, ids, grads):
    half_width = grads[0][0].shape[0]
    grad_lanes = [lanes_of for unused, lanes_of in grads]
    count = sum(high - low for low, high in grad_lanes)
    return pl.pallas_call(
        functools.partial(kernel, grad_lanes),
        in_specs=[SMEM] + [VMEM] * (2 + len(grads)),
        out_specs=[VMEM] * len(shapes),
        out_shape=[jax.ShapeDtypeStruct(shape, F32) for shape in shapes],
        scratch_shapes=[
            pltpu.VMEM((count, 128), jnp.int32),
            pltpu.VMEM((2 * (-(-half_width // 16) * 16), count), BF16),
        ],
        compiler_params=PARAMS,
        cost_estimate=COST,
    )(spot, *ids, *[g for g, unused in grads])


def call(kernel, ins, shapes):
    return pl.pallas_call(
        kernel,
        in_specs=[VMEM] * len(ins),
        out_specs=[VMEM] * len(shapes),
        out_shape=[jax.ShapeDtypeStruct(shape, F32) for shape in shapes],
        compiler_params=PARAMS,
        cost_estimate=COST,
    )(*ins)


def sums_kernel(heights, here, there, *refs):
    streams, groups = len(heights), 1 + max(g for g, unused in here)
    own, got, sends, keeps = refs[:streams], refs[streams : streams + groups], refs[streams + groups : -streams], refs[-streams:]
    for s in range(streams):
        half = keeps[s].shape[0]
        group, rows = rows_of(here, heights, s)
        out, out_rows = rows_of(there, heights, s)
        sends[out][:, out_rows] = own[s][half:] + got[group][half:, rows]
        keeps[s][...] = own[s][:half] + got[group][:half, rows]


def halves(own, got, orders, step):
    heights = [x.shape[1] for x in own]
    half, width = own[0].shape[0] // 2, own[0].shape[2]
    unused, here = grouped(orders, step, heights)
    groups, there = grouped(orders, step + 1, heights)
    shapes = [(half, height, width) for height in [h for unused, h in groups] + heights]
    out = call(functools.partial(sums_kernel, heights, here, there), [*own, *got], shapes)
    return out[: len(groups)], out[len(groups) :]


def join_kernel(heights, here, there, *refs):
    groups = 1 + max(g for g, unused in here)
    own, got, outs = refs[:groups], refs[groups : 2 * groups], refs[2 * groups :]
    count = own[0].shape[0]
    for s in range(len(heights)):
        group, rows = rows_of(here, heights, s)
        out, out_rows = rows_of(there, heights, s)
        outs[out][:count, out_rows] = own[group][:, rows]
        outs[out][count:, out_rows] = got[group][:, rows]


def join(have, got, orders, step, heights):
    count, width = have[0].shape[0], have[0].shape[2]
    unused, here = grouped(orders, step, heights)
    groups, there = grouped(orders, step - 1, heights)
    shapes = [(2 * count, height, width) for unused, height in groups]
    return call(functools.partial(join_kernel, heights, here, there), [*have, *got], shapes)


def z_sums_kernel(spans, *refs):
    streams = len(spans)
    own, got, outs = refs[:streams], refs[streams : 2 * streams], refs[2 * streams :]
    for place, out in enumerate(outs):
        for s, (low, high) in enumerate(spans):
            out[0, low:high] = own[s][place] + got[s][place]


def squares_kernel(heights, here, *refs):
    streams, groups = len(heights), 1 + max(g for g, unused in here)
    own, got, rels = refs[:streams], refs[streams : streams + groups], refs[streams + groups : -streams - 2]
    totals, rel_total, out = refs[-streams - 2 : -2], refs[-2], refs[-1]
    squares = jnp.zeros((1, out.shape[1]), F32)
    for s in range(streams):
        group, rows = rows_of(here, heights, s)
        total = own[s][0] + got[group][0, rows]
        totals[s][0] = total
        squares += jnp.sum(total * total, axis=0, keepdims=True)
    total = sum(ref[0] for ref in rels)
    rel_total[0] = total
    out[0:1] = squares
    out[1:2] = jnp.sum(total * total, axis=0, keepdims=True)


def update_kernel(spans, rel_spans, pieces, there, features, *refs):
    streams, groups = len(spans), 1 + max(g for g, unused in there)
    totals, news = refs[:streams], refs[-groups:]
    rel_total, mine, other, hub_ref, hub_sums, rel_ref, rel_sums = refs[streams:-groups]
    width = rel_ref.shape[1]
    squares = mine[...] + other[...]
    hub_scale = step_rate / jnp.sqrt(hub_sums[...] + squares[0:1] * (1.0 / features))
    rel_squares = sum(squares[1:2, b * width : (b + 1) * width] for b in range(3))
    rel_scale = step_rate / jnp.sqrt(rel_sums[...] + rel_squares * (1.0 / features))
    for s, (low, high) in enumerate(spans):
        new, base = there[s]
        first, end = rel_spans[s]
        middle = base + high - low
        news[new][0, base:middle] = hub_ref[low:high] - totals[s][0] * hub_scale
        news[new][0, middle : middle + end - first] = jnp.zeros((end - first, news[new].shape[2]), F32)
    for block, s, low, count in pieces:
        new, base = there[s]
        base += spans[s][1] - spans[s][0]
        lanes, first = slice(block * width, (block + 1) * width), rel_spans[s][0]
        news[new][0, base : base + count, lanes] = (
            rel_ref[low : low + count] - rel_total[0, first : first + count, lanes] * rel_scale
        )


def join_all_kernel(heights, here, there, *refs):
    groups = 1 + max(g for g, unused in here)
    join_kernel(heights, here, there, *refs[:-1])
    base = 0
    for s, height in enumerate(heights):
        group, rows = rows_of(here, heights, s)
        for i, ref in enumerate((refs[group], refs[groups + group])):
            count = ref.shape[0]
            refs[-1][i * count : (i + 1) * count, base : base + height] = ref[:, rows]
        base += height


def join_all(have, got, orders, step, heights):
    count, width = 2 * have[0].shape[0], have[0].shape[2]
    unused, here = grouped(orders, step, heights)
    groups, there = grouped(orders, step - 1, heights)
    shapes = [(count, height, width) for height in [h for unused, h in groups] + [sum(heights)]]
    *have, near = call(functools.partial(join_all_kernel, heights, here, there), [*have, *got], shapes)
    return have, near


def chunk_copies(part, base, first, order, span, chip, component, out_ref, sems, at):
    low, high = span
    width = part.shape[2]
    for index in range(part.shape[0]):
        chunk = chip ^ gather_bits(first + index, order)
        lanes = pl.ds(pl.multiple_of(chunk * width, width), width)
        target = out_ref.at[component, pl.ds(low, high - low), lanes]
        yield pltpu.make_async_copy(part.at[index, pl.ds(base, high - low)], target, sems.at[at + index])


def component_of(spot_ref, mine):
    return spot_ref[1] if mine else 1 - spot_ref[1]


def near_kernel(orders, spans, bases, mine, spot_ref, near_ref, *refs):
    component = component_of(spot_ref, mine)
    out_ref, sems = refs[-2:]
    copies = []
    for order, span, base in zip(orders, spans, bases):
        copies += chunk_copies(near_ref, base, 0, order, span, spot_ref[0], component, out_ref, sems, len(copies))
    for copy in copies:
        copy.start()
    for copy in copies:
        copy.wait()


def far_kernel(orders, spans, bases, pieces, by_copy, mine, spot_ref, near_ref, *refs):
    component = component_of(spot_ref, mine)
    streams = len(orders)
    fars = refs[:streams]
    hub_out, rel_out, hub_all, rel_all, sems = refs[-5:]
    half = near_ref.shape[0]
    hub_width, rel_width = hub_out.shape[2] // (2 * half), rel_out.shape[2] // (2 * half)
    copies = []
    if by_copy:
        for far, order, span in zip(fars, orders, spans):
            copies += chunk_copies(far, 0, half, order, span, spot_ref[0], component, hub_out, sems, len(copies))
        for copy in copies:
            copy.start()
    for chunk in range(2 * half):
        place = spot_ref[0] ^ chunk
        for s, (low, high) in enumerate(spans):
            index = spread_bits(place, orders[s])
            spot = index & (half - 1)
            height, end = high - low, fars[s].shape[1]
            if not by_copy:
                value = jnp.where(index >= half, fars[s][spot, :height], near_ref[spot, bases[s] : bases[s] + height])
                hub_all[low:high, chunk * hub_width : (chunk + 1) * hub_width] = value
            value = jnp.where(index >= half, fars[s][spot, height:], near_ref[spot, bases[s] + height : bases[s] + end])
            for block, stream, row, count in pieces:
                if stream == s:
                    part = value[:count, block * rel_width : (block + 1) * rel_width]
                    rel_all[row : row + count, chunk * rel_width : (chunk + 1) * rel_width] = part
    copies.append(pltpu.make_async_copy(rel_all, rel_out.at[component], sems.at[len(copies)]))
    copies[-1].start()
    if not by_copy:
        copies.append(pltpu.make_async_copy(hub_all, hub_out.at[component], sems.at[len(copies)]))
        copies[-1].start()
    for copy in copies:
        copy.wait()


def placed(kernel, scratch, spot, near, fars, outs, earlier):
    sems = pltpu.SemaphoreType.DMA((3 * near.shape[0] + 2,))
    return pl.pallas_call(
        kernel,
        in_specs=[SMEM] + [VMEM] * (1 + len(fars)) + [HBM] * len(earlier),
        out_specs=[HBM] * len(outs),
        out_shape=[jax.ShapeDtypeStruct(shape, F32) for shape in outs],
        scratch_shapes=scratch + [sems],
        input_output_aliases={2 + len(fars) + i: i for i in range(len(earlier))},
        compiler_params=PARAMS,
        cost_estimate=pl.CostEstimate(flops=0, bytes_accessed=4 * outs[0][1] * outs[0][2], transcendentals=0),
    )(spot, near, *fars, *earlier)


def adagrad(table, state, grads):
    new_state = state + jnp.sum(grads * grads, axis=0, keepdims=True) * (1.0 / grads.shape[0])
    return table - grads * (step_rate / jnp.sqrt(new_state)), new_state


def keep_and_send(core, first, second):
    return jnp.where(core == 0, first, second), jnp.where(core == 0, second, first)


def table_counts(rows, negs, weight):
    place = lax.broadcasted_iota(jnp.int32, (rows, negs.shape[1]), 0)
    return jnp.sum(jnp.where(place == negs, weight, 0.0), axis=1, keepdims=True)


def turned(x, r, half):
    x0, x1, r0, r1 = x[:half], x[half:], r[:half], r[half:]
    return jnp.concatenate([x0 * r0 - x1 * r1, x0 * r1 + x1 * r0], axis=0)


def turned_back(x, r, half):
    x0, x1, r0, r1 = x[:half], x[half:], r[:half], r[half:]
    return x0 * r0 + x1 * r1, x1 * r0 - x0 * r1


EDGE_TILE = 512


def edge_span(step):
    return pl.ds(pl.multiple_of(step * EDGE_TILE, EDGE_TILE), EDGE_TILE)


def bucket_kernel(
    bucket, core_ref, heads_ref, tails_ref, negs_ref, left_ref, left_sums_ref, right_ref, right_sums_ref, rel_ref, hub_ref,
    left_out, left_sums_out, right_out, keep_out, send_out,
    left_parts, both_parts, left_grad, both_grad,
):
    features, rows = left_ref.shape
    half = features // 2
    core = core_ref[1]
    edges = heads_ref.shape[1]
    hubs = keep_out.shape[1] - edges
    at = slice(bucket, bucket + 1)
    weight = 1.0 / (negs_ref.shape[1] + hubs)
    counts = table_counts(rows, negs_ref[at], weight)
    stack_into(left_parts, left_ref[...])
    stack_into(both_parts, right_ref[...], slice(0, rows))
    stack_into(both_parts, hub_ref[...], slice(rows, rows + hubs))
    left_grad[...] = jnp.zeros_like(left_grad)
    both_grad[...] = jnp.zeros_like(both_grad)

    @pl.loop(0, edges // EDGE_TILE)
    def _(step):
        span = edge_span(step)
        tail_here = lax.broadcasted_iota(jnp.int32, (rows, EDGE_TILE), 0) == tails_ref[at, span]
        head_hot = onehot(0, rows, heads_ref[at, span])
        h = dot2(left_parts[...], head_hot, NN)
        r = rel_ref[:, span]
        q = split(turned(h, r, half))
        scores = dot3((both_parts[:features], both_parts[features:]), q, TN)
        chance = jax.nn.sigmoid(scores[:rows])
        coef = jnp.concatenate(
            [
                counts * chance + jnp.where(tail_here, chance - 1.0, 0.0),
                weight * jax.nn.sigmoid(scores[rows:]),
            ],
            axis=0,
        )
        coef = split(coef)
        dq = dot3_stacked(both_parts[...], coef, NN)
        both_grad[...] += dot3_stacked(stack(q), coef, NT)
        dh = jnp.concatenate(turned_back(dq, r, half), axis=0)
        left_grad[...] += dot2(stack(split(dh)), head_hot, NT)
        out_span = pl.ds(pl.multiple_of(hubs + step * EDGE_TILE, 128), EDGE_TILE)
        keep_out[:, out_span], send_out[:, out_span] = keep_and_send(core, *turned_back(dq, h, half))

    left_out[...], left_sums_out[...] = adagrad(left_ref[...], left_sums_ref[...], left_grad[...])
    new_right, new_sums = adagrad(right_ref[...], right_sums_ref[...], both_grad[:, :rows])
    right_out[:features] = new_right
    right_out[features:] = jnp.broadcast_to(new_sums, (right_out.shape[0] - features, rows))
    keep_out[:, :hubs], send_out[:, :hubs] = keep_and_send(core, both_grad[:half, rows:], both_grad[half:, rows:])


def bucket_step(bucket, core, heads, tails, negs, left, left_sums, right, right_sums, rel_rows, hub_rows):
    features, rows = left.shape
    edges, hubs = heads.shape[1], hub_rows.shape[1]
    width = rows + hubs
    shapes = [(features, rows), (1, rows), (features + 8, rows)] + [(features // 2, hubs + edges)] * 2
    return pl.pallas_call(
        functools.partial(bucket_kernel, bucket),
        in_specs=[SMEM] + [VMEM] * 9,
        out_specs=[VMEM] * 5,
        out_shape=[jax.ShapeDtypeStruct(shape, F32) for shape in shapes],
        scratch_shapes=[
            pltpu.VMEM((2 * features, rows), BF16),
            pltpu.VMEM((2 * features, width), BF16),
            pltpu.VMEM((features, rows), F32),
            pltpu.VMEM((features, width), F32),
        ],
        compiler_params=PARAMS,
        cost_estimate=COST,
    )(core, heads, tails, negs, left, left_sums, right, right_sums, rel_rows, hub_rows)


def hub_kernel(
    bucket, negatives, core_ref, heads_ref, left_ref, rel_ref, hub_ref,
    query_grad, hub_keep, hub_send,
    left_parts, hub_parts, hub_grad,
):
    features, rows = left_ref.shape
    half = features // 2
    edges, hubs = heads_ref.shape[1], hub_keep.shape[1]
    at = slice(bucket, bucket + 1)
    weight = 1.0 / (negatives + hubs)
    stack_into(left_parts, left_ref[...])
    stack_into(hub_parts, hub_ref[...])
    hub_grad[...] = jnp.zeros_like(hub_grad)

    @pl.loop(0, edges // EDGE_TILE)
    def _(step):
        span = edge_span(step)
        head_hot = onehot(0, rows, heads_ref[at, span])
        h = dot2(left_parts[...], head_hot, NN)
        q = split(turned(h, rel_ref[:, span], half))
        coef = split(weight * jax.nn.sigmoid(dot3((hub_parts[:features], hub_parts[features:]), q, TN)))
        query_grad[:, span] = dot3_stacked(hub_parts[...], coef, NN)
        hub_grad[...] += dot3_stacked(stack(q), coef, NT)

    hub_keep[...], hub_send[...] = keep_and_send(core_ref[1], hub_grad[:half], hub_grad[half:])


def hub_step(bucket, negatives, core, heads, left, rel_rows, hub_rows):
    features, rows = left.shape
    edges, hubs = heads.shape[1], hub_rows.shape[1]
    shapes = [(features, edges)] + [(features // 2, hubs)] * 2
    return pl.pallas_call(
        functools.partial(hub_kernel, bucket, negatives),
        in_specs=[SMEM] + [VMEM] * 4,
        out_specs=[VMEM] * 3,
        out_shape=[jax.ShapeDtypeStruct(shape, F32) for shape in shapes],
        scratch_shapes=[
            pltpu.VMEM((2 * features, rows), BF16),
            pltpu.VMEM((2 * features, hubs), BF16),
            pltpu.VMEM((features, hubs), F32),
        ],
        compiler_params=PARAMS,
        cost_estimate=COST,
    )(core, heads, left, rel_rows, hub_rows)


def tables_kernel(
    bucket, hubs, core_ref, heads_ref, tails_ref, negs_ref, query_grad,
    left_ref, left_sums_ref, right_ref, rel_ref,
    left_out, right_out, rel_keep, rel_send,
    left_parts, right_parts, left_grad, right_grad,
):
    features, rows = left_ref.shape
    half = features // 2
    edges = heads_ref.shape[1]
    at = slice(bucket, bucket + 1)
    core = core_ref[1]
    counts = table_counts(rows, negs_ref[at], 1.0 / (negs_ref.shape[1] + hubs))
    stack_into(left_parts, left_ref[...])
    stack_into(right_parts, right_ref[:features])
    left_grad[...] = jnp.zeros_like(left_grad)
    right_grad[...] = jnp.zeros_like(right_grad)

    @pl.loop(0, edges // EDGE_TILE)
    def _(step):
        span = edge_span(step)
        tail_here = lax.broadcasted_iota(jnp.int32, (rows, EDGE_TILE), 0) == tails_ref[at, span]
        head_hot = onehot(0, rows, heads_ref[at, span])
        h = dot2(left_parts[...], head_hot, NN)
        r = rel_ref[:, span]
        q = split(turned(h, r, half))
        chance = jax.nn.sigmoid(dot3((right_parts[:features], right_parts[features:]), q, TN))
        coef = split(counts * chance + jnp.where(tail_here, chance - 1.0, 0.0))
        dq = dot3_stacked(right_parts[...], coef, NN) + query_grad[:, span]
        right_grad[...] += dot3_stacked(stack(q), coef, NT)
        rel_keep[:, span], rel_send[:, span] = keep_and_send(core, *turned_back(dq, h, half))
        dh = jnp.concatenate(turned_back(dq, r, half), axis=0)
        left_grad[...] += dot2(stack(split(dh)), head_hot, NT)

    left_out[...], unused = adagrad(left_ref[...], left_sums_ref[...], left_grad[...])
    right_out[...], unused = adagrad(right_ref[:features], right_ref[features : features + 1], right_grad[...])


def tables_step(bucket, hubs, core, heads, tails, negs, query_grad, left, left_sums, right, rel_rows):
    features, rows = left.shape
    edges = heads.shape[1]
    shapes = [(features, rows)] * 2 + [(features // 2, edges)] * 2
    return pl.pallas_call(
        functools.partial(tables_kernel, bucket, hubs),
        in_specs=[SMEM] + [VMEM] * 8,
        out_specs=[VMEM] * 4,
        out_shape=[jax.ShapeDtypeStruct(shape, F32) for shape in shapes],
        scratch_shapes=[pltpu.VMEM((2 * features, rows), BF16)] * 2
        + [pltpu.VMEM((features, rows), F32)] * 2,
        compiler_params=PARAMS,
        cost_estimate=COST,
    )(core, heads, tails, negs, query_grad, left, left_sums, right, rel_rows)


def from_behind(x, axis, by):
    size = lax.axis_size(axis)
    return lax.ppermute(x, axis, [(i, (i + by) % size) for i in range(size)])


def flipped(x, axis, bit):
    return lax.ppermute(x, axis, [(i, i ^ (1 << bit)) for i in range(lax.axis_size(axis))])


def flipped_by(x, axis, offset):
    return lax.ppermute(x, axis, [(i, i ^ offset) for i in range(lax.axis_size(axis))])


def other_core(x):
    return flipped(x, "blk", 0)


def across(x, place):
    sub_bits = lax.axis_size("sub").bit_length() - 1
    if place < sub_bits:
        return flipped(x, "sub", place)
    return flipped(x, "blk", place - sub_bits + 1)


def stream_orders():
    sub_bits = lax.axis_size("sub").bit_length() - 1
    bits = sub_bits + lax.axis_size("blk").bit_length() - 2
    x, y, z, far = sub_bits, sub_bits + 1, 0, 1
    rest = [p for p in range(bits) if p not in (x, y, z, far)]
    return [[x, y, z, far] + rest, [y, z, x, far] + rest, [z, x, far, y] + rest]


def plane_orders(sub_bits, bits):
    plane, depth = list(range(sub_bits, bits)), list(range(sub_bits - 1, -1, -1))
    return [plane + depth, plane[1:] + plane[:1] + depth]


def row_spans(rows, parts):
    ends = [-(-rows * (i + 1) // (8 * parts)) * 8 for i in range(parts - 1)] + [rows]
    return list(zip([0] + ends[:-1], ends))


def shards(
    left_emb, left_state, right_emb, right_state, relation_emb, relation_state, hub_emb, hub_state,
    heads, relations, tails, negatives, hub_ids,
):
    components, half_width, row_count = left_emb.shape
    features = components * half_width
    rel_count, hub_count = relation_emb.shape[2], hub_emb.shape[2]
    left = left_emb.reshape(features, row_count)
    right = right_emb.reshape(features, row_count)
    left_sums = left_state.reshape(1, row_count)
    right_sums = right_state.reshape(1, row_count)
    buckets, edges = heads.shape
    hubs = hub_ids.shape[1]

    orders = stream_orders()
    streams, stages = len(orders), len(orders[0])
    chunks, depth = 1 << stages, lax.axis_size("sub")
    sub_bits = depth.bit_length() - 1
    planes = chunks // depth
    spans = row_spans(half_width, streams)
    rel_orders = plane_orders(sub_bits, stages)
    plane_spans, plane_pieces = rel_layout(half_width, len(rel_orders))
    rel_spans, joint_pieces = rel_layout(half_width, streams)
    heights, rel_heights, plane_heights = [[high - low for low, high in x] for x in (spans, rel_spans, plane_spans)]
    joint_heights = [h + r for h, r in zip(heights, rel_heights)]
    bases = [sum(joint_heights[:s]) for s in range(streams)]
    width = hub_count // chunks
    hub_lanes, rel_lanes = (0, hubs), (hubs, hubs + edges)

    def exchanged(parts, step):
        return [across(x, place) for x, (place, unused) in zip(parts, grouped(orders, step, heights)[0])]

    def in_turn(first, then):
        return lax.optimization_barrier((first, then))

    blk = lax.axis_index("blk")
    spot = jnp.stack([(blk >> 1) * depth + lax.axis_index("sub"), blk & 1]).astype(jnp.int32)
    far_ids = other_core((hub_ids, relations))
    hub_rows, rel_rows, spot, owned = gather_rows(
        spot, hub_emb.reshape(features, hub_count), hub_ids, hub_state[None],
        relation_emb.reshape(features, rel_count), relations, relation_state[None], chunks,
    )
    far_ids, hub_rows = in_turn(far_ids, hub_rows)
    keeps, fars = [], []
    for b in range(buckets - 1):
        if b > 0:
            right, right_sums = right[:features], right[features : features + 1]
        left, left_sums, right, keep, send = bucket_step(
            b, spot, heads, tails, negatives, left, left_sums, right, right_sums, rel_rows[b], hub_rows[b]
        )
        right = from_behind(right, "blk", 1)
        keeps.append(keep)
        fars.append(other_core(send))
    last = buckets - 1
    query_grad, hub_keep, hub_send = hub_step(
        last, negatives.shape[1], spot, heads, left, rel_rows[last], hub_rows[last]
    )
    hub_far = other_core(hub_send)
    grads = lambda early, late, lanes: [(x, lanes) for x in early] + [(late, (0, late.shape[1]))]
    groups, where = grouped(orders, 0, heights)
    parts = chunk_columns(
        functools.partial(hub_chunks_kernel, orders, spans, where),
        [(chunks // 2, height, width) for height in [h for unused, h in groups] + heights],
        spot, (hub_ids, far_ids[0]), grads(keeps, hub_keep, hub_lanes) + grads(fars, hub_far, hub_lanes),
    )
    send, own = parts[: len(groups)], parts[len(groups) :]
    got = exchanged(send, 0)
    left, right, rel_keep, rel_send = tables_step(
        last, hubs, spot, heads, tails, negatives, query_grad, left, left_sums, right, rel_rows[last]
    )
    rel_far = other_core(rel_send)

    rel_keep, got = in_turn(rel_keep, got)
    send, own = halves(own, got, orders, 0)
    got = exchanged(send, 1)
    own, rel_far = in_turn(own, rel_far)
    parts = chunk_columns(
        functools.partial(rel_chunks_kernel, rel_orders, plane_pieces, rel_count),
        [(chunks // 2, height, width) for height in plane_heights * 2],
        spot, (relations, far_ids[1]), grads(keeps, rel_keep, rel_lanes) + grads(fars, rel_far, rel_lanes),
    )
    rel_send, rel_own = parts[: len(rel_orders)], parts[len(rel_orders) :]
    rel_got = [across(x, order[0]) for x, order in zip(rel_send, rel_orders)]
    for step in range(1, stages - 1):
        rel_own, got = in_turn(rel_own, got)
        send, own = halves(own, got, orders, step)
        got = exchanged(send, step + 1)
        if step < stages - sub_bits:
            own, rel_got = in_turn(own, rel_got)
            rel_send, rel_own = halves(rel_own, rel_got, rel_orders, step - 1)
            rel_got = [across(x, order[step]) for x, order in zip(rel_send, rel_orders)]
    own, rel_got = in_turn(own, rel_got)
    rel_own, *rel_out = call(
        functools.partial(z_sums_kernel, plane_spans), [*rel_own, *rel_got], [(1, plane_spans[-1][1], width)] * depth
    )
    rel_got = [flipped_by(x, "sub", q + 1) for q, x in enumerate(rel_out)]

    *totals, rel_total, squares = call(
        functools.partial(squares_kernel, heights, grouped(orders, stages - 1, heights)[1]),
        [*own, *got, rel_own, *rel_got], [x.shape for x in own] + [rel_own.shape, (2, width)],
    )
    hub_own, rel_own, hub_sums, rel_sums = owned
    groups, there = grouped(orders, stages - 1, joint_heights)
    have = call(
        functools.partial(update_kernel, spans, rel_spans, joint_pieces, there, features),
        [*totals, rel_total, squares, other_core(squares), hub_own, hub_sums, rel_own, rel_sums],
        [(1, height, width) for unused, height in groups],
    )
    for step in range(stages - 1, 1, -1):
        have = join(have, exchanged(have, step), orders, step, joint_heights)
    have, near = join_all(have, exchanged(have, 1), orders, 1, joint_heights)
    got = exchanged(have, 0)
    far_near = other_core(near)

    shapes = [hub_emb.shape, relation_emb.shape]
    by_copy = width % 128 == 0
    hub_new = []
    if by_copy:
        near_step = functools.partial(near_kernel, orders, spans, bases)
        hub_new = placed(functools.partial(near_step, True), [], spot, near, [], shapes[:1], [])
        hub_new = placed(functools.partial(near_step, False), [], spot, far_near, [], shapes[:1], hub_new)
        got, hub_new = in_turn(got, hub_new)
    far_step = functools.partial(far_kernel, orders, spans, bases, joint_pieces, by_copy)
    scratch = [
        pltpu.VMEM((8, 128) if by_copy else (half_width, hub_count), F32),
        pltpu.VMEM((half_width, rel_count), F32),
    ]
    far_got = other_core(got)
    out = placed(functools.partial(far_step, True), scratch, spot, near, got, shapes, hub_new)
    hub_new, rel_new = placed(functools.partial(far_step, False), scratch, spot, far_near, far_got, shapes, out)
    return (
        left.reshape(components, half_width, row_count),
        right.reshape(components, half_width, row_count),
        rel_new,
        hub_new,
    )


def solution(mesh):
    both = ("blk", "sub")
    block, table, whole = P(None, None, both), P(None, both), P()
    return jax.shard_map(
        shards,
        mesh=mesh,
        in_specs=(block, P(both), block, P(both), whole, whole, whole, whole, table, table, table, table, table),
        out_specs=(block, block, whole, whole),
        check_vma=False,
    )
```

```python
import functools
import jax
import jax.numpy as jnp
from jax import lax
from jax.experimental import pallas as pl
from jax.experimental.pallas import tpu as pltpu
from jax.sharding import PartitionSpec as P

step_rate = 0.25
F32, BF16 = jnp.float32, jnp.bfloat16
NN = (((1,), (0,)), ((), ()))
NT = (((1,), (1,)), ((), ()))
TN = (((0,), (0,)), ((), ()))
VMEM = pl.BlockSpec(memory_space=pltpu.VMEM)
SMEM = pl.BlockSpec(memory_space=pltpu.SMEM)
PARAMS = pltpu.CompilerParams(vmem_limit_bytes=12 * 1024 * 1024)
GATHER_PARAMS = pltpu.CompilerParams(vmem_limit_bytes=50 * 1024 * 1024)
HBM = pl.BlockSpec(memory_space=pltpu.HBM)
COST = pl.CostEstimate(flops=10000, bytes_accessed=10000, transcendentals=0)


def split(x):
    hi = x.astype(BF16)
    return hi, (x - hi.astype(F32)).astype(BF16)


def dot(a, b, dims):
    return lax.dot_general(a, b, dims, preferred_element_type=F32)


def dot3(a, b, dims):
    return dot(a[0], b[0], dims) + (dot(a[0], b[1], dims) + dot(a[1], b[0], dims))


def dot2(stacked, onehot, dims):
    half = stacked.shape[0] // 2
    both = dot(stacked, onehot, dims)
    return both[:half] + both[half:]


def stack(parts):
    return jnp.concatenate(parts, axis=0)


def stack_into(ref, x, lanes=slice(None)):
    rows, half = x.shape[0], ref.shape[0] // 2
    hi, lo = split(x)
    ref[:rows, lanes] = hi
    ref[half : half + rows, lanes] = lo
    if half > rows:
        blank = jnp.zeros((half - rows, x.shape[1]), BF16)
        ref[rows:half, lanes] = blank
        ref[half + rows :, lanes] = blank


def dot3_stacked(stacked, b, dims):
    half = stacked.shape[0] // 2
    both = dot(stacked, b[0], dims)
    return both[:half] + (both[half:] + dot(stacked[:half], b[1], dims))


def onehot(first, rows, idx):
    place = lax.broadcasted_iota(jnp.int32, (rows, idx.shape[1]), 0) + first
    return jnp.where(place == idx, 1.0, 0.0).astype(BF16)


def laid_out(idx):
    return jnp.concatenate([idx[b : b + 1] for b in range(idx.shape[0])], axis=1)


def take_owned(spot_ref, chunks, span, first, piece_of, out_ref):
    width = out_ref.shape[1]
    for chunk in range(chunks):
        if first <= chunk * width < first + span:

            @pl.when(spot_ref[0] == chunk)
            def _():
                out_ref[...] = piece_of(slice(chunk * width - first, (chunk + 1) * width - first))


def gather_kernel(hub_steps, rel_steps, spot_ref, hub_ids, rel_ids, hub_ref, rel_ref, *refs):
    buckets = hub_ids.shape[0]
    hub_outs, rel_outs = refs[:buckets], refs[buckets : 2 * buckets]
    spot_out, hub_own, rel_own = refs[2 * buckets : 2 * buckets + 3]
    hub_buf, rel_buf, hub_idx, rel_idx, stacked, sems = refs[2 * buckets + 3 :]
    hub_tile, rel_tile = hub_buf.shape[2], rel_buf.shape[2]
    chunks = hub_ref.shape[1] // hub_own.shape[1]
    half = hub_own.shape[0]
    steps = [(hub_ref, hub_buf, hub_tile, k) for k in range(hub_steps)]
    steps += [(rel_ref, rel_buf, rel_tile, k) for k in range(rel_steps)]
    copies = [
        pltpu.make_async_copy(table.at[:, pl.ds(k * tile, tile)], buf.at[k % 2], sems.at[i])
        for i, (table, buf, tile, k) in enumerate(steps)
    ]
    id_copies = [
        pltpu.make_async_copy(ids, out, sems.at[len(copies) + i])
        for i, (ids, out) in enumerate([(hub_ids, hub_idx), (rel_ids, rel_idx)])
    ]
    for copy in [*id_copies, copies[0]]:
        copy.start()
    spot_out[0] = spot_ref[0]
    spot_out[1] = spot_ref[1]
    for copy in id_copies:
        copy.wait()
    rows = pl.ds(pl.multiple_of(spot_ref[1] * half, 8), half)
    for i, (table, buf, tile, k) in enumerate(steps):
        if i + 1 < len(steps):
            copies[i + 1].start()
        idx, outs, own = (hub_idx, hub_outs, hub_own) if table is hub_ref else (rel_idx, rel_outs, rel_own)
        count = idx.shape[1]
        hot = onehot(k * tile, tile, laid_out(idx[...]))
        copies[i].wait()
        stack_into(stacked, buf[k % 2], slice(0, tile))
        part = dot2(stacked[:, :tile], hot, NN)
        for b, out in enumerate(outs):
            here = part[:, b * count : (b + 1) * count]
            out[...] = here if k == 0 else out[...] + here
        take_owned(spot_ref, chunks, tile, k * tile, lambda lanes: buf[k % 2, rows, lanes], own)


def gather_rows(spot, hub_table, hub_idx, rel_table, rel_idx, chunks):
    features = hub_table.shape[0]
    hub_steps, rel_steps = 4, 2
    hub_tile, rel_tile = hub_table.shape[1] // hub_steps, rel_table.shape[1] // rel_steps
    buckets, hubs = hub_idx.shape
    edges = rel_idx.shape[1]
    hub_width, rel_width = hub_table.shape[1] // chunks, rel_table.shape[1] // chunks
    shapes = [(features, hubs)] * buckets + [(features, edges)] * buckets
    own_shapes = [(features // 2, hub_width), (features // 2, rel_width)]
    floats = lambda shapes: [jax.ShapeDtypeStruct(shape, F32) for shape in shapes]
    out = pl.pallas_call(
        functools.partial(gather_kernel, hub_steps, rel_steps),
        in_specs=[SMEM] + [HBM] * 4,
        out_specs=[VMEM] * len(shapes) + [SMEM] + [VMEM] * len(own_shapes),
        out_shape=floats(shapes) + [jax.ShapeDtypeStruct((2,), jnp.int32)] + floats(own_shapes),
        scratch_shapes=[
            pltpu.VMEM((2, features, hub_tile), F32),
            pltpu.VMEM((2, features, rel_tile), F32),
            pltpu.VMEM(hub_idx.shape, jnp.int32),
            pltpu.VMEM(rel_idx.shape, jnp.int32),
            pltpu.VMEM((2 * features, max(hub_tile, rel_tile)), BF16),
            pltpu.SemaphoreType.DMA((hub_steps + rel_steps + 2,)),
        ],
        compiler_params=GATHER_PARAMS,
        cost_estimate=COST,
    )(spot, hub_idx, rel_idx, hub_table, rel_table)
    return out[:buckets], out[buckets : 2 * buckets], out[2 * buckets], out[2 * buckets + 1 :]


def spread_bits(place, order):
    bits = len(order)
    return sum((((place >> p) & 1) << (bits - 1 - i)) for i, p in enumerate(order))


def gather_bits(index, order):
    bits = len(order)
    return sum((((index >> (bits - 1 - i)) & 1) << p) for i, p in enumerate(order))


def load_columns(id_refs, grad_refs, idx_down, stacked):
    idx = jnp.concatenate([laid_out(ref[...]) for ref in id_refs], axis=1)
    idx_down[...] = jnp.transpose(jnp.broadcast_to(idx, (128, idx.shape[1])))
    at = 0
    for ref, (low, high) in grad_refs:
        width = high - low
        stack_into(stacked, ref[:, low:high], slice(at, at + width))
        at += width


def onehot_across(idx_down, targets):
    width = targets.shape[1]
    idx = idx_down[...]
    wide = jnp.concatenate([idx] * -(-width // 128), axis=1)[:, :width]
    return jnp.where(wide == targets, 1.0, 0.0).astype(BF16)


def grouped(orders, step, heights):
    groups, where = [], []
    for s, order in enumerate(orders):
        for g, (place, members) in enumerate(groups):
            if place == order[step]:
                where.append((g, sum(heights[m] for m in members)))
                members.append(s)
                break
        else:
            where.append((len(groups), 0))
            groups.append((order[step], [s]))
    return [(place, sum(heights[m] for m in members)) for place, members in groups], where


def rows_of(where, heights, s):
    group, base = where[s]
    return group, slice(base, base + heights[s])


def put_chunk(place, orders, heights, where, sends, keeps, s, value):
    index, half = spread_bits(place, orders[s]), keeps[s].shape[0]
    if index < half:
        keeps[s][index] = value
    else:
        group, rows = rows_of(where, heights, s)
        sends[group][index - half, rows] = value


def chunk_refs(grad_lanes, refs):
    ids, refs = refs[:2], refs[2:]
    grads, refs = list(zip(refs, grad_lanes)), refs[len(grad_lanes) :]
    return ids, grads, refs[:-2], refs[-2:]


def hub_chunks_kernel(orders, spans, where, grad_lanes, spot_ref, *refs):
    ids, grads, outs, (idx_down, stacked) = chunk_refs(grad_lanes, refs)
    load_columns(ids, grads, idx_down, stacked)
    streams = len(orders)
    sends, keeps = outs[:-streams], outs[-streams:]
    heights = [high - low for low, high in spans]
    chunks, width = 2 * keeps[0].shape[0], keeps[0].shape[2]
    lane = lax.broadcasted_iota(jnp.int32, (1, width), 1)
    for place in range(chunks):
        hot = onehot_across(idx_down, lane + (spot_ref[0] ^ place) * width)
        chunk = dot2(stacked[...], hot, NN)
        for s, (low, high) in enumerate(spans):
            put_chunk(place, orders, heights, where, sends, keeps, s, chunk[low:high])


def rel_layout(half_width, streams):
    blocks = row_spans(half_width, 3)
    spans = row_spans(max(high - low for low, high in blocks), streams)
    pieces = []
    for block, (low, high) in enumerate(blocks):
        for s, (first, end) in enumerate(spans):
            count = min(end, high - low) - first
            if count > 0:
                pieces.append((block, s, low + first, count))
    return spans, pieces


def rel_chunks_kernel(orders, pieces, rows, grad_lanes, spot_ref, *refs):
    ids, grads, outs, (idx_down, stacked) = chunk_refs(grad_lanes, refs)
    load_columns(ids, grads, idx_down, stacked)
    for ref in outs:
        ref[...] = jnp.zeros_like(ref)
    streams = len(orders)
    sends, keeps = outs[:streams], outs[streams:]
    half, lanes = keeps[0].shape[0], keeps[0].shape[2]
    chunks = 2 * half
    width = rows // chunks
    group = lanes // width
    lane = lax.broadcasted_iota(jnp.int32, (1, lanes), 1)
    for first in range(0, chunks, group):
        targets = jnp.full((1, lanes), -1, jnp.int32)
        places = range(first, min(first + group, chunks))
        for slot, place in enumerate(places):
            here = (lane >= slot * width) & (lane < (slot + 1) * width)
            targets = jnp.where(here, lane + ((spot_ref[0] ^ place) * width - slot * width), targets)
        dense = dot2(stacked[...], onehot_across(idx_down, targets), NN)
        for slot, place in enumerate(places):
            chunk = dense[:, slot * width : (slot + 1) * width]
            for block, s, low, count in pieces:
                index = spread_bits(place, orders[s])
                out = sends[s].at[index - half] if index >= half else keeps[s].at[index]
                out[:count, block * width : (block + 1) * width] = chunk[low : low + count]


def chunk_columns(kernel, shapes, spot, ids, grads):
    half_width = grads[0][0].shape[0]
    grad_lanes = [lanes_of for unused, lanes_of in grads]
    count = sum(high - low for low, high in grad_lanes)
    return pl.pallas_call(
        functools.partial(kernel, grad_lanes),
        in_specs=[SMEM] + [VMEM] * (2 + len(grads)),
        out_specs=[VMEM] * len(shapes),
        out_shape=[jax.ShapeDtypeStruct(shape, F32) for shape in shapes],
        scratch_shapes=[
            pltpu.VMEM((count, 128), jnp.int32),
            pltpu.VMEM((2 * (-(-half_width // 16) * 16), count), BF16),
        ],
        compiler_params=PARAMS,
        cost_estimate=COST,
    )(spot, *ids, *[g for g, unused in grads])


def call(kernel, ins, shapes):
    return pl.pallas_call(
        kernel,
        in_specs=[VMEM] * len(ins),
        out_specs=[VMEM] * len(shapes),
        out_shape=[jax.ShapeDtypeStruct(shape, F32) for shape in shapes],
        compiler_params=PARAMS,
        cost_estimate=COST,
    )(*ins)


def sums_kernel(heights, here, there, *refs):
    streams, groups = len(heights), 1 + max(g for g, unused in here)
    own, got, sends, keeps = refs[:streams], refs[streams : streams + groups], refs[streams + groups : -streams], refs[-streams:]
    for s in range(streams):
        half = keeps[s].shape[0]
        group, rows = rows_of(here, heights, s)
        out, out_rows = rows_of(there, heights, s)
        sends[out][:, out_rows] = own[s][half:] + got[group][half:, rows]
        keeps[s][...] = own[s][:half] + got[group][:half, rows]


def halves(own, got, orders, step):
    heights = [x.shape[1] for x in own]
    half, width = own[0].shape[0] // 2, own[0].shape[2]
    unused, here = grouped(orders, step, heights)
    groups, there = grouped(orders, step + 1, heights)
    shapes = [(half, height, width) for height in [h for unused, h in groups] + heights]
    out = call(functools.partial(sums_kernel, heights, here, there), [*own, *got], shapes)
    return out[: len(groups)], out[len(groups) :]


def join_kernel(heights, here, there, *refs):
    groups = 1 + max(g for g, unused in here)
    own, got, outs = refs[:groups], refs[groups : 2 * groups], refs[2 * groups :]
    count = own[0].shape[0]
    for s in range(len(heights)):
        group, rows = rows_of(here, heights, s)
        out, out_rows = rows_of(there, heights, s)
        outs[out][:count, out_rows] = own[group][:, rows]
        outs[out][count:, out_rows] = got[group][:, rows]


def join(have, got, orders, step, heights):
    count, width = have[0].shape[0], have[0].shape[2]
    unused, here = grouped(orders, step, heights)
    groups, there = grouped(orders, step - 1, heights)
    shapes = [(2 * count, height, width) for unused, height in groups]
    return call(functools.partial(join_kernel, heights, here, there), [*have, *got], shapes)


def z_sums_kernel(spans, *refs):
    streams = len(spans)
    own, got, outs = refs[:streams], refs[streams : 2 * streams], refs[2 * streams :]
    for place, out in enumerate(outs):
        for s, (low, high) in enumerate(spans):
            out[0, low:high] = own[s][place] + got[s][place]


def squares_kernel(heights, here, *refs):
    streams, groups = len(heights), 1 + max(g for g, unused in here)
    own, got, rels = refs[:streams], refs[streams : streams + groups], refs[streams + groups : -streams - 2]
    totals, rel_total, out = refs[-streams - 2 : -2], refs[-2], refs[-1]
    squares = jnp.zeros((1, out.shape[1]), F32)
    for s in range(streams):
        group, rows = rows_of(here, heights, s)
        total = own[s][0] + got[group][0, rows]
        totals[s][0] = total
        squares += jnp.sum(total * total, axis=0, keepdims=True)
    total = sum(ref[0] for ref in rels)
    rel_total[0] = total
    out[0:1] = squares
    out[1:2] = jnp.sum(total * total, axis=0, keepdims=True)


def update_kernel(spans, rel_spans, pieces, there, features, spot_ref, *refs):
    streams, groups = len(spans), 1 + max(g for g, unused in there)
    totals, (hub_sums, rel_sums), news = refs[:streams], refs[-2:], refs[-groups - 2 : -2]
    rel_total, mine, other, hub_ref, hub_all, rel_ref, rel_all = refs[streams : -groups - 2]
    chunks = hub_all.shape[1] // hub_ref.shape[1]
    take_owned(spot_ref, chunks, hub_all.shape[1], 0, lambda lanes: hub_all[:, lanes], hub_sums)
    take_owned(spot_ref, chunks, rel_all.shape[1], 0, lambda lanes: rel_all[:, lanes], rel_sums)
    width = rel_ref.shape[1]
    squares = mine[...] + other[...]
    hub_scale = step_rate / jnp.sqrt(hub_sums[...] + squares[0:1] * (1.0 / features))
    rel_squares = sum(squares[1:2, b * width : (b + 1) * width] for b in range(3))
    rel_scale = step_rate / jnp.sqrt(rel_sums[...] + rel_squares * (1.0 / features))
    for s, (low, high) in enumerate(spans):
        new, base = there[s]
        first, end = rel_spans[s]
        middle = base + high - low
        news[new][0, base:middle] = hub_ref[low:high] - totals[s][0] * hub_scale
        news[new][0, middle : middle + end - first] = jnp.zeros((end - first, news[new].shape[2]), F32)
    for block, s, low, count in pieces:
        new, base = there[s]
        base += spans[s][1] - spans[s][0]
        lanes, first = slice(block * width, (block + 1) * width), rel_spans[s][0]
        news[new][0, base : base + count, lanes] = (
            rel_ref[low : low + count] - rel_total[0, first : first + count, lanes] * rel_scale
        )


def join_all_kernel(heights, here, there, *refs):
    groups = 1 + max(g for g, unused in here)
    join_kernel(heights, here, there, *refs[:-1])
    base = 0
    for s, height in enumerate(heights):
        group, rows = rows_of(here, heights, s)
        for i, ref in enumerate((refs[group], refs[groups + group])):
            count = ref.shape[0]
            refs[-1][i * count : (i + 1) * count, base : base + height] = ref[:, rows]
        base += height


def join_all(have, got, orders, step, heights):
    count, width = 2 * have[0].shape[0], have[0].shape[2]
    unused, here = grouped(orders, step, heights)
    groups, there = grouped(orders, step - 1, heights)
    shapes = [(count, height, width) for height in [h for unused, h in groups] + [sum(heights)]]
    *have, near = call(functools.partial(join_all_kernel, heights, here, there), [*have, *got], shapes)
    return have, near


def chunk_copies(part, base, first, order, span, chip, component, out_ref, sems, at):
    low, high = span
    width = part.shape[2]
    for index in range(part.shape[0]):
        chunk = chip ^ gather_bits(first + index, order)
        lanes = pl.ds(pl.multiple_of(chunk * width, width), width)
        target = out_ref.at[component, pl.ds(low, high - low), lanes]
        yield pltpu.make_async_copy(part.at[index, pl.ds(base, high - low)], target, sems.at[at + index])


def component_of(spot_ref, mine):
    return spot_ref[1] if mine else 1 - spot_ref[1]


def near_kernel(orders, spans, bases, mine, spot_ref, near_ref, *refs):
    component = component_of(spot_ref, mine)
    out_ref, sems = refs[-2:]
    copies = []
    for order, span, base in zip(orders, spans, bases):
        copies += chunk_copies(near_ref, base, 0, order, span, spot_ref[0], component, out_ref, sems, len(copies))
    for copy in copies:
        copy.start()
    for copy in copies:
        copy.wait()


def far_kernel(orders, spans, bases, pieces, by_copy, mine, spot_ref, near_ref, *refs):
    component = component_of(spot_ref, mine)
    streams = len(orders)
    fars = refs[:streams]
    hub_out, rel_out, hub_all, rel_all, sems = refs[-5:]
    half = near_ref.shape[0]
    hub_width, rel_width = hub_out.shape[2] // (2 * half), rel_out.shape[2] // (2 * half)
    copies = []
    if by_copy:
        for far, order, span in zip(fars, orders, spans):
            copies += chunk_copies(far, 0, half, order, span, spot_ref[0], component, hub_out, sems, len(copies))
        for copy in copies:
            copy.start()
    for chunk in range(2 * half):
        place = spot_ref[0] ^ chunk
        for s, (low, high) in enumerate(spans):
            index = spread_bits(place, orders[s])
            spot = index & (half - 1)
            height, end = high - low, fars[s].shape[1]
            if not by_copy:
                value = jnp.where(index >= half, fars[s][spot, :height], near_ref[spot, bases[s] : bases[s] + height])
                hub_all[low:high, chunk * hub_width : (chunk + 1) * hub_width] = value
            value = jnp.where(index >= half, fars[s][spot, height:], near_ref[spot, bases[s] + height : bases[s] + end])
            for block, stream, row, count in pieces:
                if stream == s:
                    part = value[:count, block * rel_width : (block + 1) * rel_width]
                    rel_all[row : row + count, chunk * rel_width : (chunk + 1) * rel_width] = part
    copies.append(pltpu.make_async_copy(rel_all, rel_out.at[component], sems.at[len(copies)]))
    copies[-1].start()
    if not by_copy:
        copies.append(pltpu.make_async_copy(hub_all, hub_out.at[component], sems.at[len(copies)]))
        copies[-1].start()
    for copy in copies:
        copy.wait()


def placed(kernel, scratch, spot, near, fars, outs, earlier):
    sems = pltpu.SemaphoreType.DMA((3 * near.shape[0] + 2,))
    return pl.pallas_call(
        kernel,
        in_specs=[SMEM] + [VMEM] * (1 + len(fars)) + [HBM] * len(earlier),
        out_specs=[HBM] * len(outs),
        out_shape=[jax.ShapeDtypeStruct(shape, F32) for shape in outs],
        scratch_shapes=scratch + [sems],
        input_output_aliases={2 + len(fars) + i: i for i in range(len(earlier))},
        compiler_params=PARAMS,
        cost_estimate=pl.CostEstimate(flops=0, bytes_accessed=4 * outs[0][1] * outs[0][2], transcendentals=0),
    )(spot, near, *fars, *earlier)


def adagrad(table, state, grads):
    new_state = state + jnp.sum(grads * grads, axis=0, keepdims=True) * (1.0 / grads.shape[0])
    return table - grads * (step_rate / jnp.sqrt(new_state)), new_state


def keep_and_send(core, first, second):
    return jnp.where(core == 0, first, second), jnp.where(core == 0, second, first)


def table_counts(rows, negs, weight):
    place = lax.broadcasted_iota(jnp.int32, (rows, negs.shape[1]), 0)
    return jnp.sum(jnp.where(place == negs, weight, 0.0), axis=1, keepdims=True)


def turned(x, r, half):
    x0, x1, r0, r1 = x[:half], x[half:], r[:half], r[half:]
    return jnp.concatenate([x0 * r0 - x1 * r1, x0 * r1 + x1 * r0], axis=0)


def turned_back(x, r, half):
    x0, x1, r0, r1 = x[:half], x[half:], r[:half], r[half:]
    return x0 * r0 + x1 * r1, x1 * r0 - x0 * r1


EDGE_TILE = 512


def edge_span(step):
    return pl.ds(pl.multiple_of(step * EDGE_TILE, EDGE_TILE), EDGE_TILE)


def bucket_kernel(
    bucket, core_ref, heads_ref, tails_ref, negs_ref, left_ref, left_sums_ref, right_ref, right_sums_ref, rel_ref, hub_ref,
    left_out, left_sums_out, right_out, keep_out, send_out,
    left_parts, both_parts, left_grad, both_grad,
):
    features, rows = left_ref.shape
    half = features // 2
    core = core_ref[1]
    edges = heads_ref.shape[1]
    hubs = keep_out.shape[1] - edges
    at = slice(bucket, bucket + 1)
    weight = 1.0 / (negs_ref.shape[1] + hubs)
    counts = table_counts(rows, negs_ref[at], weight)
    stack_into(left_parts, left_ref[...])
    stack_into(both_parts, right_ref[...], slice(0, rows))
    stack_into(both_parts, hub_ref[...], slice(rows, rows + hubs))
    left_grad[...] = jnp.zeros_like(left_grad)
    both_grad[...] = jnp.zeros_like(both_grad)

    @pl.loop(0, edges // EDGE_TILE)
    def _(step):
        span = edge_span(step)
        tail_here = lax.broadcasted_iota(jnp.int32, (rows, EDGE_TILE), 0) == tails_ref[at, span]
        head_hot = onehot(0, rows, heads_ref[at, span])
        h = dot2(left_parts[...], head_hot, NN)
        r = rel_ref[:, span]
        q = split(turned(h, r, half))
        scores = dot3((both_parts[:features], both_parts[features:]), q, TN)
        chance = jax.nn.sigmoid(scores[:rows])
        coef = jnp.concatenate(
            [
                counts * chance + jnp.where(tail_here, chance - 1.0, 0.0),
                weight * jax.nn.sigmoid(scores[rows:]),
            ],
            axis=0,
        )
        coef = split(coef)
        dq = dot3_stacked(both_parts[...], coef, NN)
        both_grad[...] += dot3_stacked(stack(q), coef, NT)
        dh = jnp.concatenate(turned_back(dq, r, half), axis=0)
        left_grad[...] += dot2(stack(split(dh)), head_hot, NT)
        out_span = pl.ds(pl.multiple_of(hubs + step * EDGE_TILE, 128), EDGE_TILE)
        keep_out[:, out_span], send_out[:, out_span] = keep_and_send(core, *turned_back(dq, h, half))

    left_out[...], left_sums_out[...] = adagrad(left_ref[...], left_sums_ref[...], left_grad[...])
    new_right, new_sums = adagrad(right_ref[...], right_sums_ref[...], both_grad[:, :rows])
    right_out[:features] = new_right
    right_out[features:] = jnp.broadcast_to(new_sums, (right_out.shape[0] - features, rows))
    keep_out[:, :hubs], send_out[:, :hubs] = keep_and_send(core, both_grad[:half, rows:], both_grad[half:, rows:])


def bucket_step(bucket, core, heads, tails, negs, left, left_sums, right, right_sums, rel_rows, hub_rows):
    features, rows = left.shape
    edges, hubs = heads.shape[1], hub_rows.shape[1]
    width = rows + hubs
    shapes = [(features, rows), (1, rows), (features + 8, rows)] + [(features // 2, hubs + edges)] * 2
    return pl.pallas_call(
        functools.partial(bucket_kernel, bucket),
        in_specs=[SMEM] + [VMEM] * 9,
        out_specs=[VMEM] * 5,
        out_shape=[jax.ShapeDtypeStruct(shape, F32) for shape in shapes],
        scratch_shapes=[
            pltpu.VMEM((2 * features, rows), BF16),
            pltpu.VMEM((2 * features, width), BF16),
            pltpu.VMEM((features, rows), F32),
            pltpu.VMEM((features, width), F32),
        ],
        compiler_params=PARAMS,
        cost_estimate=COST,
    )(core, heads, tails, negs, left, left_sums, right, right_sums, rel_rows, hub_rows)


def hub_kernel(
    bucket, negatives, core_ref, heads_ref, left_ref, rel_ref, hub_ref,
    query_grad, hub_keep, hub_send,
    left_parts, hub_parts, hub_grad,
):
    features, rows = left_ref.shape
    half = features // 2
    edges, hubs = heads_ref.shape[1], hub_keep.shape[1]
    at = slice(bucket, bucket + 1)
    weight = 1.0 / (negatives + hubs)
    stack_into(left_parts, left_ref[...])
    stack_into(hub_parts, hub_ref[...])
    hub_grad[...] = jnp.zeros_like(hub_grad)

    @pl.loop(0, edges // EDGE_TILE)
    def _(step):
        span = edge_span(step)
        head_hot = onehot(0, rows, heads_ref[at, span])
        h = dot2(left_parts[...], head_hot, NN)
        q = split(turned(h, rel_ref[:, span], half))
        coef = split(weight * jax.nn.sigmoid(dot3((hub_parts[:features], hub_parts[features:]), q, TN)))
        query_grad[:, span] = dot3_stacked(hub_parts[...], coef, NN)
        hub_grad[...] += dot3_stacked(stack(q), coef, NT)

    hub_keep[...], hub_send[...] = keep_and_send(core_ref[1], hub_grad[:half], hub_grad[half:])


def hub_step(bucket, negatives, core, heads, left, rel_rows, hub_rows):
    features, rows = left.shape
    edges, hubs = heads.shape[1], hub_rows.shape[1]
    shapes = [(features, edges)] + [(features // 2, hubs)] * 2
    return pl.pallas_call(
        functools.partial(hub_kernel, bucket, negatives),
        in_specs=[SMEM] + [VMEM] * 4,
        out_specs=[VMEM] * 3,
        out_shape=[jax.ShapeDtypeStruct(shape, F32) for shape in shapes],
        scratch_shapes=[
            pltpu.VMEM((2 * features, rows), BF16),
            pltpu.VMEM((2 * features, hubs), BF16),
            pltpu.VMEM((features, hubs), F32),
        ],
        compiler_params=PARAMS,
        cost_estimate=COST,
    )(core, heads, left, rel_rows, hub_rows)


def tables_kernel(
    bucket, hubs, core_ref, heads_ref, tails_ref, negs_ref, query_grad,
    left_ref, left_sums_ref, right_ref, rel_ref,
    left_out, right_out, rel_keep, rel_send,
    left_parts, right_parts, left_grad, right_grad,
):
    features, rows = left_ref.shape
    half = features // 2
    edges = heads_ref.shape[1]
    at = slice(bucket, bucket + 1)
    core = core_ref[1]
    counts = table_counts(rows, negs_ref[at], 1.0 / (negs_ref.shape[1] + hubs))
    stack_into(left_parts, left_ref[...])
    stack_into(right_parts, right_ref[:features])
    left_grad[...] = jnp.zeros_like(left_grad)
    right_grad[...] = jnp.zeros_like(right_grad)

    @pl.loop(0, edges // EDGE_TILE)
    def _(step):
        span = edge_span(step)
        tail_here = lax.broadcasted_iota(jnp.int32, (rows, EDGE_TILE), 0) == tails_ref[at, span]
        head_hot = onehot(0, rows, heads_ref[at, span])
        h = dot2(left_parts[...], head_hot, NN)
        r = rel_ref[:, span]
        q = split(turned(h, r, half))
        chance = jax.nn.sigmoid(dot3((right_parts[:features], right_parts[features:]), q, TN))
        coef = split(counts * chance + jnp.where(tail_here, chance - 1.0, 0.0))
        dq = dot3_stacked(right_parts[...], coef, NN) + query_grad[:, span]
        right_grad[...] += dot3_stacked(stack(q), coef, NT)
        rel_keep[:, span], rel_send[:, span] = keep_and_send(core, *turned_back(dq, h, half))
        dh = jnp.concatenate(turned_back(dq, r, half), axis=0)
        left_grad[...] += dot2(stack(split(dh)), head_hot, NT)

    left_out[...], unused = adagrad(left_ref[...], left_sums_ref[...], left_grad[...])
    right_out[...], unused = adagrad(right_ref[:features], right_ref[features : features + 1], right_grad[...])


def tables_step(bucket, hubs, core, heads, tails, negs, query_grad, left, left_sums, right, rel_rows):
    features, rows = left.shape
    edges = heads.shape[1]
    shapes = [(features, rows)] * 2 + [(features // 2, edges)] * 2
    return pl.pallas_call(
        functools.partial(tables_kernel, bucket, hubs),
        in_specs=[SMEM] + [VMEM] * 8,
        out_specs=[VMEM] * 4,
        out_shape=[jax.ShapeDtypeStruct(shape, F32) for shape in shapes],
        scratch_shapes=[pltpu.VMEM((2 * features, rows), BF16)] * 2
        + [pltpu.VMEM((features, rows), F32)] * 2,
        compiler_params=PARAMS,
        cost_estimate=COST,
    )(core, heads, tails, negs, query_grad, left, left_sums, right, rel_rows)


def from_behind(x, axis, by):
    size = lax.axis_size(axis)
    return lax.ppermute(x, axis, [(i, (i + by) % size) for i in range(size)])


def flipped(x, axis, bit):
    return lax.ppermute(x, axis, [(i, i ^ (1 << bit)) for i in range(lax.axis_size(axis))])


def flipped_by(x, axis, offset):
    return lax.ppermute(x, axis, [(i, i ^ offset) for i in range(lax.axis_size(axis))])


def other_core(x):
    return flipped(x, "blk", 0)


def across(x, place):
    sub_bits = lax.axis_size("sub").bit_length() - 1
    if place < sub_bits:
        return flipped(x, "sub", place)
    return flipped(x, "blk", place - sub_bits + 1)


def stream_orders():
    sub_bits = lax.axis_size("sub").bit_length() - 1
    bits = sub_bits + lax.axis_size("blk").bit_length() - 2
    x, y, z, far = sub_bits, sub_bits + 1, 0, 1
    rest = [p for p in range(bits) if p not in (x, y, z, far)]
    return [[x, y, z, far] + rest, [y, z, x, far] + rest, [z, x, far, y] + rest]


def plane_orders(sub_bits, bits):
    plane, depth = list(range(sub_bits, bits)), list(range(sub_bits - 1, -1, -1))
    return [plane + depth, plane[1:] + plane[:1] + depth]


def row_spans(rows, parts):
    ends = [-(-rows * (i + 1) // (8 * parts)) * 8 for i in range(parts - 1)] + [rows]
    return list(zip([0] + ends[:-1], ends))


def shards(
    left_emb, left_state, right_emb, right_state, relation_emb, relation_state, hub_emb, hub_state,
    heads, relations, tails, negatives, hub_ids,
):
    components, half_width, row_count = left_emb.shape
    features = components * half_width
    rel_count, hub_count = relation_emb.shape[2], hub_emb.shape[2]
    left = left_emb.reshape(features, row_count)
    right = right_emb.reshape(features, row_count)
    left_sums = left_state.reshape(1, row_count)
    right_sums = right_state.reshape(1, row_count)
    buckets, edges = heads.shape
    hubs = hub_ids.shape[1]

    orders = stream_orders()
    streams, stages = len(orders), len(orders[0])
    chunks, depth = 1 << stages, lax.axis_size("sub")
    sub_bits = depth.bit_length() - 1
    planes = chunks // depth
    spans = row_spans(half_width, streams)
    rel_orders = plane_orders(sub_bits, stages)
    plane_spans, plane_pieces = rel_layout(half_width, len(rel_orders))
    rel_spans, joint_pieces = rel_layout(half_width, streams)
    heights, rel_heights, plane_heights = [[high - low for low, high in x] for x in (spans, rel_spans, plane_spans)]
    joint_heights = [h + r for h, r in zip(heights, rel_heights)]
    bases = [sum(joint_heights[:s]) for s in range(streams)]
    width = hub_count // chunks
    hub_lanes, rel_lanes = (0, hubs), (hubs, hubs + edges)

    def exchanged(parts, step):
        return [across(x, place) for x, (place, unused) in zip(parts, grouped(orders, step, heights)[0])]

    def in_turn(first, then):
        return lax.optimization_barrier((first, then))

    blk = lax.axis_index("blk")
    spot = jnp.stack([(blk >> 1) * depth + lax.axis_index("sub"), blk & 1]).astype(jnp.int32)
    far_ids = other_core((hub_ids, relations))
    hub_rows, rel_rows, spot, owned = gather_rows(
        spot, hub_emb.reshape(features, hub_count), hub_ids, relation_emb.reshape(features, rel_count), relations, chunks
    )
    far_ids, hub_rows = in_turn(far_ids, hub_rows)
    keeps, fars = [], []
    for b in range(buckets - 1):
        if b > 0:
            right, right_sums = right[:features], right[features : features + 1]
        left, left_sums, right, keep, send = bucket_step(
            b, spot, heads, tails, negatives, left, left_sums, right, right_sums, rel_rows[b], hub_rows[b]
        )
        right = from_behind(right, "blk", 1)
        keeps.append(keep)
        fars.append(other_core(send))
    last = buckets - 1
    query_grad, hub_keep, hub_send = hub_step(
        last, negatives.shape[1], spot, heads, left, rel_rows[last], hub_rows[last]
    )
    hub_far = other_core(hub_send)
    grads = lambda early, late, lanes: [(x, lanes) for x in early] + [(late, (0, late.shape[1]))]
    groups, where = grouped(orders, 0, heights)
    parts = chunk_columns(
        functools.partial(hub_chunks_kernel, orders, spans, where),
        [(chunks // 2, height, width) for height in [h for unused, h in groups] + heights],
        spot, (hub_ids, far_ids[0]), grads(keeps, hub_keep, hub_lanes) + grads(fars, hub_far, hub_lanes),
    )
    send, own = parts[: len(groups)], parts[len(groups) :]
    got = exchanged(send, 0)
    left, right, rel_keep, rel_send = tables_step(
        last, hubs, spot, heads, tails, negatives, query_grad, left, left_sums, right, rel_rows[last]
    )
    rel_far = other_core(rel_send)

    parts = chunk_columns(
        functools.partial(rel_chunks_kernel, rel_orders, plane_pieces, rel_count),
        [(chunks // 2, height, width) for height in plane_heights * 2],
        spot, (relations, far_ids[1]), grads(keeps, rel_keep, rel_lanes) + grads(fars, rel_far, rel_lanes),
    )
    rel_send, rel_own = parts[: len(rel_orders)], parts[len(rel_orders) :]
    rel_got = [across(x, order[0]) for x, order in zip(rel_send, rel_orders)]
    plane_steps = stages - sub_bits
    for step in range(stages - 1):
        if 0 < step < plane_steps:
            own, rel_got = in_turn(own, rel_got)
            rel_send, rel_own = halves(rel_own, rel_got, rel_orders, step - 1)
            rel_got = [across(x, order[step]) for x, order in zip(rel_send, rel_orders)]
        elif step == plane_steps:
            own, rel_got = in_turn(own, rel_got)
            rel_own, *rel_out = call(
                functools.partial(z_sums_kernel, plane_spans), [*rel_own, *rel_got],
                [(1, plane_spans[-1][1], width)] * depth,
            )
            rel_got = [flipped_by(x, "sub", q + 1) for q, x in enumerate(rel_out)]
        rel_own, got = in_turn(rel_own, got)
        send, own = halves(own, got, orders, step)
        got = exchanged(send, step + 1)

    *totals, rel_total, squares = call(
        functools.partial(squares_kernel, heights, grouped(orders, stages - 1, heights)[1]),
        [*own, *got, rel_own, *rel_got], [x.shape for x in own] + [rel_own.shape, (2, width)],
    )
    hub_own, rel_own = owned
    groups, there = grouped(orders, stages - 1, joint_heights)
    ins = [
        *totals, rel_total, squares, other_core(squares),
        hub_own, hub_state[None], rel_own, relation_state[None],
    ]
    have = pl.pallas_call(
        functools.partial(update_kernel, spans, rel_spans, joint_pieces, there, features),
        in_specs=[SMEM] + [VMEM] * len(ins),
        out_specs=[VMEM] * len(groups),
        out_shape=[jax.ShapeDtypeStruct((1, height, width), F32) for unused, height in groups],
        scratch_shapes=[pltpu.VMEM((1, x.shape[1]), F32) for x in owned],
        compiler_params=PARAMS,
        cost_estimate=COST,
    )(spot, *ins)
    for step in range(stages - 1, 1, -1):
        have = join(have, exchanged(have, step), orders, step, joint_heights)
    have, near = join_all(have, exchanged(have, 1), orders, 1, joint_heights)
    got = exchanged(have, 0)
    far_near = other_core(near)

    shapes = [hub_emb.shape, relation_emb.shape]
    by_copy = width % 128 == 0
    hub_new = []
    if by_copy:
        near_step = functools.partial(near_kernel, orders, spans, bases)
        hub_new = placed(functools.partial(near_step, True), [], spot, near, [], shapes[:1], [])
        hub_new = placed(functools.partial(near_step, False), [], spot, far_near, [], shapes[:1], hub_new)
        got, hub_new = in_turn(got, hub_new)
    far_step = functools.partial(far_kernel, orders, spans, bases, joint_pieces, by_copy)
    scratch = [
        pltpu.VMEM((8, 128) if by_copy else (half_width, hub_count), F32),
        pltpu.VMEM((half_width, rel_count), F32),
    ]
    far_got = other_core(got)
    out = placed(functools.partial(far_step, True), scratch, spot, near, got, shapes, hub_new)
    hub_new, rel_new = placed(functools.partial(far_step, False), scratch, spot, far_near, far_got, shapes, out)
    return (
        left.reshape(components, half_width, row_count),
        right.reshape(components, half_width, row_count),
        rel_new,
        hub_new,
    )


def solution(mesh):
    both = ("blk", "sub")
    block, table, whole = P(None, None, both), P(None, both), P()
    return jax.shard_map(
        shards,
        mesh=mesh,
        in_specs=(block, P(both), block, P(both), whole, whole, whole, whole, table, table, table, table, table),
        out_specs=(block, block, whole, whole),
        check_vma=False,
    )
```

```python
import functools
import jax
import jax.numpy as jnp
from jax import lax
from jax.experimental import pallas as pl
from jax.experimental.pallas import tpu as pltpu
from jax.sharding import PartitionSpec as P

step_rate = 0.25
F32, BF16 = jnp.float32, jnp.bfloat16
NN = (((1,), (0,)), ((), ()))
NT = (((1,), (1,)), ((), ()))
TN = (((0,), (0,)), ((), ()))
VMEM = pl.BlockSpec(memory_space=pltpu.VMEM)
SMEM = pl.BlockSpec(memory_space=pltpu.SMEM)
PARAMS = pltpu.CompilerParams(vmem_limit_bytes=12 * 1024 * 1024)
GATHER_PARAMS = pltpu.CompilerParams(vmem_limit_bytes=50 * 1024 * 1024)
HBM = pl.BlockSpec(memory_space=pltpu.HBM)
COST = pl.CostEstimate(flops=10000, bytes_accessed=10000, transcendentals=0)


def split(x):
    hi = x.astype(BF16)
    return hi, (x - hi.astype(F32)).astype(BF16)


def dot(a, b, dims):
    return lax.dot_general(a, b, dims, preferred_element_type=F32)


def dot3(a, b, dims):
    return dot(a[0], b[0], dims) + (dot(a[0], b[1], dims) + dot(a[1], b[0], dims))


def dot2(stacked, onehot, dims):
    half = stacked.shape[0] // 2
    both = dot(stacked, onehot, dims)
    return both[:half] + both[half:]


def stack(parts):
    return jnp.concatenate(parts, axis=0)


def stack_into(ref, x, lanes=slice(None)):
    rows, half = x.shape[0], ref.shape[0] // 2
    hi, lo = split(x)
    ref[:rows, lanes] = hi
    ref[half : half + rows, lanes] = lo
    if half > rows:
        blank = jnp.zeros((half - rows, x.shape[1]), BF16)
        ref[rows:half, lanes] = blank
        ref[half + rows :, lanes] = blank


def dot3_stacked(stacked, b, dims):
    half = stacked.shape[0] // 2
    both = dot(stacked, b[0], dims)
    return both[:half] + (both[half:] + dot(stacked[:half], b[1], dims))


def hot_where(here):
    return jnp.where(here, jnp.ones((), BF16), jnp.zeros((), BF16))


def onehot(first, rows, idx):
    place = lax.broadcasted_iota(jnp.int16, (rows, idx.shape[1]), 0)
    return hot_where(place == (idx - first).astype(jnp.int16))


def laid_out(idx):
    return jnp.concatenate([idx[b : b + 1] for b in range(idx.shape[0])], axis=1)


def take_owned(spot_ref, chunks, span, first, piece_of, out_ref):
    width = out_ref.shape[1]
    for chunk in range(chunks):
        if first <= chunk * width < first + span:

            @pl.when(spot_ref[0] == chunk)
            def _():
                out_ref[...] = piece_of(slice(chunk * width - first, (chunk + 1) * width - first))


def gather_kernel(hub_steps, rel_steps, spot_ref, hub_ids, rel_ids, hub_ref, rel_ref, *refs):
    buckets = hub_ids.shape[0]
    hub_outs, rel_outs = refs[:buckets], refs[buckets : 2 * buckets]
    spot_out, hub_own, rel_own = refs[2 * buckets : 2 * buckets + 3]
    hub_buf, rel_buf, hub_idx, rel_idx, stacked, sems = refs[2 * buckets + 3 :]
    hub_tile, rel_tile = hub_buf.shape[2], rel_buf.shape[2]
    chunks = hub_ref.shape[1] // hub_own.shape[1]
    half = hub_own.shape[0]
    steps = [(hub_ref, hub_buf, hub_tile, k) for k in range(hub_steps)]
    steps += [(rel_ref, rel_buf, rel_tile, k) for k in range(rel_steps)]
    copies = [
        pltpu.make_async_copy(table.at[:, pl.ds(k * tile, tile)], buf.at[k % 2], sems.at[i])
        for i, (table, buf, tile, k) in enumerate(steps)
    ]
    id_copies = [
        pltpu.make_async_copy(ids, out, sems.at[len(copies) + i])
        for i, (ids, out) in enumerate([(hub_ids, hub_idx), (rel_ids, rel_idx)])
    ]
    for copy in [*id_copies, copies[0]]:
        copy.start()
    spot_out[0] = spot_ref[0]
    spot_out[1] = spot_ref[1]
    for copy in id_copies:
        copy.wait()
    rows = pl.ds(pl.multiple_of(spot_ref[1] * half, 8), half)
    for i, (table, buf, tile, k) in enumerate(steps):
        if i + 1 < len(steps):
            copies[i + 1].start()
        idx, outs, own = (hub_idx, hub_outs, hub_own) if table is hub_ref else (rel_idx, rel_outs, rel_own)
        count = idx.shape[1]
        hot = onehot(k * tile, tile, laid_out(idx[...]))
        copies[i].wait()
        stack_into(stacked, buf[k % 2], slice(0, tile))
        part = dot2(stacked[:, :tile], hot, NN)
        for b, out in enumerate(outs):
            here = part[:, b * count : (b + 1) * count]
            out[...] = here if k == 0 else out[...] + here
        take_owned(spot_ref, chunks, tile, k * tile, lambda lanes: buf[k % 2, rows, lanes], own)


def gather_rows(spot, hub_table, hub_idx, rel_table, rel_idx, chunks):
    features = hub_table.shape[0]
    hub_steps, rel_steps = 4, 2
    hub_tile, rel_tile = hub_table.shape[1] // hub_steps, rel_table.shape[1] // rel_steps
    buckets, hubs = hub_idx.shape
    edges = rel_idx.shape[1]
    hub_width, rel_width = hub_table.shape[1] // chunks, rel_table.shape[1] // chunks
    shapes = [(features, hubs)] * buckets + [(features, edges)] * buckets
    own_shapes = [(features // 2, hub_width), (features // 2, rel_width)]
    floats = lambda shapes: [jax.ShapeDtypeStruct(shape, F32) for shape in shapes]
    out = pl.pallas_call(
        functools.partial(gather_kernel, hub_steps, rel_steps),
        in_specs=[SMEM] + [HBM] * 4,
        out_specs=[VMEM] * len(shapes) + [SMEM] + [VMEM] * len(own_shapes),
        out_shape=floats(shapes) + [jax.ShapeDtypeStruct((2,), jnp.int32)] + floats(own_shapes),
        scratch_shapes=[
            pltpu.VMEM((2, features, hub_tile), F32),
            pltpu.VMEM((2, features, rel_tile), F32),
            pltpu.VMEM(hub_idx.shape, jnp.int32),
            pltpu.VMEM(rel_idx.shape, jnp.int32),
            pltpu.VMEM((2 * features, max(hub_tile, rel_tile)), BF16),
            pltpu.SemaphoreType.DMA((hub_steps + rel_steps + 2,)),
        ],
        compiler_params=GATHER_PARAMS,
        cost_estimate=COST,
    )(spot, hub_idx, rel_idx, hub_table, rel_table)
    return out[:buckets], out[buckets : 2 * buckets], out[2 * buckets], out[2 * buckets + 1 :]


def spread_bits(place, order):
    bits = len(order)
    return sum((((place >> p) & 1) << (bits - 1 - i)) for i, p in enumerate(order))


def gather_bits(index, order):
    bits = len(order)
    return sum((((index >> (bits - 1 - i)) & 1) << p) for i, p in enumerate(order))


def load_columns(id_refs, grad_refs, idx_down, stacked):
    idx = jnp.concatenate([laid_out(ref[...]) for ref in id_refs], axis=1)
    idx_down[...] = jnp.transpose(jnp.broadcast_to(idx, (128, idx.shape[1]))).astype(jnp.int16)
    at = 0
    for ref, (low, high) in grad_refs:
        width = high - low
        stack_into(stacked, ref[:, low:high], slice(at, at + width))
        at += width


def onehot_across(idx_down, targets):
    width = targets.shape[1]
    idx = idx_down[...]
    wide = jnp.concatenate([idx] * -(-width // 128), axis=1)[:, :width]
    return hot_where(wide == targets.astype(jnp.int16))


def grouped(orders, step, heights):
    groups, where = [], []
    for s, order in enumerate(orders):
        for g, (place, members) in enumerate(groups):
            if place == order[step]:
                where.append((g, sum(heights[m] for m in members)))
                members.append(s)
                break
        else:
            where.append((len(groups), 0))
            groups.append((order[step], [s]))
    return [(place, sum(heights[m] for m in members)) for place, members in groups], where


def rows_of(where, heights, s):
    group, base = where[s]
    return group, slice(base, base + heights[s])


def put_chunk(place, orders, heights, where, sends, keeps, s, value):
    index, half = spread_bits(place, orders[s]), keeps[s].shape[0]
    if index < half:
        keeps[s][index] = value
    else:
        group, rows = rows_of(where, heights, s)
        sends[group][index - half, rows] = value


def chunk_refs(grad_lanes, refs):
    ids, refs = refs[:2], refs[2:]
    grads, refs = list(zip(refs, grad_lanes)), refs[len(grad_lanes) :]
    return ids, grads, refs[:-2], refs[-2:]


def hub_chunks_kernel(orders, spans, where, grad_lanes, spot_ref, *refs):
    ids, grads, outs, (idx_down, stacked) = chunk_refs(grad_lanes, refs)
    load_columns(ids, grads, idx_down, stacked)
    streams = len(orders)
    sends, keeps = outs[:-streams], outs[-streams:]
    heights = [high - low for low, high in spans]
    chunks, width = 2 * keeps[0].shape[0], keeps[0].shape[2]
    lane = lax.broadcasted_iota(jnp.int32, (1, width), 1)
    for place in range(chunks):
        hot = onehot_across(idx_down, lane + (spot_ref[0] ^ place) * width)
        chunk = dot2(stacked[...], hot, NN)
        for s, (low, high) in enumerate(spans):
            put_chunk(place, orders, heights, where, sends, keeps, s, chunk[low:high])


def rel_layout(half_width, streams):
    blocks = row_spans(half_width, 3)
    spans = row_spans(max(high - low for low, high in blocks), streams)
    pieces = []
    for block, (low, high) in enumerate(blocks):
        for s, (first, end) in enumerate(spans):
            count = min(end, high - low) - first
            if count > 0:
                pieces.append((block, s, low + first, count))
    return spans, pieces


def rel_chunks_kernel(orders, pieces, rows, grad_lanes, spot_ref, *refs):
    ids, grads, outs, (idx_down, stacked) = chunk_refs(grad_lanes, refs)
    load_columns(ids, grads, idx_down, stacked)
    for ref in outs:
        ref[...] = jnp.zeros_like(ref)
    streams = len(orders)
    sends, keeps = outs[:streams], outs[streams:]
    half, lanes = keeps[0].shape[0], keeps[0].shape[2]
    chunks = 2 * half
    width = rows // chunks
    group = lanes // width
    lane = lax.broadcasted_iota(jnp.int32, (1, lanes), 1)
    for first in range(0, chunks, group):
        targets = jnp.full((1, lanes), -1, jnp.int32)
        places = range(first, min(first + group, chunks))
        for slot, place in enumerate(places):
            here = (lane >= slot * width) & (lane < (slot + 1) * width)
            targets = jnp.where(here, lane + ((spot_ref[0] ^ place) * width - slot * width), targets)
        dense = dot2(stacked[...], onehot_across(idx_down, targets), NN)
        for slot, place in enumerate(places):
            chunk = dense[:, slot * width : (slot + 1) * width]
            for block, s, low, count in pieces:
                index = spread_bits(place, orders[s])
                out = sends[s].at[index - half] if index >= half else keeps[s].at[index]
                out[:count, block * width : (block + 1) * width] = chunk[low : low + count]


def chunk_columns(kernel, shapes, spot, ids, grads):
    half_width = grads[0][0].shape[0]
    grad_lanes = [lanes_of for unused, lanes_of in grads]
    count = sum(high - low for low, high in grad_lanes)
    return pl.pallas_call(
        functools.partial(kernel, grad_lanes),
        in_specs=[SMEM] + [VMEM] * (2 + len(grads)),
        out_specs=[VMEM] * len(shapes),
        out_shape=[jax.ShapeDtypeStruct(shape, F32) for shape in shapes],
        scratch_shapes=[
            pltpu.VMEM((count, 128), jnp.int16),
            pltpu.VMEM((2 * (-(-half_width // 16) * 16), count), BF16),
        ],
        compiler_params=PARAMS,
        cost_estimate=COST,
    )(spot, *ids, *[g for g, unused in grads])


def call(kernel, ins, shapes):
    return pl.pallas_call(
        kernel,
        in_specs=[VMEM] * len(ins),
        out_specs=[VMEM] * len(shapes),
        out_shape=[jax.ShapeDtypeStruct(shape, F32) for shape in shapes],
        compiler_params=PARAMS,
        cost_estimate=COST,
    )(*ins)


def sums_kernel(heights, here, there, *refs):
    streams, groups = len(heights), 1 + max(g for g, unused in here)
    own, got, sends, keeps = refs[:streams], refs[streams : streams + groups], refs[streams + groups : -streams], refs[-streams:]
    for s in range(streams):
        half = keeps[s].shape[0]
        group, rows = rows_of(here, heights, s)
        out, out_rows = rows_of(there, heights, s)
        sends[out][:, out_rows] = own[s][half:] + got[group][half:, rows]
        keeps[s][...] = own[s][:half] + got[group][:half, rows]


def halves(own, got, orders, step):
    heights = [x.shape[1] for x in own]
    half, width = own[0].shape[0] // 2, own[0].shape[2]
    unused, here = grouped(orders, step, heights)
    groups, there = grouped(orders, step + 1, heights)
    shapes = [(half, height, width) for height in [h for unused, h in groups] + heights]
    out = call(functools.partial(sums_kernel, heights, here, there), [*own, *got], shapes)
    return out[: len(groups)], out[len(groups) :]


def join_kernel(heights, here, there, *refs):
    groups = 1 + max(g for g, unused in here)
    own, got, outs = refs[:groups], refs[groups : 2 * groups], refs[2 * groups :]
    count = own[0].shape[0]
    for s in range(len(heights)):
        group, rows = rows_of(here, heights, s)
        out, out_rows = rows_of(there, heights, s)
        outs[out][:count, out_rows] = own[group][:, rows]
        outs[out][count:, out_rows] = got[group][:, rows]


def join(have, got, orders, step, heights):
    count, width = have[0].shape[0], have[0].shape[2]
    unused, here = grouped(orders, step, heights)
    groups, there = grouped(orders, step - 1, heights)
    shapes = [(2 * count, height, width) for unused, height in groups]
    return call(functools.partial(join_kernel, heights, here, there), [*have, *got], shapes)


def z_sums_kernel(spans, *refs):
    streams = len(spans)
    own, got, outs = refs[:streams], refs[streams : 2 * streams], refs[2 * streams :]
    for place, out in enumerate(outs):
        for s, (low, high) in enumerate(spans):
            out[0, low:high] = own[s][place] + got[s][place]


def squares_kernel(heights, here, *refs):
    streams, groups = len(heights), 1 + max(g for g, unused in here)
    own, got, rels = refs[:streams], refs[streams : streams + groups], refs[streams + groups : -streams - 2]
    totals, rel_total, out = refs[-streams - 2 : -2], refs[-2], refs[-1]
    squares = jnp.zeros((1, out.shape[1]), F32)
    for s in range(streams):
        group, rows = rows_of(here, heights, s)
        total = own[s][0] + got[group][0, rows]
        totals[s][0] = total
        squares += jnp.sum(total * total, axis=0, keepdims=True)
    total = sum(ref[0] for ref in rels)
    rel_total[0] = total
    out[0:1] = squares
    out[1:2] = jnp.sum(total * total, axis=0, keepdims=True)


def update_kernel(spans, rel_spans, pieces, there, features, spot_ref, *refs):
    streams, groups = len(spans), 1 + max(g for g, unused in there)
    totals, (hub_sums, rel_sums), news = refs[:streams], refs[-2:], refs[-groups - 2 : -2]
    rel_total, mine, other, hub_ref, hub_all, rel_ref, rel_all = refs[streams : -groups - 2]
    chunks = hub_all.shape[1] // hub_ref.shape[1]
    take_owned(spot_ref, chunks, hub_all.shape[1], 0, lambda lanes: hub_all[:, lanes], hub_sums)
    take_owned(spot_ref, chunks, rel_all.shape[1], 0, lambda lanes: rel_all[:, lanes], rel_sums)
    width = rel_ref.shape[1]
    squares = mine[...] + other[...]
    hub_scale = step_rate / jnp.sqrt(hub_sums[...] + squares[0:1] * (1.0 / features))
    rel_squares = sum(squares[1:2, b * width : (b + 1) * width] for b in range(3))
    rel_scale = step_rate / jnp.sqrt(rel_sums[...] + rel_squares * (1.0 / features))
    for s, (low, high) in enumerate(spans):
        new, base = there[s]
        first, end = rel_spans[s]
        middle = base + high - low
        news[new][0, base:middle] = hub_ref[low:high] - totals[s][0] * hub_scale
        news[new][0, middle : middle + end - first] = jnp.zeros((end - first, news[new].shape[2]), F32)
    for block, s, low, count in pieces:
        new, base = there[s]
        base += spans[s][1] - spans[s][0]
        lanes, first = slice(block * width, (block + 1) * width), rel_spans[s][0]
        news[new][0, base : base + count, lanes] = (
            rel_ref[low : low + count] - rel_total[0, first : first + count, lanes] * rel_scale
        )


def join_all_kernel(heights, here, there, *refs):
    groups = 1 + max(g for g, unused in here)
    join_kernel(heights, here, there, *refs[:-1])
    base = 0
    for s, height in enumerate(heights):
        group, rows = rows_of(here, heights, s)
        for i, ref in enumerate((refs[group], refs[groups + group])):
            count = ref.shape[0]
            refs[-1][i * count : (i + 1) * count, base : base + height] = ref[:, rows]
        base += height


def join_all(have, got, orders, step, heights):
    count, width = 2 * have[0].shape[0], have[0].shape[2]
    unused, here = grouped(orders, step, heights)
    groups, there = grouped(orders, step - 1, heights)
    shapes = [(count, height, width) for height in [h for unused, h in groups] + [sum(heights)]]
    *have, near = call(functools.partial(join_all_kernel, heights, here, there), [*have, *got], shapes)
    return have, near


def chunk_copies(part, base, first, order, span, chip, component, out_ref, sems, at):
    low, high = span
    width = part.shape[2]
    for index in range(part.shape[0]):
        chunk = chip ^ gather_bits(first + index, order)
        lanes = pl.ds(pl.multiple_of(chunk * width, width), width)
        target = out_ref.at[component, pl.ds(low, high - low), lanes]
        yield pltpu.make_async_copy(part.at[index, pl.ds(base, high - low)], target, sems.at[at + index])


def component_of(spot_ref, mine):
    return spot_ref[1] if mine else 1 - spot_ref[1]


def near_kernel(orders, spans, bases, mine, spot_ref, near_ref, *refs):
    component = component_of(spot_ref, mine)
    out_ref, sems = refs[-2:]
    copies = []
    for order, span, base in zip(orders, spans, bases):
        copies += chunk_copies(near_ref, base, 0, order, span, spot_ref[0], component, out_ref, sems, len(copies))
    for copy in copies:
        copy.start()
    for copy in copies:
        copy.wait()


def far_kernel(orders, spans, bases, pieces, by_copy, mine, spot_ref, near_ref, *refs):
    component = component_of(spot_ref, mine)
    streams = len(orders)
    fars = refs[:streams]
    hub_out, rel_out, hub_all, rel_all, sems = refs[-5:]
    half = near_ref.shape[0]
    hub_width, rel_width = hub_out.shape[2] // (2 * half), rel_out.shape[2] // (2 * half)
    copies = []
    if by_copy:
        for far, order, span in zip(fars, orders, spans):
            copies += chunk_copies(far, 0, half, order, span, spot_ref[0], component, hub_out, sems, len(copies))
        for copy in copies:
            copy.start()
    for chunk in range(2 * half):
        place = spot_ref[0] ^ chunk
        for s, (low, high) in enumerate(spans):
            index = spread_bits(place, orders[s])
            spot = index & (half - 1)
            height, end = high - low, fars[s].shape[1]
            if not by_copy:
                value = jnp.where(index >= half, fars[s][spot, :height], near_ref[spot, bases[s] : bases[s] + height])
                hub_all[low:high, chunk * hub_width : (chunk + 1) * hub_width] = value
            value = jnp.where(index >= half, fars[s][spot, height:], near_ref[spot, bases[s] + height : bases[s] + end])
            for block, stream, row, count in pieces:
                if stream == s:
                    part = value[:count, block * rel_width : (block + 1) * rel_width]
                    rel_all[row : row + count, chunk * rel_width : (chunk + 1) * rel_width] = part
    copies.append(pltpu.make_async_copy(rel_all, rel_out.at[component], sems.at[len(copies)]))
    copies[-1].start()
    if not by_copy:
        copies.append(pltpu.make_async_copy(hub_all, hub_out.at[component], sems.at[len(copies)]))
        copies[-1].start()
    for copy in copies:
        copy.wait()


def placed(kernel, scratch, spot, near, fars, outs, earlier):
    sems = pltpu.SemaphoreType.DMA((3 * near.shape[0] + 2,))
    return pl.pallas_call(
        kernel,
        in_specs=[SMEM] + [VMEM] * (1 + len(fars)) + [HBM] * len(earlier),
        out_specs=[HBM] * len(outs),
        out_shape=[jax.ShapeDtypeStruct(shape, F32) for shape in outs],
        scratch_shapes=scratch + [sems],
        input_output_aliases={2 + len(fars) + i: i for i in range(len(earlier))},
        compiler_params=PARAMS,
        cost_estimate=pl.CostEstimate(flops=0, bytes_accessed=4 * outs[0][1] * outs[0][2], transcendentals=0),
    )(spot, near, *fars, *earlier)


def adagrad(table, state, grads):
    new_state = state + jnp.sum(grads * grads, axis=0, keepdims=True) * (1.0 / grads.shape[0])
    return table - grads * (step_rate / jnp.sqrt(new_state)), new_state


def keep_and_send(core, first, second):
    return jnp.where(core == 0, first, second), jnp.where(core == 0, second, first)


def table_counts(rows, negs, weight):
    place = lax.broadcasted_iota(jnp.int32, (rows, negs.shape[1]), 0)
    return jnp.sum(jnp.where(place == negs, weight, 0.0), axis=1, keepdims=True)


def turned(x, r, half):
    x0, x1, r0, r1 = x[:half], x[half:], r[:half], r[half:]
    return jnp.concatenate([x0 * r0 - x1 * r1, x0 * r1 + x1 * r0], axis=0)


def turned_back(x, r, half):
    x0, x1, r0, r1 = x[:half], x[half:], r[:half], r[half:]
    return x0 * r0 + x1 * r1, x1 * r0 - x0 * r1


EDGE_TILE = 512


def bucket_kernel(
    bucket, core_ref, heads_ref, tails_ref, negs_ref, left_ref, left_sums_ref, right_ref, right_sums_ref, rel_ref, hub_ref,
    left_out, left_sums_out, right_out, keep_out, send_out,
    left_parts, both_parts,
):
    features, rows = left_ref.shape
    half = features // 2
    core = core_ref[1]
    edges = heads_ref.shape[1]
    hubs = keep_out.shape[1] - edges
    at = slice(bucket, bucket + 1)
    weight = 1.0 / (negs_ref.shape[1] + hubs)
    counts = table_counts(rows, negs_ref[at], weight)
    stack_into(left_parts, left_ref[...])
    stack_into(both_parts, right_ref[...], slice(0, rows))
    stack_into(both_parts, hub_ref[...], slice(rows, rows + hubs))

    tail_here = lax.broadcasted_iota(jnp.int32, (rows, edges), 0) == tails_ref[at]
    head_hot = onehot(0, rows, heads_ref[at])
    h = dot2(left_parts[...], head_hot, NN)
    r = rel_ref[...]
    q = split(turned(h, r, half))
    scores = dot3((both_parts[:features], both_parts[features:]), q, TN)
    chance = jax.nn.sigmoid(scores[:rows])
    coef = jnp.concatenate(
        [
            counts * chance + jnp.where(tail_here, chance - 1.0, 0.0),
            weight * jax.nn.sigmoid(scores[rows:]),
        ],
        axis=0,
    )
    coef = split(coef)
    dq = dot3_stacked(both_parts[...], coef, NN)
    both_grad = dot3_stacked(stack(q), coef, NT)
    dh = jnp.concatenate(turned_back(dq, r, half), axis=0)
    left_grad = dot2(stack(split(dh)), head_hot, NT)
    keep_out[:, hubs:], send_out[:, hubs:] = keep_and_send(core, *turned_back(dq, h, half))

    left_out[...], left_sums_out[...] = adagrad(left_ref[...], left_sums_ref[...], left_grad)
    new_right, new_sums = adagrad(right_ref[...], right_sums_ref[...], both_grad[:, :rows])
    right_out[:features] = new_right
    right_out[features:] = jnp.broadcast_to(new_sums, (right_out.shape[0] - features, rows))
    keep_out[:, :hubs], send_out[:, :hubs] = keep_and_send(core, both_grad[:half, rows:], both_grad[half:, rows:])


def bucket_step(bucket, core, heads, tails, negs, left, left_sums, right, right_sums, rel_rows, hub_rows):
    features, rows = left.shape
    edges, hubs = heads.shape[1], hub_rows.shape[1]
    width = rows + hubs
    shapes = [(features, rows), (1, rows), (features + 8, rows)] + [(features // 2, hubs + edges)] * 2
    return pl.pallas_call(
        functools.partial(bucket_kernel, bucket),
        in_specs=[SMEM] + [VMEM] * 9,
        out_specs=[VMEM] * 5,
        out_shape=[jax.ShapeDtypeStruct(shape, F32) for shape in shapes],
        scratch_shapes=[
            pltpu.VMEM((2 * features, rows), BF16),
            pltpu.VMEM((2 * features, width), BF16),
        ],
        compiler_params=PARAMS,
        cost_estimate=COST,
    )(core, heads, tails, negs, left, left_sums, right, right_sums, rel_rows, hub_rows)


def hub_kernel(
    bucket, negatives, core_ref, heads_ref, left_ref, rel_ref, hub_ref,
    query_grad, hub_keep, hub_send,
    left_parts, hub_parts,
):
    features, rows = left_ref.shape
    half = features // 2
    edges, hubs = heads_ref.shape[1], hub_keep.shape[1]
    at = slice(bucket, bucket + 1)
    weight = 1.0 / (negatives + hubs)
    stack_into(left_parts, left_ref[...])
    stack_into(hub_parts, hub_ref[...])

    head_hot = onehot(0, rows, heads_ref[at])
    h = dot2(left_parts[...], head_hot, NN)
    q = split(turned(h, rel_ref[...], half))
    coef = split(weight * jax.nn.sigmoid(dot3((hub_parts[:features], hub_parts[features:]), q, TN)))
    query_grad[...] = dot3_stacked(hub_parts[...], coef, NN)
    hub_grad = dot3_stacked(stack(q), coef, NT)

    hub_keep[...], hub_send[...] = keep_and_send(core_ref[1], hub_grad[:half], hub_grad[half:])


def hub_step(bucket, negatives, core, heads, left, rel_rows, hub_rows):
    features, rows = left.shape
    edges, hubs = heads.shape[1], hub_rows.shape[1]
    shapes = [(features, edges)] + [(features // 2, hubs)] * 2
    return pl.pallas_call(
        functools.partial(hub_kernel, bucket, negatives),
        in_specs=[SMEM] + [VMEM] * 4,
        out_specs=[VMEM] * 3,
        out_shape=[jax.ShapeDtypeStruct(shape, F32) for shape in shapes],
        scratch_shapes=[
            pltpu.VMEM((2 * features, rows), BF16),
            pltpu.VMEM((2 * features, hubs), BF16),
        ],
        compiler_params=PARAMS,
        cost_estimate=COST,
    )(core, heads, left, rel_rows, hub_rows)


def tables_kernel(
    bucket, hubs, core_ref, heads_ref, tails_ref, negs_ref, query_grad,
    left_ref, left_sums_ref, right_ref, rel_ref,
    left_out, right_out, rel_keep, rel_send,
    left_parts, right_parts,
):
    features, rows = left_ref.shape
    half = features // 2
    edges = heads_ref.shape[1]
    at = slice(bucket, bucket + 1)
    core = core_ref[1]
    counts = table_counts(rows, negs_ref[at], 1.0 / (negs_ref.shape[1] + hubs))
    stack_into(left_parts, left_ref[...])
    stack_into(right_parts, right_ref[:features])

    tail_here = lax.broadcasted_iota(jnp.int32, (rows, edges), 0) == tails_ref[at]
    head_hot = onehot(0, rows, heads_ref[at])
    h = dot2(left_parts[...], head_hot, NN)
    r = rel_ref[...]
    q = split(turned(h, r, half))
    chance = jax.nn.sigmoid(dot3((right_parts[:features], right_parts[features:]), q, TN))
    coef = split(counts * chance + jnp.where(tail_here, chance - 1.0, 0.0))
    dq = dot3_stacked(right_parts[...], coef, NN) + query_grad[...]
    right_grad = dot3_stacked(stack(q), coef, NT)
    rel_keep[...], rel_send[...] = keep_and_send(core, *turned_back(dq, h, half))
    dh = jnp.concatenate(turned_back(dq, r, half), axis=0)
    left_grad = dot2(stack(split(dh)), head_hot, NT)

    left_out[...], unused = adagrad(left_ref[...], left_sums_ref[...], left_grad)
    right_out[...], unused = adagrad(right_ref[:features], right_ref[features : features + 1], right_grad)


def tables_step(bucket, hubs, core, heads, tails, negs, query_grad, left, left_sums, right, rel_rows):
    features, rows = left.shape
    edges = heads.shape[1]
    shapes = [(features, rows)] * 2 + [(features // 2, edges)] * 2
    return pl.pallas_call(
        functools.partial(tables_kernel, bucket, hubs),
        in_specs=[SMEM] + [VMEM] * 8,
        out_specs=[VMEM] * 4,
        out_shape=[jax.ShapeDtypeStruct(shape, F32) for shape in shapes],
        scratch_shapes=[pltpu.VMEM((2 * features, rows), BF16)] * 2,
        compiler_params=PARAMS,
        cost_estimate=COST,
    )(core, heads, tails, negs, query_grad, left, left_sums, right, rel_rows)


def from_behind(x, axis, by):
    size = lax.axis_size(axis)
    return lax.ppermute(x, axis, [(i, (i + by) % size) for i in range(size)])


def flipped(x, axis, bit):
    return lax.ppermute(x, axis, [(i, i ^ (1 << bit)) for i in range(lax.axis_size(axis))])


def flipped_by(x, axis, offset):
    return lax.ppermute(x, axis, [(i, i ^ offset) for i in range(lax.axis_size(axis))])


def other_core(x):
    return flipped(x, "blk", 0)


def across(x, place):
    sub_bits = lax.axis_size("sub").bit_length() - 1
    if place < sub_bits:
        return flipped(x, "sub", place)
    return flipped(x, "blk", place - sub_bits + 1)


def stream_orders():
    sub_bits = lax.axis_size("sub").bit_length() - 1
    bits = sub_bits + lax.axis_size("blk").bit_length() - 2
    x, y, z, far = sub_bits, sub_bits + 1, 0, 1
    rest = [p for p in range(bits) if p not in (x, y, z, far)]
    return [[x, y, z, far] + rest, [y, z, x, far] + rest, [z, x, y, far] + rest]


def plane_orders(sub_bits, bits):
    plane, depth = list(range(sub_bits, bits)), list(range(sub_bits - 1, -1, -1))
    return [plane + depth, plane[1:] + plane[:1] + depth]


def row_spans(rows, parts):
    ends = [-(-rows * (i + 1) // (8 * parts)) * 8 for i in range(parts - 1)] + [rows]
    return list(zip([0] + ends[:-1], ends))


def shards(
    left_emb, left_state, right_emb, right_state, relation_emb, relation_state, hub_emb, hub_state,
    heads, relations, tails, negatives, hub_ids,
):
    components, half_width, row_count = left_emb.shape
    features = components * half_width
    rel_count, hub_count = relation_emb.shape[2], hub_emb.shape[2]
    left = left_emb.reshape(features, row_count)
    right = right_emb.reshape(features, row_count)
    left_sums = left_state.reshape(1, row_count)
    right_sums = right_state.reshape(1, row_count)
    buckets, edges = heads.shape
    hubs = hub_ids.shape[1]

    orders = stream_orders()
    streams, stages = len(orders), len(orders[0])
    chunks, depth = 1 << stages, lax.axis_size("sub")
    sub_bits = depth.bit_length() - 1
    planes = chunks // depth
    spans = row_spans(half_width, streams)
    rel_orders = plane_orders(sub_bits, stages)
    plane_spans, plane_pieces = rel_layout(half_width, len(rel_orders))
    rel_spans, joint_pieces = rel_layout(half_width, streams)
    heights, rel_heights, plane_heights = [[high - low for low, high in x] for x in (spans, rel_spans, plane_spans)]
    joint_heights = [h + r for h, r in zip(heights, rel_heights)]
    bases = [sum(joint_heights[:s]) for s in range(streams)]
    width = hub_count // chunks
    hub_lanes, rel_lanes = (0, hubs), (hubs, hubs + edges)

    def exchanged(parts, step):
        return [across(x, place) for x, (place, unused) in zip(parts, grouped(orders, step, heights)[0])]

    def in_turn(first, then):
        return lax.optimization_barrier((first, then))

    blk = lax.axis_index("blk")
    spot = jnp.stack([(blk >> 1) * depth + lax.axis_index("sub"), blk & 1]).astype(jnp.int32)
    far_ids = other_core((hub_ids, relations))
    hub_rows, rel_rows, spot, owned = gather_rows(
        spot, hub_emb.reshape(features, hub_count), hub_ids, relation_emb.reshape(features, rel_count), relations, chunks
    )
    far_ids, hub_rows = in_turn(far_ids, hub_rows)
    keeps, fars = [], []
    for b in range(buckets - 1):
        if b > 0:
            right = from_behind(right, "blk", 1)
            right, right_sums = right[:features], right[features : features + 1]
        left, left_sums, right, keep, send = bucket_step(
            b, spot, heads, tails, negatives, left, left_sums, right, right_sums, rel_rows[b], hub_rows[b]
        )
        keeps.append(keep)
        fars.append(other_core(send))
    last = buckets - 1
    query_grad, hub_keep, hub_send = hub_step(
        last, negatives.shape[1], spot, heads, left, rel_rows[last], hub_rows[last]
    )
    right, hub_send = in_turn(right, hub_send)
    hub_far = other_core(hub_send)
    right = from_behind(right, "blk", 1)
    grads = lambda early, late, lanes: [(x, lanes) for x in early] + [(late, (0, late.shape[1]))]
    groups, where = grouped(orders, 0, heights)
    parts = chunk_columns(
        functools.partial(hub_chunks_kernel, orders, spans, where),
        [(chunks // 2, height, width) for height in [h for unused, h in groups] + heights],
        spot, (hub_ids, far_ids[0]), grads(keeps, hub_keep, hub_lanes) + grads(fars, hub_far, hub_lanes),
    )
    send, own = parts[: len(groups)], parts[len(groups) :]
    got = exchanged(send, 0)
    left, right, rel_keep, rel_send = tables_step(
        last, hubs, spot, heads, tails, negatives, query_grad, left, left_sums, right, rel_rows[last]
    )
    rel_far = other_core(rel_send)

    parts = chunk_columns(
        functools.partial(rel_chunks_kernel, rel_orders, plane_pieces, rel_count),
        [(chunks // 2, height, width) for height in plane_heights * 2],
        spot, (relations, far_ids[1]), grads(keeps, rel_keep, rel_lanes) + grads(fars, rel_far, rel_lanes),
    )
    rel_send, rel_own = parts[: len(rel_orders)], parts[len(rel_orders) :]
    rel_got = [across(x, order[0]) for x, order in zip(rel_send, rel_orders)]
    plane_steps = stages - sub_bits
    for step in range(stages - 1):
        if 0 < step < plane_steps:
            own, rel_got = in_turn(own, rel_got)
            rel_send, rel_own = halves(rel_own, rel_got, rel_orders, step - 1)
            rel_got = [across(x, order[step]) for x, order in zip(rel_send, rel_orders)]
        elif step == plane_steps:
            own, rel_got = in_turn(own, rel_got)
            rel_own, *rel_out = call(
                functools.partial(z_sums_kernel, plane_spans), [*rel_own, *rel_got],
                [(1, plane_spans[-1][1], width)] * depth,
            )
            rel_got = [flipped_by(x, "sub", q + 1) for q, x in enumerate(rel_out)]
        rel_own, got = in_turn(rel_own, got)
        send, own = halves(own, got, orders, step)
        got = exchanged(send, step + 1)

    *totals, rel_total, squares = call(
        functools.partial(squares_kernel, heights, grouped(orders, stages - 1, heights)[1]),
        [*own, *got, rel_own, *rel_got], [x.shape for x in own] + [rel_own.shape, (2, width)],
    )
    hub_own, rel_own = owned
    groups, there = grouped(orders, stages - 1, joint_heights)
    ins = [
        *totals, rel_total, squares, other_core(squares),
        hub_own, hub_state[None], rel_own, relation_state[None],
    ]
    have = pl.pallas_call(
        functools.partial(update_kernel, spans, rel_spans, joint_pieces, there, features),
        in_specs=[SMEM] + [VMEM] * len(ins),
        out_specs=[VMEM] * len(groups),
        out_shape=[jax.ShapeDtypeStruct((1, height, width), F32) for unused, height in groups],
        scratch_shapes=[pltpu.VMEM((1, x.shape[1]), F32) for x in owned],
        compiler_params=PARAMS,
        cost_estimate=COST,
    )(spot, *ins)
    for step in range(stages - 1, 1, -1):
        have = join(have, exchanged(have, step), orders, step, joint_heights)
    have, near = join_all(have, exchanged(have, 1), orders, 1, joint_heights)
    got = exchanged(have, 0)
    far_near = other_core(near)

    shapes = [hub_emb.shape, relation_emb.shape]
    by_copy = width % 128 == 0
    hub_new = []
    if by_copy:
        near_step = functools.partial(near_kernel, orders, spans, bases)
        hub_new = placed(functools.partial(near_step, True), [], spot, near, [], shapes[:1], [])
        hub_new = placed(functools.partial(near_step, False), [], spot, far_near, [], shapes[:1], hub_new)
        got, hub_new = in_turn(got, hub_new)
    far_step = functools.partial(far_kernel, orders, spans, bases, joint_pieces, by_copy)
    scratch = [
        pltpu.VMEM((8, 128) if by_copy else (half_width, hub_count), F32),
        pltpu.VMEM((half_width, rel_count), F32),
    ]
    far_got = other_core(got)
    out = placed(functools.partial(far_step, True), scratch, spot, near, got, shapes, hub_new)
    hub_new, rel_new = placed(functools.partial(far_step, False), scratch, spot, far_near, far_got, shapes, out)
    return (
        left.reshape(components, half_width, row_count),
        right.reshape(components, half_width, row_count),
        rel_new,
        hub_new,
    )


def solution(mesh):
    both = ("blk", "sub")
    block, table, whole = P(None, None, both), P(None, both), P()
    return jax.shard_map(
        shards,
        mesh=mesh,
        in_specs=(block, P(both), block, P(both), whole, whole, whole, whole, table, table, table, table, table),
        out_specs=(block, block, whole, whole),
        check_vma=False,
    )
```

```python
import functools
import jax
import jax.numpy as jnp
from jax import lax
from jax.experimental import pallas as pl
from jax.experimental.pallas import tpu as pltpu
from jax.sharding import PartitionSpec as P

step_rate = 0.25
F32, BF16 = jnp.float32, jnp.bfloat16
NN = (((1,), (0,)), ((), ()))
NT = (((1,), (1,)), ((), ()))
TN = (((0,), (0,)), ((), ()))
VMEM = pl.BlockSpec(memory_space=pltpu.VMEM)
SMEM = pl.BlockSpec(memory_space=pltpu.SMEM)
PARAMS = pltpu.CompilerParams(vmem_limit_bytes=12 * 1024 * 1024)
GATHER_PARAMS = pltpu.CompilerParams(vmem_limit_bytes=50 * 1024 * 1024)
HBM = pl.BlockSpec(memory_space=pltpu.HBM)
COST = pl.CostEstimate(flops=10000, bytes_accessed=10000, transcendentals=0)


def split(x):
    hi = x.astype(BF16)
    return hi, (x - hi.astype(F32)).astype(BF16)


def dot(a, b, dims):
    return lax.dot_general(a, b, dims, preferred_element_type=F32)


def dot3(a, b, dims):
    return dot(a[0], b[0], dims) + (dot(a[0], b[1], dims) + dot(a[1], b[0], dims))


def dot2(stacked, onehot, dims):
    half = stacked.shape[0] // 2
    both = dot(stacked, onehot, dims)
    return both[:half] + both[half:]


def stack(parts):
    return jnp.concatenate(parts, axis=0)


def stack_into(ref, x, lanes=slice(None)):
    rows, half = x.shape[0], ref.shape[0] // 2
    hi, lo = split(x)
    ref[:rows, lanes] = hi
    ref[half : half + rows, lanes] = lo
    if half > rows:
        blank = jnp.zeros((half - rows, x.shape[1]), BF16)
        ref[rows:half, lanes] = blank
        ref[half + rows :, lanes] = blank


def dot3_stacked(stacked, b, dims):
    half = stacked.shape[0] // 2
    both = dot(stacked, b[0], dims)
    return both[:half] + (both[half:] + dot(stacked[:half], b[1], dims))


def hot_where(here):
    return jnp.where(here, jnp.ones((), BF16), jnp.zeros((), BF16))


def onehot(first, rows, idx):
    place = lax.broadcasted_iota(jnp.int16, (rows, idx.shape[1]), 0)
    return hot_where(place == (idx - first).astype(jnp.int16))


def laid_out(idx):
    return jnp.concatenate([idx[b : b + 1] for b in range(idx.shape[0])], axis=1)


def take_owned(spot_ref, chunks, span, first, piece_of, out_ref):
    width = out_ref.shape[1]
    for chunk in range(chunks):
        if first <= chunk * width < first + span:

            @pl.when(spot_ref[0] == chunk)
            def _():
                out_ref[...] = piece_of(slice(chunk * width - first, (chunk + 1) * width - first))


def gather_kernel(hub_steps, rel_steps, spot_ref, hub_ids, rel_ids, hub_ref, rel_ref, *refs):
    buckets = hub_ids.shape[0]
    hub_outs, rel_outs = refs[:buckets], refs[buckets : 2 * buckets]
    spot_out, hub_own, rel_own = refs[2 * buckets : 2 * buckets + 3]
    hub_buf, rel_buf, hub_idx, rel_idx, stacked, sems = refs[2 * buckets + 3 :]
    hub_tile, rel_tile = hub_buf.shape[2], rel_buf.shape[2]
    chunks = hub_ref.shape[1] // hub_own.shape[1]
    half = hub_own.shape[0]
    steps = [(hub_ref, hub_buf, hub_tile, k) for k in range(hub_steps)]
    steps += [(rel_ref, rel_buf, rel_tile, k) for k in range(rel_steps)]
    copies = [
        pltpu.make_async_copy(table.at[:, pl.ds(k * tile, tile)], buf.at[k % 2], sems.at[i])
        for i, (table, buf, tile, k) in enumerate(steps)
    ]
    id_copies = [
        pltpu.make_async_copy(ids, out, sems.at[len(copies) + i])
        for i, (ids, out) in enumerate([(hub_ids, hub_idx), (rel_ids, rel_idx)])
    ]
    for copy in [*id_copies, copies[0]]:
        copy.start()
    spot_out[0] = spot_ref[0]
    spot_out[1] = spot_ref[1]
    for copy in id_copies:
        copy.wait()
    rows = pl.ds(pl.multiple_of(spot_ref[1] * half, 8), half)
    for i, (table, buf, tile, k) in enumerate(steps):
        if i + 1 < len(steps):
            copies[i + 1].start()
        idx, outs, own = (hub_idx, hub_outs, hub_own) if table is hub_ref else (rel_idx, rel_outs, rel_own)
        count = idx.shape[1]
        hot = onehot(k * tile, tile, laid_out(idx[...]))
        copies[i].wait()
        stack_into(stacked, buf[k % 2], slice(0, tile))
        part = dot2(stacked[:, :tile], hot, NN)
        for b, out in enumerate(outs):
            here = part[:, b * count : (b + 1) * count]
            out[...] = here if k == 0 else out[...] + here
        take_owned(spot_ref, chunks, tile, k * tile, lambda lanes: buf[k % 2, rows, lanes], own)


def gather_rows(spot, hub_table, hub_idx, rel_table, rel_idx, chunks):
    features = hub_table.shape[0]
    hub_steps, rel_steps = 4, 2
    hub_tile, rel_tile = hub_table.shape[1] // hub_steps, rel_table.shape[1] // rel_steps
    buckets, hubs = hub_idx.shape
    edges = rel_idx.shape[1]
    hub_width, rel_width = hub_table.shape[1] // chunks, rel_table.shape[1] // chunks
    shapes = [(features, hubs)] * buckets + [(features, edges)] * buckets
    own_shapes = [(features // 2, hub_width), (features // 2, rel_width)]
    floats = lambda shapes: [jax.ShapeDtypeStruct(shape, F32) for shape in shapes]
    out = pl.pallas_call(
        functools.partial(gather_kernel, hub_steps, rel_steps),
        in_specs=[SMEM] + [HBM] * 4,
        out_specs=[VMEM] * len(shapes) + [SMEM] + [VMEM] * len(own_shapes),
        out_shape=floats(shapes) + [jax.ShapeDtypeStruct((2,), jnp.int32)] + floats(own_shapes),
        scratch_shapes=[
            pltpu.VMEM((2, features, hub_tile), F32),
            pltpu.VMEM((2, features, rel_tile), F32),
            pltpu.VMEM(hub_idx.shape, jnp.int32),
            pltpu.VMEM(rel_idx.shape, jnp.int32),
            pltpu.VMEM((2 * features, max(hub_tile, rel_tile)), BF16),
            pltpu.SemaphoreType.DMA((hub_steps + rel_steps + 2,)),
        ],
        compiler_params=GATHER_PARAMS,
        cost_estimate=COST,
    )(spot, hub_idx, rel_idx, hub_table, rel_table)
    return out[:buckets], out[buckets : 2 * buckets], out[2 * buckets], out[2 * buckets + 1 :]


def spread_bits(place, order):
    bits = len(order)
    return sum((((place >> p) & 1) << (bits - 1 - i)) for i, p in enumerate(order))


def gather_bits(index, order):
    bits = len(order)
    return sum((((index >> (bits - 1 - i)) & 1) << p) for i, p in enumerate(order))


def load_columns(id_refs, grad_refs, idx_down, stacked):
    idx = jnp.concatenate([laid_out(ref[...]) for ref in id_refs], axis=1)
    idx_down[...] = jnp.transpose(jnp.broadcast_to(idx, (128, idx.shape[1]))).astype(jnp.int16)
    at = 0
    for ref, (low, high) in grad_refs:
        width = high - low
        stack_into(stacked, ref[:, low:high], slice(at, at + width))
        at += width


def onehot_across(idx_down, targets):
    width = targets.shape[1]
    idx = idx_down[...]
    wide = jnp.concatenate([idx] * -(-width // 128), axis=1)[:, :width]
    return hot_where(wide == targets.astype(jnp.int16))


def grouped(orders, step, heights):
    groups, where = [], []
    for s, order in enumerate(orders):
        for g, (place, members) in enumerate(groups):
            if place == order[step]:
                where.append((g, sum(heights[m] for m in members)))
                members.append(s)
                break
        else:
            where.append((len(groups), 0))
            groups.append((order[step], [s]))
    return [(place, sum(heights[m] for m in members)) for place, members in groups], where


def rows_of(where, heights, s):
    group, base = where[s]
    return group, slice(base, base + heights[s])


def put_chunk(place, orders, heights, where, sends, keeps, s, value):
    index, half = spread_bits(place, orders[s]), keeps[s].shape[0]
    if index < half:
        keeps[s][index] = value
    else:
        group, rows = rows_of(where, heights, s)
        sends[group][index - half, rows] = value


def chunk_refs(grad_lanes, refs):
    ids, refs = refs[:2], refs[2:]
    grads, refs = list(zip(refs, grad_lanes)), refs[len(grad_lanes) :]
    return ids, grads, refs[:-2], refs[-2:]


def hub_chunks_kernel(orders, spans, where, grad_lanes, spot_ref, *refs):
    ids, grads, outs, (idx_down, stacked) = chunk_refs(grad_lanes, refs)
    load_columns(ids, grads, idx_down, stacked)
    streams = len(orders)
    sends, keeps = outs[:-streams], outs[-streams:]
    heights = [high - low for low, high in spans]
    chunks, width = 2 * keeps[0].shape[0], keeps[0].shape[2]
    lane = lax.broadcasted_iota(jnp.int32, (1, width), 1)
    for place in range(chunks):
        hot = onehot_across(idx_down, lane + (spot_ref[0] ^ place) * width)
        chunk = dot2(stacked[...], hot, NN)
        for s, (low, high) in enumerate(spans):
            put_chunk(place, orders, heights, where, sends, keeps, s, chunk[low:high])


def rel_layout(half_width, streams):
    blocks = row_spans(half_width, 3)
    spans = row_spans(max(high - low for low, high in blocks), streams)
    pieces = []
    for block, (low, high) in enumerate(blocks):
        for s, (first, end) in enumerate(spans):
            count = min(end, high - low) - first
            if count > 0:
                pieces.append((block, s, low + first, count))
    return spans, pieces


def rel_chunks_kernel(orders, pieces, rows, grad_lanes, spot_ref, *refs):
    ids, grads, outs, (idx_down, stacked) = chunk_refs(grad_lanes, refs)
    load_columns(ids, grads, idx_down, stacked)
    for ref in outs:
        ref[...] = jnp.zeros_like(ref)
    streams = len(orders)
    sends, keeps = outs[:streams], outs[streams:]
    half, lanes = keeps[0].shape[0], keeps[0].shape[2]
    chunks = 2 * half
    width = rows // chunks
    group = lanes // width
    lane = lax.broadcasted_iota(jnp.int32, (1, lanes), 1)
    for first in range(0, chunks, group):
        targets = jnp.full((1, lanes), -1, jnp.int32)
        places = range(first, min(first + group, chunks))
        for slot, place in enumerate(places):
            here = (lane >= slot * width) & (lane < (slot + 1) * width)
            targets = jnp.where(here, lane + ((spot_ref[0] ^ place) * width - slot * width), targets)
        dense = dot2(stacked[...], onehot_across(idx_down, targets), NN)
        for slot, place in enumerate(places):
            chunk = dense[:, slot * width : (slot + 1) * width]
            for block, s, low, count in pieces:
                index = spread_bits(place, orders[s])
                out = sends[s].at[index - half] if index >= half else keeps[s].at[index]
                out[:count, block * width : (block + 1) * width] = chunk[low : low + count]


def chunk_columns(kernel, shapes, spot, ids, grads):
    half_width = grads[0][0].shape[0]
    grad_lanes = [lanes_of for unused, lanes_of in grads]
    count = sum(high - low for low, high in grad_lanes)
    return pl.pallas_call(
        functools.partial(kernel, grad_lanes),
        in_specs=[SMEM] + [VMEM] * (2 + len(grads)),
        out_specs=[VMEM] * len(shapes),
        out_shape=[jax.ShapeDtypeStruct(shape, F32) for shape in shapes],
        scratch_shapes=[
            pltpu.VMEM((count, 128), jnp.int16),
            pltpu.VMEM((2 * (-(-half_width // 16) * 16), count), BF16),
        ],
        compiler_params=PARAMS,
        cost_estimate=COST,
    )(spot, *ids, *[g for g, unused in grads])


def call(kernel, ins, shapes):
    return pl.pallas_call(
        kernel,
        in_specs=[VMEM] * len(ins),
        out_specs=[VMEM] * len(shapes),
        out_shape=[jax.ShapeDtypeStruct(shape, F32) for shape in shapes],
        compiler_params=PARAMS,
        cost_estimate=COST,
    )(*ins)


def sums_kernel(heights, here, there, *refs):
    streams, groups = len(heights), 1 + max(g for g, unused in here)
    own, got, sends, keeps = refs[:streams], refs[streams : streams + groups], refs[streams + groups : -streams], refs[-streams:]
    for s in range(streams):
        half = keeps[s].shape[0]
        group, rows = rows_of(here, heights, s)
        out, out_rows = rows_of(there, heights, s)
        sends[out][:, out_rows] = own[s][half:] + got[group][half:, rows]
        keeps[s][...] = own[s][:half] + got[group][:half, rows]


def halves(own, got, orders, step):
    heights = [x.shape[1] for x in own]
    half, width = own[0].shape[0] // 2, own[0].shape[2]
    unused, here = grouped(orders, step, heights)
    groups, there = grouped(orders, step + 1, heights)
    shapes = [(half, height, width) for height in [h for unused, h in groups] + heights]
    out = call(functools.partial(sums_kernel, heights, here, there), [*own, *got], shapes)
    return out[: len(groups)], out[len(groups) :]


def join_kernel(heights, here, there, *refs):
    groups = 1 + max(g for g, unused in here)
    own, got, outs = refs[:groups], refs[groups : 2 * groups], refs[2 * groups :]
    count = own[0].shape[0]
    for s in range(len(heights)):
        group, rows = rows_of(here, heights, s)
        out, out_rows = rows_of(there, heights, s)
        outs[out][:count, out_rows] = own[group][:, rows]
        outs[out][count:, out_rows] = got[group][:, rows]


def join(have, got, orders, step, heights):
    count, width = have[0].shape[0], have[0].shape[2]
    unused, here = grouped(orders, step, heights)
    groups, there = grouped(orders, step - 1, heights)
    shapes = [(2 * count, height, width) for unused, height in groups]
    return call(functools.partial(join_kernel, heights, here, there), [*have, *got], shapes)


def z_sums_kernel(spans, *refs):
    streams = len(spans)
    own, got, outs = refs[:streams], refs[streams : 2 * streams], refs[2 * streams :]
    for place, out in enumerate(outs):
        for s, (low, high) in enumerate(spans):
            out[0, low:high] = own[s][place] + got[s][place]


def squares_kernel(heights, here, *refs):
    streams, groups = len(heights), 1 + max(g for g, unused in here)
    own, got, rels = refs[:streams], refs[streams : streams + groups], refs[streams + groups : -streams - 2]
    totals, rel_total, out = refs[-streams - 2 : -2], refs[-2], refs[-1]
    squares = jnp.zeros((1, out.shape[1]), F32)
    for s in range(streams):
        group, rows = rows_of(here, heights, s)
        total = own[s][0] + got[group][0, rows]
        totals[s][0] = total
        squares += jnp.sum(total * total, axis=0, keepdims=True)
    total = sum(ref[0] for ref in rels)
    rel_total[0] = total
    out[0:1] = squares
    out[1:2] = jnp.sum(total * total, axis=0, keepdims=True)


def update_kernel(spans, rel_spans, pieces, there, features, spot_ref, *refs):
    streams, groups = len(spans), 1 + max(g for g, unused in there)
    totals, (hub_sums, rel_sums), news = refs[:streams], refs[-2:], refs[-groups - 2 : -2]
    rel_total, mine, other, hub_ref, hub_all, rel_ref, rel_all = refs[streams : -groups - 2]
    chunks = hub_all.shape[1] // hub_ref.shape[1]
    take_owned(spot_ref, chunks, hub_all.shape[1], 0, lambda lanes: hub_all[:, lanes], hub_sums)
    take_owned(spot_ref, chunks, rel_all.shape[1], 0, lambda lanes: rel_all[:, lanes], rel_sums)
    width = rel_ref.shape[1]
    squares = mine[...] + other[...]
    hub_scale = step_rate / jnp.sqrt(hub_sums[...] + squares[0:1] * (1.0 / features))
    rel_squares = sum(squares[1:2, b * width : (b + 1) * width] for b in range(3))
    rel_scale = step_rate / jnp.sqrt(rel_sums[...] + rel_squares * (1.0 / features))
    for s, (low, high) in enumerate(spans):
        new, base = there[s]
        first, end = rel_spans[s]
        middle = base + high - low
        news[new][0, base:middle] = hub_ref[low:high] - totals[s][0] * hub_scale
        news[new][0, middle : middle + end - first] = jnp.zeros((end - first, news[new].shape[2]), F32)
    for block, s, low, count in pieces:
        new, base = there[s]
        base += spans[s][1] - spans[s][0]
        lanes, first = slice(block * width, (block + 1) * width), rel_spans[s][0]
        news[new][0, base : base + count, lanes] = (
            rel_ref[low : low + count] - rel_total[0, first : first + count, lanes] * rel_scale
        )


def join_all_kernel(heights, here, there, *refs):
    groups = 1 + max(g for g, unused in here)
    join_kernel(heights, here, there, *refs[:-1])
    base = 0
    for s, height in enumerate(heights):
        group, rows = rows_of(here, heights, s)
        for i, ref in enumerate((refs[group], refs[groups + group])):
            count = ref.shape[0]
            refs[-1][i * count : (i + 1) * count, base : base + height] = ref[:, rows]
        base += height


def join_all(have, got, orders, step, heights):
    count, width = 2 * have[0].shape[0], have[0].shape[2]
    unused, here = grouped(orders, step, heights)
    groups, there = grouped(orders, step - 1, heights)
    shapes = [(count, height, width) for height in [h for unused, h in groups] + [sum(heights)]]
    *have, near = call(functools.partial(join_all_kernel, heights, here, there), [*have, *got], shapes)
    return have, near


def chunk_copies(part, base, first, order, span, chip, component, out_ref, sems, at):
    low, high = span
    width = part.shape[2]
    for index in range(part.shape[0]):
        chunk = chip ^ gather_bits(first + index, order)
        lanes = pl.ds(pl.multiple_of(chunk * width, width), width)
        target = out_ref.at[component, pl.ds(low, high - low), lanes]
        yield pltpu.make_async_copy(part.at[index, pl.ds(base, high - low)], target, sems.at[at + index])


def component_of(spot_ref, mine):
    return spot_ref[1] if mine else 1 - spot_ref[1]


def near_kernel(orders, spans, bases, mine, spot_ref, near_ref, *refs):
    component = component_of(spot_ref, mine)
    out_ref, sems = refs[-2:]
    copies = []
    for order, span, base in zip(orders, spans, bases):
        copies += chunk_copies(near_ref, base, 0, order, span, spot_ref[0], component, out_ref, sems, len(copies))
    for copy in copies:
        copy.start()
    for copy in copies:
        copy.wait()


def far_kernel(orders, spans, bases, pieces, by_copy, mine, spot_ref, near_ref, *refs):
    component = component_of(spot_ref, mine)
    streams = len(orders)
    fars = refs[:streams]
    hub_out, rel_out, hub_all, rel_all, sems = refs[-5:]
    half = near_ref.shape[0]
    hub_width, rel_width = hub_out.shape[2] // (2 * half), rel_out.shape[2] // (2 * half)
    copies = []
    if by_copy:
        for far, order, span in zip(fars, orders, spans):
            copies += chunk_copies(far, 0, half, order, span, spot_ref[0], component, hub_out, sems, len(copies))
        for copy in copies:
            copy.start()
    for chunk in range(2 * half):
        place = spot_ref[0] ^ chunk
        for s, (low, high) in enumerate(spans):
            index = spread_bits(place, orders[s])
            spot = index & (half - 1)
            height, end = high - low, fars[s].shape[1]
            if not by_copy:
                value = jnp.where(index >= half, fars[s][spot, :height], near_ref[spot, bases[s] : bases[s] + height])
                hub_all[low:high, chunk * hub_width : (chunk + 1) * hub_width] = value
            value = jnp.where(index >= half, fars[s][spot, height:], near_ref[spot, bases[s] + height : bases[s] + end])
            for block, stream, row, count in pieces:
                if stream == s:
                    part = value[:count, block * rel_width : (block + 1) * rel_width]
                    rel_all[row : row + count, chunk * rel_width : (chunk + 1) * rel_width] = part
    copies.append(pltpu.make_async_copy(rel_all, rel_out.at[component], sems.at[len(copies)]))
    copies[-1].start()
    if not by_copy:
        copies.append(pltpu.make_async_copy(hub_all, hub_out.at[component], sems.at[len(copies)]))
        copies[-1].start()
    for copy in copies:
        copy.wait()


def placed(kernel, scratch, spot, near, fars, outs, earlier):
    sems = pltpu.SemaphoreType.DMA((3 * near.shape[0] + 2,))
    return pl.pallas_call(
        kernel,
        in_specs=[SMEM] + [VMEM] * (1 + len(fars)) + [HBM] * len(earlier),
        out_specs=[HBM] * len(outs),
        out_shape=[jax.ShapeDtypeStruct(shape, F32) for shape in outs],
        scratch_shapes=scratch + [sems],
        input_output_aliases={2 + len(fars) + i: i for i in range(len(earlier))},
        compiler_params=PARAMS,
        cost_estimate=pl.CostEstimate(flops=0, bytes_accessed=4 * outs[0][1] * outs[0][2], transcendentals=0),
    )(spot, near, *fars, *earlier)


def adagrad(table, state, grads):
    new_state = state + jnp.sum(grads * grads, axis=0, keepdims=True) * (1.0 / grads.shape[0])
    return table - grads * (step_rate / jnp.sqrt(new_state)), new_state


def keep_and_send(core, first, second):
    return jnp.where(core == 0, first, second), jnp.where(core == 0, second, first)


def table_counts(rows, negs, weight):
    place = lax.broadcasted_iota(jnp.int32, (rows, negs.shape[1]), 0)
    return jnp.sum(jnp.where(place == negs, weight, 0.0), axis=1, keepdims=True)


def turned(x, r, half):
    x0, x1, r0, r1 = x[:half], x[half:], r[:half], r[half:]
    return jnp.concatenate([x0 * r0 - x1 * r1, x0 * r1 + x1 * r0], axis=0)


def turned_back(x, r, half):
    x0, x1, r0, r1 = x[:half], x[half:], r[:half], r[half:]
    return x0 * r0 + x1 * r1, x1 * r0 - x0 * r1


EDGE_TILE = 512


def bucket_kernel(
    bucket, core_ref, heads_ref, tails_ref, negs_ref, left_ref, left_sums_ref, right_ref, right_sums_ref, rel_ref, hub_ref,
    left_out, left_sums_out, right_out, keep_out, send_out,
    left_parts, both_parts,
):
    features, rows = left_ref.shape
    half = features // 2
    core = core_ref[1]
    edges = heads_ref.shape[1]
    hubs = keep_out.shape[1] - edges
    at = slice(bucket, bucket + 1)
    weight = 1.0 / (negs_ref.shape[1] + hubs)
    counts = table_counts(rows, negs_ref[at], weight)
    stack_into(left_parts, left_ref[...])
    stack_into(both_parts, right_ref[...], slice(0, rows))
    stack_into(both_parts, hub_ref[...], slice(rows, rows + hubs))

    tail_here = lax.broadcasted_iota(jnp.int32, (rows, edges), 0) == tails_ref[at]
    head_hot = onehot(0, rows, heads_ref[at])
    h = dot2(left_parts[...], head_hot, NN)
    r = rel_ref[...]
    q = split(turned(h, r, half))
    scores = dot3((both_parts[:features], both_parts[features:]), q, TN)
    chance = jax.nn.sigmoid(scores[:rows])
    coef = jnp.concatenate(
        [
            counts * chance + jnp.where(tail_here, chance - 1.0, 0.0),
            weight * jax.nn.sigmoid(scores[rows:]),
        ],
        axis=0,
    )
    coef = split(coef)
    dq = dot3_stacked(both_parts[...], coef, NN)
    both_grad = dot3_stacked(stack(q), coef, NT)
    dh = jnp.concatenate(turned_back(dq, r, half), axis=0)
    left_grad = dot2(stack(split(dh)), head_hot, NT)
    keep_out[:, hubs:], send_out[:, hubs:] = keep_and_send(core, *turned_back(dq, h, half))

    left_out[...], left_sums_out[...] = adagrad(left_ref[...], left_sums_ref[...], left_grad)
    new_right, new_sums = adagrad(right_ref[...], right_sums_ref[...], both_grad[:, :rows])
    right_out[:features] = new_right
    right_out[features:] = jnp.broadcast_to(new_sums, (right_out.shape[0] - features, rows))
    keep_out[:, :hubs], send_out[:, :hubs] = keep_and_send(core, both_grad[:half, rows:], both_grad[half:, rows:])


def bucket_step(bucket, core, heads, tails, negs, left, left_sums, right, right_sums, rel_rows, hub_rows):
    features, rows = left.shape
    edges, hubs = heads.shape[1], hub_rows.shape[1]
    width = rows + hubs
    shapes = [(features, rows), (1, rows), (features + 8, rows)] + [(features // 2, hubs + edges)] * 2
    return pl.pallas_call(
        functools.partial(bucket_kernel, bucket),
        in_specs=[SMEM] + [VMEM] * 9,
        out_specs=[VMEM] * 5,
        out_shape=[jax.ShapeDtypeStruct(shape, F32) for shape in shapes],
        scratch_shapes=[
            pltpu.VMEM((2 * features, rows), BF16),
            pltpu.VMEM((2 * features, width), BF16),
        ],
        compiler_params=PARAMS,
        cost_estimate=COST,
    )(core, heads, tails, negs, left, left_sums, right, right_sums, rel_rows, hub_rows)


def hub_kernel(
    bucket, negatives, core_ref, heads_ref, left_ref, rel_ref, hub_ref,
    query_grad, hub_keep, hub_send,
    left_parts, hub_parts,
):
    features, rows = left_ref.shape
    half = features // 2
    edges, hubs = heads_ref.shape[1], hub_keep.shape[1]
    at = slice(bucket, bucket + 1)
    weight = 1.0 / (negatives + hubs)
    stack_into(left_parts, left_ref[...])
    stack_into(hub_parts, hub_ref[...])

    head_hot = onehot(0, rows, heads_ref[at])
    h = dot2(left_parts[...], head_hot, NN)
    q = split(turned(h, rel_ref[...], half))
    coef = split(weight * jax.nn.sigmoid(dot3((hub_parts[:features], hub_parts[features:]), q, TN)))
    query_grad[...] = dot3_stacked(hub_parts[...], coef, NN)
    hub_grad = dot3_stacked(stack(q), coef, NT)

    hub_keep[...], hub_send[...] = keep_and_send(core_ref[1], hub_grad[:half], hub_grad[half:])


def hub_step(bucket, negatives, core, heads, left, rel_rows, hub_rows):
    features, rows = left.shape
    edges, hubs = heads.shape[1], hub_rows.shape[1]
    shapes = [(features, edges)] + [(features // 2, hubs)] * 2
    return pl.pallas_call(
        functools.partial(hub_kernel, bucket, negatives),
        in_specs=[SMEM] + [VMEM] * 4,
        out_specs=[VMEM] * 3,
        out_shape=[jax.ShapeDtypeStruct(shape, F32) for shape in shapes],
        scratch_shapes=[
            pltpu.VMEM((2 * features, rows), BF16),
            pltpu.VMEM((2 * features, hubs), BF16),
        ],
        compiler_params=PARAMS,
        cost_estimate=COST,
    )(core, heads, left, rel_rows, hub_rows)


def tables_kernel(
    bucket, hubs, core_ref, heads_ref, tails_ref, negs_ref, query_grad,
    left_ref, left_sums_ref, right_ref, rel_ref,
    left_out, right_out, rel_keep, rel_send,
    left_parts, right_parts,
):
    features, rows = left_ref.shape
    half = features // 2
    edges = heads_ref.shape[1]
    at = slice(bucket, bucket + 1)
    core = core_ref[1]
    counts = table_counts(rows, negs_ref[at], 1.0 / (negs_ref.shape[1] + hubs))
    stack_into(left_parts, left_ref[...])
    stack_into(right_parts, right_ref[:features])

    tail_here = lax.broadcasted_iota(jnp.int32, (rows, edges), 0) == tails_ref[at]
    head_hot = onehot(0, rows, heads_ref[at])
    h = dot2(left_parts[...], head_hot, NN)
    r = rel_ref[...]
    q = split(turned(h, r, half))
    chance = jax.nn.sigmoid(dot3((right_parts[:features], right_parts[features:]), q, TN))
    coef = split(counts * chance + jnp.where(tail_here, chance - 1.0, 0.0))
    dq = dot3_stacked(right_parts[...], coef, NN) + query_grad[...]
    right_grad = dot3_stacked(stack(q), coef, NT)
    rel_keep[...], rel_send[...] = keep_and_send(core, *turned_back(dq, h, half))
    dh = jnp.concatenate(turned_back(dq, r, half), axis=0)
    left_grad = dot2(stack(split(dh)), head_hot, NT)

    left_out[...], unused = adagrad(left_ref[...], left_sums_ref[...], left_grad)
    right_out[...], unused = adagrad(right_ref[:features], right_ref[features : features + 1], right_grad)


def tables_step(bucket, hubs, core, heads, tails, negs, query_grad, left, left_sums, right, rel_rows):
    features, rows = left.shape
    edges = heads.shape[1]
    shapes = [(features, rows)] * 2 + [(features // 2, edges)] * 2
    return pl.pallas_call(
        functools.partial(tables_kernel, bucket, hubs),
        in_specs=[SMEM] + [VMEM] * 8,
        out_specs=[VMEM] * 4,
        out_shape=[jax.ShapeDtypeStruct(shape, F32) for shape in shapes],
        scratch_shapes=[pltpu.VMEM((2 * features, rows), BF16)] * 2,
        compiler_params=PARAMS,
        cost_estimate=COST,
    )(core, heads, tails, negs, query_grad, left, left_sums, right, rel_rows)


def from_behind(x, axis, by):
    size = lax.axis_size(axis)
    return lax.ppermute(x, axis, [(i, (i + by) % size) for i in range(size)])


def flipped(x, axis, bit):
    return lax.ppermute(x, axis, [(i, i ^ (1 << bit)) for i in range(lax.axis_size(axis))])


def flipped_by(x, axis, offset):
    return lax.ppermute(x, axis, [(i, i ^ offset) for i in range(lax.axis_size(axis))])


def other_core(x):
    return flipped(x, "blk", 0)


def across(x, place):
    sub_bits = lax.axis_size("sub").bit_length() - 1
    if place < sub_bits:
        return flipped(x, "sub", place)
    return flipped(x, "blk", place - sub_bits + 1)


def stream_orders():
    sub_bits = lax.axis_size("sub").bit_length() - 1
    bits = sub_bits + lax.axis_size("blk").bit_length() - 2
    x, y, z, far = sub_bits, sub_bits + 1, 0, 1
    rest = [p for p in range(bits) if p not in (x, y, z, far)]
    return [[x, y, z, far] + rest, [y, z, x, far] + rest, [z, x, far, y] + rest]


def plane_orders(sub_bits, bits):
    plane, depth = list(range(sub_bits, bits)), list(range(sub_bits - 1, -1, -1))
    return [plane + depth, plane[1:] + plane[:1] + depth]


def row_spans(rows, parts):
    ends = [-(-rows * (i + 1) // (8 * parts)) * 8 for i in range(parts - 1)] + [rows]
    return list(zip([0] + ends[:-1], ends))


def shards(
    left_emb, left_state, right_emb, right_state, relation_emb, relation_state, hub_emb, hub_state,
    heads, relations, tails, negatives, hub_ids,
):
    components, half_width, row_count = left_emb.shape
    features = components * half_width
    rel_count, hub_count = relation_emb.shape[2], hub_emb.shape[2]
    left = left_emb.reshape(features, row_count)
    right = right_emb.reshape(features, row_count)
    left_sums = left_state.reshape(1, row_count)
    right_sums = right_state.reshape(1, row_count)
    buckets, edges = heads.shape
    hubs = hub_ids.shape[1]

    orders = stream_orders()
    streams, stages = len(orders), len(orders[0])
    chunks, depth = 1 << stages, lax.axis_size("sub")
    sub_bits = depth.bit_length() - 1
    planes = chunks // depth
    spans = row_spans(half_width, streams)
    rel_orders = plane_orders(sub_bits, stages)
    plane_spans, plane_pieces = rel_layout(half_width, len(rel_orders))
    rel_spans, joint_pieces = rel_layout(half_width, streams)
    heights, rel_heights, plane_heights = [[high - low for low, high in x] for x in (spans, rel_spans, plane_spans)]
    joint_heights = [h + r for h, r in zip(heights, rel_heights)]
    bases = [sum(joint_heights[:s]) for s in range(streams)]
    width = hub_count // chunks
    hub_lanes, rel_lanes = (0, hubs), (hubs, hubs + edges)

    def exchanged(parts, step):
        return [across(x, place) for x, (place, unused) in zip(parts, grouped(orders, step, heights)[0])]

    def in_turn(first, then):
        return lax.optimization_barrier((first, then))

    blk = lax.axis_index("blk")
    spot = jnp.stack([(blk >> 1) * depth + lax.axis_index("sub"), blk & 1]).astype(jnp.int32)
    far_ids = other_core((hub_ids, relations))
    hub_rows, rel_rows, spot, owned = gather_rows(
        spot, hub_emb.reshape(features, hub_count), hub_ids, relation_emb.reshape(features, rel_count), relations, chunks
    )
    far_ids, hub_rows = in_turn(far_ids, hub_rows)
    keeps, sends = [], []
    for b in range(buckets - 1):
        if b > 0:
            right, right_sums = right[:features], right[features : features + 1]
        left, left_sums, right, keep, send = bucket_step(
            b, spot, heads, tails, negatives, left, left_sums, right, right_sums, rel_rows[b], hub_rows[b]
        )
        right = from_behind(right, "blk", 1)
        keeps.append(keep)
        sends.append(send)
    last = buckets - 1
    query_grad, hub_keep, hub_send = hub_step(
        last, negatives.shape[1], spot, heads, left, rel_rows[last], hub_rows[last]
    )
    sends, hub_send = in_turn(sends, hub_send)
    hub_far = other_core(hub_send)
    fars = [other_core(x) for x in sends]
    grads = lambda early, late, lanes: [(x, lanes) for x in early] + [(late, (0, late.shape[1]))]
    groups, where = grouped(orders, 0, heights)
    parts = chunk_columns(
        functools.partial(hub_chunks_kernel, orders, spans, where),
        [(chunks // 2, height, width) for height in [h for unused, h in groups] + heights],
        spot, (hub_ids, far_ids[0]), grads(keeps, hub_keep, hub_lanes) + grads(fars, hub_far, hub_lanes),
    )
    send, own = parts[: len(groups)], parts[len(groups) :]
    got = exchanged(send, 0)
    left, right, rel_keep, rel_send = tables_step(
        last, hubs, spot, heads, tails, negatives, query_grad, left, left_sums, right, rel_rows[last]
    )
    rel_far = other_core(rel_send)

    parts = chunk_columns(
        functools.partial(rel_chunks_kernel, rel_orders, plane_pieces, rel_count),
        [(chunks // 2, height, width) for height in plane_heights * 2],
        spot, (relations, far_ids[1]), grads(keeps, rel_keep, rel_lanes) + grads(fars, rel_far, rel_lanes),
    )
    rel_send, rel_own = parts[: len(rel_orders)], parts[len(rel_orders) :]
    rel_got = [across(x, order[0]) for x, order in zip(rel_send, rel_orders)]
    plane_steps = stages - sub_bits
    for step in range(stages - 1):
        if 0 < step < plane_steps:
            own, rel_got = in_turn(own, rel_got)
            rel_send, rel_own = halves(rel_own, rel_got, rel_orders, step - 1)
            rel_got = [across(x, order[step]) for x, order in zip(rel_send, rel_orders)]
        elif step == plane_steps:
            own, rel_got = in_turn(own, rel_got)
            rel_own, *rel_out = call(
                functools.partial(z_sums_kernel, plane_spans), [*rel_own, *rel_got],
                [(1, plane_spans[-1][1], width)] * depth,
            )
            rel_got = [flipped_by(x, "sub", q + 1) for q, x in enumerate(rel_out)]
        rel_own, got = in_turn(rel_own, got)
        send, own = halves(own, got, orders, step)
        got = exchanged(send, step + 1)

    *totals, rel_total, squares = call(
        functools.partial(squares_kernel, heights, grouped(orders, stages - 1, heights)[1]),
        [*own, *got, rel_own, *rel_got], [x.shape for x in own] + [rel_own.shape, (2, width)],
    )
    hub_own, rel_own = owned
    groups, there = grouped(orders, stages - 1, joint_heights)
    ins = [
        *totals, rel_total, squares, other_core(squares),
        hub_own, hub_state[None], rel_own, relation_state[None],
    ]
    have = pl.pallas_call(
        functools.partial(update_kernel, spans, rel_spans, joint_pieces, there, features),
        in_specs=[SMEM] + [VMEM] * len(ins),
        out_specs=[VMEM] * len(groups),
        out_shape=[jax.ShapeDtypeStruct((1, height, width), F32) for unused, height in groups],
        scratch_shapes=[pltpu.VMEM((1, x.shape[1]), F32) for x in owned],
        compiler_params=PARAMS,
        cost_estimate=COST,
    )(spot, *ins)
    for step in range(stages - 1, 1, -1):
        have = join(have, exchanged(have, step), orders, step, joint_heights)
    have, near = join_all(have, exchanged(have, 1), orders, 1, joint_heights)
    got = exchanged(have, 0)
    far_near = other_core(near)

    shapes = [hub_emb.shape, relation_emb.shape]
    by_copy = width % 128 == 0
    hub_new = []
    if by_copy:
        near_step = functools.partial(near_kernel, orders, spans, bases)
        hub_new = placed(functools.partial(near_step, True), [], spot, near, [], shapes[:1], [])
        hub_new = placed(functools.partial(near_step, False), [], spot, far_near, [], shapes[:1], hub_new)
        got, hub_new = in_turn(got, hub_new)
    far_step = functools.partial(far_kernel, orders, spans, bases, joint_pieces, by_copy)
    scratch = [
        pltpu.VMEM((8, 128) if by_copy else (half_width, hub_count), F32),
        pltpu.VMEM((half_width, rel_count), F32),
    ]
    far_got = other_core(got)
    out = placed(functools.partial(far_step, True), scratch, spot, near, got, shapes, hub_new)
    hub_new, rel_new = placed(functools.partial(far_step, False), scratch, spot, far_near, far_got, shapes, out)
    return (
        left.reshape(components, half_width, row_count),
        right.reshape(components, half_width, row_count),
        rel_new,
        hub_new,
    )


def solution(mesh):
    both = ("blk", "sub")
    block, table, whole = P(None, None, both), P(None, both), P()
    return jax.shard_map(
        shards,
        mesh=mesh,
        in_specs=(block, P(both), block, P(both), whole, whole, whole, whole, table, table, table, table, table),
        out_specs=(block, block, whole, whole),
        check_vma=False,
    )
```

```python
import functools
import jax
import jax.numpy as jnp
from jax import lax
from jax.experimental import pallas as pl
from jax.experimental.pallas import tpu as pltpu
from jax.sharding import PartitionSpec as P

step_rate = 0.25
F32, BF16 = jnp.float32, jnp.bfloat16
NN = (((1,), (0,)), ((), ()))
NT = (((1,), (1,)), ((), ()))
TN = (((0,), (0,)), ((), ()))
VMEM = pl.BlockSpec(memory_space=pltpu.VMEM)
SMEM = pl.BlockSpec(memory_space=pltpu.SMEM)
PARAMS = pltpu.CompilerParams(vmem_limit_bytes=12 * 1024 * 1024)
GATHER_PARAMS = pltpu.CompilerParams(vmem_limit_bytes=50 * 1024 * 1024)
HBM = pl.BlockSpec(memory_space=pltpu.HBM)
COST = pl.CostEstimate(flops=10000, bytes_accessed=10000, transcendentals=0)


def split(x):
    hi = x.astype(BF16)
    return hi, (x - hi.astype(F32)).astype(BF16)


def dot(a, b, dims):
    return lax.dot_general(a, b, dims, preferred_element_type=F32)


def dot3(a, b, dims):
    return dot(a[0], b[0], dims) + (dot(a[0], b[1], dims) + dot(a[1], b[0], dims))


def dot2(stacked, onehot, dims):
    half = stacked.shape[0] // 2
    both = dot(stacked, onehot, dims)
    return both[:half] + both[half:]


def stack(parts):
    return jnp.concatenate(parts, axis=0)


def stack_into(ref, x, lanes=slice(None)):
    rows, half = x.shape[0], ref.shape[0] // 2
    hi, lo = split(x)
    ref[:rows, lanes] = hi
    ref[half : half + rows, lanes] = lo
    if half > rows:
        blank = jnp.zeros((half - rows, x.shape[1]), BF16)
        ref[rows:half, lanes] = blank
        ref[half + rows :, lanes] = blank


def dot3_stacked(stacked, b, dims):
    half = stacked.shape[0] // 2
    both = dot(stacked, b[0], dims)
    return both[:half] + (both[half:] + dot(stacked[:half], b[1], dims))


def hot_where(here):
    return jnp.where(here, jnp.ones((), BF16), jnp.zeros((), BF16))


def onehot(first, rows, idx):
    place = lax.broadcasted_iota(jnp.int16, (rows, idx.shape[1]), 0)
    return hot_where(place == (idx - first).astype(jnp.int16))


def laid_out(idx):
    return jnp.concatenate([idx[b : b + 1] for b in range(idx.shape[0])], axis=1)


def take_owned(spot_ref, chunks, span, first, piece_of, out_ref):
    width = out_ref.shape[1]
    for chunk in range(chunks):
        if first <= chunk * width < first + span:

            @pl.when(spot_ref[0] == chunk)
            def _():
                out_ref[...] = piece_of(slice(chunk * width - first, (chunk + 1) * width - first))


def gather_kernel(hub_steps, rel_steps, spot_ref, hub_ids, rel_ids, hub_ref, rel_ref, *refs):
    buckets = hub_ids.shape[0]
    hub_outs, rel_outs = refs[:buckets], refs[buckets : 2 * buckets]
    spot_out, hub_own, rel_own = refs[2 * buckets : 2 * buckets + 3]
    hub_buf, rel_buf, hub_idx, rel_idx, stacked, sems = refs[2 * buckets + 3 :]
    hub_tile, rel_tile = hub_buf.shape[2], rel_buf.shape[2]
    chunks = hub_ref.shape[1] // hub_own.shape[1]
    half = hub_own.shape[0]
    steps = [(hub_ref, hub_buf, hub_tile, k) for k in range(hub_steps)]
    steps += [(rel_ref, rel_buf, rel_tile, k) for k in range(rel_steps)]
    copies = [
        pltpu.make_async_copy(table.at[:, pl.ds(k * tile, tile)], buf.at[k % 2], sems.at[i])
        for i, (table, buf, tile, k) in enumerate(steps)
    ]
    id_copies = [
        pltpu.make_async_copy(ids, out, sems.at[len(copies) + i])
        for i, (ids, out) in enumerate([(hub_ids, hub_idx), (rel_ids, rel_idx)])
    ]
    for copy in [*id_copies, copies[0]]:
        copy.start()
    spot_out[0] = spot_ref[0]
    spot_out[1] = spot_ref[1]
    for copy in id_copies:
        copy.wait()
    rows = pl.ds(pl.multiple_of(spot_ref[1] * half, 8), half)
    for i, (table, buf, tile, k) in enumerate(steps):
        if i + 1 < len(steps):
            copies[i + 1].start()
        idx, outs, own = (hub_idx, hub_outs, hub_own) if table is hub_ref else (rel_idx, rel_outs, rel_own)
        count = idx.shape[1]
        hot = onehot(k * tile, tile, laid_out(idx[...]))
        copies[i].wait()
        stack_into(stacked, buf[k % 2], slice(0, tile))
        part = dot2(stacked[:, :tile], hot, NN)
        for b, out in enumerate(outs):
            here = part[:, b * count : (b + 1) * count]
            out[...] = here if k == 0 else out[...] + here
        take_owned(spot_ref, chunks, tile, k * tile, lambda lanes: buf[k % 2, rows, lanes], own)


def gather_rows(spot, hub_table, hub_idx, rel_table, rel_idx, chunks):
    features = hub_table.shape[0]
    hub_steps, rel_steps = 4, 2
    hub_tile, rel_tile = hub_table.shape[1] // hub_steps, rel_table.shape[1] // rel_steps
    buckets, hubs = hub_idx.shape
    edges = rel_idx.shape[1]
    hub_width, rel_width = hub_table.shape[1] // chunks, rel_table.shape[1] // chunks
    shapes = [(features, hubs)] * buckets + [(features, edges)] * buckets
    own_shapes = [(features // 2, hub_width), (features // 2, rel_width)]
    floats = lambda shapes: [jax.ShapeDtypeStruct(shape, F32) for shape in shapes]
    out = pl.pallas_call(
        functools.partial(gather_kernel, hub_steps, rel_steps),
        in_specs=[SMEM] + [HBM] * 4,
        out_specs=[VMEM] * len(shapes) + [SMEM] + [VMEM] * len(own_shapes),
        out_shape=floats(shapes) + [jax.ShapeDtypeStruct((2,), jnp.int32)] + floats(own_shapes),
        scratch_shapes=[
            pltpu.VMEM((2, features, hub_tile), F32),
            pltpu.VMEM((2, features, rel_tile), F32),
            pltpu.VMEM(hub_idx.shape, jnp.int32),
            pltpu.VMEM(rel_idx.shape, jnp.int32),
            pltpu.VMEM((2 * features, max(hub_tile, rel_tile)), BF16),
            pltpu.SemaphoreType.DMA((hub_steps + rel_steps + 2,)),
        ],
        compiler_params=GATHER_PARAMS,
        cost_estimate=COST,
    )(spot, hub_idx, rel_idx, hub_table, rel_table)
    return out[:buckets], out[buckets : 2 * buckets], out[2 * buckets], out[2 * buckets + 1 :]


def spread_bits(place, order):
    bits = len(order)
    return sum((((place >> p) & 1) << (bits - 1 - i)) for i, p in enumerate(order))


def gather_bits(index, order):
    bits = len(order)
    return sum((((index >> (bits - 1 - i)) & 1) << p) for i, p in enumerate(order))


def load_columns(id_refs, grad_refs, idx_down, stacked):
    idx = jnp.concatenate([laid_out(ref[...]) for ref in id_refs], axis=1)
    idx_down[...] = jnp.transpose(jnp.broadcast_to(idx, (128, idx.shape[1]))).astype(jnp.int16)
    at = 0
    for ref, (low, high) in grad_refs:
        width = high - low
        stack_into(stacked, ref[:, low:high], slice(at, at + width))
        at += width


def onehot_across(idx_down, targets):
    width = targets.shape[1]
    idx = idx_down[...]
    wide = jnp.concatenate([idx] * -(-width // 128), axis=1)[:, :width]
    return hot_where(wide == targets.astype(jnp.int16))


def grouped(orders, step, heights):
    groups, where = [], []
    for s, order in enumerate(orders):
        for g, (place, members) in enumerate(groups):
            if place == order[step]:
                where.append((g, sum(heights[m] for m in members)))
                members.append(s)
                break
        else:
            where.append((len(groups), 0))
            groups.append((order[step], [s]))
    return [(place, sum(heights[m] for m in members)) for place, members in groups], where


def rows_of(where, heights, s):
    group, base = where[s]
    return group, slice(base, base + heights[s])


def put_chunk(place, orders, heights, where, sends, keeps, s, value):
    index, half = spread_bits(place, orders[s]), keeps[s].shape[0]
    if index < half:
        keeps[s][index] = value
    else:
        group, rows = rows_of(where, heights, s)
        sends[group][index - half, rows] = value


def chunk_refs(grad_lanes, refs):
    ids, refs = refs[:2], refs[2:]
    grads, refs = list(zip(refs, grad_lanes)), refs[len(grad_lanes) :]
    return ids, grads, refs[:-2], refs[-2:]


def hub_chunks_kernel(orders, spans, where, grad_lanes, spot_ref, *refs):
    ids, grads, outs, (idx_down, stacked) = chunk_refs(grad_lanes, refs)
    load_columns(ids, grads, idx_down, stacked)
    streams = len(orders)
    sends, keeps = outs[:-streams], outs[-streams:]
    heights = [high - low for low, high in spans]
    chunks, width = 2 * keeps[0].shape[0], keeps[0].shape[2]
    lane = lax.broadcasted_iota(jnp.int32, (1, width), 1)
    for place in range(chunks):
        hot = onehot_across(idx_down, lane + (spot_ref[0] ^ place) * width)
        chunk = dot2(stacked[...], hot, NN)
        for s, (low, high) in enumerate(spans):
            put_chunk(place, orders, heights, where, sends, keeps, s, chunk[low:high])


def packed_map(half_width, width, lanes):
    rows = half_width // 24 * 8
    gap, extra = lanes - 3 * width, half_width - 3 * rows
    entries = [(rows * b, 0, width, 0, b * width, rows) for b in range(3)]
    for i in range(-(-width // gap)):
        entries.append((3 * rows, i * gap, min(gap, width - i * gap), extra * i, 3 * width, extra))
    return rows, entries


def split_pieces(entries, spans):
    pieces = []
    for row, lane, lanes, to, to_lane, count in entries:
        for s, (first, end) in enumerate(spans):
            low, high = max(to, first), min(to + count, end)
            if low < high:
                pieces.append((s, row + low - to, high - low, lane, lanes, low - first, to_lane))
    return pieces


def rel_chunks_kernel(orders, pieces, rows, grad_lanes, spot_ref, *refs):
    ids, grads, outs, (idx_down, stacked) = chunk_refs(grad_lanes, refs)
    load_columns(ids, grads, idx_down, stacked)
    for ref in outs:
        ref[...] = jnp.zeros_like(ref)
    streams = len(orders)
    sends, keeps = outs[:streams], outs[streams:]
    half, lanes = keeps[0].shape[0], keeps[0].shape[2]
    chunks = 2 * half
    width = rows // chunks
    group = lanes // width
    lane = lax.broadcasted_iota(jnp.int32, (1, lanes), 1)
    for first in range(0, chunks, group):
        targets = jnp.full((1, lanes), -1, jnp.int32)
        places = range(first, min(first + group, chunks))
        for slot, place in enumerate(places):
            here = (lane >= slot * width) & (lane < (slot + 1) * width)
            targets = jnp.where(here, lane + ((spot_ref[0] ^ place) * width - slot * width), targets)
        dense = dot2(stacked[...], onehot_across(idx_down, targets), NN)
        for slot, place in enumerate(places):
            chunk = dense[:, slot * width : (slot + 1) * width]
            for s, row, count, low, wide, to, to_lane in pieces:
                index = spread_bits(place, orders[s])
                out = sends[s].at[index - half] if index >= half else keeps[s].at[index]
                out[to : to + count, to_lane : to_lane + wide] = chunk[row : row + count, low : low + wide]


def chunk_columns(kernel, shapes, spot, ids, grads):
    half_width = grads[0][0].shape[0]
    grad_lanes = [lanes_of for unused, lanes_of in grads]
    count = sum(high - low for low, high in grad_lanes)
    return pl.pallas_call(
        functools.partial(kernel, grad_lanes),
        in_specs=[SMEM] + [VMEM] * (2 + len(grads)),
        out_specs=[VMEM] * len(shapes),
        out_shape=[jax.ShapeDtypeStruct(shape, F32) for shape in shapes],
        scratch_shapes=[
            pltpu.VMEM((count, 128), jnp.int16),
            pltpu.VMEM((2 * (-(-half_width // 16) * 16), count), BF16),
        ],
        compiler_params=PARAMS,
        cost_estimate=COST,
    )(spot, *ids, *[g for g, unused in grads])


def call(kernel, ins, shapes):
    return pl.pallas_call(
        kernel,
        in_specs=[VMEM] * len(ins),
        out_specs=[VMEM] * len(shapes),
        out_shape=[jax.ShapeDtypeStruct(shape, F32) for shape in shapes],
        compiler_params=PARAMS,
        cost_estimate=COST,
    )(*ins)


def sums_kernel(heights, here, there, *refs):
    streams, groups = len(heights), 1 + max(g for g, unused in here)
    own, got, sends, keeps = refs[:streams], refs[streams : streams + groups], refs[streams + groups : -streams], refs[-streams:]
    for s in range(streams):
        half = keeps[s].shape[0]
        group, rows = rows_of(here, heights, s)
        out, out_rows = rows_of(there, heights, s)
        sends[out][:, out_rows] = own[s][half:] + got[group][half:, rows]
        keeps[s][...] = own[s][:half] + got[group][:half, rows]


def halves(own, got, orders, step):
    heights = [x.shape[1] for x in own]
    half, width = own[0].shape[0] // 2, own[0].shape[2]
    unused, here = grouped(orders, step, heights)
    groups, there = grouped(orders, step + 1, heights)
    shapes = [(half, height, width) for height in [h for unused, h in groups] + heights]
    out = call(functools.partial(sums_kernel, heights, here, there), [*own, *got], shapes)
    return out[: len(groups)], out[len(groups) :]


def join_kernel(heights, here, there, *refs):
    groups = 1 + max(g for g, unused in here)
    own, got, outs = refs[:groups], refs[groups : 2 * groups], refs[2 * groups :]
    count = own[0].shape[0]
    for s in range(len(heights)):
        group, rows = rows_of(here, heights, s)
        out, out_rows = rows_of(there, heights, s)
        outs[out][:count, out_rows] = own[group][:, rows]
        outs[out][count:, out_rows] = got[group][:, rows]


def join(have, got, orders, step, heights):
    count, width = have[0].shape[0], have[0].shape[2]
    unused, here = grouped(orders, step, heights)
    groups, there = grouped(orders, step - 1, heights)
    shapes = [(2 * count, height, width) for unused, height in groups]
    return call(functools.partial(join_kernel, heights, here, there), [*have, *got], shapes)


def last_sums_kernel(heights, here, there, spans, carried, *refs):
    streams, planes = len(heights), len(spans)
    groups, out_groups = [1 + max(g for g, unused in where) for where in (here, there)]
    rels, outs = refs[streams + groups : streams + groups + 2 * planes], refs[streams + groups + 2 * planes :]
    sums_kernel(heights, here, there, *refs[: streams + groups], *outs[: out_groups + streams])
    rel_outs = list(outs[out_groups + streams :])
    for place in range(rels[0].shape[0]):
        group, base = carried[place] if place in carried else (None, 0)
        out = rel_outs.pop(0) if group is None else outs[group]
        for s, (low, high) in enumerate(spans):
            out[0, base + low : base + high] = rels[s][place] + rels[planes + s][place]


def squares_kernel(heights, here, entries, carried, *refs):
    streams, groups = len(heights), 1 + max(g for g, unused in here)
    own, got, rels = refs[:streams], refs[streams : streams + groups], refs[streams + groups : -streams - 2]
    totals, rel_total, out = refs[-streams - 2 : -2], refs[-2], refs[-1]
    squares = jnp.zeros((1, out.shape[1]), F32)
    for s in range(streams):
        group, rows = rows_of(here, heights, s)
        total = own[s][0] + got[group][0, rows]
        totals[s][0] = total
        squares += jnp.sum(total * total, axis=0, keepdims=True)
    height = rel_total.shape[1]
    total = sum(ref[0] for ref in rels)
    for group, base in carried.values():
        total = total + got[group][0, base : base + height]
    rel_total[0] = total
    out[0:1] = squares
    out[1:2] = jnp.zeros_like(squares)
    square = total * total
    for row, lane, lanes, to, to_lane, count in entries:
        part = jnp.sum(square[to : to + count, to_lane : to_lane + lanes], axis=0, keepdims=True)
        out[1:2, lane : lane + lanes] += part


def update_kernel(spans, rel_spans, pieces, there, features, spot_ref, *refs):
    streams, groups = len(spans), 1 + max(g for g, unused in there)
    totals, (hub_sums, rel_sums), news = refs[:streams], refs[-2:], refs[-groups - 2 : -2]
    rel_total, mine, other, hub_ref, hub_all, rel_ref, rel_all = refs[streams : -groups - 2]
    chunks = hub_all.shape[1] // hub_ref.shape[1]
    take_owned(spot_ref, chunks, hub_all.shape[1], 0, lambda lanes: hub_all[:, lanes], hub_sums)
    take_owned(spot_ref, chunks, rel_all.shape[1], 0, lambda lanes: rel_all[:, lanes], rel_sums)
    width = rel_ref.shape[1]
    squares = mine[...] + other[...]
    hub_scale = step_rate / jnp.sqrt(hub_sums[...] + squares[0:1] * (1.0 / features))
    rel_scale = step_rate / jnp.sqrt(rel_sums[...] + squares[1:2, :width] * (1.0 / features))
    for s, (low, high) in enumerate(spans):
        new, base = there[s]
        first, end = rel_spans[s]
        middle = base + high - low
        news[new][0, base:middle] = hub_ref[low:high] - totals[s][0] * hub_scale
        news[new][0, middle : middle + end - first] = jnp.zeros((end - first, news[new].shape[2]), F32)
    for s, row, count, low, wide, to, to_lane in pieces:
        new, base = there[s]
        base += spans[s][1] - spans[s][0] + to
        lanes, first = slice(to_lane, to_lane + wide), rel_spans[s][0] + to
        news[new][0, base : base + count, lanes] = (
            rel_ref[row : row + count, low : low + wide]
            - rel_total[0, first : first + count, lanes] * rel_scale[:, low : low + wide]
        )


def join_all_kernel(heights, here, there, *refs):
    groups = 1 + max(g for g, unused in here)
    join_kernel(heights, here, there, *refs[:-1])
    base = 0
    for s, height in enumerate(heights):
        group, rows = rows_of(here, heights, s)
        for i, ref in enumerate((refs[group], refs[groups + group])):
            count = ref.shape[0]
            refs[-1][i * count : (i + 1) * count, base : base + height] = ref[:, rows]
        base += height


def join_all(have, got, orders, step, heights):
    count, width = 2 * have[0].shape[0], have[0].shape[2]
    unused, here = grouped(orders, step, heights)
    groups, there = grouped(orders, step - 1, heights)
    shapes = [(count, height, width) for height in [h for unused, h in groups] + [sum(heights)]]
    *have, near = call(functools.partial(join_all_kernel, heights, here, there), [*have, *got], shapes)
    return have, near


def chunk_copies(part, base, first, order, span, chip, component, out_ref, sems, at):
    low, high = span
    width = part.shape[2]
    for index in range(part.shape[0]):
        chunk = chip ^ gather_bits(first + index, order)
        lanes = pl.ds(pl.multiple_of(chunk * width, width), width)
        target = out_ref.at[component, pl.ds(low, high - low), lanes]
        yield pltpu.make_async_copy(part.at[index, pl.ds(base, high - low)], target, sems.at[at + index])


def component_of(spot_ref, mine):
    return spot_ref[1] if mine else 1 - spot_ref[1]


def near_kernel(orders, spans, bases, mine, spot_ref, near_ref, *refs):
    component = component_of(spot_ref, mine)
    out_ref, sems = refs[-2:]
    copies = []
    for order, span, base in zip(orders, spans, bases):
        copies += chunk_copies(near_ref, base, 0, order, span, spot_ref[0], component, out_ref, sems, len(copies))
    for copy in copies:
        copy.start()
    for copy in copies:
        copy.wait()


def far_kernel(orders, spans, bases, pieces, by_copy, mine, spot_ref, near_ref, *refs):
    component = component_of(spot_ref, mine)
    streams = len(orders)
    fars = refs[:streams]
    hub_out, rel_out, hub_all, rel_all, sems = refs[-5:]
    half = near_ref.shape[0]
    hub_width, rel_width = hub_out.shape[2] // (2 * half), rel_out.shape[2] // (2 * half)
    copies = []
    if by_copy:
        for far, order, span in zip(fars, orders, spans):
            copies += chunk_copies(far, 0, half, order, span, spot_ref[0], component, hub_out, sems, len(copies))
        for copy in copies:
            copy.start()
    for chunk in range(2 * half):
        place = spot_ref[0] ^ chunk
        for s, (low, high) in enumerate(spans):
            index = spread_bits(place, orders[s])
            spot = index & (half - 1)
            height, end = high - low, fars[s].shape[1]
            if not by_copy:
                value = jnp.where(index >= half, fars[s][spot, :height], near_ref[spot, bases[s] : bases[s] + height])
                hub_all[low:high, chunk * hub_width : (chunk + 1) * hub_width] = value
            value = jnp.where(index >= half, fars[s][spot, height:], near_ref[spot, bases[s] + height : bases[s] + end])
            for stream, row, count, low, wide, to, to_lane in pieces:
                if stream == s:
                    at = chunk * rel_width + low
                    rel_all[row : row + count, at : at + wide] = value[to : to + count, to_lane : to_lane + wide]
    copies.append(pltpu.make_async_copy(rel_all, rel_out.at[component], sems.at[len(copies)]))
    copies[-1].start()
    if not by_copy:
        copies.append(pltpu.make_async_copy(hub_all, hub_out.at[component], sems.at[len(copies)]))
        copies[-1].start()
    for copy in copies:
        copy.wait()


def placed(kernel, scratch, spot, near, fars, outs, earlier):
    sems = pltpu.SemaphoreType.DMA((3 * near.shape[0] + 2,))
    return pl.pallas_call(
        kernel,
        in_specs=[SMEM] + [VMEM] * (1 + len(fars)) + [HBM] * len(earlier),
        out_specs=[HBM] * len(outs),
        out_shape=[jax.ShapeDtypeStruct(shape, F32) for shape in outs],
        scratch_shapes=scratch + [sems],
        input_output_aliases={2 + len(fars) + i: i for i in range(len(earlier))},
        compiler_params=PARAMS,
        cost_estimate=pl.CostEstimate(flops=0, bytes_accessed=4 * outs[0][1] * outs[0][2], transcendentals=0),
    )(spot, near, *fars, *earlier)


def adagrad(table, state, grads):
    new_state = state + jnp.sum(grads * grads, axis=0, keepdims=True) * (1.0 / grads.shape[0])
    return table - grads * (step_rate / jnp.sqrt(new_state)), new_state


def keep_and_send(core, first, second):
    return jnp.where(core == 0, first, second), jnp.where(core == 0, second, first)


def table_counts(rows, negs, weight):
    place = lax.broadcasted_iota(jnp.int32, (rows, negs.shape[1]), 0)
    return jnp.sum(jnp.where(place == negs, weight, 0.0), axis=1, keepdims=True)


def turned(x, r, half):
    x0, x1, r0, r1 = x[:half], x[half:], r[:half], r[half:]
    return jnp.concatenate([x0 * r0 - x1 * r1, x0 * r1 + x1 * r0], axis=0)


def turned_back(x, r, half):
    x0, x1, r0, r1 = x[:half], x[half:], r[:half], r[half:]
    return x0 * r0 + x1 * r1, x1 * r0 - x0 * r1


EDGE_TILE = 512


def bucket_kernel(
    bucket, core_ref, heads_ref, tails_ref, negs_ref, left_ref, left_sums_ref, right_ref, right_sums_ref, rel_ref, hub_ref,
    left_out, left_sums_out, right_out, keep_out, send_out,
    left_parts, both_parts,
):
    features, rows = left_ref.shape
    half = features // 2
    core = core_ref[1]
    edges = heads_ref.shape[1]
    hubs = keep_out.shape[1] - edges
    at = slice(bucket, bucket + 1)
    weight = 1.0 / (negs_ref.shape[1] + hubs)
    counts = table_counts(rows, negs_ref[at], weight)
    stack_into(left_parts, left_ref[...])
    stack_into(both_parts, right_ref[...], slice(0, rows))
    stack_into(both_parts, hub_ref[...], slice(rows, rows + hubs))

    tail_here = lax.broadcasted_iota(jnp.int32, (rows, edges), 0) == tails_ref[at]
    head_hot = onehot(0, rows, heads_ref[at])
    h = dot2(left_parts[...], head_hot, NN)
    r = rel_ref[...]
    q = split(turned(h, r, half))
    scores = dot3((both_parts[:features], both_parts[features:]), q, TN)
    chance = jax.nn.sigmoid(scores[:rows])
    coef = jnp.concatenate(
        [
            counts * chance + jnp.where(tail_here, chance - 1.0, 0.0),
            weight * jax.nn.sigmoid(scores[rows:]),
        ],
        axis=0,
    )
    coef = split(coef)
    dq = dot3_stacked(both_parts[...], coef, NN)
    both_grad = dot3_stacked(stack(q), coef, NT)
    dh = jnp.concatenate(turned_back(dq, r, half), axis=0)
    left_grad = dot2(stack(split(dh)), head_hot, NT)
    keep_out[:, hubs:], send_out[:, hubs:] = keep_and_send(core, *turned_back(dq, h, half))

    left_out[...], left_sums_out[...] = adagrad(left_ref[...], left_sums_ref[...], left_grad)
    new_right, new_sums = adagrad(right_ref[...], right_sums_ref[...], both_grad[:, :rows])
    right_out[:features] = new_right
    right_out[features:] = jnp.broadcast_to(new_sums, (right_out.shape[0] - features, rows))
    keep_out[:, :hubs], send_out[:, :hubs] = keep_and_send(core, both_grad[:half, rows:], both_grad[half:, rows:])


def bucket_step(bucket, core, heads, tails, negs, left, left_sums, right, right_sums, rel_rows, hub_rows):
    features, rows = left.shape
    edges, hubs = heads.shape[1], hub_rows.shape[1]
    width = rows + hubs
    shapes = [(features, rows), (1, rows), (features + 8, rows)] + [(features // 2, hubs + edges)] * 2
    return pl.pallas_call(
        functools.partial(bucket_kernel, bucket),
        in_specs=[SMEM] + [VMEM] * 9,
        out_specs=[VMEM] * 5,
        out_shape=[jax.ShapeDtypeStruct(shape, F32) for shape in shapes],
        scratch_shapes=[
            pltpu.VMEM((2 * features, rows), BF16),
            pltpu.VMEM((2 * features, width), BF16),
        ],
        compiler_params=PARAMS,
        cost_estimate=COST,
    )(core, heads, tails, negs, left, left_sums, right, right_sums, rel_rows, hub_rows)


def hub_kernel(
    bucket, negatives, core_ref, heads_ref, left_ref, rel_ref, hub_ref,
    query_grad, hub_keep, hub_send,
    left_parts, hub_parts,
):
    features, rows = left_ref.shape
    half = features // 2
    edges, hubs = heads_ref.shape[1], hub_keep.shape[1]
    at = slice(bucket, bucket + 1)
    weight = 1.0 / (negatives + hubs)
    stack_into(left_parts, left_ref[...])
    stack_into(hub_parts, hub_ref[...])

    head_hot = onehot(0, rows, heads_ref[at])
    h = dot2(left_parts[...], head_hot, NN)
    q = split(turned(h, rel_ref[...], half))
    coef = split(weight * jax.nn.sigmoid(dot3((hub_parts[:features], hub_parts[features:]), q, TN)))
    query_grad[...] = dot3_stacked(hub_parts[...], coef, NN)
    hub_grad = dot3_stacked(stack(q), coef, NT)

    hub_keep[...], hub_send[...] = keep_and_send(core_ref[1], hub_grad[:half], hub_grad[half:])


def hub_step(bucket, negatives, core, heads, left, rel_rows, hub_rows):
    features, rows = left.shape
    edges, hubs = heads.shape[1], hub_rows.shape[1]
    shapes = [(features, edges)] + [(features // 2, hubs)] * 2
    return pl.pallas_call(
        functools.partial(hub_kernel, bucket, negatives),
        in_specs=[SMEM] + [VMEM] * 4,
        out_specs=[VMEM] * 3,
        out_shape=[jax.ShapeDtypeStruct(shape, F32) for shape in shapes],
        scratch_shapes=[
            pltpu.VMEM((2 * features, rows), BF16),
            pltpu.VMEM((2 * features, hubs), BF16),
        ],
        compiler_params=PARAMS,
        cost_estimate=COST,
    )(core, heads, left, rel_rows, hub_rows)


def tables_kernel(
    bucket, hubs, core_ref, heads_ref, tails_ref, negs_ref, query_grad,
    left_ref, left_sums_ref, right_ref, rel_ref,
    left_out, right_out, rel_keep, rel_send,
    left_parts, right_parts,
):
    features, rows = left_ref.shape
    half = features // 2
    edges = heads_ref.shape[1]
    at = slice(bucket, bucket + 1)
    core = core_ref[1]
    counts = table_counts(rows, negs_ref[at], 1.0 / (negs_ref.shape[1] + hubs))
    stack_into(left_parts, left_ref[...])
    stack_into(right_parts, right_ref[:features])

    tail_here = lax.broadcasted_iota(jnp.int32, (rows, edges), 0) == tails_ref[at]
    head_hot = onehot(0, rows, heads_ref[at])
    h = dot2(left_parts[...], head_hot, NN)
    r = rel_ref[...]
    q = split(turned(h, r, half))
    chance = jax.nn.sigmoid(dot3((right_parts[:features], right_parts[features:]), q, TN))
    coef = split(counts * chance + jnp.where(tail_here, chance - 1.0, 0.0))
    dq = dot3_stacked(right_parts[...], coef, NN) + query_grad[...]
    right_grad = dot3_stacked(stack(q), coef, NT)
    rel_keep[...], rel_send[...] = keep_and_send(core, *turned_back(dq, h, half))
    dh = jnp.concatenate(turned_back(dq, r, half), axis=0)
    left_grad = dot2(stack(split(dh)), head_hot, NT)

    left_out[...], unused = adagrad(left_ref[...], left_sums_ref[...], left_grad)
    right_out[...], unused = adagrad(right_ref[:features], right_ref[features : features + 1], right_grad)


def tables_step(bucket, hubs, core, heads, tails, negs, query_grad, left, left_sums, right, rel_rows):
    features, rows = left.shape
    edges = heads.shape[1]
    shapes = [(features, rows)] * 2 + [(features // 2, edges)] * 2
    return pl.pallas_call(
        functools.partial(tables_kernel, bucket, hubs),
        in_specs=[SMEM] + [VMEM] * 8,
        out_specs=[VMEM] * 4,
        out_shape=[jax.ShapeDtypeStruct(shape, F32) for shape in shapes],
        scratch_shapes=[pltpu.VMEM((2 * features, rows), BF16)] * 2,
        compiler_params=PARAMS,
        cost_estimate=COST,
    )(core, heads, tails, negs, query_grad, left, left_sums, right, rel_rows)


def from_behind(x, axis, by):
    size = lax.axis_size(axis)
    return lax.ppermute(x, axis, [(i, (i + by) % size) for i in range(size)])


def flipped(x, axis, bit):
    return lax.ppermute(x, axis, [(i, i ^ (1 << bit)) for i in range(lax.axis_size(axis))])


def flipped_by(x, axis, offset):
    return lax.ppermute(x, axis, [(i, i ^ offset) for i in range(lax.axis_size(axis))])


def other_core(x):
    return flipped(x, "blk", 0)


def across(x, place):
    sub_bits = lax.axis_size("sub").bit_length() - 1
    if place < sub_bits:
        return flipped(x, "sub", place)
    return flipped(x, "blk", place - sub_bits + 1)


def stream_orders():
    sub_bits = lax.axis_size("sub").bit_length() - 1
    bits = sub_bits + lax.axis_size("blk").bit_length() - 2
    x, y, z, far = sub_bits, sub_bits + 1, 0, 1
    rest = [p for p in range(bits) if p not in (x, y, z, far)]
    return [[x, y, z, far] + rest, [y, z, x, far] + rest, [z, x, far, y] + rest]


def plane_orders(sub_bits, bits):
    plane, depth = list(range(sub_bits, bits)), list(range(sub_bits - 1, -1, -1))
    return [plane + depth, plane[1:] + plane[:1] + depth]


def row_spans(rows, parts):
    ends = [-(-rows * (i + 1) // (8 * parts)) * 8 for i in range(parts - 1)] + [rows]
    return list(zip([0] + ends[:-1], ends))


def shards(
    left_emb, left_state, right_emb, right_state, relation_emb, relation_state, hub_emb, hub_state,
    heads, relations, tails, negatives, hub_ids,
):
    components, half_width, row_count = left_emb.shape
    features = components * half_width
    rel_count, hub_count = relation_emb.shape[2], hub_emb.shape[2]
    left = left_emb.reshape(features, row_count)
    right = right_emb.reshape(features, row_count)
    left_sums = left_state.reshape(1, row_count)
    right_sums = right_state.reshape(1, row_count)
    buckets, edges = heads.shape
    hubs = hub_ids.shape[1]

    orders = stream_orders()
    streams, stages = len(orders), len(orders[0])
    chunks, depth = 1 << stages, lax.axis_size("sub")
    sub_bits = depth.bit_length() - 1
    planes = chunks // depth
    spans = row_spans(half_width, streams)
    rel_orders = plane_orders(sub_bits, stages)
    width, rel_width = hub_count // chunks, rel_count // chunks
    rel_height, entries = packed_map(half_width, rel_width, width)
    plane_spans = row_spans(rel_height, len(rel_orders))
    share = -(-(half_width + rel_height) // (8 * streams)) * 8
    ends = [share * (s + 1) - spans[s][1] for s in range(streams - 1)] + [rel_height]
    rel_spans = list(zip([0] + ends[:-1], ends))
    plane_pieces, joint_pieces = split_pieces(entries, plane_spans), split_pieces(entries, rel_spans)
    heights, rel_heights, plane_heights = [[high - low for low, high in x] for x in (spans, rel_spans, plane_spans)]
    joint_heights = [h + r for h, r in zip(heights, rel_heights)]
    bases = [sum(joint_heights[:s]) for s in range(streams)]
    hub_lanes, rel_lanes = (0, hubs), (hubs, hubs + edges)

    def exchanged(parts, step):
        return [across(x, place) for x, (place, unused) in zip(parts, grouped(orders, step, heights)[0])]

    def in_turn(first, then):
        return lax.optimization_barrier((first, then))

    blk = lax.axis_index("blk")
    spot = jnp.stack([(blk >> 1) * depth + lax.axis_index("sub"), blk & 1]).astype(jnp.int32)
    far_ids = other_core((hub_ids, relations))
    hub_rows, rel_rows, spot, owned = gather_rows(
        spot, hub_emb.reshape(features, hub_count), hub_ids, relation_emb.reshape(features, rel_count), relations, chunks
    )
    far_ids, hub_rows = in_turn(far_ids, hub_rows)
    keeps, sends = [], []
    for b in range(buckets - 1):
        if b > 0:
            right, right_sums = right[:features], right[features : features + 1]
        left, left_sums, right, keep, send = bucket_step(
            b, spot, heads, tails, negatives, left, left_sums, right, right_sums, rel_rows[b], hub_rows[b]
        )
        right = from_behind(right, "blk", 1)
        keeps.append(keep)
        sends.append(send)
    last = buckets - 1
    query_grad, hub_keep, hub_send = hub_step(
        last, negatives.shape[1], spot, heads, left, rel_rows[last], hub_rows[last]
    )
    sends, hub_send = in_turn(sends, hub_send)
    hub_far = other_core(hub_send)
    fars = [other_core(x) for x in sends]
    grads = lambda early, late, lanes: [(x, lanes) for x in early] + [(late, (0, late.shape[1]))]
    groups, where = grouped(orders, 0, heights)
    parts = chunk_columns(
        functools.partial(hub_chunks_kernel, orders, spans, where),
        [(chunks // 2, height, width) for height in [h for unused, h in groups] + heights],
        spot, (hub_ids, far_ids[0]), grads(keeps, hub_keep, hub_lanes) + grads(fars, hub_far, hub_lanes),
    )
    send, own = parts[: len(groups)], parts[len(groups) :]
    got = exchanged(send, 0)
    left, right, rel_keep, rel_send = tables_step(
        last, hubs, spot, heads, tails, negatives, query_grad, left, left_sums, right, rel_rows[last]
    )
    rel_far = other_core(rel_send)

    parts = chunk_columns(
        functools.partial(rel_chunks_kernel, rel_orders, plane_pieces, rel_count),
        [(chunks // 2, height, width) for height in plane_heights * 2],
        spot, (relations, far_ids[1]), grads(keeps, rel_keep, rel_lanes) + grads(fars, rel_far, rel_lanes),
    )
    rel_send, rel_own = parts[: len(rel_orders)], parts[len(rel_orders) :]
    rel_got = [across(x, order[0]) for x, order in zip(rel_send, rel_orders)]
    plane_steps = stages - sub_bits
    for step in range(stages - 2):
        if 0 < step < plane_steps:
            own, rel_got = in_turn(own, rel_got)
            rel_send, rel_own = halves(rel_own, rel_got, rel_orders, step - 1)
            rel_got = [across(x, order[step]) for x, order in zip(rel_send, rel_orders)]
        rel_own, got = in_turn(rel_own, got)
        send, own = halves(own, got, orders, step)
        got = exchanged(send, step + 1)

    here = grouped(orders, stages - 2, heights)[1]
    groups, there = grouped(orders, stages - 1, heights)
    carried = {1 << place: (g, height) for g, (place, height) in enumerate(groups) if place < sub_bits}
    tall = [height + (rel_height if place < sub_bits else 0) for place, height in groups]
    alone = [q for q in range(depth) if q not in carried]
    parts = call(
        functools.partial(last_sums_kernel, heights, here, there, plane_spans, carried),
        [*own, *got, *rel_own, *rel_got],
        [(1, height, width) for height in tall + heights + [rel_height] * len(alone)],
    )
    send, own, rel_parts = parts[: len(groups)], parts[len(groups) : len(groups) + streams], parts[len(groups) + streams :]
    got = exchanged(send, stages - 1)
    rel_got = [flipped_by(x, "sub", q) for q, x in zip(alone[1:], rel_parts[1:])]
    *totals, rel_total, squares = call(
        functools.partial(squares_kernel, heights, there, entries, carried),
        [*own, *got, rel_parts[0], *rel_got], [x.shape for x in own] + [rel_parts[0].shape, (2, width)],
    )
    hub_own, rel_own = owned
    groups, there = grouped(orders, stages - 1, joint_heights)
    ins = [
        *totals, rel_total, squares, other_core(squares),
        hub_own, hub_state[None], rel_own, relation_state[None],
    ]
    have = pl.pallas_call(
        functools.partial(update_kernel, spans, rel_spans, joint_pieces, there, features),
        in_specs=[SMEM] + [VMEM] * len(ins),
        out_specs=[VMEM] * len(groups),
        out_shape=[jax.ShapeDtypeStruct((1, height, width), F32) for unused, height in groups],
        scratch_shapes=[pltpu.VMEM((1, x.shape[1]), F32) for x in owned],
        compiler_params=PARAMS,
        cost_estimate=COST,
    )(spot, *ins)
    for step in range(stages - 1, 1, -1):
        have = join(have, exchanged(have, step), orders, step, joint_heights)
    have, near = join_all(have, exchanged(have, 1), orders, 1, joint_heights)
    got = exchanged(have, 0)
    far_near = other_core(near)

    shapes = [hub_emb.shape, relation_emb.shape]
    by_copy = width % 128 == 0
    hub_new = []
    if by_copy:
        near_step = functools.partial(near_kernel, orders, spans, bases)
        hub_new = placed(functools.partial(near_step, True), [], spot, near, [], shapes[:1], [])
        hub_new = placed(functools.partial(near_step, False), [], spot, far_near, [], shapes[:1], hub_new)
        got, hub_new = in_turn(got, hub_new)
    far_step = functools.partial(far_kernel, orders, spans, bases, joint_pieces, by_copy)
    scratch = [
        pltpu.VMEM((8, 128) if by_copy else (half_width, hub_count), F32),
        pltpu.VMEM((half_width, rel_count), F32),
    ]
    far_got = other_core(got)
    out = placed(functools.partial(far_step, True), scratch, spot, near, got, shapes, hub_new)
    hub_new, rel_new = placed(functools.partial(far_step, False), scratch, spot, far_near, far_got, shapes, out)
    return (
        left.reshape(components, half_width, row_count),
        right.reshape(components, half_width, row_count),
        rel_new,
        hub_new,
    )


def solution(mesh):
    both = ("blk", "sub")
    block, table, whole = P(None, None, both), P(None, both), P()
    return jax.shard_map(
        shards,
        mesh=mesh,
        in_specs=(block, P(both), block, P(both), whole, whole, whole, whole, table, table, table, table, table),
        out_specs=(block, block, whole, whole),
        check_vma=False,
    )
```

```python
import functools
import jax
import jax.numpy as jnp
from jax import lax
from jax.experimental import pallas as pl
from jax.experimental.pallas import tpu as pltpu
from jax.sharding import PartitionSpec as P

step_rate = 0.25
F32, BF16 = jnp.float32, jnp.bfloat16
NN = (((1,), (0,)), ((), ()))
NT = (((1,), (1,)), ((), ()))
TN = (((0,), (0,)), ((), ()))
VMEM = pl.BlockSpec(memory_space=pltpu.VMEM)
SMEM = pl.BlockSpec(memory_space=pltpu.SMEM)
PARAMS = pltpu.CompilerParams(vmem_limit_bytes=12 * 1024 * 1024)
GATHER_PARAMS = pltpu.CompilerParams(vmem_limit_bytes=50 * 1024 * 1024)
HBM = pl.BlockSpec(memory_space=pltpu.HBM)
COST = pl.CostEstimate(flops=10000, bytes_accessed=10000, transcendentals=0)


def split(x):
    hi = x.astype(BF16)
    return hi, (x - hi.astype(F32)).astype(BF16)


def dot(a, b, dims):
    return lax.dot_general(a, b, dims, preferred_element_type=F32)


def dot3(a, b, dims):
    return dot(a[0], b[0], dims) + (dot(a[0], b[1], dims) + dot(a[1], b[0], dims))


def dot2(stacked, onehot, dims):
    half = stacked.shape[0] // 2
    both = dot(stacked, onehot, dims)
    return both[:half] + both[half:]


def stack(parts):
    return jnp.concatenate(parts, axis=0)


def stack_into(ref, x, lanes=slice(None)):
    rows, half = x.shape[0], ref.shape[0] // 2
    hi, lo = split(x)
    ref[:rows, lanes] = hi
    ref[half : half + rows, lanes] = lo
    if half > rows:
        blank = jnp.zeros((half - rows, x.shape[1]), BF16)
        ref[rows:half, lanes] = blank
        ref[half + rows :, lanes] = blank


def dot3_stacked(stacked, b, dims):
    half = stacked.shape[0] // 2
    both = dot(stacked, b[0], dims)
    return both[:half] + (both[half:] + dot(stacked[:half], b[1], dims))


def hot_where(here):
    return jnp.where(here, jnp.ones((), BF16), jnp.zeros((), BF16))


def onehot(first, rows, idx):
    place = lax.broadcasted_iota(jnp.int16, (rows, idx.shape[1]), 0)
    return hot_where(place == (idx - first).astype(jnp.int16))


def laid_out(idx):
    return jnp.concatenate([idx[b : b + 1] for b in range(idx.shape[0])], axis=1)


def take_owned(spot_ref, chunks, span, first, piece_of, out_ref):
    width = out_ref.shape[1]
    for chunk in range(chunks):
        if first <= chunk * width < first + span:

            @pl.when(spot_ref[0] == chunk)
            def _():
                out_ref[...] = piece_of(slice(chunk * width - first, (chunk + 1) * width - first))


def gather_kernel(hub_steps, rel_steps, spot_ref, hub_ids, rel_ids, hub_ref, rel_ref, *refs):
    buckets = hub_ids.shape[0]
    hub_outs, rel_outs = refs[:buckets], refs[buckets : 2 * buckets]
    spot_out, hub_own, rel_own = refs[2 * buckets : 2 * buckets + 3]
    hub_buf, rel_buf, hub_idx, rel_idx, stacked, sems = refs[2 * buckets + 3 :]
    hub_tile, rel_tile = hub_buf.shape[2], rel_buf.shape[2]
    chunks = hub_ref.shape[1] // hub_own.shape[1]
    half = hub_own.shape[0]
    steps = [(hub_ref, hub_buf, hub_tile, k) for k in range(hub_steps)]
    steps += [(rel_ref, rel_buf, rel_tile, k) for k in range(rel_steps)]
    copies = [
        pltpu.make_async_copy(table.at[:, pl.ds(k * tile, tile)], buf.at[k % 2], sems.at[i])
        for i, (table, buf, tile, k) in enumerate(steps)
    ]
    id_copies = [
        pltpu.make_async_copy(ids, out, sems.at[len(copies) + i])
        for i, (ids, out) in enumerate([(hub_ids, hub_idx), (rel_ids, rel_idx)])
    ]
    for copy in [*id_copies, copies[0]]:
        copy.start()
    spot_out[0] = spot_ref[0]
    spot_out[1] = spot_ref[1]
    for copy in id_copies:
        copy.wait()
    rows = pl.ds(pl.multiple_of(spot_ref[1] * half, 8), half)
    for i, (table, buf, tile, k) in enumerate(steps):
        if i + 1 < len(steps):
            copies[i + 1].start()
        idx, outs, own = (hub_idx, hub_outs, hub_own) if table is hub_ref else (rel_idx, rel_outs, rel_own)
        count = idx.shape[1]
        hot = onehot(k * tile, tile, laid_out(idx[...]))
        copies[i].wait()
        stack_into(stacked, buf[k % 2], slice(0, tile))
        part = dot2(stacked[:, :tile], hot, NN)
        for b, out in enumerate(outs):
            here = part[:, b * count : (b + 1) * count]
            out[...] = here if k == 0 else out[...] + here
        take_owned(spot_ref, chunks, tile, k * tile, lambda lanes: buf[k % 2, rows, lanes], own)


def gather_rows(spot, hub_table, hub_idx, rel_table, rel_idx, chunks):
    features = hub_table.shape[0]
    hub_steps, rel_steps = 4, 2
    hub_tile, rel_tile = hub_table.shape[1] // hub_steps, rel_table.shape[1] // rel_steps
    buckets, hubs = hub_idx.shape
    edges = rel_idx.shape[1]
    hub_width, rel_width = hub_table.shape[1] // chunks, rel_table.shape[1] // chunks
    shapes = [(features, hubs)] * buckets + [(features, edges)] * buckets
    own_shapes = [(features // 2, hub_width), (features // 2, rel_width)]
    floats = lambda shapes: [jax.ShapeDtypeStruct(shape, F32) for shape in shapes]
    out = pl.pallas_call(
        functools.partial(gather_kernel, hub_steps, rel_steps),
        in_specs=[SMEM] + [HBM] * 4,
        out_specs=[VMEM] * len(shapes) + [SMEM] + [VMEM] * len(own_shapes),
        out_shape=floats(shapes) + [jax.ShapeDtypeStruct((2,), jnp.int32)] + floats(own_shapes),
        scratch_shapes=[
            pltpu.VMEM((2, features, hub_tile), F32),
            pltpu.VMEM((2, features, rel_tile), F32),
            pltpu.VMEM(hub_idx.shape, jnp.int32),
            pltpu.VMEM(rel_idx.shape, jnp.int32),
            pltpu.VMEM((2 * features, max(hub_tile, rel_tile)), BF16),
            pltpu.SemaphoreType.DMA((hub_steps + rel_steps + 2,)),
        ],
        compiler_params=GATHER_PARAMS,
        cost_estimate=COST,
    )(spot, hub_idx, rel_idx, hub_table, rel_table)
    return out[:buckets], out[buckets : 2 * buckets], out[2 * buckets], out[2 * buckets + 1 :]


def spread_bits(place, order):
    bits = len(order)
    return sum((((place >> p) & 1) << (bits - 1 - i)) for i, p in enumerate(order))


def gather_bits(index, order):
    bits = len(order)
    return sum((((index >> (bits - 1 - i)) & 1) << p) for i, p in enumerate(order))


def load_columns(id_refs, grad_refs, idx_down, stacked):
    idx = jnp.concatenate([laid_out(ref[...]) for ref in id_refs], axis=1)
    idx_down[...] = jnp.transpose(jnp.broadcast_to(idx, (128, idx.shape[1]))).astype(jnp.int16)
    at = 0
    for ref, (low, high) in grad_refs:
        width = high - low
        stack_into(stacked, ref[:, low:high], slice(at, at + width))
        at += width


def onehot_across(idx_down, targets):
    width = targets.shape[1]
    idx = idx_down[...]
    wide = jnp.concatenate([idx] * -(-width // 128), axis=1)[:, :width]
    return hot_where(wide == targets.astype(jnp.int16))


def grouped(orders, step, heights):
    groups, where = [], []
    for s, order in enumerate(orders):
        for g, (place, members) in enumerate(groups):
            if place == order[step]:
                where.append((g, sum(heights[m] for m in members)))
                members.append(s)
                break
        else:
            where.append((len(groups), 0))
            groups.append((order[step], [s]))
    return [(place, sum(heights[m] for m in members)) for place, members in groups], where


def rows_of(where, heights, s):
    group, base = where[s]
    return group, slice(base, base + heights[s])


def put_chunk(place, orders, heights, where, sends, keeps, s, value):
    index, half = spread_bits(place, orders[s]), keeps[s].shape[0]
    if index < half:
        keeps[s][index] = value
    else:
        group, rows = rows_of(where, heights, s)
        sends[group][index - half, rows] = value


def chunk_refs(grad_lanes, refs):
    ids, refs = refs[:2], refs[2:]
    grads, refs = list(zip(refs, grad_lanes)), refs[len(grad_lanes) :]
    return ids, grads, refs[:-2], refs[-2:]


def hub_chunks_kernel(orders, spans, where, grad_lanes, spot_ref, *refs):
    ids, grads, outs, (idx_down, stacked) = chunk_refs(grad_lanes, refs)
    load_columns(ids, grads, idx_down, stacked)
    streams = len(orders)
    sends, keeps = outs[:-streams], outs[-streams:]
    heights = [high - low for low, high in spans]
    chunks, width = 2 * keeps[0].shape[0], keeps[0].shape[2]
    lane = lax.broadcasted_iota(jnp.int32, (1, width), 1)
    for place in range(chunks):
        hot = onehot_across(idx_down, lane + (spot_ref[0] ^ place) * width)
        chunk = dot2(stacked[...], hot, NN)
        for s, (low, high) in enumerate(spans):
            put_chunk(place, orders, heights, where, sends, keeps, s, chunk[low:high])


def packed_map(half_width, width, lanes):
    rows = half_width // 24 * 8
    gap, extra = lanes - 3 * width, half_width - 3 * rows
    entries = [(rows * b, 0, width, 0, b * width, rows) for b in range(3)]
    for i in range(-(-width // gap)):
        entries.append((3 * rows, i * gap, min(gap, width - i * gap), extra * i, 3 * width, extra))
    return rows, entries


def split_pieces(entries, spans):
    pieces = []
    for row, lane, lanes, to, to_lane, count in entries:
        for s, (first, end) in enumerate(spans):
            low, high = max(to, first), min(to + count, end)
            if low < high:
                pieces.append((s, row + low - to, high - low, lane, lanes, low - first, to_lane))
    return pieces


def rel_chunks_kernel(orders, pieces, rows, grad_lanes, spot_ref, *refs):
    ids, grads, outs, (idx_down, stacked) = chunk_refs(grad_lanes, refs)
    load_columns(ids, grads, idx_down, stacked)
    for ref in outs:
        ref[...] = jnp.zeros_like(ref)
    streams = len(orders)
    sends, keeps = outs[:streams], outs[streams:]
    half, lanes = keeps[0].shape[0], keeps[0].shape[2]
    chunks = 2 * half
    width = rows // chunks
    group = lanes // width
    lane = lax.broadcasted_iota(jnp.int32, (1, lanes), 1)
    for first in range(0, chunks, group):
        targets = jnp.full((1, lanes), -1, jnp.int32)
        places = range(first, min(first + group, chunks))
        for slot, place in enumerate(places):
            here = (lane >= slot * width) & (lane < (slot + 1) * width)
            targets = jnp.where(here, lane + ((spot_ref[0] ^ place) * width - slot * width), targets)
        dense = dot2(stacked[...], onehot_across(idx_down, targets), NN)
        for slot, place in enumerate(places):
            chunk = dense[:, slot * width : (slot + 1) * width]
            for s, row, count, low, wide, to, to_lane in pieces:
                index = spread_bits(place, orders[s])
                out = sends[s].at[index - half] if index >= half else keeps[s].at[index]
                out[to : to + count, to_lane : to_lane + wide] = chunk[row : row + count, low : low + wide]


def chunk_columns(kernel, shapes, spot, ids, grads):
    half_width = grads[0][0].shape[0]
    grad_lanes = [lanes_of for unused, lanes_of in grads]
    count = sum(high - low for low, high in grad_lanes)
    return pl.pallas_call(
        functools.partial(kernel, grad_lanes),
        in_specs=[SMEM] + [VMEM] * (2 + len(grads)),
        out_specs=[VMEM] * len(shapes),
        out_shape=[jax.ShapeDtypeStruct(shape, F32) for shape in shapes],
        scratch_shapes=[
            pltpu.VMEM((count, 128), jnp.int16),
            pltpu.VMEM((2 * (-(-half_width // 16) * 16), count), BF16),
        ],
        compiler_params=PARAMS,
        cost_estimate=COST,
    )(spot, *ids, *[g for g, unused in grads])


def call(kernel, ins, shapes):
    return pl.pallas_call(
        kernel,
        in_specs=[VMEM] * len(ins),
        out_specs=[VMEM] * len(shapes),
        out_shape=[jax.ShapeDtypeStruct(shape, F32) for shape in shapes],
        compiler_params=PARAMS,
        cost_estimate=COST,
    )(*ins)


def sums_kernel(heights, here, there, *refs):
    streams, groups = len(heights), 1 + max(g for g, unused in here)
    own, got, sends, keeps = refs[:streams], refs[streams : streams + groups], refs[streams + groups : -streams], refs[-streams:]
    for s in range(streams):
        half = keeps[s].shape[0]
        group, rows = rows_of(here, heights, s)
        out, out_rows = rows_of(there, heights, s)
        sends[out][:, out_rows] = own[s][half:] + got[group][half:, rows]
        keeps[s][...] = own[s][:half] + got[group][:half, rows]


def halves(own, got, orders, step):
    heights = [x.shape[1] for x in own]
    half, width = own[0].shape[0] // 2, own[0].shape[2]
    unused, here = grouped(orders, step, heights)
    groups, there = grouped(orders, step + 1, heights)
    shapes = [(half, height, width) for height in [h for unused, h in groups] + heights]
    out = call(functools.partial(sums_kernel, heights, here, there), [*own, *got], shapes)
    return out[: len(groups)], out[len(groups) :]


def join_kernel(heights, here, there, *refs):
    groups = 1 + max(g for g, unused in here)
    own, got, outs = refs[:groups], refs[groups : 2 * groups], refs[2 * groups :]
    count = own[0].shape[0]
    for s in range(len(heights)):
        group, rows = rows_of(here, heights, s)
        out, out_rows = rows_of(there, heights, s)
        outs[out][:count, out_rows] = own[group][:, rows]
        outs[out][count:, out_rows] = got[group][:, rows]


def join(have, got, orders, step, heights):
    count, width = have[0].shape[0], have[0].shape[2]
    unused, here = grouped(orders, step, heights)
    groups, there = grouped(orders, step - 1, heights)
    shapes = [(2 * count, height, width) for unused, height in groups]
    return call(functools.partial(join_kernel, heights, here, there), [*have, *got], shapes)


def last_sums_kernel(heights, here, there, spans, *refs):
    streams, planes = len(heights), len(spans)
    groups, out_groups = [1 + max(g for g, unused in where) for where in (here, there)]
    rels, outs = refs[streams + groups : streams + groups + 2 * planes], refs[streams + groups + 2 * planes :]
    sums_kernel(heights, here, there, *refs[: streams + groups], *outs[: out_groups + streams])
    for place, out in enumerate(outs[out_groups + streams :]):
        for s, (low, high) in enumerate(spans):
            out[0, low:high] = rels[s][place] + rels[planes + s][place]


def squares_kernel(heights, here, entries, *refs):
    streams, groups = len(heights), 1 + max(g for g, unused in here)
    own, got, rels = refs[:streams], refs[streams : streams + groups], refs[streams + groups : -streams - 2]
    totals, rel_total, out = refs[-streams - 2 : -2], refs[-2], refs[-1]
    squares = jnp.zeros((1, out.shape[1]), F32)
    for s in range(streams):
        group, rows = rows_of(here, heights, s)
        total = own[s][0] + got[group][0, rows]
        totals[s][0] = total
        squares += jnp.sum(total * total, axis=0, keepdims=True)
    total = sum(ref[0] for ref in rels)
    rel_total[0] = total
    out[0:1] = squares
    out[1:2] = jnp.zeros_like(squares)
    square = total * total
    for row, lane, lanes, to, to_lane, count in entries:
        part = jnp.sum(square[to : to + count, to_lane : to_lane + lanes], axis=0, keepdims=True)
        out[1:2, lane : lane + lanes] += part


def update_kernel(spans, rel_spans, pieces, there, features, spot_ref, *refs):
    streams, groups = len(spans), 1 + max(g for g, unused in there)
    totals, (hub_sums, rel_sums), news = refs[:streams], refs[-2:], refs[-groups - 2 : -2]
    rel_total, mine, other, hub_ref, hub_all, rel_ref, rel_all = refs[streams : -groups - 2]
    chunks = hub_all.shape[1] // hub_ref.shape[1]
    take_owned(spot_ref, chunks, hub_all.shape[1], 0, lambda lanes: hub_all[:, lanes], hub_sums)
    take_owned(spot_ref, chunks, rel_all.shape[1], 0, lambda lanes: rel_all[:, lanes], rel_sums)
    width = rel_ref.shape[1]
    squares = mine[...] + other[...]
    hub_scale = step_rate / jnp.sqrt(hub_sums[...] + squares[0:1] * (1.0 / features))
    rel_scale = step_rate / jnp.sqrt(rel_sums[...] + squares[1:2, :width] * (1.0 / features))
    for s, (low, high) in enumerate(spans):
        new, base = there[s]
        first, end = rel_spans[s]
        middle = base + high - low
        news[new][0, base:middle] = hub_ref[low:high] - totals[s][0] * hub_scale
        news[new][0, middle : middle + end - first] = jnp.zeros((end - first, news[new].shape[2]), F32)
    for s, row, count, low, wide, to, to_lane in pieces:
        new, base = there[s]
        base += spans[s][1] - spans[s][0] + to
        lanes, first = slice(to_lane, to_lane + wide), rel_spans[s][0] + to
        news[new][0, base : base + count, lanes] = (
            rel_ref[row : row + count, low : low + wide]
            - rel_total[0, first : first + count, lanes] * rel_scale[:, low : low + wide]
        )


def join_all_kernel(heights, here, there, *refs):
    groups = 1 + max(g for g, unused in here)
    join_kernel(heights, here, there, *refs[:-1])
    base = 0
    for s, height in enumerate(heights):
        group, rows = rows_of(here, heights, s)
        for i, ref in enumerate((refs[group], refs[groups + group])):
            count = ref.shape[0]
            refs[-1][i * count : (i + 1) * count, base : base + height] = ref[:, rows]
        base += height


def join_all(have, got, orders, step, heights):
    count, width = 2 * have[0].shape[0], have[0].shape[2]
    unused, here = grouped(orders, step, heights)
    groups, there = grouped(orders, step - 1, heights)
    shapes = [(count, height, width) for height in [h for unused, h in groups] + [sum(heights)]]
    *have, near = call(functools.partial(join_all_kernel, heights, here, there), [*have, *got], shapes)
    return have, near


def chunk_copies(part, base, first, order, span, chip, component, out_ref, sems, at):
    low, high = span
    width = part.shape[2]
    for index in range(part.shape[0]):
        chunk = chip ^ gather_bits(first + index, order)
        lanes = pl.ds(pl.multiple_of(chunk * width, width), width)
        target = out_ref.at[component, pl.ds(low, high - low), lanes]
        yield pltpu.make_async_copy(part.at[index, pl.ds(base, high - low)], target, sems.at[at + index])


def component_of(spot_ref, mine):
    return spot_ref[1] if mine else 1 - spot_ref[1]


def near_kernel(orders, spans, bases, mine, spot_ref, near_ref, *refs):
    component = component_of(spot_ref, mine)
    out_ref, sems = refs[-2:]
    copies = []
    for order, span, base in zip(orders, spans, bases):
        copies += chunk_copies(near_ref, base, 0, order, span, spot_ref[0], component, out_ref, sems, len(copies))
    for copy in copies:
        copy.start()
    for copy in copies:
        copy.wait()


def far_kernel(orders, spans, bases, pieces, by_copy, mine, spot_ref, near_ref, *refs):
    component = component_of(spot_ref, mine)
    streams = len(orders)
    fars = refs[:streams]
    hub_out, rel_out, hub_all, rel_all, sems = refs[-5:]
    half = near_ref.shape[0]
    hub_width, rel_width = hub_out.shape[2] // (2 * half), rel_out.shape[2] // (2 * half)
    copies = []
    if by_copy:
        for far, order, span in zip(fars, orders, spans):
            copies += chunk_copies(far, 0, half, order, span, spot_ref[0], component, hub_out, sems, len(copies))
        for copy in copies:
            copy.start()
    for chunk in range(2 * half):
        place = spot_ref[0] ^ chunk
        for s, (low, high) in enumerate(spans):
            index = spread_bits(place, orders[s])
            spot = index & (half - 1)
            height, end = high - low, fars[s].shape[1]
            if not by_copy:
                value = jnp.where(index >= half, fars[s][spot, :height], near_ref[spot, bases[s] : bases[s] + height])
                hub_all[low:high, chunk * hub_width : (chunk + 1) * hub_width] = value
            value = jnp.where(index >= half, fars[s][spot, height:], near_ref[spot, bases[s] + height : bases[s] + end])
            for stream, row, count, low, wide, to, to_lane in pieces:
                if stream == s:
                    at = chunk * rel_width + low
                    rel_all[row : row + count, at : at + wide] = value[to : to + count, to_lane : to_lane + wide]
    copies.append(pltpu.make_async_copy(rel_all, rel_out.at[component], sems.at[len(copies)]))
    copies[-1].start()
    if not by_copy:
        copies.append(pltpu.make_async_copy(hub_all, hub_out.at[component], sems.at[len(copies)]))
        copies[-1].start()
    for copy in copies:
        copy.wait()


def placed(kernel, scratch, spot, near, fars, outs, earlier):
    sems = pltpu.SemaphoreType.DMA((3 * near.shape[0] + 2,))
    return pl.pallas_call(
        kernel,
        in_specs=[SMEM] + [VMEM] * (1 + len(fars)) + [HBM] * len(earlier),
        out_specs=[HBM] * len(outs),
        out_shape=[jax.ShapeDtypeStruct(shape, F32) for shape in outs],
        scratch_shapes=scratch + [sems],
        input_output_aliases={2 + len(fars) + i: i for i in range(len(earlier))},
        compiler_params=PARAMS,
        cost_estimate=pl.CostEstimate(flops=0, bytes_accessed=4 * outs[0][1] * outs[0][2], transcendentals=0),
    )(spot, near, *fars, *earlier)


def adagrad(table, state, grads):
    new_state = state + jnp.sum(grads * grads, axis=0, keepdims=True) * (1.0 / grads.shape[0])
    return table - grads * (step_rate / jnp.sqrt(new_state)), new_state


def keep_and_send(core, first, second):
    return jnp.where(core == 0, first, second), jnp.where(core == 0, second, first)


def table_counts(rows, negs, weight):
    place = lax.broadcasted_iota(jnp.int32, (rows, negs.shape[1]), 0)
    return jnp.sum(jnp.where(place == negs, weight, 0.0), axis=1, keepdims=True)


def turned(x, r, half):
    x0, x1, r0, r1 = x[:half], x[half:], r[:half], r[half:]
    return jnp.concatenate([x0 * r0 - x1 * r1, x0 * r1 + x1 * r0], axis=0)


def turned_back(x, r, half):
    x0, x1, r0, r1 = x[:half], x[half:], r[:half], r[half:]
    return x0 * r0 + x1 * r1, x1 * r0 - x0 * r1


EDGE_TILE = 512


def bucket_kernel(
    bucket, core_ref, heads_ref, tails_ref, negs_ref, left_ref, left_sums_ref, right_ref, right_sums_ref, rel_ref, hub_ref,
    left_out, left_sums_out, right_out, keep_out, send_out,
    left_parts, both_parts,
):
    features, rows = left_ref.shape
    half = features // 2
    core = core_ref[1]
    edges = heads_ref.shape[1]
    hubs = keep_out.shape[1] - edges
    at = slice(bucket, bucket + 1)
    weight = 1.0 / (negs_ref.shape[1] + hubs)
    counts = table_counts(rows, negs_ref[at], weight)
    stack_into(left_parts, left_ref[...])
    stack_into(both_parts, right_ref[...], slice(0, rows))
    stack_into(both_parts, hub_ref[...], slice(rows, rows + hubs))

    tail_here = lax.broadcasted_iota(jnp.int32, (rows, edges), 0) == tails_ref[at]
    head_hot = onehot(0, rows, heads_ref[at])
    h = dot2(left_parts[...], head_hot, NN)
    r = rel_ref[...]
    q = split(turned(h, r, half))
    scores = dot3((both_parts[:features], both_parts[features:]), q, TN)
    chance = jax.nn.sigmoid(scores[:rows])
    coef = jnp.concatenate(
        [
            counts * chance + jnp.where(tail_here, chance - 1.0, 0.0),
            weight * jax.nn.sigmoid(scores[rows:]),
        ],
        axis=0,
    )
    coef = split(coef)
    dq = dot3_stacked(both_parts[...], coef, NN)
    both_grad = dot3_stacked(stack(q), coef, NT)
    dh = jnp.concatenate(turned_back(dq, r, half), axis=0)
    left_grad = dot2(stack(split(dh)), head_hot, NT)
    keep_out[:, hubs:], send_out[:, hubs:] = keep_and_send(core, *turned_back(dq, h, half))

    left_out[...], left_sums_out[...] = adagrad(left_ref[...], left_sums_ref[...], left_grad)
    new_right, new_sums = adagrad(right_ref[...], right_sums_ref[...], both_grad[:, :rows])
    right_out[:features] = new_right
    right_out[features:] = jnp.broadcast_to(new_sums, (right_out.shape[0] - features, rows))
    keep_out[:, :hubs], send_out[:, :hubs] = keep_and_send(core, both_grad[:half, rows:], both_grad[half:, rows:])


def bucket_step(bucket, core, heads, tails, negs, left, left_sums, right, right_sums, rel_rows, hub_rows):
    features, rows = left.shape
    edges, hubs = heads.shape[1], hub_rows.shape[1]
    width = rows + hubs
    shapes = [(features, rows), (1, rows), (features + 8, rows)] + [(features // 2, hubs + edges)] * 2
    return pl.pallas_call(
        functools.partial(bucket_kernel, bucket),
        in_specs=[SMEM] + [VMEM] * 9,
        out_specs=[VMEM] * 5,
        out_shape=[jax.ShapeDtypeStruct(shape, F32) for shape in shapes],
        scratch_shapes=[
            pltpu.VMEM((2 * features, rows), BF16),
            pltpu.VMEM((2 * features, width), BF16),
        ],
        compiler_params=PARAMS,
        cost_estimate=COST,
    )(core, heads, tails, negs, left, left_sums, right, right_sums, rel_rows, hub_rows)


def hub_kernel(
    bucket, negatives, core_ref, heads_ref, left_ref, rel_ref, hub_ref,
    query_grad, hub_keep, hub_send,
    left_parts, hub_parts,
):
    features, rows = left_ref.shape
    half = features // 2
    edges, hubs = heads_ref.shape[1], hub_keep.shape[1]
    at = slice(bucket, bucket + 1)
    weight = 1.0 / (negatives + hubs)
    stack_into(left_parts, left_ref[...])
    stack_into(hub_parts, hub_ref[...])

    head_hot = onehot(0, rows, heads_ref[at])
    h = dot2(left_parts[...], head_hot, NN)
    q = split(turned(h, rel_ref[...], half))
    coef = split(weight * jax.nn.sigmoid(dot3((hub_parts[:features], hub_parts[features:]), q, TN)))
    query_grad[...] = dot3_stacked(hub_parts[...], coef, NN)
    hub_grad = dot3_stacked(stack(q), coef, NT)

    hub_keep[...], hub_send[...] = keep_and_send(core_ref[1], hub_grad[:half], hub_grad[half:])


def hub_step(bucket, negatives, core, heads, left, rel_rows, hub_rows):
    features, rows = left.shape
    edges, hubs = heads.shape[1], hub_rows.shape[1]
    shapes = [(features, edges)] + [(features // 2, hubs)] * 2
    return pl.pallas_call(
        functools.partial(hub_kernel, bucket, negatives),
        in_specs=[SMEM] + [VMEM] * 4,
        out_specs=[VMEM] * 3,
        out_shape=[jax.ShapeDtypeStruct(shape, F32) for shape in shapes],
        scratch_shapes=[
            pltpu.VMEM((2 * features, rows), BF16),
            pltpu.VMEM((2 * features, hubs), BF16),
        ],
        compiler_params=PARAMS,
        cost_estimate=COST,
    )(core, heads, left, rel_rows, hub_rows)


def tables_kernel(
    bucket, hubs, core_ref, heads_ref, tails_ref, negs_ref, query_grad,
    left_ref, left_sums_ref, right_ref, rel_ref,
    left_out, right_out, rel_keep, rel_send,
    left_parts, right_parts,
):
    features, rows = left_ref.shape
    half = features // 2
    edges = heads_ref.shape[1]
    at = slice(bucket, bucket + 1)
    core = core_ref[1]
    counts = table_counts(rows, negs_ref[at], 1.0 / (negs_ref.shape[1] + hubs))
    stack_into(left_parts, left_ref[...])
    stack_into(right_parts, right_ref[:features])

    tail_here = lax.broadcasted_iota(jnp.int32, (rows, edges), 0) == tails_ref[at]
    head_hot = onehot(0, rows, heads_ref[at])
    h = dot2(left_parts[...], head_hot, NN)
    r = rel_ref[...]
    q = split(turned(h, r, half))
    chance = jax.nn.sigmoid(dot3((right_parts[:features], right_parts[features:]), q, TN))
    coef = split(counts * chance + jnp.where(tail_here, chance - 1.0, 0.0))
    dq = dot3_stacked(right_parts[...], coef, NN) + query_grad[...]
    right_grad = dot3_stacked(stack(q), coef, NT)
    rel_keep[...], rel_send[...] = keep_and_send(core, *turned_back(dq, h, half))
    dh = jnp.concatenate(turned_back(dq, r, half), axis=0)
    left_grad = dot2(stack(split(dh)), head_hot, NT)

    left_out[...], unused = adagrad(left_ref[...], left_sums_ref[...], left_grad)
    right_out[...], unused = adagrad(right_ref[:features], right_ref[features : features + 1], right_grad)


def tables_step(bucket, hubs, core, heads, tails, negs, query_grad, left, left_sums, right, rel_rows):
    features, rows = left.shape
    edges = heads.shape[1]
    shapes = [(features, rows)] * 2 + [(features // 2, edges)] * 2
    return pl.pallas_call(
        functools.partial(tables_kernel, bucket, hubs),
        in_specs=[SMEM] + [VMEM] * 8,
        out_specs=[VMEM] * 4,
        out_shape=[jax.ShapeDtypeStruct(shape, F32) for shape in shapes],
        scratch_shapes=[pltpu.VMEM((2 * features, rows), BF16)] * 2,
        compiler_params=PARAMS,
        cost_estimate=COST,
    )(core, heads, tails, negs, query_grad, left, left_sums, right, rel_rows)


def from_behind(x, axis, by):
    size = lax.axis_size(axis)
    return lax.ppermute(x, axis, [(i, (i + by) % size) for i in range(size)])


def flipped(x, axis, bit):
    return lax.ppermute(x, axis, [(i, i ^ (1 << bit)) for i in range(lax.axis_size(axis))])


def flipped_by(x, axis, offset):
    return lax.ppermute(x, axis, [(i, i ^ offset) for i in range(lax.axis_size(axis))])


def other_core(x):
    return flipped(x, "blk", 0)


def across(x, place):
    sub_bits = lax.axis_size("sub").bit_length() - 1
    if place < sub_bits:
        return flipped(x, "sub", place)
    return flipped(x, "blk", place - sub_bits + 1)


def stream_orders(gathering):
    sub_bits = lax.axis_size("sub").bit_length() - 1
    bits = sub_bits + lax.axis_size("blk").bit_length() - 2
    x, y, z, far = sub_bits, sub_bits + 1, 0, 1
    rest = [p for p in range(bits) if p not in (x, y, z, far)]
    last = [y, far] if gathering else [far, y]
    return [[x, y, z, far] + rest, [y, z, x, far] + rest, [z, x, *last] + rest]


def plane_orders(sub_bits, bits):
    plane, depth = list(range(sub_bits, bits)), list(range(sub_bits - 1, -1, -1))
    return [plane + depth, plane[1:] + plane[:1] + depth]


def row_spans(rows, parts):
    ends = [-(-rows * (i + 1) // (8 * parts)) * 8 for i in range(parts - 1)] + [rows]
    return list(zip([0] + ends[:-1], ends))


def shards(
    left_emb, left_state, right_emb, right_state, relation_emb, relation_state, hub_emb, hub_state,
    heads, relations, tails, negatives, hub_ids,
):
    components, half_width, row_count = left_emb.shape
    features = components * half_width
    rel_count, hub_count = relation_emb.shape[2], hub_emb.shape[2]
    left = left_emb.reshape(features, row_count)
    right = right_emb.reshape(features, row_count)
    left_sums = left_state.reshape(1, row_count)
    right_sums = right_state.reshape(1, row_count)
    buckets, edges = heads.shape
    hubs = hub_ids.shape[1]

    orders, back_orders = stream_orders(False), stream_orders(True)
    streams, stages = len(orders), len(orders[0])
    chunks, depth = 1 << stages, lax.axis_size("sub")
    sub_bits = depth.bit_length() - 1
    planes = chunks // depth
    spans = row_spans(half_width, streams)
    rel_orders = plane_orders(sub_bits, stages)
    width, rel_width = hub_count // chunks, rel_count // chunks
    rel_height, entries = packed_map(half_width, rel_width, width)
    plane_spans = row_spans(rel_height, len(rel_orders))
    share = -(-(half_width + rel_height) // (8 * streams)) * 8
    ends = [share * (s + 1) - spans[s][1] for s in range(streams - 1)] + [rel_height]
    rel_spans = list(zip([0] + ends[:-1], ends))
    plane_pieces, joint_pieces = split_pieces(entries, plane_spans), split_pieces(entries, rel_spans)
    heights, rel_heights, plane_heights = [[high - low for low, high in x] for x in (spans, rel_spans, plane_spans)]
    joint_heights = [h + r for h, r in zip(heights, rel_heights)]
    bases = [sum(joint_heights[:s]) for s in range(streams)]
    hub_lanes, rel_lanes = (0, hubs), (hubs, hubs + edges)

    def exchanged(parts, step, orders=orders):
        return [across(x, place) for x, (place, unused) in zip(parts, grouped(orders, step, heights)[0])]

    def in_turn(first, then):
        return lax.optimization_barrier((first, then))

    blk = lax.axis_index("blk")
    spot = jnp.stack([(blk >> 1) * depth + lax.axis_index("sub"), blk & 1]).astype(jnp.int32)
    far_ids = other_core((hub_ids, relations))
    hub_rows, rel_rows, spot, owned = gather_rows(
        spot, hub_emb.reshape(features, hub_count), hub_ids, relation_emb.reshape(features, rel_count), relations, chunks
    )
    far_ids, hub_rows = in_turn(far_ids, hub_rows)
    keeps, sends = [], []
    for b in range(buckets - 1):
        if b > 0:
            right, right_sums = right[:features], right[features : features + 1]
        left, left_sums, right, keep, send = bucket_step(
            b, spot, heads, tails, negatives, left, left_sums, right, right_sums, rel_rows[b], hub_rows[b]
        )
        right = from_behind(right, "blk", 1)
        keeps.append(keep)
        sends.append(send)
    last = buckets - 1
    query_grad, hub_keep, hub_send = hub_step(
        last, negatives.shape[1], spot, heads, left, rel_rows[last], hub_rows[last]
    )
    sends, hub_send = in_turn(sends, hub_send)
    hub_far = other_core(hub_send)
    fars = [other_core(x) for x in sends]
    grads = lambda early, late, lanes: [(x, lanes) for x in early] + [(late, (0, late.shape[1]))]
    groups, where = grouped(orders, 0, heights)
    parts = chunk_columns(
        functools.partial(hub_chunks_kernel, orders, spans, where),
        [(chunks // 2, height, width) for height in [h for unused, h in groups] + heights],
        spot, (hub_ids, far_ids[0]), grads(keeps, hub_keep, hub_lanes) + grads(fars, hub_far, hub_lanes),
    )
    send, own = parts[: len(groups)], parts[len(groups) :]
    got = exchanged(send, 0)
    left, right, rel_keep, rel_send = tables_step(
        last, hubs, spot, heads, tails, negatives, query_grad, left, left_sums, right, rel_rows[last]
    )
    rel_far = other_core(rel_send)

    parts = chunk_columns(
        functools.partial(rel_chunks_kernel, rel_orders, plane_pieces, rel_count),
        [(chunks // 2, height, width) for height in plane_heights * 2],
        spot, (relations, far_ids[1]), grads(keeps, rel_keep, rel_lanes) + grads(fars, rel_far, rel_lanes),
    )
    rel_send, rel_own = parts[: len(rel_orders)], parts[len(rel_orders) :]
    rel_got = [across(x, order[0]) for x, order in zip(rel_send, rel_orders)]
    plane_steps = stages - sub_bits
    for step in range(stages - 2):
        if 0 < step < plane_steps:
            own, rel_got = in_turn(own, rel_got)
            rel_send, rel_own = halves(rel_own, rel_got, rel_orders, step - 1)
            rel_got = [across(x, order[step]) for x, order in zip(rel_send, rel_orders)]
        rel_own, got = in_turn(rel_own, got)
        send, own = halves(own, got, orders, step)
        got = exchanged(send, step + 1)

    here = grouped(orders, stages - 2, heights)[1]
    groups, there = grouped(orders, stages - 1, heights)
    parts = call(
        functools.partial(last_sums_kernel, heights, here, there, plane_spans),
        [*own, *got, *rel_own, *rel_got],
        [(1, height, width) for height in [h for unused, h in groups] + heights + [rel_height] * depth],
    )
    send, own, rel_parts = parts[: len(groups)], parts[len(groups) : len(groups) + streams], parts[len(groups) + streams :]
    got = exchanged(send, stages - 1)
    rel_got = [flipped_by(x, "sub", q + 1) for q, x in enumerate(rel_parts[1:])]
    *totals, rel_total, squares = call(
        functools.partial(squares_kernel, heights, there, entries),
        [*own, *got, rel_parts[0], *rel_got], [x.shape for x in own] + [rel_parts[0].shape, (2, width)],
    )
    hub_own, rel_own = owned
    groups, there = grouped(back_orders, stages - 1, joint_heights)
    ins = [
        *totals, rel_total, squares, other_core(squares),
        hub_own, hub_state[None], rel_own, relation_state[None],
    ]
    have = pl.pallas_call(
        functools.partial(update_kernel, spans, rel_spans, joint_pieces, there, features),
        in_specs=[SMEM] + [VMEM] * len(ins),
        out_specs=[VMEM] * len(groups),
        out_shape=[jax.ShapeDtypeStruct((1, height, width), F32) for unused, height in groups],
        scratch_shapes=[pltpu.VMEM((1, x.shape[1]), F32) for x in owned],
        compiler_params=PARAMS,
        cost_estimate=COST,
    )(spot, *ins)
    for step in range(stages - 1, 1, -1):
        have = join(have, exchanged(have, step, back_orders), back_orders, step, joint_heights)
    have, near = join_all(have, exchanged(have, 1, back_orders), back_orders, 1, joint_heights)
    got = exchanged(have, 0, back_orders)
    far_near = other_core(near)

    shapes = [hub_emb.shape, relation_emb.shape]
    by_copy = width % 128 == 0
    hub_new = []
    if by_copy:
        near_step = functools.partial(near_kernel, back_orders, spans, bases)
        hub_new = placed(functools.partial(near_step, True), [], spot, near, [], shapes[:1], [])
        hub_new = placed(functools.partial(near_step, False), [], spot, far_near, [], shapes[:1], hub_new)
        got, hub_new = in_turn(got, hub_new)
    far_step = functools.partial(far_kernel, back_orders, spans, bases, joint_pieces, by_copy)
    scratch = [
        pltpu.VMEM((8, 128) if by_copy else (half_width, hub_count), F32),
        pltpu.VMEM((half_width, rel_count), F32),
    ]
    far_got = other_core(got)
    out = placed(functools.partial(far_step, True), scratch, spot, near, got, shapes, hub_new)
    hub_new, rel_new = placed(functools.partial(far_step, False), scratch, spot, far_near, far_got, shapes, out)
    return (
        left.reshape(components, half_width, row_count),
        right.reshape(components, half_width, row_count),
        rel_new,
        hub_new,
    )


def solution(mesh):
    both = ("blk", "sub")
    block, table, whole = P(None, None, both), P(None, both), P()
    return jax.shard_map(
        shards,
        mesh=mesh,
        in_specs=(block, P(both), block, P(both), whole, whole, whole, whole, table, table, table, table, table),
        out_specs=(block, block, whole, whole),
        check_vma=False,
    )
```

```python
import functools
import jax
import jax.numpy as jnp
from jax import lax
from jax.experimental import pallas as pl
from jax.experimental.pallas import tpu as pltpu
from jax.sharding import PartitionSpec as P

step_rate = 0.25
F32, BF16 = jnp.float32, jnp.bfloat16
NN = (((1,), (0,)), ((), ()))
NT = (((1,), (1,)), ((), ()))
TN = (((0,), (0,)), ((), ()))
VMEM = pl.BlockSpec(memory_space=pltpu.VMEM)
SMEM = pl.BlockSpec(memory_space=pltpu.SMEM)
PARAMS = pltpu.CompilerParams(vmem_limit_bytes=12 * 1024 * 1024)
GATHER_PARAMS = pltpu.CompilerParams(vmem_limit_bytes=50 * 1024 * 1024)
HBM = pl.BlockSpec(memory_space=pltpu.HBM)
COST = pl.CostEstimate(flops=10000, bytes_accessed=10000, transcendentals=0)


def split(x):
    hi = x.astype(BF16)
    return hi, (x - hi.astype(F32)).astype(BF16)


def dot(a, b, dims):
    return lax.dot_general(a, b, dims, preferred_element_type=F32)


def dot3(a, b, dims):
    return dot(a[0], b[0], dims) + (dot(a[0], b[1], dims) + dot(a[1], b[0], dims))


def dot2(stacked, onehot, dims):
    half = stacked.shape[0] // 2
    both = dot(stacked, onehot, dims)
    return both[:half] + both[half:]


def stack(parts):
    return jnp.concatenate(parts, axis=0)


def stack_into(ref, x, lanes=slice(None)):
    rows, half = x.shape[0], ref.shape[0] // 2
    hi, lo = split(x)
    ref[:rows, lanes] = hi
    ref[half : half + rows, lanes] = lo
    if half > rows:
        blank = jnp.zeros((half - rows, x.shape[1]), BF16)
        ref[rows:half, lanes] = blank
        ref[half + rows :, lanes] = blank


def dot3_stacked(stacked, b, dims):
    half = stacked.shape[0] // 2
    both = dot(stacked, b[0], dims)
    return both[:half] + (both[half:] + dot(stacked[:half], b[1], dims))


def hot_where(here):
    return jnp.where(here, jnp.ones((), BF16), jnp.zeros((), BF16))


def onehot(first, rows, idx):
    place = lax.broadcasted_iota(jnp.int16, (rows, idx.shape[1]), 0)
    return hot_where(place == (idx - first).astype(jnp.int16))


def laid_out(idx):
    return jnp.concatenate([idx[b : b + 1] for b in range(idx.shape[0])], axis=1)


def take_owned(spot_ref, chunks, span, first, piece_of, out_ref):
    width = out_ref.shape[1]
    for chunk in range(chunks):
        if first <= chunk * width < first + span:

            @pl.when(spot_ref[0] == chunk)
            def _():
                out_ref[...] = piece_of(slice(chunk * width - first, (chunk + 1) * width - first))


def gather_kernel(hub_steps, rel_steps, spot_ref, hub_ids, rel_ids, hub_ref, rel_ref, *refs):
    buckets = hub_ids.shape[0]
    hub_outs, rel_outs = refs[:buckets], refs[buckets : 2 * buckets]
    spot_out, hub_own, rel_own = refs[2 * buckets : 2 * buckets + 3]
    hub_buf, rel_buf, hub_idx, rel_idx, stacked, sems = refs[2 * buckets + 3 :]
    hub_tile, rel_tile = hub_buf.shape[2], rel_buf.shape[2]
    chunks = hub_ref.shape[1] // hub_own.shape[1]
    half = hub_own.shape[0]
    steps = [(hub_ref, hub_buf, hub_tile, k) for k in range(hub_steps)]
    steps += [(rel_ref, rel_buf, rel_tile, k) for k in range(rel_steps)]
    copies = [
        pltpu.make_async_copy(table.at[:, pl.ds(k * tile, tile)], buf.at[k % 2], sems.at[i])
        for i, (table, buf, tile, k) in enumerate(steps)
    ]
    id_copies = [
        pltpu.make_async_copy(ids, out, sems.at[len(copies) + i])
        for i, (ids, out) in enumerate([(hub_ids, hub_idx), (rel_ids, rel_idx)])
    ]
    for copy in [*id_copies, copies[0]]:
        copy.start()
    spot_out[0] = spot_ref[0]
    spot_out[1] = spot_ref[1]
    for copy in id_copies:
        copy.wait()
    rows = pl.ds(pl.multiple_of(spot_ref[1] * half, 8), half)
    for i, (table, buf, tile, k) in enumerate(steps):
        if i + 1 < len(steps):
            copies[i + 1].start()
        idx, outs, own = (hub_idx, hub_outs, hub_own) if table is hub_ref else (rel_idx, rel_outs, rel_own)
        count = idx.shape[1]
        hot = onehot(k * tile, tile, laid_out(idx[...]))
        copies[i].wait()
        stack_into(stacked, buf[k % 2], slice(0, tile))
        part = dot2(stacked[:, :tile], hot, NN)
        for b, out in enumerate(outs):
            here = part[:, b * count : (b + 1) * count]
            out[...] = here if k == 0 else out[...] + here
        take_owned(spot_ref, chunks, tile, k * tile, lambda lanes: buf[k % 2, rows, lanes], own)


def gather_rows(spot, hub_table, hub_idx, rel_table, rel_idx, chunks):
    features = hub_table.shape[0]
    hub_steps, rel_steps = 4, 2
    hub_tile, rel_tile = hub_table.shape[1] // hub_steps, rel_table.shape[1] // rel_steps
    buckets, hubs = hub_idx.shape
    edges = rel_idx.shape[1]
    hub_width, rel_width = hub_table.shape[1] // chunks, rel_table.shape[1] // chunks
    shapes = [(features, hubs)] * buckets + [(features, edges)] * buckets
    own_shapes = [(features // 2, hub_width), (features // 2, rel_width)]
    floats = lambda shapes: [jax.ShapeDtypeStruct(shape, F32) for shape in shapes]
    out = pl.pallas_call(
        functools.partial(gather_kernel, hub_steps, rel_steps),
        in_specs=[SMEM] + [HBM] * 4,
        out_specs=[VMEM] * len(shapes) + [SMEM] + [VMEM] * len(own_shapes),
        out_shape=floats(shapes) + [jax.ShapeDtypeStruct((2,), jnp.int32)] + floats(own_shapes),
        scratch_shapes=[
            pltpu.VMEM((2, features, hub_tile), F32),
            pltpu.VMEM((2, features, rel_tile), F32),
            pltpu.VMEM(hub_idx.shape, jnp.int32),
            pltpu.VMEM(rel_idx.shape, jnp.int32),
            pltpu.VMEM((2 * features, max(hub_tile, rel_tile)), BF16),
            pltpu.SemaphoreType.DMA((hub_steps + rel_steps + 2,)),
        ],
        compiler_params=GATHER_PARAMS,
        cost_estimate=COST,
    )(spot, hub_idx, rel_idx, hub_table, rel_table)
    return out[:buckets], out[buckets : 2 * buckets], out[2 * buckets], out[2 * buckets + 1 :]


def spread_bits(place, order):
    bits = len(order)
    return sum((((place >> p) & 1) << (bits - 1 - i)) for i, p in enumerate(order))


def gather_bits(index, order):
    bits = len(order)
    return sum((((index >> (bits - 1 - i)) & 1) << p) for i, p in enumerate(order))


def load_columns(id_refs, grad_refs, idx_down, stacked):
    idx = jnp.concatenate([laid_out(ref[...]) for ref in id_refs], axis=1)
    idx_down[...] = jnp.transpose(jnp.broadcast_to(idx, (128, idx.shape[1]))).astype(jnp.int16)
    at = 0
    for ref, (low, high) in grad_refs:
        width = high - low
        stack_into(stacked, ref[:, low:high], slice(at, at + width))
        at += width


def onehot_across(idx_down, targets):
    width = targets.shape[1]
    idx = idx_down[...]
    wide = jnp.concatenate([idx] * -(-width // 128), axis=1)[:, :width]
    return hot_where(wide == targets.astype(jnp.int16))


def grouped(orders, step, heights):
    groups, where = [], []
    for s, order in enumerate(orders):
        for g, (place, members) in enumerate(groups):
            if place == order[step]:
                where.append((g, sum(heights[m] for m in members)))
                members.append(s)
                break
        else:
            where.append((len(groups), 0))
            groups.append((order[step], [s]))
    return [(place, sum(heights[m] for m in members)) for place, members in groups], where


def rows_of(where, heights, s):
    group, base = where[s]
    return group, slice(base, base + heights[s])


def put_chunk(place, orders, heights, where, sends, keeps, s, value):
    index, half = spread_bits(place, orders[s]), keeps[s].shape[0]
    if index < half:
        keeps[s][index] = value
    else:
        group, rows = rows_of(where, heights, s)
        sends[group][index - half, rows] = value


def chunk_refs(grad_lanes, refs):
    ids, refs = refs[:2], refs[2:]
    grads, refs = list(zip(refs, grad_lanes)), refs[len(grad_lanes) :]
    return ids, grads, refs[:-2], refs[-2:]


def hub_chunks_kernel(orders, spans, where, grad_lanes, spot_ref, *refs):
    ids, grads, outs, (idx_down, stacked) = chunk_refs(grad_lanes, refs)
    load_columns(ids, grads, idx_down, stacked)
    streams = len(orders)
    sends, keeps = outs[:-streams], outs[-streams:]
    heights = [high - low for low, high in spans]
    chunks, width = 2 * keeps[0].shape[0], keeps[0].shape[2]
    lane = lax.broadcasted_iota(jnp.int32, (1, width), 1)
    for place in range(chunks):
        hot = onehot_across(idx_down, lane + (spot_ref[0] ^ place) * width)
        chunk = dot2(stacked[...], hot, NN)
        for s, (low, high) in enumerate(spans):
            put_chunk(place, orders, heights, where, sends, keeps, s, chunk[low:high])


def packed_map(half_width, width, lanes):
    rows = half_width // 24 * 8
    gap, extra = lanes - 3 * width, half_width - 3 * rows
    entries = [(rows * b, 0, width, 0, b * width, rows) for b in range(3)]
    for i in range(-(-width // gap)):
        entries.append((3 * rows, i * gap, min(gap, width - i * gap), extra * i, 3 * width, extra))
    return rows, entries


def split_pieces(entries, spans):
    pieces = []
    for row, lane, lanes, to, to_lane, count in entries:
        for s, (first, end) in enumerate(spans):
            low, high = max(to, first), min(to + count, end)
            if low < high:
                pieces.append((s, row + low - to, high - low, lane, lanes, low - first, to_lane))
    return pieces


def rel_chunks_kernel(orders, pieces, rows, grad_lanes, spot_ref, *refs):
    ids, grads, outs, (idx_down, stacked) = chunk_refs(grad_lanes, refs)
    load_columns(ids, grads, idx_down, stacked)
    for ref in outs:
        ref[...] = jnp.zeros_like(ref)
    streams = len(orders)
    sends, keeps = outs[:streams], outs[streams:]
    half, lanes = keeps[0].shape[0], keeps[0].shape[2]
    chunks = 2 * half
    width = rows // chunks
    group = lanes // width
    lane = lax.broadcasted_iota(jnp.int32, (1, lanes), 1)
    for first in range(0, chunks, group):
        targets = jnp.full((1, lanes), -1, jnp.int32)
        places = range(first, min(first + group, chunks))
        for slot, place in enumerate(places):
            here = (lane >= slot * width) & (lane < (slot + 1) * width)
            targets = jnp.where(here, lane + ((spot_ref[0] ^ place) * width - slot * width), targets)
        dense = dot2(stacked[...], onehot_across(idx_down, targets), NN)
        for slot, place in enumerate(places):
            chunk = dense[:, slot * width : (slot + 1) * width]
            for s, row, count, low, wide, to, to_lane in pieces:
                index = spread_bits(place, orders[s])
                out = sends[s].at[index - half] if index >= half else keeps[s].at[index]
                out[to : to + count, to_lane : to_lane + wide] = chunk[row : row + count, low : low + wide]


def chunk_columns(kernel, shapes, spot, ids, grads):
    half_width = grads[0][0].shape[0]
    grad_lanes = [lanes_of for unused, lanes_of in grads]
    count = sum(high - low for low, high in grad_lanes)
    return pl.pallas_call(
        functools.partial(kernel, grad_lanes),
        in_specs=[SMEM] + [VMEM] * (2 + len(grads)),
        out_specs=[VMEM] * len(shapes),
        out_shape=[jax.ShapeDtypeStruct(shape, F32) for shape in shapes],
        scratch_shapes=[
            pltpu.VMEM((count, 128), jnp.int16),
            pltpu.VMEM((2 * (-(-half_width // 16) * 16), count), BF16),
        ],
        compiler_params=PARAMS,
        cost_estimate=COST,
    )(spot, *ids, *[g for g, unused in grads])


def call(kernel, ins, shapes):
    return pl.pallas_call(
        kernel,
        in_specs=[VMEM] * len(ins),
        out_specs=[VMEM] * len(shapes),
        out_shape=[jax.ShapeDtypeStruct(shape, F32) for shape in shapes],
        compiler_params=PARAMS,
        cost_estimate=COST,
    )(*ins)


def sums_kernel(heights, here, there, *refs):
    streams, groups = len(heights), 1 + max(g for g, unused in here)
    own, got, sends, keeps = refs[:streams], refs[streams : streams + groups], refs[streams + groups : -streams], refs[-streams:]
    for s in range(streams):
        half = keeps[s].shape[0]
        group, rows = rows_of(here, heights, s)
        out, out_rows = rows_of(there, heights, s)
        sends[out][:, out_rows] = own[s][half:] + got[group][half:, rows]
        keeps[s][...] = own[s][:half] + got[group][:half, rows]


def halves(own, got, orders, step):
    heights = [x.shape[1] for x in own]
    half, width = own[0].shape[0] // 2, own[0].shape[2]
    unused, here = grouped(orders, step, heights)
    groups, there = grouped(orders, step + 1, heights)
    shapes = [(half, height, width) for height in [h for unused, h in groups] + heights]
    out = call(functools.partial(sums_kernel, heights, here, there), [*own, *got], shapes)
    return out[: len(groups)], out[len(groups) :]


def split_kernel(bases, *refs):
    streams = len(bases)
    for got, base, out in zip(refs[:streams], bases, refs[streams:]):
        out[...] = got[:, base : base + out.shape[1]]


def extend_kernel(bases, *refs):
    streams = len(bases)
    held, owned, got, outs = [refs[i * streams : (i + 1) * streams] for i in range(4)]
    for s, base in enumerate(bases):
        count, height = held[s].shape[0], held[s].shape[1]
        outs[s][:count] = held[s][...]
        outs[s][count] = owned[s][0, base : base + height]
        outs[s][count + 1 :] = got[s][...]


def near_chunks_kernel(bases, *refs):
    streams = len(bases)
    new, held, owned, out = refs[0], refs[1 : streams + 1], refs[streams + 1 : -1], refs[-1]
    out[0] = new[0]
    for s, base in enumerate(bases):
        count, height = held[s].shape[0], held[s].shape[1]
        out[1 : count + 1, base : base + height] = held[s][...]
        out[count + 1, base : base + height] = owned[s][0, base : base + height]


def last_sums_kernel(heights, here, there, spans, *refs):
    streams, planes = len(heights), len(spans)
    groups, out_groups = [1 + max(g for g, unused in where) for where in (here, there)]
    rels, outs = refs[streams + groups : streams + groups + 2 * planes], refs[streams + groups + 2 * planes :]
    sums_kernel(heights, here, there, *refs[: streams + groups], *outs[: out_groups + streams])
    for place, out in enumerate(outs[out_groups + streams :]):
        for s, (low, high) in enumerate(spans):
            out[0, low:high] = rels[s][place] + rels[planes + s][place]


def squares_kernel(heights, here, entries, *refs):
    streams, groups = len(heights), 1 + max(g for g, unused in here)
    own, got, rels = refs[:streams], refs[streams : streams + groups], refs[streams + groups : -streams - 2]
    totals, rel_total, out = refs[-streams - 2 : -2], refs[-2], refs[-1]
    squares = jnp.zeros((1, out.shape[1]), F32)
    for s in range(streams):
        group, rows = rows_of(here, heights, s)
        total = own[s][0] + got[group][0, rows]
        totals[s][0] = total
        squares += jnp.sum(total * total, axis=0, keepdims=True)
    total = sum(ref[0] for ref in rels)
    rel_total[0] = total
    out[0:1] = squares
    out[1:2] = jnp.zeros_like(squares)
    square = total * total
    for row, lane, lanes, to, to_lane, count in entries:
        part = jnp.sum(square[to : to + count, to_lane : to_lane + lanes], axis=0, keepdims=True)
        out[1:2, lane : lane + lanes] += part


def update_kernel(spans, rel_spans, pieces, there, features, spot_ref, *refs):
    streams, groups = len(spans), 1 + max(g for g, unused in there)
    totals, (hub_sums, rel_sums), news = refs[:streams], refs[-2:], refs[-groups - 2 : -2]
    rel_total, mine, other, hub_ref, hub_all, rel_ref, rel_all = refs[streams : -groups - 2]
    chunks = hub_all.shape[1] // hub_ref.shape[1]
    take_owned(spot_ref, chunks, hub_all.shape[1], 0, lambda lanes: hub_all[:, lanes], hub_sums)
    take_owned(spot_ref, chunks, rel_all.shape[1], 0, lambda lanes: rel_all[:, lanes], rel_sums)
    width = rel_ref.shape[1]
    squares = mine[...] + other[...]
    hub_scale = step_rate / jnp.sqrt(hub_sums[...] + squares[0:1] * (1.0 / features))
    rel_scale = step_rate / jnp.sqrt(rel_sums[...] + squares[1:2, :width] * (1.0 / features))
    for s, (low, high) in enumerate(spans):
        new, base = there[s]
        first, end = rel_spans[s]
        middle = base + high - low
        news[new][0, base:middle] = hub_ref[low:high] - totals[s][0] * hub_scale
        news[new][0, middle : middle + end - first] = jnp.zeros((end - first, news[new].shape[2]), F32)
    for s, row, count, low, wide, to, to_lane in pieces:
        new, base = there[s]
        base += spans[s][1] - spans[s][0] + to
        lanes, first = slice(to_lane, to_lane + wide), rel_spans[s][0] + to
        news[new][0, base : base + count, lanes] = (
            rel_ref[row : row + count, low : low + wide]
            - rel_total[0, first : first + count, lanes] * rel_scale[:, low : low + wide]
        )


def chunk_copies(part, base, first, order, span, chip, component, out_ref, sems, at):
    low, high = span
    width = part.shape[2]
    for index in range(part.shape[0]):
        chunk = chip ^ gather_bits(first + index, order)
        lanes = pl.ds(pl.multiple_of(chunk * width, width), width)
        target = out_ref.at[component, pl.ds(low, high - low), lanes]
        yield pltpu.make_async_copy(part.at[index, pl.ds(base, high - low)], target, sems.at[at + index])


def component_of(spot_ref, mine):
    return spot_ref[1] if mine else 1 - spot_ref[1]


def near_kernel(orders, spans, bases, mine, spot_ref, near_ref, *refs):
    component = component_of(spot_ref, mine)
    out_ref, sems = refs[-2:]
    copies = []
    for order, span, base in zip(orders, spans, bases):
        copies += chunk_copies(near_ref, base, 0, order, span, spot_ref[0], component, out_ref, sems, len(copies))
    for copy in copies:
        copy.start()
    for copy in copies:
        copy.wait()


def far_kernel(orders, spans, bases, pieces, by_copy, mine, spot_ref, near_ref, *refs):
    component = component_of(spot_ref, mine)
    streams = len(orders)
    fars = refs[:streams]
    hub_out, rel_out, hub_all, rel_all, sems = refs[-5:]
    known = near_ref.shape[0]
    chunks = known + fars[0].shape[0]
    hub_width, rel_width = hub_out.shape[2] // chunks, rel_out.shape[2] // chunks
    copies = []
    if by_copy:
        for far, order, span in zip(fars, orders, spans):
            copies += chunk_copies(far, 0, known, order, span, spot_ref[0], component, hub_out, sems, len(copies))
        for copy in copies:
            copy.start()
    for chunk in range(chunks):
        place = spot_ref[0] ^ chunk
        for s, (low, high) in enumerate(spans):
            index = spread_bits(place, orders[s])
            near_at, far_at = jnp.minimum(index, known - 1), jnp.maximum(index - known, 0)
            height, base, end = high - low, bases[s], fars[s].shape[1]
            if not by_copy:
                value = jnp.where(index >= known, fars[s][far_at, :height], near_ref[near_at, base : base + height])
                hub_all[low:high, chunk * hub_width : (chunk + 1) * hub_width] = value
            value = jnp.where(index >= known, fars[s][far_at, height:], near_ref[near_at, base + height : base + end])
            for stream, row, count, low, wide, to, to_lane in pieces:
                if stream == s:
                    at = chunk * rel_width + low
                    rel_all[row : row + count, at : at + wide] = value[to : to + count, to_lane : to_lane + wide]
    copies.append(pltpu.make_async_copy(rel_all, rel_out.at[component], sems.at[len(copies)]))
    copies[-1].start()
    if not by_copy:
        copies.append(pltpu.make_async_copy(hub_all, hub_out.at[component], sems.at[len(copies)]))
        copies[-1].start()
    for copy in copies:
        copy.wait()


def placed(kernel, scratch, spot, near, fars, outs, earlier):
    sems = pltpu.SemaphoreType.DMA((3 * near.shape[0] + 2,))
    return pl.pallas_call(
        kernel,
        in_specs=[SMEM] + [VMEM] * (1 + len(fars)) + [HBM] * len(earlier),
        out_specs=[HBM] * len(outs),
        out_shape=[jax.ShapeDtypeStruct(shape, F32) for shape in outs],
        scratch_shapes=scratch + [sems],
        input_output_aliases={2 + len(fars) + i: i for i in range(len(earlier))},
        compiler_params=PARAMS,
        cost_estimate=pl.CostEstimate(flops=0, bytes_accessed=4 * outs[0][1] * outs[0][2], transcendentals=0),
    )(spot, near, *fars, *earlier)


def adagrad(table, state, grads):
    new_state = state + jnp.sum(grads * grads, axis=0, keepdims=True) * (1.0 / grads.shape[0])
    return table - grads * (step_rate / jnp.sqrt(new_state)), new_state


def keep_and_send(core, first, second):
    return jnp.where(core == 0, first, second), jnp.where(core == 0, second, first)


def table_counts(rows, negs, weight):
    place = lax.broadcasted_iota(jnp.int32, (rows, negs.shape[1]), 0)
    return jnp.sum(jnp.where(place == negs, weight, 0.0), axis=1, keepdims=True)


def turned(x, r, half):
    x0, x1, r0, r1 = x[:half], x[half:], r[:half], r[half:]
    return jnp.concatenate([x0 * r0 - x1 * r1, x0 * r1 + x1 * r0], axis=0)


def turned_back(x, r, half):
    x0, x1, r0, r1 = x[:half], x[half:], r[:half], r[half:]
    return x0 * r0 + x1 * r1, x1 * r0 - x0 * r1


EDGE_TILE = 512


def bucket_kernel(
    bucket, core_ref, heads_ref, tails_ref, negs_ref, left_ref, left_sums_ref, right_ref, right_sums_ref, rel_ref, hub_ref,
    left_out, left_sums_out, right_out, keep_out, send_out,
    left_parts, both_parts,
):
    features, rows = left_ref.shape
    half = features // 2
    core = core_ref[1]
    edges = heads_ref.shape[1]
    hubs = keep_out.shape[1] - edges
    at = slice(bucket, bucket + 1)
    weight = 1.0 / (negs_ref.shape[1] + hubs)
    counts = table_counts(rows, negs_ref[at], weight)
    stack_into(left_parts, left_ref[...])
    stack_into(both_parts, right_ref[...], slice(0, rows))
    stack_into(both_parts, hub_ref[...], slice(rows, rows + hubs))

    tail_here = lax.broadcasted_iota(jnp.int32, (rows, edges), 0) == tails_ref[at]
    head_hot = onehot(0, rows, heads_ref[at])
    h = dot2(left_parts[...], head_hot, NN)
    r = rel_ref[...]
    q = split(turned(h, r, half))
    scores = dot3((both_parts[:features], both_parts[features:]), q, TN)
    chance = jax.nn.sigmoid(scores[:rows])
    coef = jnp.concatenate(
        [
            counts * chance + jnp.where(tail_here, chance - 1.0, 0.0),
            weight * jax.nn.sigmoid(scores[rows:]),
        ],
        axis=0,
    )
    coef = split(coef)
    dq = dot3_stacked(both_parts[...], coef, NN)
    both_grad = dot3_stacked(stack(q), coef, NT)
    dh = jnp.concatenate(turned_back(dq, r, half), axis=0)
    left_grad = dot2(stack(split(dh)), head_hot, NT)
    keep_out[:, hubs:], send_out[:, hubs:] = keep_and_send(core, *turned_back(dq, h, half))

    left_out[...], left_sums_out[...] = adagrad(left_ref[...], left_sums_ref[...], left_grad)
    new_right, new_sums = adagrad(right_ref[...], right_sums_ref[...], both_grad[:, :rows])
    right_out[:features] = new_right
    right_out[features:] = jnp.broadcast_to(new_sums, (right_out.shape[0] - features, rows))
    keep_out[:, :hubs], send_out[:, :hubs] = keep_and_send(core, both_grad[:half, rows:], both_grad[half:, rows:])


def bucket_step(bucket, core, heads, tails, negs, left, left_sums, right, right_sums, rel_rows, hub_rows):
    features, rows = left.shape
    edges, hubs = heads.shape[1], hub_rows.shape[1]
    width = rows + hubs
    shapes = [(features, rows), (1, rows), (features + 8, rows)] + [(features // 2, hubs + edges)] * 2
    return pl.pallas_call(
        functools.partial(bucket_kernel, bucket),
        in_specs=[SMEM] + [VMEM] * 9,
        out_specs=[VMEM] * 5,
        out_shape=[jax.ShapeDtypeStruct(shape, F32) for shape in shapes],
        scratch_shapes=[
            pltpu.VMEM((2 * features, rows), BF16),
            pltpu.VMEM((2 * features, width), BF16),
        ],
        compiler_params=PARAMS,
        cost_estimate=COST,
    )(core, heads, tails, negs, left, left_sums, right, right_sums, rel_rows, hub_rows)


def hub_kernel(
    bucket, negatives, core_ref, heads_ref, left_ref, rel_ref, hub_ref,
    query_grad, hub_keep, hub_send,
    left_parts, hub_parts,
):
    features, rows = left_ref.shape
    half = features // 2
    edges, hubs = heads_ref.shape[1], hub_keep.shape[1]
    at = slice(bucket, bucket + 1)
    weight = 1.0 / (negatives + hubs)
    stack_into(left_parts, left_ref[...])
    stack_into(hub_parts, hub_ref[...])

    head_hot = onehot(0, rows, heads_ref[at])
    h = dot2(left_parts[...], head_hot, NN)
    q = split(turned(h, rel_ref[...], half))
    coef = split(weight * jax.nn.sigmoid(dot3((hub_parts[:features], hub_parts[features:]), q, TN)))
    query_grad[...] = dot3_stacked(hub_parts[...], coef, NN)
    hub_grad = dot3_stacked(stack(q), coef, NT)

    hub_keep[...], hub_send[...] = keep_and_send(core_ref[1], hub_grad[:half], hub_grad[half:])


def hub_step(bucket, negatives, core, heads, left, rel_rows, hub_rows):
    features, rows = left.shape
    edges, hubs = heads.shape[1], hub_rows.shape[1]
    shapes = [(features, edges)] + [(features // 2, hubs)] * 2
    return pl.pallas_call(
        functools.partial(hub_kernel, bucket, negatives),
        in_specs=[SMEM] + [VMEM] * 4,
        out_specs=[VMEM] * 3,
        out_shape=[jax.ShapeDtypeStruct(shape, F32) for shape in shapes],
        scratch_shapes=[
            pltpu.VMEM((2 * features, rows), BF16),
            pltpu.VMEM((2 * features, hubs), BF16),
        ],
        compiler_params=PARAMS,
        cost_estimate=COST,
    )(core, heads, left, rel_rows, hub_rows)


def tables_kernel(
    bucket, hubs, core_ref, heads_ref, tails_ref, negs_ref, query_grad,
    left_ref, left_sums_ref, right_ref, rel_ref,
    left_out, right_out, rel_keep, rel_send,
    left_parts, right_parts,
):
    features, rows = left_ref.shape
    half = features // 2
    edges = heads_ref.shape[1]
    at = slice(bucket, bucket + 1)
    core = core_ref[1]
    counts = table_counts(rows, negs_ref[at], 1.0 / (negs_ref.shape[1] + hubs))
    stack_into(left_parts, left_ref[...])
    stack_into(right_parts, right_ref[:features])

    tail_here = lax.broadcasted_iota(jnp.int32, (rows, edges), 0) == tails_ref[at]
    head_hot = onehot(0, rows, heads_ref[at])
    h = dot2(left_parts[...], head_hot, NN)
    r = rel_ref[...]
    q = split(turned(h, r, half))
    chance = jax.nn.sigmoid(dot3((right_parts[:features], right_parts[features:]), q, TN))
    coef = split(counts * chance + jnp.where(tail_here, chance - 1.0, 0.0))
    dq = dot3_stacked(right_parts[...], coef, NN) + query_grad[...]
    right_grad = dot3_stacked(stack(q), coef, NT)
    rel_keep[...], rel_send[...] = keep_and_send(core, *turned_back(dq, h, half))
    dh = jnp.concatenate(turned_back(dq, r, half), axis=0)
    left_grad = dot2(stack(split(dh)), head_hot, NT)

    left_out[...], unused = adagrad(left_ref[...], left_sums_ref[...], left_grad)
    right_out[...], unused = adagrad(right_ref[:features], right_ref[features : features + 1], right_grad)


def tables_step(bucket, hubs, core, heads, tails, negs, query_grad, left, left_sums, right, rel_rows):
    features, rows = left.shape
    edges = heads.shape[1]
    shapes = [(features, rows)] * 2 + [(features // 2, edges)] * 2
    return pl.pallas_call(
        functools.partial(tables_kernel, bucket, hubs),
        in_specs=[SMEM] + [VMEM] * 8,
        out_specs=[VMEM] * 4,
        out_shape=[jax.ShapeDtypeStruct(shape, F32) for shape in shapes],
        scratch_shapes=[pltpu.VMEM((2 * features, rows), BF16)] * 2,
        compiler_params=PARAMS,
        cost_estimate=COST,
    )(core, heads, tails, negs, query_grad, left, left_sums, right, rel_rows)


def from_behind(x, axis, by):
    size = lax.axis_size(axis)
    return lax.ppermute(x, axis, [(i, (i + by) % size) for i in range(size)])


def flipped(x, axis, bit):
    return lax.ppermute(x, axis, [(i, i ^ (1 << bit)) for i in range(lax.axis_size(axis))])


def flipped_by(x, axis, offset):
    return lax.ppermute(x, axis, [(i, i ^ offset) for i in range(lax.axis_size(axis))])


def other_core(x):
    return flipped(x, "blk", 0)


def across(x, place):
    sub_bits = lax.axis_size("sub").bit_length() - 1
    if place < sub_bits:
        return flipped(x, "sub", place)
    return flipped(x, "blk", place - sub_bits + 1)


def stream_orders(gathering):
    sub_bits = lax.axis_size("sub").bit_length() - 1
    bits = sub_bits + lax.axis_size("blk").bit_length() - 2
    x, y, z, far = sub_bits, sub_bits + 1, 0, 1
    rest = [p for p in range(bits) if p not in (x, y, z, far)]
    last = [y, far] if gathering else [far, y]
    return [[x, y, z, far] + rest, [y, z, x, far] + rest, [z, x, *last] + rest]


def plane_orders(sub_bits, bits):
    plane, depth = list(range(sub_bits, bits)), list(range(sub_bits - 1, -1, -1))
    return [plane + depth, plane[1:] + plane[:1] + depth]


def row_spans(rows, parts):
    ends = [-(-rows * (i + 1) // (8 * parts)) * 8 for i in range(parts - 1)] + [rows]
    return list(zip([0] + ends[:-1], ends))


def shards(
    left_emb, left_state, right_emb, right_state, relation_emb, relation_state, hub_emb, hub_state,
    heads, relations, tails, negatives, hub_ids,
):
    components, half_width, row_count = left_emb.shape
    features = components * half_width
    rel_count, hub_count = relation_emb.shape[2], hub_emb.shape[2]
    left = left_emb.reshape(features, row_count)
    right = right_emb.reshape(features, row_count)
    left_sums = left_state.reshape(1, row_count)
    right_sums = right_state.reshape(1, row_count)
    buckets, edges = heads.shape
    hubs = hub_ids.shape[1]

    orders, back_orders = stream_orders(False), stream_orders(True)
    streams, stages = len(orders), len(orders[0])
    chunks, depth = 1 << stages, lax.axis_size("sub")
    sub_bits = depth.bit_length() - 1
    planes = chunks // depth
    spans = row_spans(half_width, streams)
    rel_orders = plane_orders(sub_bits, stages)
    width, rel_width = hub_count // chunks, rel_count // chunks
    rel_height, entries = packed_map(half_width, rel_width, width)
    plane_spans = row_spans(rel_height, len(rel_orders))
    share = -(-(half_width + rel_height) // (8 * streams)) * 8
    ends = [share * (s + 1) - spans[s][1] for s in range(streams - 1)] + [rel_height]
    rel_spans = list(zip([0] + ends[:-1], ends))
    plane_pieces, joint_pieces = split_pieces(entries, plane_spans), split_pieces(entries, rel_spans)
    heights, rel_heights, plane_heights = [[high - low for low, high in x] for x in (spans, rel_spans, plane_spans)]
    joint_heights = [h + r for h, r in zip(heights, rel_heights)]
    bases = [sum(joint_heights[:s]) for s in range(streams)]
    hub_lanes, rel_lanes = (0, hubs), (hubs, hubs + edges)

    def exchanged(parts, step, orders=orders):
        return [across(x, place) for x, (place, unused) in zip(parts, grouped(orders, step, heights)[0])]

    def in_turn(first, then):
        return lax.optimization_barrier((first, then))

    blk = lax.axis_index("blk")
    spot = jnp.stack([(blk >> 1) * depth + lax.axis_index("sub"), blk & 1]).astype(jnp.int32)
    far_ids = other_core((hub_ids, relations))
    hub_rows, rel_rows, spot, owned = gather_rows(
        spot, hub_emb.reshape(features, hub_count), hub_ids, relation_emb.reshape(features, rel_count), relations, chunks
    )
    far_ids, hub_rows = in_turn(far_ids, hub_rows)
    keeps, sends = [], []
    for b in range(buckets - 1):
        if b > 0:
            right, right_sums = right[:features], right[features : features + 1]
        left, left_sums, right, keep, send = bucket_step(
            b, spot, heads, tails, negatives, left, left_sums, right, right_sums, rel_rows[b], hub_rows[b]
        )
        right = from_behind(right, "blk", 1)
        keeps.append(keep)
        sends.append(send)
    last = buckets - 1
    query_grad, hub_keep, hub_send = hub_step(
        last, negatives.shape[1], spot, heads, left, rel_rows[last], hub_rows[last]
    )
    sends, hub_send = in_turn(sends, hub_send)
    hub_far = other_core(hub_send)
    fars = [other_core(x) for x in sends]
    grads = lambda early, late, lanes: [(x, lanes) for x in early] + [(late, (0, late.shape[1]))]
    groups, where = grouped(orders, 0, heights)
    parts = chunk_columns(
        functools.partial(hub_chunks_kernel, orders, spans, where),
        [(chunks // 2, height, width) for height in [h for unused, h in groups] + heights],
        spot, (hub_ids, far_ids[0]), grads(keeps, hub_keep, hub_lanes) + grads(fars, hub_far, hub_lanes),
    )
    send, own = parts[: len(groups)], parts[len(groups) :]
    got = exchanged(send, 0)
    left, right, rel_keep, rel_send = tables_step(
        last, hubs, spot, heads, tails, negatives, query_grad, left, left_sums, right, rel_rows[last]
    )
    rel_far = other_core(rel_send)

    parts = chunk_columns(
        functools.partial(rel_chunks_kernel, rel_orders, plane_pieces, rel_count),
        [(chunks // 2, height, width) for height in plane_heights * 2],
        spot, (relations, far_ids[1]), grads(keeps, rel_keep, rel_lanes) + grads(fars, rel_far, rel_lanes),
    )
    rel_send, rel_own = parts[: len(rel_orders)], parts[len(rel_orders) :]
    rel_got = [across(x, order[0]) for x, order in zip(rel_send, rel_orders)]
    plane_steps = stages - sub_bits
    for step in range(stages - 2):
        if 0 < step < plane_steps:
            own, rel_got = in_turn(own, rel_got)
            rel_send, rel_own = halves(rel_own, rel_got, rel_orders, step - 1)
            rel_got = [across(x, order[step]) for x, order in zip(rel_send, rel_orders)]
        rel_own, got = in_turn(rel_own, got)
        send, own = halves(own, got, orders, step)
        got = exchanged(send, step + 1)

    here = grouped(orders, stages - 2, heights)[1]
    groups, there = grouped(orders, stages - 1, heights)
    parts = call(
        functools.partial(last_sums_kernel, heights, here, there, plane_spans),
        [*own, *got, *rel_own, *rel_got],
        [(1, height, width) for height in [h for unused, h in groups] + heights + [rel_height] * depth],
    )
    send, own, rel_parts = parts[: len(groups)], parts[len(groups) : len(groups) + streams], parts[len(groups) + streams :]
    got = exchanged(send, stages - 1)
    rel_got = [flipped_by(x, "sub", q + 1) for q, x in enumerate(rel_parts[1:])]
    *totals, rel_total, squares = call(
        functools.partial(squares_kernel, heights, there, entries),
        [*own, *got, rel_parts[0], *rel_got], [x.shape for x in own] + [rel_parts[0].shape, (2, width)],
    )
    hub_own, rel_own = owned
    there = [(0, base) for base in bases]
    ins = [
        *totals, rel_total, squares, other_core(squares),
        hub_own, hub_state[None], rel_own, relation_state[None],
    ]
    [new] = pl.pallas_call(
        functools.partial(update_kernel, spans, rel_spans, joint_pieces, there, features),
        in_specs=[SMEM] + [VMEM] * len(ins),
        out_specs=[VMEM],
        out_shape=[jax.ShapeDtypeStruct((1, sum(joint_heights), width), F32)],
        scratch_shapes=[pltpu.VMEM((1, x.shape[1]), F32) for x in owned],
        compiler_params=PARAMS,
        cost_estimate=COST,
    )(spot, *ins)
    partners = [across(new, place) for place in range(stages)]
    owned_at = lambda step: [partners[order[step]] for order in back_orders]
    shapes = lambda count: [(count, height, width) for height in joint_heights]
    have = call(functools.partial(split_kernel, bases), owned_at(stages - 1), shapes(1))
    for step in range(stages - 2, 0, -1):
        got = [across(x, order[step]) for x, order in zip(have, back_orders)]
        have = call(
            functools.partial(extend_kernel, bases), [*have, *owned_at(step), *got], shapes(2 * have[0].shape[0] + 1)
        )
    got = [across(x, order[0]) for x, order in zip(have, back_orders)]
    [near] = call(
        functools.partial(near_chunks_kernel, bases), [new, *have, *owned_at(0)],
        [(have[0].shape[0] + 2, sum(joint_heights), width)],
    )
    far_near = other_core(near)

    shapes = [hub_emb.shape, relation_emb.shape]
    by_copy = width % 128 == 0
    hub_new = []
    if by_copy:
        near_step = functools.partial(near_kernel, back_orders, spans, bases)
        hub_new = placed(functools.partial(near_step, True), [], spot, near, [], shapes[:1], [])
        hub_new = placed(functools.partial(near_step, False), [], spot, far_near, [], shapes[:1], hub_new)
        got, hub_new = in_turn(got, hub_new)
    far_step = functools.partial(far_kernel, back_orders, spans, bases, joint_pieces, by_copy)
    scratch = [
        pltpu.VMEM((8, 128) if by_copy else (half_width, hub_count), F32),
        pltpu.VMEM((half_width, rel_count), F32),
    ]
    far_got = other_core(got)
    out = placed(functools.partial(far_step, True), scratch, spot, near, got, shapes, hub_new)
    hub_new, rel_new = placed(functools.partial(far_step, False), scratch, spot, far_near, far_got, shapes, out)
    return (
        left.reshape(components, half_width, row_count),
        right.reshape(components, half_width, row_count),
        rel_new,
        hub_new,
    )


def solution(mesh):
    both = ("blk", "sub")
    block, table, whole = P(None, None, both), P(None, both), P()
    return jax.shard_map(
        shards,
        mesh=mesh,
        in_specs=(block, P(both), block, P(both), whole, whole, whole, whole, table, table, table, table, table),
        out_specs=(block, block, whole, whole),
        check_vma=False,
    )
```

```python
import functools
import jax
import jax.numpy as jnp
from jax import lax
from jax.experimental import pallas as pl
from jax.experimental.pallas import tpu as pltpu
from jax.sharding import PartitionSpec as P

step_rate = 0.25
F32, BF16 = jnp.float32, jnp.bfloat16
NN = (((1,), (0,)), ((), ()))
NT = (((1,), (1,)), ((), ()))
TN = (((0,), (0,)), ((), ()))
VMEM = pl.BlockSpec(memory_space=pltpu.VMEM)
SMEM = pl.BlockSpec(memory_space=pltpu.SMEM)
PARAMS = pltpu.CompilerParams(vmem_limit_bytes=12 * 1024 * 1024)
GATHER_PARAMS = pltpu.CompilerParams(vmem_limit_bytes=50 * 1024 * 1024)
HBM = pl.BlockSpec(memory_space=pltpu.HBM)
COST = pl.CostEstimate(flops=10000, bytes_accessed=10000, transcendentals=0)


def split(x):
    hi = x.astype(BF16)
    return hi, (x - hi.astype(F32)).astype(BF16)


def dot(a, b, dims):
    return lax.dot_general(a, b, dims, preferred_element_type=F32)


def dot3(a, b, dims):
    return dot(a[0], b[0], dims) + (dot(a[0], b[1], dims) + dot(a[1], b[0], dims))


def dot2(stacked, onehot, dims):
    half = stacked.shape[0] // 2
    both = dot(stacked, onehot, dims)
    return both[:half] + both[half:]


def stack(parts):
    return jnp.concatenate(parts, axis=0)


def stack_into(ref, x, lanes=slice(None)):
    rows, half = x.shape[0], ref.shape[0] // 2
    hi, lo = split(x)
    ref[:rows, lanes] = hi
    ref[half : half + rows, lanes] = lo
    if half > rows:
        blank = jnp.zeros((half - rows, x.shape[1]), BF16)
        ref[rows:half, lanes] = blank
        ref[half + rows :, lanes] = blank


def dot3_stacked(stacked, b, dims):
    half = stacked.shape[0] // 2
    both = dot(stacked, b[0], dims)
    return both[:half] + (both[half:] + dot(stacked[:half], b[1], dims))


def hot_where(here):
    return jnp.where(here, jnp.ones((), BF16), jnp.zeros((), BF16))


def onehot(first, rows, idx):
    place = lax.broadcasted_iota(jnp.int16, (rows, idx.shape[1]), 0)
    return hot_where(place == (idx - first).astype(jnp.int16))


def laid_out(idx):
    return jnp.concatenate([idx[b : b + 1] for b in range(idx.shape[0])], axis=1)


def take_owned(spot_ref, chunks, span, first, piece_of, out_ref):
    width = out_ref.shape[1]
    for chunk in range(chunks):
        if first <= chunk * width < first + span:

            @pl.when(spot_ref[0] == chunk)
            def _():
                out_ref[...] = piece_of(slice(chunk * width - first, (chunk + 1) * width - first))


def gather_kernel(hub_steps, rel_steps, spot_ref, hub_ids, rel_ids, hub_ref, rel_ref, *refs):
    buckets = hub_ids.shape[0]
    hub_outs, rel_outs = refs[:buckets], refs[buckets : 2 * buckets]
    spot_out, hub_own, rel_own = refs[2 * buckets : 2 * buckets + 3]
    hub_buf, rel_buf, hub_idx, rel_idx, stacked, sems = refs[2 * buckets + 3 :]
    hub_tile, rel_tile = hub_buf.shape[2], rel_buf.shape[2]
    chunks = hub_ref.shape[1] // hub_own.shape[1]
    half = hub_own.shape[0]
    steps = [(rel_ref, rel_buf, rel_tile, k) for k in range(rel_steps)]
    steps += [(hub_ref, hub_buf, hub_tile, k) for k in range(hub_steps)]
    copies = [
        pltpu.make_async_copy(table.at[:, pl.ds(k * tile, tile)], buf.at[k % 2], sems.at[i])
        for i, (table, buf, tile, k) in enumerate(steps)
    ]
    id_copies = [
        pltpu.make_async_copy(ids, out, sems.at[len(copies) + i])
        for i, (ids, out) in enumerate([(hub_ids, hub_idx), (rel_ids, rel_idx)])
    ]
    ahead = rel_steps + 2
    for copy in [*id_copies, *copies[:ahead]]:
        copy.start()
    spot_out[0] = spot_ref[0]
    spot_out[1] = spot_ref[1]
    for copy in id_copies:
        copy.wait()
    rows = pl.ds(pl.multiple_of(spot_ref[1] * half, 8), half)
    for i, (table, buf, tile, k) in enumerate(steps):
        idx, outs, own = (hub_idx, hub_outs, hub_own) if table is hub_ref else (rel_idx, rel_outs, rel_own)
        count = idx.shape[1]
        hot = onehot(k * tile, tile, laid_out(idx[...]))
        copies[i].wait()
        stack_into(stacked, buf[k % 2], slice(0, tile))
        part = dot2(stacked[:, :tile], hot, NN)
        for b, out in enumerate(outs):
            here = part[:, b * count : (b + 1) * count]
            out[...] = here if k == 0 else out[...] + here
        take_owned(spot_ref, chunks, tile, k * tile, lambda lanes: buf[k % 2, rows, lanes], own)
        if i >= rel_steps and i + 2 < len(steps):
            copies[i + 2].start()


def gather_rows(spot, hub_table, hub_idx, rel_table, rel_idx, chunks):
    features = hub_table.shape[0]
    hub_steps, rel_steps = 4, 2
    hub_tile, rel_tile = hub_table.shape[1] // hub_steps, rel_table.shape[1] // rel_steps
    buckets, hubs = hub_idx.shape
    edges = rel_idx.shape[1]
    hub_width, rel_width = hub_table.shape[1] // chunks, rel_table.shape[1] // chunks
    shapes = [(features, hubs)] * buckets + [(features, edges)] * buckets
    own_shapes = [(features // 2, hub_width), (features // 2, rel_width)]
    floats = lambda shapes: [jax.ShapeDtypeStruct(shape, F32) for shape in shapes]
    out = pl.pallas_call(
        functools.partial(gather_kernel, hub_steps, rel_steps),
        in_specs=[SMEM] + [HBM] * 4,
        out_specs=[VMEM] * len(shapes) + [SMEM] + [VMEM] * len(own_shapes),
        out_shape=floats(shapes) + [jax.ShapeDtypeStruct((2,), jnp.int32)] + floats(own_shapes),
        scratch_shapes=[
            pltpu.VMEM((2, features, hub_tile), F32),
            pltpu.VMEM((2, features, rel_tile), F32),
            pltpu.VMEM(hub_idx.shape, jnp.int32),
            pltpu.VMEM(rel_idx.shape, jnp.int32),
            pltpu.VMEM((2 * features, max(hub_tile, rel_tile)), BF16),
            pltpu.SemaphoreType.DMA((hub_steps + rel_steps + 2,)),
        ],
        compiler_params=GATHER_PARAMS,
        cost_estimate=COST,
    )(spot, hub_idx, rel_idx, hub_table, rel_table)
    return out[:buckets], out[buckets : 2 * buckets], out[2 * buckets], out[2 * buckets + 1 :]


def spread_bits(place, order):
    bits = len(order)
    return sum((((place >> p) & 1) << (bits - 1 - i)) for i, p in enumerate(order))


def gather_bits(index, order):
    bits = len(order)
    return sum((((index >> (bits - 1 - i)) & 1) << p) for i, p in enumerate(order))


def load_columns(id_refs, grad_refs, idx_down, stacked):
    idx = jnp.concatenate([laid_out(ref[...]) for ref in id_refs], axis=1)
    idx_down[...] = jnp.transpose(jnp.broadcast_to(idx, (128, idx.shape[1]))).astype(jnp.int16)
    at = 0
    for ref, (low, high) in grad_refs:
        width = high - low
        stack_into(stacked, ref[:, low:high], slice(at, at + width))
        at += width


def onehot_across(idx_down, targets):
    width = targets.shape[1]
    idx = idx_down[...]
    wide = jnp.concatenate([idx] * -(-width // 128), axis=1)[:, :width]
    return hot_where(wide == targets.astype(jnp.int16))


def grouped(orders, step, heights):
    groups, where = [], []
    for s, order in enumerate(orders):
        for g, (place, members) in enumerate(groups):
            if place == order[step]:
                where.append((g, sum(heights[m] for m in members)))
                members.append(s)
                break
        else:
            where.append((len(groups), 0))
            groups.append((order[step], [s]))
    return [(place, sum(heights[m] for m in members)) for place, members in groups], where


def rows_of(where, heights, s):
    group, base = where[s]
    return group, slice(base, base + heights[s])


def put_chunk(place, orders, heights, where, sends, keeps, s, value):
    index, half = spread_bits(place, orders[s]), keeps[s].shape[0]
    if index < half:
        keeps[s][index] = value
    else:
        group, rows = rows_of(where, heights, s)
        sends[group][index - half, rows] = value


def chunk_refs(grad_lanes, refs):
    ids, refs = refs[:2], refs[2:]
    grads, refs = list(zip(refs, grad_lanes)), refs[len(grad_lanes) :]
    return ids, grads, refs[:-2], refs[-2:]


def hub_chunks_kernel(orders, spans, where, grad_lanes, spot_ref, *refs):
    ids, grads, outs, (idx_down, stacked) = chunk_refs(grad_lanes, refs)
    load_columns(ids, grads, idx_down, stacked)
    streams = len(orders)
    sends, keeps = outs[:-streams], outs[-streams:]
    heights = [high - low for low, high in spans]
    chunks, width = 2 * keeps[0].shape[0], keeps[0].shape[2]
    lane = lax.broadcasted_iota(jnp.int32, (1, width), 1)
    for place in range(chunks):
        hot = onehot_across(idx_down, lane + (spot_ref[0] ^ place) * width)
        chunk = dot2(stacked[...], hot, NN)
        for s, (low, high) in enumerate(spans):
            put_chunk(place, orders, heights, where, sends, keeps, s, chunk[low:high])


def packed_map(half_width, width, lanes):
    rows = half_width // 24 * 8
    gap, extra = lanes - 3 * width, half_width - 3 * rows
    entries = [(rows * b, 0, width, 0, b * width, rows) for b in range(3)]
    for i in range(-(-width // gap)):
        entries.append((3 * rows, i * gap, min(gap, width - i * gap), extra * i, 3 * width, extra))
    return rows, entries


def split_pieces(entries, spans):
    pieces = []
    for row, lane, lanes, to, to_lane, count in entries:
        for s, (first, end) in enumerate(spans):
            low, high = max(to, first), min(to + count, end)
            if low < high:
                pieces.append((s, row + low - to, high - low, lane, lanes, low - first, to_lane))
    return pieces


def rel_chunks_kernel(orders, pieces, rows, grad_lanes, spot_ref, *refs):
    ids, grads, outs, (idx_down, stacked) = chunk_refs(grad_lanes, refs)
    load_columns(ids, grads, idx_down, stacked)
    for ref in outs:
        ref[...] = jnp.zeros_like(ref)
    streams = len(orders)
    sends, keeps = outs[:streams], outs[streams:]
    half, lanes = keeps[0].shape[0], keeps[0].shape[2]
    chunks = 2 * half
    width = rows // chunks
    group = lanes // width
    lane = lax.broadcasted_iota(jnp.int32, (1, lanes), 1)
    for first in range(0, chunks, group):
        targets = jnp.full((1, lanes), -1, jnp.int32)
        places = range(first, min(first + group, chunks))
        for slot, place in enumerate(places):
            here = (lane >= slot * width) & (lane < (slot + 1) * width)
            targets = jnp.where(here, lane + ((spot_ref[0] ^ place) * width - slot * width), targets)
        dense = dot2(stacked[...], onehot_across(idx_down, targets), NN)
        for slot, place in enumerate(places):
            chunk = dense[:, slot * width : (slot + 1) * width]
            for s, row, count, low, wide, to, to_lane in pieces:
                index = spread_bits(place, orders[s])
                out = sends[s].at[index - half] if index >= half else keeps[s].at[index]
                out[to : to + count, to_lane : to_lane + wide] = chunk[row : row + count, low : low + wide]


def chunk_columns(kernel, shapes, spot, ids, grads):
    half_width = grads[0][0].shape[0]
    grad_lanes = [lanes_of for unused, lanes_of in grads]
    count = sum(high - low for low, high in grad_lanes)
    return pl.pallas_call(
        functools.partial(kernel, grad_lanes),
        in_specs=[SMEM] + [VMEM] * (2 + len(grads)),
        out_specs=[VMEM] * len(shapes),
        out_shape=[jax.ShapeDtypeStruct(shape, F32) for shape in shapes],
        scratch_shapes=[
            pltpu.VMEM((count, 128), jnp.int16),
            pltpu.VMEM((2 * (-(-half_width // 16) * 16), count), BF16),
        ],
        compiler_params=PARAMS,
        cost_estimate=COST,
    )(spot, *ids, *[g for g, unused in grads])


def call(kernel, ins, shapes, cost=None):
    return pl.pallas_call(
        kernel,
        in_specs=[VMEM] * len(ins),
        out_specs=[VMEM] * len(shapes),
        out_shape=[jax.ShapeDtypeStruct(shape, F32) for shape in shapes],
        compiler_params=PARAMS,
        cost_estimate=cost or COST,
    )(*ins)


def sums_kernel(heights, here, there, *refs):
    streams, groups = len(heights), 1 + max(g for g, unused in here)
    own, got, sends, keeps = refs[:streams], refs[streams : streams + groups], refs[streams + groups : -streams], refs[-streams:]
    for s in range(streams):
        half = keeps[s].shape[0]
        group, rows = rows_of(here, heights, s)
        out, out_rows = rows_of(there, heights, s)
        sends[out][:, out_rows] = own[s][half:] + got[group][half:, rows]
        keeps[s][...] = own[s][:half] + got[group][:half, rows]


def halves(own, got, orders, step):
    heights = [x.shape[1] for x in own]
    half, width = own[0].shape[0] // 2, own[0].shape[2]
    unused, here = grouped(orders, step, heights)
    groups, there = grouped(orders, step + 1, heights)
    shapes = [(half, height, width) for height in [h for unused, h in groups] + heights]
    out = call(functools.partial(sums_kernel, heights, here, there), [*own, *got], shapes)
    return out[: len(groups)], out[len(groups) :]


def split_kernel(bases, *refs):
    streams = len(bases)
    for got, base, out in zip(refs[:streams], bases, refs[streams:]):
        out[...] = got[:, base : base + out.shape[1]]


def extend_kernel(bases, *refs):
    streams = len(bases)
    held, owned, got, outs = [refs[i * streams : (i + 1) * streams] for i in range(4)]
    for s, base in enumerate(bases):
        count, height = held[s].shape[0], held[s].shape[1]
        outs[s][:count] = held[s][...]
        outs[s][count] = owned[s][0, base : base + height]
        outs[s][count + 1 :] = got[s][...]


def near_chunks_kernel(bases, *refs):
    streams = len(bases)
    new, held, owned, out = refs[0], refs[1 : streams + 1], refs[streams + 1 : -1], refs[-1]
    out[0] = new[0]
    for s, base in enumerate(bases):
        count, height = held[s].shape[0], held[s].shape[1]
        out[1 : count + 1, base : base + height] = held[s][...]
        out[count + 1, base : base + height] = owned[s][0, base : base + height]


def last_sums_kernel(heights, here, there, spans, *refs):
    streams, planes = len(heights), len(spans)
    groups, out_groups = [1 + max(g for g, unused in where) for where in (here, there)]
    rels, outs = refs[streams + groups : streams + groups + 2 * planes], refs[streams + groups + 2 * planes :]
    sums_kernel(heights, here, there, *refs[: streams + groups], *outs[: out_groups + streams])
    for place, out in enumerate(outs[out_groups + streams :]):
        for s, (low, high) in enumerate(spans):
            out[0, low:high] = rels[s][place] + rels[planes + s][place]


def squares_kernel(heights, here, entries, *refs):
    streams, groups = len(heights), 1 + max(g for g, unused in here)
    own, got, rels = refs[:streams], refs[streams : streams + groups], refs[streams + groups : -streams - 2]
    totals, rel_total, out = refs[-streams - 2 : -2], refs[-2], refs[-1]
    squares = jnp.zeros((1, out.shape[1]), F32)
    for s in range(streams):
        group, rows = rows_of(here, heights, s)
        total = own[s][0] + got[group][0, rows]
        totals[s][0] = total
        squares += jnp.sum(total * total, axis=0, keepdims=True)
    total = sum(ref[0] for ref in rels)
    rel_total[0] = total
    out[0:1] = squares
    out[1:2] = jnp.zeros_like(squares)
    square = total * total
    for row, lane, lanes, to, to_lane, count in entries:
        part = jnp.sum(square[to : to + count, to_lane : to_lane + lanes], axis=0, keepdims=True)
        out[1:2, lane : lane + lanes] += part


def update_kernel(spans, rel_spans, pieces, there, features, spot_ref, *refs):
    streams, groups = len(spans), 1 + max(g for g, unused in there)
    totals, (hub_sums, rel_sums), news = refs[:streams], refs[-2:], refs[-groups - 2 : -2]
    rel_total, mine, other, hub_ref, hub_all, rel_ref, rel_all = refs[streams : -groups - 2]
    chunks = hub_all.shape[1] // hub_ref.shape[1]
    take_owned(spot_ref, chunks, hub_all.shape[1], 0, lambda lanes: hub_all[:, lanes], hub_sums)
    take_owned(spot_ref, chunks, rel_all.shape[1], 0, lambda lanes: rel_all[:, lanes], rel_sums)
    width = rel_ref.shape[1]
    squares = mine[...] + other[...]
    hub_scale = step_rate / jnp.sqrt(hub_sums[...] + squares[0:1] * (1.0 / features))
    rel_scale = step_rate / jnp.sqrt(rel_sums[...] + squares[1:2, :width] * (1.0 / features))
    for s, (low, high) in enumerate(spans):
        new, base = there[s]
        first, end = rel_spans[s]
        middle = base + high - low
        news[new][0, base:middle] = hub_ref[low:high] - totals[s][0] * hub_scale
        news[new][0, middle : middle + end - first] = jnp.zeros((end - first, news[new].shape[2]), F32)
    for s, row, count, low, wide, to, to_lane in pieces:
        new, base = there[s]
        base += spans[s][1] - spans[s][0] + to
        lanes, first = slice(to_lane, to_lane + wide), rel_spans[s][0] + to
        news[new][0, base : base + count, lanes] = (
            rel_ref[row : row + count, low : low + wide]
            - rel_total[0, first : first + count, lanes] * rel_scale[:, low : low + wide]
        )


def chunk_copies(part, base, first, order, span, chip, component, out_ref, sems, at):
    low, high = span
    width = part.shape[2]
    for index in range(part.shape[0]):
        chunk = chip ^ gather_bits(first + index, order)
        lanes = pl.ds(pl.multiple_of(chunk * width, width), width)
        target = out_ref.at[component, pl.ds(low, high - low), lanes]
        yield pltpu.make_async_copy(part.at[index, pl.ds(base, high - low)], target, sems.at[at + index])


def component_of(spot_ref, mine):
    return spot_ref[1] if mine else 1 - spot_ref[1]


def near_kernel(orders, spans, bases, mine, spot_ref, near_ref, *refs):
    component = component_of(spot_ref, mine)
    out_ref, sems = refs[-2:]
    copies = []
    for order, span, base in zip(orders, spans, bases):
        copies += chunk_copies(near_ref, base, 0, order, span, spot_ref[0], component, out_ref, sems, len(copies))
    for copy in copies:
        copy.start()
    for copy in copies:
        copy.wait()


def far_kernel(orders, spans, bases, pieces, by_copy, mine, spot_ref, near_ref, *refs):
    component = component_of(spot_ref, mine)
    streams = len(orders)
    fars = refs[:streams]
    hub_out, rel_out, hub_all, rel_all, sems = refs[-5:]
    known = near_ref.shape[0]
    chunks = known + fars[0].shape[0]
    hub_width, rel_width = hub_out.shape[2] // chunks, rel_out.shape[2] // chunks
    copies = []
    if by_copy:
        for far, order, span in zip(fars, orders, spans):
            copies += chunk_copies(far, 0, known, order, span, spot_ref[0], component, hub_out, sems, len(copies))
        for copy in copies:
            copy.start()
    for chunk in range(chunks):
        place = spot_ref[0] ^ chunk
        for s, (low, high) in enumerate(spans):
            index = spread_bits(place, orders[s])
            near_at, far_at = jnp.minimum(index, known - 1), jnp.maximum(index - known, 0)
            height, base, end = high - low, bases[s], fars[s].shape[1]
            if not by_copy:
                value = jnp.where(index >= known, fars[s][far_at, :height], near_ref[near_at, base : base + height])
                hub_all[low:high, chunk * hub_width : (chunk + 1) * hub_width] = value
            value = jnp.where(index >= known, fars[s][far_at, height:], near_ref[near_at, base + height : base + end])
            for stream, row, count, low, wide, to, to_lane in pieces:
                if stream == s:
                    at = chunk * rel_width + low
                    rel_all[row : row + count, at : at + wide] = value[to : to + count, to_lane : to_lane + wide]
    copies.append(pltpu.make_async_copy(rel_all, rel_out.at[component], sems.at[len(copies)]))
    copies[-1].start()
    if not by_copy:
        copies.append(pltpu.make_async_copy(hub_all, hub_out.at[component], sems.at[len(copies)]))
        copies[-1].start()
    for copy in copies:
        copy.wait()


def placed(kernel, scratch, spot, near, fars, outs, earlier):
    sems = pltpu.SemaphoreType.DMA((3 * near.shape[0] + 2,))
    return pl.pallas_call(
        kernel,
        in_specs=[SMEM] + [VMEM] * (1 + len(fars)) + [HBM] * len(earlier),
        out_specs=[HBM] * len(outs),
        out_shape=[jax.ShapeDtypeStruct(shape, F32) for shape in outs],
        scratch_shapes=scratch + [sems],
        input_output_aliases={2 + len(fars) + i: i for i in range(len(earlier))},
        compiler_params=PARAMS,
        cost_estimate=pl.CostEstimate(flops=0, bytes_accessed=4 * outs[0][1] * outs[0][2], transcendentals=0),
    )(spot, near, *fars, *earlier)


def adagrad(table, state, grads):
    new_state = state + jnp.sum(grads * grads, axis=0, keepdims=True) * (1.0 / grads.shape[0])
    return table - grads * (step_rate / jnp.sqrt(new_state)), new_state


def keep_and_send(core, first, second):
    return jnp.where(core == 0, first, second), jnp.where(core == 0, second, first)


def table_counts(rows, negs, weight):
    place = lax.broadcasted_iota(jnp.int32, (rows, negs.shape[1]), 0)
    return jnp.sum(jnp.where(place == negs, weight, 0.0), axis=1, keepdims=True)


def turned(x, r, half):
    x0, x1, r0, r1 = x[:half], x[half:], r[:half], r[half:]
    return jnp.concatenate([x0 * r0 - x1 * r1, x0 * r1 + x1 * r0], axis=0)


def turned_back(x, r, half):
    x0, x1, r0, r1 = x[:half], x[half:], r[:half], r[half:]
    return x0 * r0 + x1 * r1, x1 * r0 - x0 * r1


EDGE_TILE = 512


def bucket_kernel(
    bucket, core_ref, heads_ref, tails_ref, negs_ref, left_ref, left_sums_ref, right_ref, right_sums_ref, rel_ref, hub_ref,
    left_out, left_sums_out, right_out, keep_out, send_out,
    left_parts, both_parts,
):
    features, rows = left_ref.shape
    half = features // 2
    core = core_ref[1]
    edges = heads_ref.shape[1]
    hubs = keep_out.shape[1] - edges
    at = slice(bucket, bucket + 1)
    weight = 1.0 / (negs_ref.shape[1] + hubs)
    counts = table_counts(rows, negs_ref[at], weight)
    stack_into(left_parts, left_ref[...])
    stack_into(both_parts, right_ref[...], slice(0, rows))
    stack_into(both_parts, hub_ref[...], slice(rows, rows + hubs))

    tail_here = lax.broadcasted_iota(jnp.int32, (rows, edges), 0) == tails_ref[at]
    head_hot = onehot(0, rows, heads_ref[at])
    h = dot2(left_parts[...], head_hot, NN)
    r = rel_ref[...]
    q = split(turned(h, r, half))
    scores = dot3((both_parts[:features], both_parts[features:]), q, TN)
    chance = jax.nn.sigmoid(scores[:rows])
    coef = jnp.concatenate(
        [
            counts * chance + jnp.where(tail_here, chance - 1.0, 0.0),
            weight * jax.nn.sigmoid(scores[rows:]),
        ],
        axis=0,
    )
    coef = split(coef)
    dq = dot3_stacked(both_parts[...], coef, NN)
    both_grad = dot3_stacked(stack(q), coef, NT)
    dh = jnp.concatenate(turned_back(dq, r, half), axis=0)
    left_grad = dot2(stack(split(dh)), head_hot, NT)
    keep_out[:, hubs:], send_out[:, hubs:] = keep_and_send(core, *turned_back(dq, h, half))

    left_out[...], left_sums_out[...] = adagrad(left_ref[...], left_sums_ref[...], left_grad)
    new_right, new_sums = adagrad(right_ref[...], right_sums_ref[...], both_grad[:, :rows])
    right_out[:features] = new_right
    right_out[features:] = jnp.broadcast_to(new_sums, (right_out.shape[0] - features, rows))
    keep_out[:, :hubs], send_out[:, :hubs] = keep_and_send(core, both_grad[:half, rows:], both_grad[half:, rows:])


def bucket_step(bucket, core, heads, tails, negs, left, left_sums, right, right_sums, rel_rows, hub_rows):
    features, rows = left.shape
    edges, hubs = heads.shape[1], hub_rows.shape[1]
    width = rows + hubs
    shapes = [(features, rows), (1, rows), (features + 8, rows)] + [(features // 2, hubs + edges)] * 2
    return pl.pallas_call(
        functools.partial(bucket_kernel, bucket),
        in_specs=[SMEM] + [VMEM] * 9,
        out_specs=[VMEM] * 5,
        out_shape=[jax.ShapeDtypeStruct(shape, F32) for shape in shapes],
        scratch_shapes=[
            pltpu.VMEM((2 * features, rows), BF16),
            pltpu.VMEM((2 * features, width), BF16),
        ],
        compiler_params=PARAMS,
        cost_estimate=COST,
    )(core, heads, tails, negs, left, left_sums, right, right_sums, rel_rows, hub_rows)


def hub_kernel(
    bucket, negatives, core_ref, heads_ref, left_ref, rel_ref, hub_ref,
    query_grad, hub_keep, hub_send,
    left_parts, hub_parts,
):
    features, rows = left_ref.shape
    half = features // 2
    edges, hubs = heads_ref.shape[1], hub_keep.shape[1]
    at = slice(bucket, bucket + 1)
    weight = 1.0 / (negatives + hubs)
    stack_into(left_parts, left_ref[...])
    stack_into(hub_parts, hub_ref[...])

    head_hot = onehot(0, rows, heads_ref[at])
    h = dot2(left_parts[...], head_hot, NN)
    q = split(turned(h, rel_ref[...], half))
    coef = split(weight * jax.nn.sigmoid(dot3((hub_parts[:features], hub_parts[features:]), q, TN)))
    query_grad[...] = dot3_stacked(hub_parts[...], coef, NN)
    hub_grad = dot3_stacked(stack(q), coef, NT)

    hub_keep[...], hub_send[...] = keep_and_send(core_ref[1], hub_grad[:half], hub_grad[half:])


def hub_step(bucket, negatives, core, heads, left, rel_rows, hub_rows):
    features, rows = left.shape
    edges, hubs = heads.shape[1], hub_rows.shape[1]
    shapes = [(features, edges)] + [(features // 2, hubs)] * 2
    return pl.pallas_call(
        functools.partial(hub_kernel, bucket, negatives),
        in_specs=[SMEM] + [VMEM] * 4,
        out_specs=[VMEM] * 3,
        out_shape=[jax.ShapeDtypeStruct(shape, F32) for shape in shapes],
        scratch_shapes=[
            pltpu.VMEM((2 * features, rows), BF16),
            pltpu.VMEM((2 * features, hubs), BF16),
        ],
        compiler_params=PARAMS,
        cost_estimate=COST,
    )(core, heads, left, rel_rows, hub_rows)


def relations_kernel(
    bucket, hubs, core_ref, heads_ref, tails_ref, negs_ref, query_grad, left_ref, right_ref, rel_ref,
    rel_keep, rel_send, query_out, coef_out, head_grad,
    left_parts, right_parts,
):
    features, rows = left_ref.shape
    half = features // 2
    edges = heads_ref.shape[1]
    at = slice(bucket, bucket + 1)
    counts = table_counts(rows, negs_ref[at], 1.0 / (negs_ref.shape[1] + hubs))
    stack_into(left_parts, left_ref[...])
    stack_into(right_parts, right_ref[:features])
    tail_here = lax.broadcasted_iota(jnp.int32, (rows, edges), 0) == tails_ref[at]
    h = dot2(left_parts[...], onehot(0, rows, heads_ref[at]), NN)
    r = rel_ref[...]
    q = split(turned(h, r, half))
    chance = jax.nn.sigmoid(dot3((right_parts[:features], right_parts[features:]), q, TN))
    coef = split(counts * chance + jnp.where(tail_here, chance - 1.0, 0.0))
    dq = dot3_stacked(right_parts[...], coef, NN) + query_grad[...]
    rel_keep[...], rel_send[...] = keep_and_send(core_ref[1], *turned_back(dq, h, half))
    query_out[...] = stack(q)
    coef_out[0], coef_out[1] = coef
    head_grad[:half], head_grad[half:] = turned_back(dq, r, half)


def relations_step(bucket, hubs, core, heads, tails, negs, query_grad, left, right, rel_rows):
    features, rows = left.shape
    edges = heads.shape[1]
    half = jax.ShapeDtypeStruct((features // 2, edges), F32)
    return pl.pallas_call(
        functools.partial(relations_kernel, bucket, hubs),
        in_specs=[SMEM] + [VMEM] * 7,
        out_specs=[VMEM] * 5,
        out_shape=[
            half,
            half,
            jax.ShapeDtypeStruct((2 * features, edges), BF16),
            jax.ShapeDtypeStruct((2, rows, edges), BF16),
            jax.ShapeDtypeStruct((features, edges), F32),
        ],
        scratch_shapes=[pltpu.VMEM((2 * features, rows), BF16)] * 2,
        compiler_params=PARAMS,
        cost_estimate=COST,
    )(core, heads, tails, negs, query_grad, left, right, rel_rows)


def tables_kernel(
    bucket, heads_ref, left_ref, left_sums_ref, right_ref, query_ref, coef_ref, head_grad, left_out, right_out
):
    features, rows = left_ref.shape
    head_hot = onehot(0, rows, heads_ref[bucket : bucket + 1])
    left_grad = dot2(stack(split(head_grad[...])), head_hot, NT)
    left_out[...], unused = adagrad(left_ref[...], left_sums_ref[...], left_grad)
    right_grad = dot3_stacked(query_ref[...], (coef_ref[0], coef_ref[1]), NT)
    right_out[...], unused = adagrad(right_ref[:features], right_ref[features : features + 1], right_grad)


def from_behind(x, axis, by):
    size = lax.axis_size(axis)
    return lax.ppermute(x, axis, [(i, (i + by) % size) for i in range(size)])


def flipped(x, axis, bit):
    return lax.ppermute(x, axis, [(i, i ^ (1 << bit)) for i in range(lax.axis_size(axis))])


def flipped_by(x, axis, offset):
    return lax.ppermute(x, axis, [(i, i ^ offset) for i in range(lax.axis_size(axis))])


def other_core(x):
    return flipped(x, "blk", 0)


def across(x, place):
    sub_bits = lax.axis_size("sub").bit_length() - 1
    if place < sub_bits:
        return flipped(x, "sub", place)
    return flipped(x, "blk", place - sub_bits + 1)


def stream_orders(gathering):
    sub_bits = lax.axis_size("sub").bit_length() - 1
    bits = sub_bits + lax.axis_size("blk").bit_length() - 2
    x, y, z, far = sub_bits, sub_bits + 1, 0, 1
    rest = [p for p in range(bits) if p not in (x, y, z, far)]
    last = [y, far] if gathering else [far, y]
    return [[x, y, z, far] + rest, [y, z, x, far] + rest, [z, x, *last] + rest]


def plane_orders(sub_bits, bits):
    plane, depth = list(range(sub_bits, bits)), list(range(sub_bits - 1, -1, -1))
    return [plane + depth, plane[1:] + plane[:1] + depth]


def row_spans(rows, parts):
    ends = [-(-rows * (i + 1) // (8 * parts)) * 8 for i in range(parts - 1)] + [rows]
    return list(zip([0] + ends[:-1], ends))


def shards(
    left_emb, left_state, right_emb, right_state, relation_emb, relation_state, hub_emb, hub_state,
    heads, relations, tails, negatives, hub_ids,
):
    components, half_width, row_count = left_emb.shape
    features = components * half_width
    rel_count, hub_count = relation_emb.shape[2], hub_emb.shape[2]
    left = left_emb.reshape(features, row_count)
    right = right_emb.reshape(features, row_count)
    left_sums = left_state.reshape(1, row_count)
    right_sums = right_state.reshape(1, row_count)
    buckets, edges = heads.shape
    hubs = hub_ids.shape[1]

    orders, back_orders = stream_orders(False), stream_orders(True)
    streams, stages = len(orders), len(orders[0])
    chunks, depth = 1 << stages, lax.axis_size("sub")
    sub_bits = depth.bit_length() - 1
    planes = chunks // depth
    spans = row_spans(half_width, streams)
    rel_orders = plane_orders(sub_bits, stages)
    width, rel_width = hub_count // chunks, rel_count // chunks
    rel_height, entries = packed_map(half_width, rel_width, width)
    plane_spans = row_spans(rel_height, len(rel_orders))
    share = -(-(half_width + rel_height) // (8 * streams)) * 8
    ends = [share * (s + 1) - spans[s][1] for s in range(streams - 1)] + [rel_height]
    rel_spans = list(zip([0] + ends[:-1], ends))
    plane_pieces, joint_pieces = split_pieces(entries, plane_spans), split_pieces(entries, rel_spans)
    heights, rel_heights, plane_heights = [[high - low for low, high in x] for x in (spans, rel_spans, plane_spans)]
    joint_heights = [h + r for h, r in zip(heights, rel_heights)]
    bases = [sum(joint_heights[:s]) for s in range(streams)]
    hub_lanes, rel_lanes = (0, hubs), (hubs, hubs + edges)

    def exchanged(parts, step, orders=orders):
        return [across(x, place) for x, (place, unused) in zip(parts, grouped(orders, step, heights)[0])]

    def in_turn(first, then):
        return lax.optimization_barrier((first, then))

    blk = lax.axis_index("blk")
    spot = jnp.stack([(blk >> 1) * depth + lax.axis_index("sub"), blk & 1]).astype(jnp.int32)
    far_ids = other_core((hub_ids, relations))
    hub_rows, rel_rows, spot, owned = gather_rows(
        spot, hub_emb.reshape(features, hub_count), hub_ids, relation_emb.reshape(features, rel_count), relations, chunks
    )
    far_ids, hub_rows = in_turn(far_ids, hub_rows)
    keeps, sends = [], []
    for b in range(buckets - 1):
        if b > 0:
            right, right_sums = right[:features], right[features : features + 1]
        left, left_sums, right, keep, send = bucket_step(
            b, spot, heads, tails, negatives, left, left_sums, right, right_sums, rel_rows[b], hub_rows[b]
        )
        right = from_behind(right, "blk", 1)
        keeps.append(keep)
        sends.append(send)
    last = buckets - 1
    query_grad, hub_keep, hub_send = hub_step(
        last, negatives.shape[1], spot, heads, left, rel_rows[last], hub_rows[last]
    )
    sends, hub_send = in_turn(sends, hub_send)
    hub_far = other_core(hub_send)
    fars = [other_core(x) for x in sends]
    grads = lambda early, late, lanes: [(x, lanes) for x in early] + [(late, (0, late.shape[1]))]
    groups, where = grouped(orders, 0, heights)
    parts = chunk_columns(
        functools.partial(hub_chunks_kernel, orders, spans, where),
        [(chunks // 2, height, width) for height in [h for unused, h in groups] + heights],
        spot, (hub_ids, far_ids[0]), grads(keeps, hub_keep, hub_lanes) + grads(fars, hub_far, hub_lanes),
    )
    send, own = parts[: len(groups)], parts[len(groups) :]
    got = exchanged(send, 0)
    rel_keep, rel_send, *parts = relations_step(
        last, hubs, spot, heads, tails, negatives, query_grad, left, right, rel_rows[last]
    )
    later = [heads, left, left_sums, right, *parts]
    rel_far = other_core(rel_send)

    parts = chunk_columns(
        functools.partial(rel_chunks_kernel, rel_orders, plane_pieces, rel_count),
        [(chunks // 2, height, width) for height in plane_heights * 2],
        spot, (relations, far_ids[1]), grads(keeps, rel_keep, rel_lanes) + grads(fars, rel_far, rel_lanes),
    )
    rel_send, rel_own = parts[: len(rel_orders)], parts[len(rel_orders) :]
    rel_got = [across(x, order[0]) for x, order in zip(rel_send, rel_orders)]
    plane_steps = stages - sub_bits
    for step in range(stages - 2):
        if 0 < step < plane_steps:
            own, rel_got = in_turn(own, rel_got)
            rel_send, rel_own = halves(rel_own, rel_got, rel_orders, step - 1)
            rel_got = [across(x, order[step]) for x, order in zip(rel_send, rel_orders)]
        rel_own, got = in_turn(rel_own, got)
        send, own = halves(own, got, orders, step)
        got = exchanged(send, step + 1)

    here = grouped(orders, stages - 2, heights)[1]
    groups, there = grouped(orders, stages - 1, heights)
    parts = call(
        functools.partial(last_sums_kernel, heights, here, there, plane_spans),
        [*own, *got, *rel_own, *rel_got],
        [(1, height, width) for height in [h for unused, h in groups] + heights + [rel_height] * depth],
    )
    send, own, rel_parts = parts[: len(groups)], parts[len(groups) : len(groups) + streams], parts[len(groups) + streams :]
    got = exchanged(send, stages - 1)
    rel_got = [flipped_by(x, "sub", q + 1) for q, x in enumerate(rel_parts[1:])]
    *totals, rel_total, squares = call(
        functools.partial(squares_kernel, heights, there, entries),
        [*own, *got, rel_parts[0], *rel_got], [x.shape for x in own] + [rel_parts[0].shape, (2, width)],
    )
    hub_own, rel_own = owned
    there = [(0, base) for base in bases]
    ins = [
        *totals, rel_total, squares, other_core(squares),
        hub_own, hub_state[None], rel_own, relation_state[None],
    ]
    [new] = pl.pallas_call(
        functools.partial(update_kernel, spans, rel_spans, joint_pieces, there, features),
        in_specs=[SMEM] + [VMEM] * len(ins),
        out_specs=[VMEM],
        out_shape=[jax.ShapeDtypeStruct((1, sum(joint_heights), width), F32)],
        scratch_shapes=[pltpu.VMEM((1, x.shape[1]), F32) for x in owned],
        compiler_params=PARAMS,
        cost_estimate=COST,
    )(spot, *ins)
    partners = [across(new, place) for place in range(stages)]
    owned_at = lambda step: [partners[order[step]] for order in back_orders]
    shapes = lambda count: [(count, height, width) for height in joint_heights]
    have = call(functools.partial(split_kernel, bases), owned_at(stages - 1), shapes(1))
    for step in range(stages - 2, 0, -1):
        got = [across(x, order[step]) for x, order in zip(have, back_orders)]
        have = call(
            functools.partial(extend_kernel, bases), [*have, *owned_at(step), *got], shapes(2 * have[0].shape[0] + 1)
        )
    got = [across(x, order[0]) for x, order in zip(have, back_orders)]
    [near] = call(
        functools.partial(near_chunks_kernel, bases), [new, *have, *owned_at(0)],
        [(have[0].shape[0] + 2, sum(joint_heights), width)],
    )
    far_near = other_core(near)

    shapes = [hub_emb.shape, relation_emb.shape]
    by_copy = width % 128 == 0
    hub_new = []
    if by_copy:
        near_step = functools.partial(near_kernel, back_orders, spans, bases)
        hub_new = placed(functools.partial(near_step, True), [], spot, near, [], shapes[:1], [])
        later, hub_new = in_turn(later, hub_new)
        left, right = call(
            functools.partial(tables_kernel, last), later, [left.shape] * 2,
            pl.CostEstimate(flops=3 * 10**9, bytes_accessed=10**7, transcendentals=0),
        )
        hub_new = placed(functools.partial(near_step, False), [], spot, far_near, [], shapes[:1], hub_new)
        got, hub_new, left, right = lax.optimization_barrier((got, hub_new, left, right))
    else:
        left, right = call(functools.partial(tables_kernel, last), later, [left.shape] * 2)
    far_step = functools.partial(far_kernel, back_orders, spans, bases, joint_pieces, by_copy)
    scratch = [
        pltpu.VMEM((8, 128) if by_copy else (half_width, hub_count), F32),
        pltpu.VMEM((half_width, rel_count), F32),
    ]
    far_got = other_core(got)
    out = placed(functools.partial(far_step, True), scratch, spot, near, got, shapes, hub_new)
    hub_new, rel_new = placed(functools.partial(far_step, False), scratch, spot, far_near, far_got, shapes, out)
    return (
        left.reshape(components, half_width, row_count),
        right.reshape(components, half_width, row_count),
        rel_new,
        hub_new,
    )


def solution(mesh):
    both = ("blk", "sub")
    block, table, whole = P(None, None, both), P(None, both), P()
    return jax.shard_map(
        shards,
        mesh=mesh,
        in_specs=(block, P(both), block, P(both), whole, whole, whole, whole, table, table, table, table, table),
        out_specs=(block, block, whole, whole),
        check_vma=False,
    )
```

```python
import functools
import jax
import jax.numpy as jnp
from jax import lax
from jax.experimental import pallas as pl
from jax.experimental.pallas import tpu as pltpu
from jax.sharding import PartitionSpec as P

step_rate = 0.25
F32, BF16 = jnp.float32, jnp.bfloat16
NN = (((1,), (0,)), ((), ()))
NT = (((1,), (1,)), ((), ()))
TN = (((0,), (0,)), ((), ()))
VMEM = pl.BlockSpec(memory_space=pltpu.VMEM)
SMEM = pl.BlockSpec(memory_space=pltpu.SMEM)
PARAMS = pltpu.CompilerParams(vmem_limit_bytes=12 * 1024 * 1024)
GATHER_PARAMS = pltpu.CompilerParams(vmem_limit_bytes=50 * 1024 * 1024)
HBM = pl.BlockSpec(memory_space=pltpu.HBM)
COST = pl.CostEstimate(flops=10000, bytes_accessed=10000, transcendentals=0)


def split(x):
    hi = x.astype(BF16)
    return hi, (x - hi.astype(F32)).astype(BF16)


def dot(a, b, dims):
    return lax.dot_general(a, b, dims, preferred_element_type=F32)


def dot3(a, b, dims):
    return dot(a[0], b[0], dims) + (dot(a[0], b[1], dims) + dot(a[1], b[0], dims))


def dot2(stacked, onehot, dims):
    half = stacked.shape[0] // 2
    both = dot(stacked, onehot, dims)
    return both[:half] + both[half:]


def stack(parts):
    return jnp.concatenate(parts, axis=0)


def stack_into(ref, x, lanes=slice(None)):
    rows, half = x.shape[0], ref.shape[0] // 2
    hi, lo = split(x)
    ref[:rows, lanes] = hi
    ref[half : half + rows, lanes] = lo
    if half > rows:
        blank = jnp.zeros((half - rows, x.shape[1]), BF16)
        ref[rows:half, lanes] = blank
        ref[half + rows :, lanes] = blank


def dot3_stacked(stacked, b, dims):
    half = stacked.shape[0] // 2
    both = dot(stacked, b[0], dims)
    return both[:half] + (both[half:] + dot(stacked[:half], b[1], dims))


def hot_where(here):
    return jnp.where(here, jnp.ones((), BF16), jnp.zeros((), BF16))


def onehot(first, rows, idx):
    place = lax.broadcasted_iota(jnp.int16, (rows, idx.shape[1]), 0)
    return hot_where(place == (idx - first).astype(jnp.int16))


def laid_out(idx):
    return jnp.concatenate([idx[b : b + 1] for b in range(idx.shape[0])], axis=1)


def take_owned(spot_ref, chunks, span, first, piece_of, out_ref):
    width = out_ref.shape[1]
    for chunk in range(chunks):
        if first <= chunk * width < first + span:

            @pl.when(spot_ref[0] == chunk)
            def _():
                out_ref[...] = piece_of(slice(chunk * width - first, (chunk + 1) * width - first))


def gather_kernel(hub_steps, rel_steps, spot_ref, hub_ids, rel_ids, hub_ref, rel_ref, *refs):
    buckets = hub_ids.shape[0]
    hub_outs, rel_outs = refs[:buckets], refs[buckets : 2 * buckets]
    spot_out, hub_own, rel_own = refs[2 * buckets : 2 * buckets + 3]
    hub_buf, rel_buf, hub_idx, rel_idx, stacked, sems = refs[2 * buckets + 3 :]
    hub_tile, rel_tile = hub_buf.shape[2], rel_buf.shape[2]
    chunks = hub_ref.shape[1] // hub_own.shape[1]
    half = hub_own.shape[0]
    steps = [(hub_ref, hub_buf, hub_tile, k) for k in range(hub_steps)]
    steps += [(rel_ref, rel_buf, rel_tile, k) for k in range(rel_steps)]
    copies = [
        pltpu.make_async_copy(table.at[:, pl.ds(k * tile, tile)], buf.at[k % 2], sems.at[i])
        for i, (table, buf, tile, k) in enumerate(steps)
    ]
    id_copies = [
        pltpu.make_async_copy(ids, out, sems.at[len(copies) + i])
        for i, (ids, out) in enumerate([(hub_ids, hub_idx), (rel_ids, rel_idx)])
    ]
    for copy in [*id_copies, copies[0]]:
        copy.start()
    spot_out[0] = spot_ref[0]
    spot_out[1] = spot_ref[1]
    for copy in id_copies:
        copy.wait()
    rows = pl.ds(pl.multiple_of(spot_ref[1] * half, 8), half)
    for i, (table, buf, tile, k) in enumerate(steps):
        if i + 1 < len(steps):
            copies[i + 1].start()
        idx, outs, own = (hub_idx, hub_outs, hub_own) if table is hub_ref else (rel_idx, rel_outs, rel_own)
        count = idx.shape[1]
        hot = onehot(k * tile, tile, laid_out(idx[...]))
        copies[i].wait()
        stack_into(stacked, buf[k % 2], slice(0, tile))
        part = dot2(stacked[:, :tile], hot, NN)
        for b, out in enumerate(outs):
            here = part[:, b * count : (b + 1) * count]
            out[...] = here if k == 0 else out[...] + here
        take_owned(spot_ref, chunks, tile, k * tile, lambda lanes: buf[k % 2, rows, lanes], own)


def gather_rows(spot, hub_table, hub_idx, rel_table, rel_idx, chunks):
    features = hub_table.shape[0]
    hub_steps, rel_steps = 4, 2
    hub_tile, rel_tile = hub_table.shape[1] // hub_steps, rel_table.shape[1] // rel_steps
    buckets, hubs = hub_idx.shape
    edges = rel_idx.shape[1]
    hub_width, rel_width = hub_table.shape[1] // chunks, rel_table.shape[1] // chunks
    shapes = [(features, hubs)] * buckets + [(features, edges)] * buckets
    own_shapes = [(features // 2, hub_width), (features // 2, rel_width)]
    floats = lambda shapes: [jax.ShapeDtypeStruct(shape, F32) for shape in shapes]
    out = pl.pallas_call(
        functools.partial(gather_kernel, hub_steps, rel_steps),
        in_specs=[SMEM] + [HBM] * 4,
        out_specs=[VMEM] * len(shapes) + [SMEM] + [VMEM] * len(own_shapes),
        out_shape=floats(shapes) + [jax.ShapeDtypeStruct((2,), jnp.int32)] + floats(own_shapes),
        scratch_shapes=[
            pltpu.VMEM((2, features, hub_tile), F32),
            pltpu.VMEM((2, features, rel_tile), F32),
            pltpu.VMEM(hub_idx.shape, jnp.int32),
            pltpu.VMEM(rel_idx.shape, jnp.int32),
            pltpu.VMEM((2 * features, max(hub_tile, rel_tile)), BF16),
            pltpu.SemaphoreType.DMA((hub_steps + rel_steps + 2,)),
        ],
        compiler_params=GATHER_PARAMS,
        cost_estimate=COST,
    )(spot, hub_idx, rel_idx, hub_table, rel_table)
    return out[:buckets], out[buckets : 2 * buckets], out[2 * buckets], out[2 * buckets + 1 :]


def spread_bits(place, order):
    bits = len(order)
    return sum((((place >> p) & 1) << (bits - 1 - i)) for i, p in enumerate(order))


def gather_bits(index, order):
    bits = len(order)
    return sum((((index >> (bits - 1 - i)) & 1) << p) for i, p in enumerate(order))


def load_columns(id_refs, grad_refs, idx_down, stacked):
    idx = jnp.concatenate([laid_out(ref[...]) for ref in id_refs], axis=1)
    idx_down[...] = jnp.transpose(jnp.broadcast_to(idx, (128, idx.shape[1]))).astype(jnp.int16)
    at = 0
    for ref, (low, high) in grad_refs:
        width = high - low
        stack_into(stacked, ref[:, low:high], slice(at, at + width))
        at += width


def onehot_across(idx_down, targets):
    width = targets.shape[1]
    idx = idx_down[...]
    wide = jnp.concatenate([idx] * -(-width // 128), axis=1)[:, :width]
    return hot_where(wide == targets.astype(jnp.int16))


def grouped(orders, step, heights):
    groups, where = [], []
    for s, order in enumerate(orders):
        for g, (place, members) in enumerate(groups):
            if place == order[step]:
                where.append((g, sum(heights[m] for m in members)))
                members.append(s)
                break
        else:
            where.append((len(groups), 0))
            groups.append((order[step], [s]))
    return [(place, sum(heights[m] for m in members)) for place, members in groups], where


def rows_of(where, heights, s):
    group, base = where[s]
    return group, slice(base, base + heights[s])


def put_chunk(place, orders, heights, where, sends, keeps, s, value):
    index, half = spread_bits(place, orders[s]), keeps[s].shape[0]
    if index < half:
        keeps[s][index] = value
    else:
        group, rows = rows_of(where, heights, s)
        sends[group][index - half, rows] = value


def chunk_refs(grad_lanes, refs):
    ids, refs = refs[:2], refs[2:]
    grads, refs = list(zip(refs, grad_lanes)), refs[len(grad_lanes) :]
    return ids, grads, refs[:-2], refs[-2:]


def hub_chunks_kernel(orders, spans, where, grad_lanes, spot_ref, *refs):
    ids, grads, outs, (idx_down, stacked) = chunk_refs(grad_lanes, refs)
    load_columns(ids, grads, idx_down, stacked)
    streams = len(orders)
    sends, keeps = outs[:-streams], outs[-streams:]
    heights = [high - low for low, high in spans]
    chunks, width = 2 * keeps[0].shape[0], keeps[0].shape[2]
    lane = lax.broadcasted_iota(jnp.int32, (1, width), 1)
    for place in range(chunks):
        hot = onehot_across(idx_down, lane + (spot_ref[0] ^ place) * width)
        chunk = dot2(stacked[...], hot, NN)
        for s, (low, high) in enumerate(spans):
            put_chunk(place, orders, heights, where, sends, keeps, s, chunk[low:high])


def packed_map(half_width, width, lanes):
    rows = half_width // 24 * 8
    gap, extra = lanes - 3 * width, half_width - 3 * rows
    entries = [(rows * b, 0, width, 0, b * width, rows) for b in range(3)]
    for i in range(-(-width // gap)):
        entries.append((3 * rows, i * gap, min(gap, width - i * gap), extra * i, 3 * width, extra))
    return rows, entries


def split_pieces(entries, spans):
    pieces = []
    for row, lane, lanes, to, to_lane, count in entries:
        for s, (first, end) in enumerate(spans):
            low, high = max(to, first), min(to + count, end)
            if low < high:
                pieces.append((s, row + low - to, high - low, lane, lanes, low - first, to_lane))
    return pieces


def rel_chunks_kernel(orders, pieces, rows, grad_lanes, spot_ref, *refs):
    ids, grads, outs, (idx_down, stacked) = chunk_refs(grad_lanes, refs)
    load_columns(ids, grads, idx_down, stacked)
    for ref in outs:
        ref[...] = jnp.zeros_like(ref)
    streams = len(orders)
    sends, keeps = outs[:streams], outs[streams:]
    half, lanes = keeps[0].shape[0], keeps[0].shape[2]
    chunks = 2 * half
    width = rows // chunks
    group = lanes // width
    lane = lax.broadcasted_iota(jnp.int32, (1, lanes), 1)
    for first in range(0, chunks, group):
        targets = jnp.full((1, lanes), -1, jnp.int32)
        places = range(first, min(first + group, chunks))
        for slot, place in enumerate(places):
            here = (lane >= slot * width) & (lane < (slot + 1) * width)
            targets = jnp.where(here, lane + ((spot_ref[0] ^ place) * width - slot * width), targets)
        dense = dot2(stacked[...], onehot_across(idx_down, targets), NN)
        for slot, place in enumerate(places):
            chunk = dense[:, slot * width : (slot + 1) * width]
            for s, row, count, low, wide, to, to_lane in pieces:
                index = spread_bits(place, orders[s])
                out = sends[s].at[index - half] if index >= half else keeps[s].at[index]
                out[to : to + count, to_lane : to_lane + wide] = chunk[row : row + count, low : low + wide]


def chunk_columns(kernel, shapes, spot, ids, grads):
    half_width = grads[0][0].shape[0]
    grad_lanes = [lanes_of for unused, lanes_of in grads]
    count = sum(high - low for low, high in grad_lanes)
    return pl.pallas_call(
        functools.partial(kernel, grad_lanes),
        in_specs=[SMEM] + [VMEM] * (2 + len(grads)),
        out_specs=[VMEM] * len(shapes),
        out_shape=[jax.ShapeDtypeStruct(shape, F32) for shape in shapes],
        scratch_shapes=[
            pltpu.VMEM((count, 128), jnp.int16),
            pltpu.VMEM((2 * (-(-half_width // 16) * 16), count), BF16),
        ],
        compiler_params=PARAMS,
        cost_estimate=COST,
    )(spot, *ids, *[g for g, unused in grads])


def call(kernel, ins, shapes):
    return pl.pallas_call(
        kernel,
        in_specs=[VMEM] * len(ins),
        out_specs=[VMEM] * len(shapes),
        out_shape=[jax.ShapeDtypeStruct(shape, F32) for shape in shapes],
        compiler_params=PARAMS,
        cost_estimate=COST,
    )(*ins)


def sums_kernel(heights, here, there, *refs):
    streams, groups = len(heights), 1 + max(g for g, unused in here)
    own, got, sends, keeps = refs[:streams], refs[streams : streams + groups], refs[streams + groups : -streams], refs[-streams:]
    for s in range(streams):
        half = keeps[s].shape[0]
        group, rows = rows_of(here, heights, s)
        out, out_rows = rows_of(there, heights, s)
        sends[out][:, out_rows] = own[s][half:] + got[group][half:, rows]
        keeps[s][...] = own[s][:half] + got[group][:half, rows]


def halves(own, got, orders, step):
    heights = [x.shape[1] for x in own]
    half, width = own[0].shape[0] // 2, own[0].shape[2]
    unused, here = grouped(orders, step, heights)
    groups, there = grouped(orders, step + 1, heights)
    shapes = [(half, height, width) for height in [h for unused, h in groups] + heights]
    out = call(functools.partial(sums_kernel, heights, here, there), [*own, *got], shapes)
    return out[: len(groups)], out[len(groups) :]


def split_kernel(bases, *refs):
    streams = len(bases)
    for got, base, out in zip(refs[:streams], bases, refs[streams:]):
        out[...] = got[:, base : base + out.shape[1]]


def extend_kernel(bases, *refs):
    streams = len(bases)
    held, owned, got, outs = [refs[i * streams : (i + 1) * streams] for i in range(4)]
    for s, base in enumerate(bases):
        count, height = held[s].shape[0], held[s].shape[1]
        outs[s][:count] = held[s][...]
        outs[s][count] = owned[s][0, base : base + height]
        outs[s][count + 1 :] = got[s][...]


def near_chunks_kernel(bases, *refs):
    streams = len(bases)
    new, held, owned, out = refs[0], refs[1 : streams + 1], refs[streams + 1 : -1], refs[-1]
    out[0] = new[0]
    for s, base in enumerate(bases):
        count, height = held[s].shape[0], held[s].shape[1]
        out[1 : count + 1, base : base + height] = held[s][...]
        out[count + 1, base : base + height] = owned[s][0, base : base + height]


def last_sums_kernel(heights, here, there, spans, *refs):
    streams, planes = len(heights), len(spans)
    groups, out_groups = [1 + max(g for g, unused in where) for where in (here, there)]
    rels, outs = refs[streams + groups : streams + groups + 2 * planes], refs[streams + groups + 2 * planes :]
    sums_kernel(heights, here, there, *refs[: streams + groups], *outs[: out_groups + streams])
    for place, out in enumerate(outs[out_groups + streams :]):
        for s, (low, high) in enumerate(spans):
            out[0, low:high] = rels[s][place] + rels[planes + s][place]


def squares_kernel(heights, here, entries, *refs):
    streams, groups = len(heights), 1 + max(g for g, unused in here)
    own, got, rels = refs[:streams], refs[streams : streams + groups], refs[streams + groups : -streams - 2]
    totals, rel_total, out = refs[-streams - 2 : -2], refs[-2], refs[-1]
    squares = jnp.zeros((1, out.shape[1]), F32)
    for s in range(streams):
        group, rows = rows_of(here, heights, s)
        total = own[s][0] + got[group][0, rows]
        totals[s][0] = total
        squares += jnp.sum(total * total, axis=0, keepdims=True)
    total = sum(ref[0] for ref in rels)
    rel_total[0] = total
    out[0:1] = squares
    out[1:2] = jnp.zeros_like(squares)
    square = total * total
    for row, lane, lanes, to, to_lane, count in entries:
        part = jnp.sum(square[to : to + count, to_lane : to_lane + lanes], axis=0, keepdims=True)
        out[1:2, lane : lane + lanes] += part


def update_kernel(spans, rel_spans, pieces, there, features, spot_ref, *refs):
    streams, groups = len(spans), 1 + max(g for g, unused in there)
    totals, (hub_sums, rel_sums), news = refs[:streams], refs[-2:], refs[-groups - 2 : -2]
    rel_total, mine, other, hub_ref, hub_all, rel_ref, rel_all = refs[streams : -groups - 2]
    chunks = hub_all.shape[1] // hub_ref.shape[1]
    take_owned(spot_ref, chunks, hub_all.shape[1], 0, lambda lanes: hub_all[:, lanes], hub_sums)
    take_owned(spot_ref, chunks, rel_all.shape[1], 0, lambda lanes: rel_all[:, lanes], rel_sums)
    width = rel_ref.shape[1]
    squares = mine[...] + other[...]
    hub_scale = step_rate / jnp.sqrt(hub_sums[...] + squares[0:1] * (1.0 / features))
    rel_scale = step_rate / jnp.sqrt(rel_sums[...] + squares[1:2, :width] * (1.0 / features))
    for s, (low, high) in enumerate(spans):
        new, base = there[s]
        first, end = rel_spans[s]
        middle = base + high - low
        news[new][0, base:middle] = hub_ref[low:high] - totals[s][0] * hub_scale
        news[new][0, middle : middle + end - first] = jnp.zeros((end - first, news[new].shape[2]), F32)
    for s, row, count, low, wide, to, to_lane in pieces:
        new, base = there[s]
        base += spans[s][1] - spans[s][0] + to
        lanes, first = slice(to_lane, to_lane + wide), rel_spans[s][0] + to
        news[new][0, base : base + count, lanes] = (
            rel_ref[row : row + count, low : low + wide]
            - rel_total[0, first : first + count, lanes] * rel_scale[:, low : low + wide]
        )


def chunk_copies(part, base, first, order, span, chip, component, out_ref, sems, at):
    low, high = span
    width = part.shape[2]
    for index in range(part.shape[0]):
        chunk = chip ^ gather_bits(first + index, order)
        lanes = pl.ds(pl.multiple_of(chunk * width, width), width)
        target = out_ref.at[component, pl.ds(low, high - low), lanes]
        yield pltpu.make_async_copy(part.at[index, pl.ds(base, high - low)], target, sems.at[at + index])


def component_of(spot_ref, mine):
    return spot_ref[1] if mine else 1 - spot_ref[1]


def near_kernel(orders, spans, bases, mine, spot_ref, near_ref, *refs):
    component = component_of(spot_ref, mine)
    out_ref, sems = refs[-2:]
    copies = []
    for order, span, base in zip(orders, spans, bases):
        copies += chunk_copies(near_ref, base, 0, order, span, spot_ref[0], component, out_ref, sems, len(copies))
    for copy in copies:
        copy.start()
    for copy in copies:
        copy.wait()


def far_kernel(orders, spans, bases, pieces, by_copy, mine, spot_ref, near_ref, *refs):
    component = component_of(spot_ref, mine)
    streams = len(orders)
    fars = refs[:streams]
    hub_out, rel_out, hub_all, rel_all, sems = refs[-5:]
    known = near_ref.shape[0]
    chunks = known + fars[0].shape[0]
    hub_width, rel_width = hub_out.shape[2] // chunks, rel_out.shape[2] // chunks
    copies = []
    if by_copy:
        for far, order, span in zip(fars, orders, spans):
            copies += chunk_copies(far, 0, known, order, span, spot_ref[0], component, hub_out, sems, len(copies))
        for copy in copies:
            copy.start()
    for chunk in range(chunks):
        place = spot_ref[0] ^ chunk
        for s, (low, high) in enumerate(spans):
            index = spread_bits(place, orders[s])
            near_at, far_at = jnp.minimum(index, known - 1), jnp.maximum(index - known, 0)
            height, base, end = high - low, bases[s], fars[s].shape[1]
            if not by_copy:
                value = jnp.where(index >= known, fars[s][far_at, :height], near_ref[near_at, base : base + height])
                hub_all[low:high, chunk * hub_width : (chunk + 1) * hub_width] = value
            value = jnp.where(index >= known, fars[s][far_at, height:], near_ref[near_at, base + height : base + end])
            for stream, row, count, low, wide, to, to_lane in pieces:
                if stream == s:
                    at = chunk * rel_width + low
                    rel_all[row : row + count, at : at + wide] = value[to : to + count, to_lane : to_lane + wide]
    copies.append(pltpu.make_async_copy(rel_all, rel_out.at[component], sems.at[len(copies)]))
    copies[-1].start()
    if not by_copy:
        copies.append(pltpu.make_async_copy(hub_all, hub_out.at[component], sems.at[len(copies)]))
        copies[-1].start()
    for copy in copies:
        copy.wait()


def placed(kernel, scratch, spot, near, fars, outs, earlier):
    sems = pltpu.SemaphoreType.DMA((3 * near.shape[0] + 2,))
    return pl.pallas_call(
        kernel,
        in_specs=[SMEM] + [VMEM] * (1 + len(fars)) + [HBM] * len(earlier),
        out_specs=[HBM] * len(outs),
        out_shape=[jax.ShapeDtypeStruct(shape, F32) for shape in outs],
        scratch_shapes=scratch + [sems],
        input_output_aliases={2 + len(fars) + i: i for i in range(len(earlier))},
        compiler_params=PARAMS,
        cost_estimate=pl.CostEstimate(flops=0, bytes_accessed=4 * outs[0][1] * outs[0][2], transcendentals=0),
    )(spot, near, *fars, *earlier)


def adagrad(table, state, grads):
    new_state = state + jnp.sum(grads * grads, axis=0, keepdims=True) * (1.0 / grads.shape[0])
    return table - grads * (step_rate / jnp.sqrt(new_state)), new_state


def keep_and_send(core, first, second):
    return jnp.where(core == 0, first, second), jnp.where(core == 0, second, first)


def table_counts(rows, negs, weight):
    place = lax.broadcasted_iota(jnp.int32, (rows, negs.shape[1]), 0)
    return jnp.sum(jnp.where(place == negs, weight, 0.0), axis=1, keepdims=True)


def turned(x, r, half):
    x0, x1, r0, r1 = x[:half], x[half:], r[:half], r[half:]
    return jnp.concatenate([x0 * r0 - x1 * r1, x0 * r1 + x1 * r0], axis=0)


def turned_back(x, r, half):
    x0, x1, r0, r1 = x[:half], x[half:], r[:half], r[half:]
    return x0 * r0 + x1 * r1, x1 * r0 - x0 * r1


EDGE_TILE = 512


def bucket_kernel(
    bucket, core_ref, heads_ref, tails_ref, negs_ref, left_ref, left_sums_ref, right_ref, right_sums_ref, rel_ref, hub_ref,
    left_out, left_sums_out, right_out, keep_out, send_out,
    left_parts, both_parts,
):
    features, rows = left_ref.shape
    half = features // 2
    core = core_ref[1]
    edges = heads_ref.shape[1]
    hubs = keep_out.shape[1] - edges
    at = slice(bucket, bucket + 1)
    weight = 1.0 / (negs_ref.shape[1] + hubs)
    counts = table_counts(rows, negs_ref[at], weight)
    stack_into(left_parts, left_ref[...])
    stack_into(both_parts, right_ref[...], slice(0, rows))
    stack_into(both_parts, hub_ref[...], slice(rows, rows + hubs))

    tail_here = lax.broadcasted_iota(jnp.int32, (rows, edges), 0) == tails_ref[at]
    head_hot = onehot(0, rows, heads_ref[at])
    h = dot2(left_parts[...], head_hot, NN)
    r = rel_ref[...]
    q = split(turned(h, r, half))
    scores = dot3((both_parts[:features], both_parts[features:]), q, TN)
    chance = jax.nn.sigmoid(scores[:rows])
    coef = jnp.concatenate(
        [
            counts * chance + jnp.where(tail_here, chance - 1.0, 0.0),
            weight * jax.nn.sigmoid(scores[rows:]),
        ],
        axis=0,
    )
    coef = split(coef)
    dq = dot3_stacked(both_parts[...], coef, NN)
    both_grad = dot3_stacked(stack(q), coef, NT)
    dh = jnp.concatenate(turned_back(dq, r, half), axis=0)
    left_grad = dot2(stack(split(dh)), head_hot, NT)
    keep_out[:, hubs:], send_out[:, hubs:] = keep_and_send(core, *turned_back(dq, h, half))

    left_out[...], left_sums_out[...] = adagrad(left_ref[...], left_sums_ref[...], left_grad)
    new_right, new_sums = adagrad(right_ref[...], right_sums_ref[...], both_grad[:, :rows])
    right_out[:features] = new_right
    right_out[features:] = jnp.broadcast_to(new_sums, (right_out.shape[0] - features, rows))
    keep_out[:, :hubs], send_out[:, :hubs] = keep_and_send(core, both_grad[:half, rows:], both_grad[half:, rows:])


def bucket_step(bucket, core, heads, tails, negs, left, left_sums, right, right_sums, rel_rows, hub_rows):
    features, rows = left.shape
    edges, hubs = heads.shape[1], hub_rows.shape[1]
    width = rows + hubs
    shapes = [(features, rows), (1, rows), (features + 8, rows)] + [(features // 2, hubs + edges)] * 2
    return pl.pallas_call(
        functools.partial(bucket_kernel, bucket),
        in_specs=[SMEM] + [VMEM] * 9,
        out_specs=[VMEM] * 5,
        out_shape=[jax.ShapeDtypeStruct(shape, F32) for shape in shapes],
        scratch_shapes=[
            pltpu.VMEM((2 * features, rows), BF16),
            pltpu.VMEM((2 * features, width), BF16),
        ],
        compiler_params=PARAMS,
        cost_estimate=COST,
    )(core, heads, tails, negs, left, left_sums, right, right_sums, rel_rows, hub_rows)


def hub_kernel(
    bucket, negatives, core_ref, heads_ref, left_ref, rel_ref, hub_ref,
    query_grad, hub_keep, hub_send,
    left_parts, hub_parts,
):
    features, rows = left_ref.shape
    half = features // 2
    edges, hubs = heads_ref.shape[1], hub_keep.shape[1]
    at = slice(bucket, bucket + 1)
    weight = 1.0 / (negatives + hubs)
    stack_into(left_parts, left_ref[...])
    stack_into(hub_parts, hub_ref[...])

    head_hot = onehot(0, rows, heads_ref[at])
    h = dot2(left_parts[...], head_hot, NN)
    q = split(turned(h, rel_ref[...], half))
    coef = split(weight * jax.nn.sigmoid(dot3((hub_parts[:features], hub_parts[features:]), q, TN)))
    query_grad[...] = dot3_stacked(hub_parts[...], coef, NN)
    hub_grad = dot3_stacked(stack(q), coef, NT)

    hub_keep[...], hub_send[...] = keep_and_send(core_ref[1], hub_grad[:half], hub_grad[half:])


def hub_step(bucket, negatives, core, heads, left, rel_rows, hub_rows):
    features, rows = left.shape
    edges, hubs = heads.shape[1], hub_rows.shape[1]
    shapes = [(features, edges)] + [(features // 2, hubs)] * 2
    return pl.pallas_call(
        functools.partial(hub_kernel, bucket, negatives),
        in_specs=[SMEM] + [VMEM] * 4,
        out_specs=[VMEM] * 3,
        out_shape=[jax.ShapeDtypeStruct(shape, F32) for shape in shapes],
        scratch_shapes=[
            pltpu.VMEM((2 * features, rows), BF16),
            pltpu.VMEM((2 * features, hubs), BF16),
        ],
        compiler_params=PARAMS,
        cost_estimate=COST,
    )(core, heads, left, rel_rows, hub_rows)


def tables_kernel(
    bucket, hubs, core_ref, heads_ref, tails_ref, negs_ref, query_grad,
    left_ref, left_sums_ref, right_ref, rel_ref,
    left_out, right_out, rel_keep, rel_send,
    left_parts, right_parts,
):
    features, rows = left_ref.shape
    half = features // 2
    edges = heads_ref.shape[1]
    at = slice(bucket, bucket + 1)
    core = core_ref[1]
    counts = table_counts(rows, negs_ref[at], 1.0 / (negs_ref.shape[1] + hubs))
    stack_into(left_parts, left_ref[...])
    stack_into(right_parts, right_ref[:features])

    tail_here = lax.broadcasted_iota(jnp.int32, (rows, edges), 0) == tails_ref[at]
    head_hot = onehot(0, rows, heads_ref[at])
    h = dot2(left_parts[...], head_hot, NN)
    r = rel_ref[...]
    q = split(turned(h, r, half))
    chance = jax.nn.sigmoid(dot3((right_parts[:features], right_parts[features:]), q, TN))
    coef = split(counts * chance + jnp.where(tail_here, chance - 1.0, 0.0))
    dq = dot3_stacked(right_parts[...], coef, NN) + query_grad[...]
    right_grad = dot3_stacked(stack(q), coef, NT)
    rel_keep[...], rel_send[...] = keep_and_send(core, *turned_back(dq, h, half))
    dh = jnp.concatenate(turned_back(dq, r, half), axis=0)
    left_grad = dot2(stack(split(dh)), head_hot, NT)

    left_out[...], unused = adagrad(left_ref[...], left_sums_ref[...], left_grad)
    right_out[...], unused = adagrad(right_ref[:features], right_ref[features : features + 1], right_grad)


def tables_step(bucket, hubs, core, heads, tails, negs, query_grad, left, left_sums, right, rel_rows):
    features, rows = left.shape
    edges = heads.shape[1]
    shapes = [(features, rows)] * 2 + [(features // 2, edges)] * 2
    return pl.pallas_call(
        functools.partial(tables_kernel, bucket, hubs),
        in_specs=[SMEM] + [VMEM] * 8,
        out_specs=[VMEM] * 4,
        out_shape=[jax.ShapeDtypeStruct(shape, F32) for shape in shapes],
        scratch_shapes=[pltpu.VMEM((2 * features, rows), BF16)] * 2,
        compiler_params=PARAMS,
        cost_estimate=COST,
    )(core, heads, tails, negs, query_grad, left, left_sums, right, rel_rows)


def from_behind(x, axis, by):
    size = lax.axis_size(axis)
    return lax.ppermute(x, axis, [(i, (i + by) % size) for i in range(size)])


def line_label(i):
    return i ^ (i >> 1)


def flipped_by(x, axis, offset):
    size = lax.axis_size(axis)
    labels = [line_label(i) if axis == "sub" else i for i in range(size)]
    return lax.ppermute(x, axis, [(i, labels.index(labels[i] ^ offset)) for i in range(size)])


def flipped(x, axis, bit):
    return flipped_by(x, axis, 1 << bit)


def other_core(x):
    return flipped(x, "blk", 0)


def across(x, place):
    sub_bits = lax.axis_size("sub").bit_length() - 1
    if place < sub_bits:
        return flipped(x, "sub", place)
    return flipped(x, "blk", place - sub_bits + 1)


def stream_orders(gathering):
    sub_bits = lax.axis_size("sub").bit_length() - 1
    bits = sub_bits + lax.axis_size("blk").bit_length() - 2
    x, y, z, far = sub_bits, sub_bits + 1, 0, 1
    rest = [p for p in range(bits) if p not in (x, y, z, far)]
    last = [y, far] if gathering else [far, y]
    return [[x, y, z, far] + rest, [y, z, x, far] + rest, [z, x, *last] + rest]


def plane_orders(sub_bits, bits):
    plane, depth = list(range(sub_bits, bits)), list(range(sub_bits - 1, -1, -1))
    return [plane + depth, plane[1:] + plane[:1] + depth]


def row_spans(rows, parts):
    ends = [-(-rows * (i + 1) // (8 * parts)) * 8 for i in range(parts - 1)] + [rows]
    return list(zip([0] + ends[:-1], ends))


def shards(
    left_emb, left_state, right_emb, right_state, relation_emb, relation_state, hub_emb, hub_state,
    heads, relations, tails, negatives, hub_ids,
):
    components, half_width, row_count = left_emb.shape
    features = components * half_width
    rel_count, hub_count = relation_emb.shape[2], hub_emb.shape[2]
    left = left_emb.reshape(features, row_count)
    right = right_emb.reshape(features, row_count)
    left_sums = left_state.reshape(1, row_count)
    right_sums = right_state.reshape(1, row_count)
    buckets, edges = heads.shape
    hubs = hub_ids.shape[1]

    orders, back_orders = stream_orders(False), stream_orders(True)
    streams, stages = len(orders), len(orders[0])
    chunks, depth = 1 << stages, lax.axis_size("sub")
    sub_bits = depth.bit_length() - 1
    planes = chunks // depth
    spans = row_spans(half_width, streams)
    rel_orders = plane_orders(sub_bits, stages)
    width, rel_width = hub_count // chunks, rel_count // chunks
    rel_height, entries = packed_map(half_width, rel_width, width)
    plane_spans = row_spans(rel_height, len(rel_orders))
    share = -(-(half_width + rel_height) // (8 * streams)) * 8
    ends = [share * (s + 1) - spans[s][1] for s in range(streams - 1)] + [rel_height]
    rel_spans = list(zip([0] + ends[:-1], ends))
    plane_pieces, joint_pieces = split_pieces(entries, plane_spans), split_pieces(entries, rel_spans)
    heights, rel_heights, plane_heights = [[high - low for low, high in x] for x in (spans, rel_spans, plane_spans)]
    joint_heights = [h + r for h, r in zip(heights, rel_heights)]
    bases = [sum(joint_heights[:s]) for s in range(streams)]
    hub_lanes, rel_lanes = (0, hubs), (hubs, hubs + edges)

    def exchanged(parts, step, orders=orders):
        return [across(x, place) for x, (place, unused) in zip(parts, grouped(orders, step, heights)[0])]

    def in_turn(first, then):
        return lax.optimization_barrier((first, then))

    blk = lax.axis_index("blk")
    spot = jnp.stack([(blk >> 1) * depth + line_label(lax.axis_index("sub")), blk & 1]).astype(jnp.int32)
    far_ids = other_core((hub_ids, relations))
    hub_rows, rel_rows, spot, owned = gather_rows(
        spot, hub_emb.reshape(features, hub_count), hub_ids, relation_emb.reshape(features, rel_count), relations, chunks
    )
    far_ids, hub_rows = in_turn(far_ids, hub_rows)
    keeps, sends = [], []
    for b in range(buckets - 1):
        if b > 0:
            right, right_sums = right[:features], right[features : features + 1]
        left, left_sums, right, keep, send = bucket_step(
            b, spot, heads, tails, negatives, left, left_sums, right, right_sums, rel_rows[b], hub_rows[b]
        )
        right = from_behind(right, "blk", 1)
        keeps.append(keep)
        sends.append(send)
    last = buckets - 1
    query_grad, hub_keep, hub_send = hub_step(
        last, negatives.shape[1], spot, heads, left, rel_rows[last], hub_rows[last]
    )
    sends, hub_send = in_turn(sends, hub_send)
    hub_far = other_core(hub_send)
    fars = [other_core(x) for x in sends]
    grads = lambda early, late, lanes: [(x, lanes) for x in early] + [(late, (0, late.shape[1]))]
    groups, where = grouped(orders, 0, heights)
    parts = chunk_columns(
        functools.partial(hub_chunks_kernel, orders, spans, where),
        [(chunks // 2, height, width) for height in [h for unused, h in groups] + heights],
        spot, (hub_ids, far_ids[0]), grads(keeps, hub_keep, hub_lanes) + grads(fars, hub_far, hub_lanes),
    )
    send, own = parts[: len(groups)], parts[len(groups) :]
    got = exchanged(send, 0)
    left, right, rel_keep, rel_send = tables_step(
        last, hubs, spot, heads, tails, negatives, query_grad, left, left_sums, right, rel_rows[last]
    )
    rel_far = other_core(rel_send)

    parts = chunk_columns(
        functools.partial(rel_chunks_kernel, rel_orders, plane_pieces, rel_count),
        [(chunks // 2, height, width) for height in plane_heights * 2],
        spot, (relations, far_ids[1]), grads(keeps, rel_keep, rel_lanes) + grads(fars, rel_far, rel_lanes),
    )
    rel_send, rel_own = parts[: len(rel_orders)], parts[len(rel_orders) :]
    rel_got = [across(x, order[0]) for x, order in zip(rel_send, rel_orders)]
    plane_steps = stages - sub_bits
    for step in range(stages - 2):
        if 0 < step < plane_steps:
            own, rel_got = in_turn(own, rel_got)
            rel_send, rel_own = halves(rel_own, rel_got, rel_orders, step - 1)
            rel_got = [across(x, order[step]) for x, order in zip(rel_send, rel_orders)]
        rel_own, got = in_turn(rel_own, got)
        send, own = halves(own, got, orders, step)
        got = exchanged(send, step + 1)

    here = grouped(orders, stages - 2, heights)[1]
    groups, there = grouped(orders, stages - 1, heights)
    parts = call(
        functools.partial(last_sums_kernel, heights, here, there, plane_spans),
        [*own, *got, *rel_own, *rel_got],
        [(1, height, width) for height in [h for unused, h in groups] + heights + [rel_height] * depth],
    )
    send, own, rel_parts = parts[: len(groups)], parts[len(groups) : len(groups) + streams], parts[len(groups) + streams :]
    got = exchanged(send, stages - 1)
    rel_got = [flipped_by(x, "sub", q + 1) for q, x in enumerate(rel_parts[1:])]
    *totals, rel_total, squares = call(
        functools.partial(squares_kernel, heights, there, entries),
        [*own, *got, rel_parts[0], *rel_got], [x.shape for x in own] + [rel_parts[0].shape, (2, width)],
    )
    hub_own, rel_own = owned
    there = [(0, base) for base in bases]
    ins = [
        *totals, rel_total, squares, other_core(squares),
        hub_own, hub_state[None], rel_own, relation_state[None],
    ]
    [new] = pl.pallas_call(
        functools.partial(update_kernel, spans, rel_spans, joint_pieces, there, features),
        in_specs=[SMEM] + [VMEM] * len(ins),
        out_specs=[VMEM],
        out_shape=[jax.ShapeDtypeStruct((1, sum(joint_heights), width), F32)],
        scratch_shapes=[pltpu.VMEM((1, x.shape[1]), F32) for x in owned],
        compiler_params=PARAMS,
        cost_estimate=COST,
    )(spot, *ins)
    partners = [across(new, place) for place in range(stages)]
    owned_at = lambda step: [partners[order[step]] for order in back_orders]
    shapes = lambda count: [(count, height, width) for height in joint_heights]
    have = call(functools.partial(split_kernel, bases), owned_at(stages - 1), shapes(1))
    for step in range(stages - 2, 0, -1):
        got = [across(x, order[step]) for x, order in zip(have, back_orders)]
        have = call(
            functools.partial(extend_kernel, bases), [*have, *owned_at(step), *got], shapes(2 * have[0].shape[0] + 1)
        )
    got = [across(x, order[0]) for x, order in zip(have, back_orders)]
    [near] = call(
        functools.partial(near_chunks_kernel, bases), [new, *have, *owned_at(0)],
        [(have[0].shape[0] + 2, sum(joint_heights), width)],
    )
    far_near = other_core(near)

    shapes = [hub_emb.shape, relation_emb.shape]
    by_copy = width % 128 == 0
    hub_new = []
    if by_copy:
        near_step = functools.partial(near_kernel, back_orders, spans, bases)
        hub_new = placed(functools.partial(near_step, True), [], spot, near, [], shapes[:1], [])
        hub_new = placed(functools.partial(near_step, False), [], spot, far_near, [], shapes[:1], hub_new)
        got, hub_new = in_turn(got, hub_new)
    far_step = functools.partial(far_kernel, back_orders, spans, bases, joint_pieces, by_copy)
    scratch = [
        pltpu.VMEM((8, 128) if by_copy else (half_width, hub_count), F32),
        pltpu.VMEM((half_width, rel_count), F32),
    ]
    far_got = other_core(got)
    out = placed(functools.partial(far_step, True), scratch, spot, near, got, shapes, hub_new)
    hub_new, rel_new = placed(functools.partial(far_step, False), scratch, spot, far_near, far_got, shapes, out)
    return (
        left.reshape(components, half_width, row_count),
        right.reshape(components, half_width, row_count),
        rel_new,
        hub_new,
    )


def solution(mesh):
    both = ("blk", "sub")
    block, table, whole = P(None, None, both), P(None, both), P()
    return jax.shard_map(
        shards,
        mesh=mesh,
        in_specs=(block, P(both), block, P(both), whole, whole, whole, whole, table, table, table, table, table),
        out_specs=(block, block, whole, whole),
        check_vma=False,
    )
```
